32 devices in a mesh: rows: 4 (over y, x), batch: 8 (over z, core).
Axes of the slice: x: 2, y: 2, z: 4, core: 2. Of those that a mesh axis runs over, the one named last changes fastest.
Arguments:
- images: float32 [64, 16, 16, 1024], P('batch', 'rows'), may hold values from -6 to 6
- w_reduce: float32 [1024, 256], replicated, may hold values from -0.1875 to 0.1875
- gain_one: float32 [256], replicated, may hold values from 0.25 to 1.75
- shift_one: float32 [256], replicated, may hold values from -3 to 3
- w_group: float32 [3, 3, 128, 512], replicated, may hold values from -0.1875 to 0.1875
- gain_two: float32 [512], replicated, may hold values from 0.25 to 1.75
- shift_two: float32 [512], replicated, may hold values from -3 to 3
- w_squeeze: float32 [256, 128], replicated, may hold values from -0.375 to 0.375
- gain_fc: float32 [128], replicated, may hold values from 0.25 to 1.75
- shift_fc: float32 [128], replicated, may hold values from -3 to 3
- w_excite: float32 [128, 512], replicated, may hold values from -0.75 to 0.75
- excite_bias: float32 [512], replicated, may hold values from -4 to 4
- w_expand: float32 [256, 1024], replicated, may hold values from -0.375 to 0.375
- gain_three: float32 [1024], replicated, may hold values from 0.25 to 1.75
- shift_three: float32 [1024], replicated, may hold values from -3 to 3
- valid_rows: int32 [64, 16], P('batch'), may hold values from 0 to 1, as said below
- valid_cols: int32 [64, 16], P('batch'), may hold values from 0 to 1, as said below
- cotangent: float32 [64, 16, 16, 1024], P('batch', 'rows'), may hold values from -6 to 6
Outputs:
- block_out: float32 [64, 16, 16, 1024], P('batch', 'rows')
- grad_images: float32 [64, 16, 16, 1024], P('batch', 'rows')
- grad_w_reduce: float32 [1024, 256], replicated
- grad_gain_one: float32 [256], replicated
- grad_shift_one: float32 [256], replicated
- grad_w_group: float32 [3, 3, 128, 512], replicated
- grad_gain_two: float32 [512], replicated
- grad_shift_two: float32 [512], replicated
- grad_w_squeeze: float32 [256, 128], replicated
- grad_gain_fc: float32 [128], replicated
- grad_shift_fc: float32 [128], replicated
- grad_w_excite: float32 [128, 512], replicated
- grad_excite_bias: float32 [512], replicated
- grad_w_expand: float32 [256, 1024], replicated
- grad_gain_three: float32 [1024], replicated
- grad_shift_three: float32 [1024], replicated
The draws below stay inside these ranges and needn't reach their ends.
Inputs may be any that keep to these rules, and one draw needn't show every extreme that they name: `valid_rows`: each image's valid rows form one run of 12, 14 or 16 consecutive rows, and its valid columns a run of the same length; at least one image is valid on the whole map. `valid_cols`: each image's valid columns form one run as long as its run of valid rows.
All inputs are finite; a program needn't handle non-finite values.
Results may differ from the reference program's by a relative error of at most 0.0003.
Values sent between devices are 32-bit elements; how exact they have to be, the bound alone decides.
No kernel may reach another device: no remote copies, remote signals or barrier semaphores. Data moves between devices by JAX's collectives and lax.ppermute only.
A program may use at most 128 MiB of HBM per device.

```python
from functools import partial
import jax
import jax.numpy as jnp
from jax import lax

CH = 1024
MID = 256
INTER = 128
HEIGHT = 16
WIDTH = 16
IMAGES = 64


def image_sides(key):
    side_pick = jax.random.randint(key, (IMAGES,), 0, 3)
    forced = jax.random.randint(jax.random.fold_in(key, 7), (), 0, IMAGES)
    side_pick = jnp.where(jnp.arange(IMAGES) == forced, 2, side_pick)
    return HEIGHT - 4 + 2 * side_pick


def valid_run(key, sides, length):
    offset = jax.random.randint(key, (IMAGES,), 0, 5) % (length - sides + 1)
    position = jnp.arange(length)[None, :]
    inside = (position >= offset[:, None]) & (position < (offset + sides)[:, None])
    return inside.astype(jnp.int32)


def draw_valid_rows(key, part):
    sides = image_sides(key)
    key = jax.random.fold_in(key, 11)
    return valid_run(key, sides, HEIGHT)


def draw_valid_cols(key, part):
    sides = image_sides(key)
    key = jax.random.fold_in(key, 23)
    return valid_run(key, sides, WIDTH)


def levels(stream_key, shape, pieces, smallest, top_value):
    loudness = 1.0
    for dim, shards_of in pieces:
        heights = jax.random.uniform(jax.random.fold_in(jax.random.fold_in(stream_key, 6), dim), (shards_of,), jnp.float32, smallest / len(pieces), top_value / len(pieces))
        loudness = loudness * jnp.repeat(jnp.exp(heights), shape[dim] // shards_of).reshape((-1,) + (1,) * (len(shape) - 1 - dim))
    return loudness


def normal_values(stream_key, extent, scale, most, split=(), kind=jnp.bfloat16):
    result = scale * jax.random.normal(stream_key, extent, jnp.float32)
    if split:
        result = result * levels(stream_key, extent, split, -0.22, 0.18)
    return jnp.clip(result, -most, most).astype(kind)


def setup_inputs(seed: int = 0) -> dict:
    arg_keys = jax.random.split(jax.random.key(seed), 19)
    return {
        "images": normal_values(arg_keys[0], (IMAGES, HEIGHT, WIDTH, CH), 1.0, 6.0, ((0, 8), (1, 4)), jnp.float32),
        "w_reduce": normal_values(arg_keys[1], (CH, MID), CH ** -0.5, 0.1875, (), jnp.float32),
        "gain_one": jnp.clip(1.0 + 0.15 * jax.random.normal(arg_keys[2], (MID,), jnp.float32), 0.25, 1.75),
        "shift_one": normal_values(arg_keys[3], (MID,), 0.5, 3.0, (), jnp.float32),
        "w_group": normal_values(arg_keys[4], (3, 3, MID // 2, 2 * MID), (9 * MID // 2) ** -0.5, 0.1875, (), jnp.float32),
        "gain_two": jnp.clip(1.0 + 0.15 * jax.random.normal(arg_keys[5], (2 * MID,), jnp.float32), 0.25, 1.75),
        "shift_two": normal_values(arg_keys[6], (2 * MID,), 0.5, 3.0, (), jnp.float32),
        "w_squeeze": normal_values(arg_keys[7], (MID, INTER), MID ** -0.5, 0.375, (), jnp.float32),
        "gain_fc": jnp.clip(1.0 + 0.15 * jax.random.normal(arg_keys[8], (INTER,), jnp.float32), 0.25, 1.75),
        "shift_fc": normal_values(arg_keys[9], (INTER,), 0.5, 3.0, (), jnp.float32),
        "w_excite": normal_values(arg_keys[10], (INTER, 2 * MID), (INTER // 2) ** -0.5, 0.75, (), jnp.float32),
        "excite_bias": normal_values(arg_keys[11], (2 * MID,), 0.7, 4.0, (), jnp.float32),
        "w_expand": normal_values(arg_keys[12], (MID, CH), MID ** -0.5, 0.375, (), jnp.float32),
        "gain_three": jnp.clip(1.0 + 0.15 * jax.random.normal(arg_keys[13], (CH,), jnp.float32), 0.25, 1.75),
        "shift_three": normal_values(arg_keys[14], (CH,), 0.5, 3.0, (), jnp.float32),
        "valid_rows": draw_valid_rows(jax.random.fold_in(arg_keys[18], 71), 0),
        "valid_cols": draw_valid_cols(jax.random.fold_in(arg_keys[18], 71), 0),
        "cotangent": normal_values(arg_keys[17], (IMAGES, HEIGHT, WIDTH, CH), 1.0, 6.0, ((0, 8), (1, 4)), jnp.float32),
    }


epsilon = 1e-05
highest = lax.Precision.HIGHEST

def smooth(values):
    return values * jax.nn.sigmoid(values)

def masked_norm(values, validity, total_count, gain, shift):
    mean_value = lax.optimization_barrier(jnp.sum(values * validity, axis=(0, 1, 2))) / total_count
    centered = values - mean_value
    variance = lax.optimization_barrier(jnp.sum(centered * centered * validity, axis=(0, 1, 2))) / total_count
    return centered * lax.rsqrt(variance + epsilon) * gain + shift

def forward(validity, pixels, images, w_reduce, gain_one, shift_one, w_group, gain_two, shift_two, w_squeeze, gain_fc, shift_fc, w_excite, excite_bias, w_expand, gain_three, shift_three):
    total_count = jnp.sum(validity)
    mid_width = w_reduce.shape[1]
    z_one = jnp.einsum('bhwc,cm->bhwm', images, w_reduce, precision=highest)
    a_one = smooth(masked_norm(z_one, validity, total_count, gain_one, shift_one)) * validity
    z_two = lax.conv_general_dilated(a_one, w_group, (1, 1), 'SAME', dimension_numbers=('NHWC', 'HWIO', 'NHWC'), feature_group_count=2, precision=highest)
    a_two = smooth(masked_norm(z_two, validity, total_count, gain_two, shift_two)) * validity
    half_first = a_two[..., :mid_width]
    half_second = a_two[..., mid_width:]
    pooled = lax.optimization_barrier(jnp.sum(half_first + half_second, axis=(1, 2))) / pixels
    f_one = jnp.dot(pooled, w_squeeze, precision=highest)
    fc_mean = lax.optimization_barrier(jnp.mean(f_one, axis=0))
    fc_var = lax.optimization_barrier(jnp.mean((f_one - fc_mean) ** 2, axis=0))
    fc_act = smooth((f_one - fc_mean) * lax.rsqrt(fc_var + epsilon) * gain_fc + shift_fc)
    logits = jnp.dot(fc_act, w_excite, precision=highest) + excite_bias
    weights = jax.nn.softmax(jnp.stack([logits[:, :mid_width], logits[:, mid_width:]]), axis=0)
    mixed = weights[0][:, None, None, :] * half_first + weights[1][:, None, None, :] * half_second
    z_three = jnp.einsum('bhwm,mc->bhwc', mixed, w_expand, precision=highest)
    pre_act = masked_norm(z_three, validity, total_count, gain_three, shift_three) + images
    return smooth(pre_act) * validity

def reference(images, w_reduce, gain_one, shift_one, w_group, gain_two, shift_two, w_squeeze, gain_fc, shift_fc, w_excite, excite_bias, w_expand, gain_three, shift_three, valid_rows, valid_cols, cotangent):
    row_valid = valid_rows.astype(jnp.float32)
    col_valid = valid_cols.astype(jnp.float32)
    validity = row_valid[:, :, None, None] * col_valid[:, None, :, None]
    pixels = (lax.optimization_barrier(jnp.sum(row_valid, axis=1)) * lax.optimization_barrier(jnp.sum(col_valid, axis=1)))[:, None]
    block_out, pullback = jax.vjp(partial(forward, validity, pixels), images, w_reduce, gain_one, shift_one, w_group, gain_two, shift_two, w_squeeze, gain_fc, shift_fc, w_excite, excite_bias, w_expand, gain_three, shift_three)
    grads = pullback(cotangent)
    return (block_out, grads[0], grads[1], grads[2], grads[3], grads[4], grads[5], grads[6], grads[7], grads[8], grads[9], grads[10], grads[11], grads[12], grads[13], grads[14])
```

```python
import functools

import jax
import jax.numpy as jnp
from jax import lax
from jax.experimental import pallas as pl
from jax.experimental.pallas import tpu as pltpu
from jax.sharding import PartitionSpec as P

epsilon = 1e-05
f32 = jnp.float32
bf16 = jnp.bfloat16
highest = lax.Precision.HIGHEST
both = ("rows", "batch")
NN = ((1,), (0,))
NT = ((1,), (1,))
TN = ((0,), (0,))


def split(values):
    high = values.astype(bf16)
    return high, (values - high.astype(f32)).astype(bf16)


def dot(left, right, dims):
    return lax.dot_general(left, right, (dims, ((), ())), preferred_element_type=f32)


def product(left, right, dims):
    return dot(left[0], right[0], dims) + (
        dot(left[0], right[1], dims) + dot(left[1], right[0], dims)
    )


def exact(left, right, dims):
    return lax.dot_general(
        left, right, (dims, ((), ())), preferred_element_type=f32, precision=highest
    )


def put(tile, row, vector):
    for j in range(vector.shape[1] // 128):
        tile[row + j : row + j + 1, :] = vector[:, j * 128 : (j + 1) * 128]


def get(tile, row, count):
    return jnp.concatenate([tile[row + j : row + j + 1, :] for j in range(count)], axis=1)


def wide(mask, width):
    return jnp.concatenate([mask] * (width // 128), axis=1)


def column_sum(values):
    return jnp.sum(values, axis=0, keepdims=True)


def image_sum(values, images):
    return jnp.sum(values.reshape(images, values.shape[0] // images, values.shape[1]), axis=1)


def per_image(vector, values):
    count, width = vector.shape
    each = values.shape[0] // count
    return jnp.broadcast_to(vector[:, None, :], (count, each, width)).reshape(values.shape[0], width)


def merge_stats(gathered, counts, width):
    groups = width // 128
    own = jnp.maximum(counts, 1.0)
    total = jnp.sum(counts, axis=0)
    means, inverses = [], []
    for j in range(groups):
        sums = gathered[:, j, :]
        squares = gathered[:, groups + j, :]
        mean = jnp.sum(sums, axis=0, keepdims=True) / total
        shift = sums / own - mean
        spread = jnp.sum(squares + counts * shift * shift, axis=0, keepdims=True) / total
        means.append(mean)
        inverses.append(lax.rsqrt(spread + epsilon))
    return jnp.concatenate(means, axis=1), jnp.concatenate(inverses, axis=1), total


def local_stats(values, mask, count):
    sums = column_sum(values * mask)
    centered = values - sums / jnp.maximum(count, 1.0)
    return sums, column_sum(centered * centered * mask)


def own_rows(extended, images):
    rows, width = extended.shape
    tall = rows // images // 16
    return extended.reshape(images, tall, 16, width)[:, 1 : tall - 1].reshape(-1, width)


def call(body, outs, ins, scratch=(), limit=40, **extra):
    specs = [jax.ShapeDtypeStruct(shape, kind) for shape, kind in outs]
    return pl.pallas_call(
        body,
        out_shape=specs,
        scratch_shapes=list(scratch),
        compiler_params=pltpu.CompilerParams(vmem_limit_bytes=limit * 2**20),
        **extra,
    )(*ins)


def share(tile):
    return lax.all_to_all(tile, both, 0, 0)


def halos(first, last):
    count = lax.axis_size("rows")
    above = lax.ppermute(last, "rows", [(i, i + 1) for i in range(count - 1)])
    below = lax.ppermute(first, "rows", [(i + 1, i) for i in range(count - 1)])
    return above, below


def reduce_kernel(rows_ref, cols_ref, x_ref, w_ref, z_ref, ext_ref, own_ref, first_ref, last_ref, pay_ref, tile):
    images = rows_ref.shape[0]
    tall = x_ref.shape[0] // images // 16
    shape = (images, tall + 2, 16, 16)
    start = lax.axis_index("rows") * tall - 1
    lane = lax.broadcasted_iota(jnp.int32, shape, 3).reshape(-1, 16)
    at_row = lax.broadcasted_iota(jnp.int32, shape, 1).reshape(-1, 16) + start
    at_col = lax.broadcasted_iota(jnp.int32, shape, 2).reshape(-1, 16)
    row_valid = per_image(rows_ref[...].astype(f32), lane)
    col_valid = per_image(cols_ref[...].astype(f32), lane)
    in_row = jnp.sum(jnp.where(lane == at_row, row_valid, 0.0), axis=1, keepdims=True)
    in_col = jnp.sum(jnp.where(lane == at_col, col_valid, 0.0), axis=1, keepdims=True)
    mask = jnp.broadcast_to(in_row * in_col, ext_ref.shape)
    ext_ref[...] = mask
    own = own_rows(mask, images)
    own_ref[...] = own
    z = product(split(x_ref[...]), split(w_ref[...]), NN)
    z_ref[...] = z
    edges = z.reshape(images, tall, 16, -1)
    first_ref[...] = edges[:, 0].reshape(first_ref.shape)
    last_ref[...] = edges[:, tall - 1].reshape(last_ref.shape)
    count = column_sum(own)
    both_counts = wide(count, z.shape[1])
    sums, squares = local_stats(z, wide(own, z.shape[1]), both_counts)
    tile[...] = jnp.zeros_like(tile)
    put(tile, 0, sums)
    put(tile, 2, squares)
    put(tile, 4, count)
    pay_ref[...] = jnp.broadcast_to(tile[...][None], pay_ref.shape)


def parts_kernel(*refs):
    half = len(refs) // 3
    for i in range(half):
        high, low = split(refs[i][...])
        refs[half + 2 * i][...] = high
        refs[half + 2 * i + 1][...] = low


def turned_kernel(x_ref, high_ref, low_ref):
    high_ref[...], low_ref[...] = split(x_ref[...].T)


def moved(values, step):
    count = values.shape[0]
    at = lax.broadcasted_iota(jnp.int32, values.shape, 0) & 15
    if step == 0:
        return values
    if step > 0:
        return jnp.where(at < 15, pltpu.roll(values, count - 1, 0), 0.0)
    return jnp.where(at > 0, pltpu.roll(values, 1, 0), 0.0)


def window(extended, images, row, width):
    tall = extended.shape[0] // images // 16
    cells = extended.reshape(images, tall, 16, extended.shape[1])
    return cells[:, row : row + tall - 2, :, width].reshape(images * (tall - 2) * 16, -1)


def conv_kernel(z_ref, above_ref, below_ref, ext_ref, own_ref, g1_ref, gain_ref, shift_ref, wh_ref, wl_ref,
                a_ref, z2_ref, first_ref, last_ref, stat_ref, pay_ref, tile, zext):
    images = zext.shape[0]
    tall = zext.shape[1] - 2
    width = z_ref.shape[1]
    group = width // 2
    gathered = g1_ref[...]
    mean, inv, total = merge_stats(gathered, gathered[:, 4, :], width)
    tile[...] = jnp.zeros_like(tile)
    put(tile, 0, mean)
    put(tile, 2, inv)
    put(tile, 4, total[None] if total.ndim == 1 else total)
    stat_ref[...] = tile[...]
    zext[:, 1 : tall + 1] = z_ref[...].reshape(images, tall, 16, width)
    zext[:, 0] = above_ref[...].reshape(images, 16, width)
    zext[:, tall + 1] = below_ref[...].reshape(images, 16, width)
    y = (zext[...].reshape(-1, width) - mean) * inv * gain_ref[...] + shift_ref[...]
    a = y * jax.nn.sigmoid(y) * wide(ext_ref[...], width)
    a_ref[...] = a
    shifted = [split(moved(a, step)) for step in (-1, 0, 1)]
    half = z2_ref.shape[1] // 2
    for g in range(2):
        cols = slice(g * group, (g + 1) * group)
        left = [
            jnp.concatenate(
                [window(shifted[tap % 3][part], images, tap // 3, cols) for tap in range(9)], axis=1
            )
            for part in range(2)
        ]
        outs = slice(g * half, (g + 1) * half)
        z2_ref[:, outs] = product(left, (wh_ref[:, outs], wl_ref[:, outs]), NN)
    z2 = z2_ref[...]
    edges = z2.reshape(images, tall, 16, -1)
    first_ref[...] = edges[:, 0].reshape(first_ref.shape)
    last_ref[...] = edges[:, tall - 1].reshape(last_ref.shape)
    own = wide(own_ref[...], z2.shape[1])
    sums, squares = local_stats(z2, own, wide(column_sum(own_ref[...]), z2.shape[1]))
    put(tile, 0, sums)
    put(tile, 4, squares)
    pay_ref[...] = jnp.broadcast_to(tile[...][None], pay_ref.shape)


def taps_kernel(images, a_ref, high_ref, low_ref):
    group = a_ref.shape[1] // 2
    a = a_ref[...]
    shifted = [moved(a, step) for step in (-1, 0, 1)]
    for g in range(2):
        cols = slice(g * group, (g + 1) * group)
        for tap in range(9):
            high, low = split(window(shifted[tap % 3], images, tap // 3, cols).T)
            high_ref[g, tap * group : (tap + 1) * group, :] = high
            low_ref[g, tap * group : (tap + 1) * group, :] = low


def pixel_count(rows_ref, cols_ref):
    rows = jnp.sum(rows_ref[...].astype(f32), axis=1, keepdims=True)
    return rows * jnp.sum(cols_ref[...].astype(f32), axis=1, keepdims=True)


def pool_kernel(z_ref, own_ref, g1_ref, g2_ref, gain_ref, shift_ref, rows_ref, cols_ref, w_ref,
                a_ref, stat_ref, pooled_ref, pay_ref):
    images = rows_ref.shape[0]
    width = z_ref.shape[1]
    mid = width // 2
    mean, inv, total = merge_stats(g2_ref[...], g1_ref[:, 4, :], width)
    put(stat_ref, 0, mean)
    put(stat_ref, 4, inv)
    y = (z_ref[...] - mean) * inv * gain_ref[...] + shift_ref[...]
    a = y * jax.nn.sigmoid(y) * wide(own_ref[...], width)
    a_ref[...] = a
    sums = image_sum(a, images)
    pooled = (sums[:, :mid] + sums[:, mid:]) / pixel_count(rows_ref, cols_ref)
    pooled_ref[...] = pooled
    pay_ref[...] = jnp.broadcast_to(exact(pooled, w_ref[...], NN)[None], pay_ref.shape)


def slope_kernel(z_ref, above_ref, below_ref, ext_ref, stat_ref, gain_ref, shift_ref, rows_ref, cols_ref,
                 slope_ref, normed_ref, sums_ref, zext):
    images = zext.shape[0]
    tall = zext.shape[1] - 2
    width = z_ref.shape[1]
    zext[:, 1 : tall + 1] = z_ref[...].reshape(images, tall, 16, width)
    zext[:, 0] = above_ref[...].reshape(images, 16, width)
    zext[:, tall + 1] = below_ref[...].reshape(images, 16, width)
    mean, inv = get(stat_ref, 0, 4), get(stat_ref, 4, 4)
    normed = (zext[...].reshape(-1, width) - mean) * inv
    y = normed * gain_ref[...] + shift_ref[...]
    sigma = jax.nn.sigmoid(y)
    slope = sigma * (1.0 + y * (1.0 - sigma)) * wide(ext_ref[...], width)
    slope_ref[...] = slope
    normed_ref[...] = normed
    pixels = pixel_count(rows_ref, cols_ref)
    inner = own_rows(slope, images)
    sums_ref[:, :width] = image_sum(inner, images) / pixels
    sums_ref[:, width:] = image_sum(inner * own_rows(normed, images), images) / pixels


def expand_kernel(g3_ref, a_ref, own_ref, gain_ref, shift_ref, w_ref, bias_ref, wh_ref, wl_ref,
                  mixed_ref, z_ref, weights_ref, normed_ref, pre_ref, act_ref, inv_ref, pay_ref, tile, acts):
    own_images = weights_ref.shape[0]
    mid = mixed_ref.shape[1]
    devices = g3_ref.shape[0]
    rows = lax.axis_size("rows")
    f_one = jnp.sum(g3_ref[...].reshape(rows, devices // rows * own_images, -1), axis=0)
    mean = jnp.mean(f_one, axis=0, keepdims=True)
    centered = f_one - mean
    inv = lax.rsqrt(jnp.mean(centered * centered, axis=0, keepdims=True) + epsilon)
    normed = centered * inv
    pre = normed * gain_ref[...] + shift_ref[...]
    normed_ref[...] = normed
    pre_ref[...] = pre
    inv_ref[...] = inv
    acts[...] = pre * jax.nn.sigmoid(pre)
    at = pl.multiple_of(lax.axis_index("batch") * own_images, own_images)
    act = acts[pl.ds(at, own_images), :]
    act_ref[...] = act
    logits = exact(act, w_ref[...], NN) + bias_ref[...]
    lead = logits[:, :mid] - logits[:, mid:]
    first, second = jax.nn.sigmoid(lead), jax.nn.sigmoid(-lead)
    weights_ref[:, :mid] = first
    weights_ref[:, mid:] = second
    a = a_ref[...]
    mixed = per_image(first, a) * a[:, :mid] + per_image(second, a) * a[:, mid:]
    mixed_ref[...] = mixed
    z_ref[...] = product(split(mixed), (wh_ref[...], wl_ref[...]), NN)
    z = z_ref[...]
    width = z.shape[1]
    own = wide(own_ref[...], width)
    sums, squares = local_stats(z, own, wide(column_sum(own_ref[...]), width))
    put(tile, 0, sums)
    put(tile, width // 128, squares)
    pay_ref[...] = jnp.broadcast_to(tile[...][None], pay_ref.shape)


def output_kernel(g1_ref, g4_ref, gain_ref, shift_ref, z_ref, x_ref, cot_ref, own_ref,
                  out_ref, grad_ref, stat_ref, pay_ref, tile, sums):
    width = z_ref.shape[1]
    step = pl.program_id(0)

    @pl.when(step == 0)
    def _():
        mean, inv, total = merge_stats(g4_ref[...], g1_ref[:, 4, :], width)
        put(stat_ref, 0, mean)
        put(stat_ref, width // 128, inv)
        sums[...] = jnp.zeros_like(sums)

    mean, inv = get(stat_ref, 0, width // 128), get(stat_ref, width // 128, width // 128)
    own = wide(own_ref[...], width)
    normed = (z_ref[...] - mean) * inv
    pre = normed * gain_ref[...] + shift_ref[...] + x_ref[...]
    sigma = jax.nn.sigmoid(pre)
    out_ref[...] = pre * sigma * own
    grad = cot_ref[...] * own * (sigma * (1.0 + pre * (1.0 - sigma)))
    grad_ref[...] = grad
    sums[0:1, :] += column_sum(grad)
    sums[1:2, :] += column_sum(grad * normed)

    @pl.when(step == pl.num_programs(0) - 1)
    def _():
        put(tile, 0, sums[0:1, :])
        put(tile, width // 128, sums[1:2, :])
        pay_ref[...] = jnp.broadcast_to(tile[...][None], pay_ref.shape)


def mixed_kernel(g5_ref, stat1_ref, stat3_ref, gain_ref, z_ref, grad_ref, own_ref, wh_ref, wl_ref, a_ref, slope_ref,
                 normed_ref, weights_ref, w_ref, dzh_ref, dzl_ref, gm_ref, first_ref, last_ref, dsum_ref, grads_ref,
                 pay_ref, tile):
    width = z_ref.shape[1]
    mid = gm_ref.shape[1]
    images = weights_ref.shape[0]
    tall = z_ref.shape[0] // images // 16
    groups = width // 128
    grads_ref[...] = jnp.sum(g5_ref[...], axis=0)
    count = wide(stat1_ref[4:5, :], width)
    mean, inv = get(stat3_ref, 0, groups), get(stat3_ref, groups, groups)
    normed = (z_ref[...] - mean) * inv
    flat = get(grads_ref, 0, groups) / count
    cross = get(grads_ref, groups, groups) / count
    dz = gain_ref[...] * inv * (grad_ref[...] - flat - normed * cross) * wide(own_ref[...], width)
    dz_high, dz_low = split(dz)
    dzh_ref[...] = dz_high
    dzl_ref[...] = dz_low
    gm = product((dz_high, dz_low), (wh_ref[...], wl_ref[...]), NT)
    gm_ref[...] = gm
    edges = gm.reshape(images, tall, 16, mid)
    first_ref[...] = edges[:, 0].reshape(first_ref.shape)
    last_ref[...] = edges[:, tall - 1].reshape(last_ref.shape)
    a = a_ref[...]
    weights = weights_ref[...]
    gate = image_sum(gm * (a[:, :mid] - a[:, mid:]), images)
    dsum = weights[:, :mid] * weights[:, mid:] * gate
    dsum_ref[...] = dsum
    tile[...] = jnp.zeros_like(tile)
    tile[:images, :] = exact(dsum, w_ref[:, :mid] - w_ref[:, mid:], NT)
    slope = own_rows(slope_ref[...], images) * jnp.concatenate([gm, gm], axis=1)
    put(tile, 8, column_sum(weights * image_sum(slope, images)))
    put(tile, 12, column_sum(weights * image_sum(slope * own_rows(normed_ref[...], images), images)))
    pay_ref[...] = jnp.broadcast_to(tile[...][None], pay_ref.shape)


def expand_grad_kernel(mixed_ref, dzh_ref, dzl_ref, act_ref, dsum_ref, out_ref, excite_ref, bias_ref):
    out_ref[...] = product(split(mixed_ref[...].T), (dzh_ref[...], dzl_ref[...]), NN)
    dsum = dsum_ref[...]
    excite_ref[...] = exact(act_ref[...], dsum, TN)
    bias_ref[...] = column_sum(dsum)


def group_kernel(g6_ref, gs_ref, pre_ref, fcn_ref, inv_ref, gfc_ref, wsq_ref, pooled_ref, gm_ref, above_ref, below_ref,
                 slope_ref, normed_ref, ext_ref, weights_ref, stat1_ref, stat2_ref, gain_ref, rows_ref, cols_ref,
                 th_ref, tl_ref,
                 dzh_ref, dzl_ref, out_ref, gains_ref, fc_ref, squeeze_ref, dext, gf, owned):
    step = pl.program_id(0)
    images = rows_ref.shape[0]
    width = normed_ref.shape[1]
    mid = width // 2

    @pl.when(step == 0)
    def _():
        rows = lax.axis_size("rows")
        devices = g6_ref.shape[0]
        shared = g6_ref[...]
        pre = pre_ref[...]
        fcn = fcn_ref[...]
        sigma = jax.nn.sigmoid(pre)
        total = pre.shape[0]
        grad = jnp.sum(shared[:, :images].reshape(rows, total, -1), axis=0) * (sigma * (1.0 + pre * (1.0 - sigma)))
        flat, cross = column_sum(grad), column_sum(grad * fcn)
        fc_ref[0:1, :] = cross
        fc_ref[1:2, :] = flat
        gf[...] = gfc_ref[...] * inv_ref[...] * (grad - flat / total - fcn * cross / total)
        at = pl.multiple_of(lax.axis_index("batch") * images, images)
        mine = gf[pl.ds(at, images), :]
        squeeze_ref[...] = exact(pooled_ref[...], mine, TN)
        spread = exact(gf[...], wsq_ref[...], NT)
        owned[...] = spread
        own_spread = owned[pl.ds(at, images), :] / pixel_count(rows_ref, cols_ref)
        slopes = jnp.sum(gs_ref[...].reshape(rows, total, -1), axis=0)
        spread = jnp.concatenate([spread, spread], axis=1)
        base = jnp.sum(shared[:, 8:], axis=0)
        flat_two = get(base, 0, width // 128) + column_sum(spread * slopes[:, :width])
        cross_two = get(base, width // 128, width // 128) + column_sum(spread * slopes[:, width:])
        put(gains_ref, 0, cross_two)
        put(gains_ref, width // 128, flat_two)
        count = wide(stat1_ref[4:5, :], width)
        inv = get(stat2_ref, width // 128, width // 128)
        tall = dext.shape[1] - 2
        dext[:, 1 : tall + 1] = gm_ref[...].reshape(images, tall, 16, mid)
        dext[:, 0] = above_ref[...].reshape(images, 16, mid)
        dext[:, tall + 1] = below_ref[...].reshape(images, 16, mid)
        gm = dext[...].reshape(-1, mid)
        weights = weights_ref[...]
        shared_part = per_image(own_spread, gm)
        upstream = jnp.concatenate(
            [
                per_image(weights[:, :mid], gm) * gm + shared_part,
                per_image(weights[:, mid:], gm) * gm + shared_part,
            ],
            axis=1,
        )
        dz = (
            gain_ref[...]
            * inv
            * (upstream * slope_ref[...] - flat_two / count - normed_ref[...] * (cross_two / count))
            * wide(ext_ref[...], width)
        )
        high, low = split(dz)
        dzh_ref[...] = high
        dzl_ref[...] = low

    for g in range(2):
        outs = slice(g * mid, (g + 1) * mid)
        right = [window(ref[...], images, 1, outs) for ref in (dzh_ref, dzl_ref)]
        out_ref[:, outs] = product((th_ref[g], tl_ref[g]), right, NN)


def input_grad_kernel(dzh_ref, dzl_ref, wh_ref, wl_ref, z_ref, stat_ref, own_ref, gain_ref, shift_ref,
                      dy_ref, pay_ref, tile):
    images = dzh_ref.shape[0] // 16 // (z_ref.shape[0] // 16 // 8 + 2)
    width = z_ref.shape[1]
    group = width // 2
    half = dzh_ref.shape[1] // 2
    taps = 3 * group
    grads = []
    for g in range(2):
        outs = slice(g * half, (g + 1) * half)
        total = None
        for row in range(3):
            left = [window(ref[...], images, 2 - row, outs) for ref in (dzh_ref, dzl_ref)]
            right = [ref[row * taps : (row + 1) * taps, outs] for ref in (wh_ref, wl_ref)]
            term = product(left, right, NT)
            total = term if total is None else total + term
        grads.append(
            moved(total[:, :group], 1)
            + total[:, group : 2 * group]
            + moved(total[:, 2 * group :], -1)
        )
    grad = jnp.concatenate(grads, axis=1)
    mean, inv = get(stat_ref, 0, 2), get(stat_ref, 2, 2)
    normed = (z_ref[...] - mean) * inv
    y = normed * gain_ref[...] + shift_ref[...]
    sigma = jax.nn.sigmoid(y)
    dy = grad * wide(own_ref[...], width) * (sigma * (1.0 + y * (1.0 - sigma)))
    dy_ref[...] = dy
    tile[...] = jnp.zeros_like(tile)
    put(tile, 0, column_sum(dy * normed))
    put(tile, 2, column_sum(dy))
    pay_ref[...] = jnp.broadcast_to(tile[...][None], pay_ref.shape)


def final_kernel(g7_ref, dy_ref, z_ref, stat_ref, gain_ref, own_ref, wh_ref, wl_ref, th_ref, tl_ref, grad_ref,
                 out_ref, reduce_ref, gains_ref):
    width = z_ref.shape[1]
    gains_ref[...] = jnp.sum(g7_ref[...], axis=0)
    cross, flat = get(gains_ref, 0, 2), get(gains_ref, 2, 2)
    count = wide(stat_ref[4:5, :], width)
    mean, inv = get(stat_ref, 0, 2), get(stat_ref, 2, 2)
    normed = (z_ref[...] - mean) * inv
    dz = gain_ref[...] * inv * (dy_ref[...] - flat / count - normed * (cross / count)) * wide(own_ref[...], width)
    parts = split(dz)
    reduce_ref[...] = product((th_ref[...], tl_ref[...]), parts, NN)
    out_ref[...] = product(parts, (wh_ref[...], wl_ref[...]), NT) + grad_ref[...]


def on_device(
    images,
    w_reduce,
    gain_one,
    shift_one,
    w_group,
    gain_two,
    shift_two,
    w_squeeze,
    gain_fc,
    shift_fc,
    w_excite,
    excite_bias,
    w_expand,
    gain_three,
    shift_three,
    valid_rows,
    valid_cols,
    cotangent,
):
    count, tall, broad, chan = images.shape
    mid = w_reduce.shape[1]
    inter = w_squeeze.shape[1]
    duo = 2 * mid
    cells = count * tall * broad
    longer = count * (tall + 2) * broad
    edge = count * broad
    devices = lax.axis_size("rows") * lax.axis_size("batch")
    all_images = count * lax.axis_size("batch")
    x = images.reshape(cells, chan)
    cot = cotangent.reshape(cells, chan)
    row = lambda v: v.reshape(1, -1)
    pay8 = ((devices, 8, 128), f32)
    pay16 = ((devices, 16, 128), f32)
    tile8 = pltpu.VMEM((8, 128), f32)
    tile16 = pltpu.VMEM((16, 128), f32)
    flat_w = w_group.reshape(9 * mid // 2, duo)

    z_one, ext, own, first, last, pay = call(
        reduce_kernel,
        [((cells, mid), f32), ((longer, 128), f32), ((cells, 128), f32), ((edge, mid), f32), ((edge, mid), f32), pay8],
        [valid_rows, valid_cols, x, w_reduce],
        [tile8],
    )
    g1 = share(pay)
    above, below = halos(first, last)
    wgh, wgl, weh, wel, wrh, wrl = call(
        parts_kernel,
        [(w.shape, bf16) for w in (flat_w, w_expand, w_reduce) for _ in range(2)],
        [flat_w, w_expand, w_reduce],
    )
    xth, xtl = call(turned_kernel, [((chan, cells), bf16)] * 2, [x])
    a_one, z_two, first, last, stat1, pay = call(
        conv_kernel,
        [((longer, mid), f32), ((cells, duo), f32), ((edge, duo), f32), ((edge, duo), f32), ((8, 128), f32), pay8],
        [z_one, above, below, ext, own, g1, row(gain_one), row(shift_one), wgh, wgl],
        [tile8, pltpu.VMEM((count, tall + 2, broad, mid), f32)],
    )
    g2 = share(pay)
    above, below = halos(first, last)
    tph, tpl = call(functools.partial(taps_kernel, count), [((2, 9 * mid // 2, cells), bf16)] * 2, [a_one])
    a_two, stat2, pooled, pay = call(
        pool_kernel,
        [((cells, duo), f32), ((8, 128), f32), ((count, mid), f32), ((devices, count, inter), f32)],
        [z_two, own, g1, g2, row(gain_two), row(shift_two), valid_rows, valid_cols, w_squeeze],
    )
    g3 = share(pay)
    slope_two, normed_two, slopes = call(
        slope_kernel,
        [((longer, duo), f32), ((longer, duo), f32), ((count, 2 * duo), f32)],
        [z_two, above, below, ext, stat2, row(gain_two), row(shift_two), valid_rows, valid_cols],
        [pltpu.VMEM((count, tall + 2, broad, duo), f32)],
    )
    gs = lax.all_gather(slopes, both)
    mixed, z_three, weights, fc_normed, fc_pre, fc_act, fc_inv, pay = call(
        expand_kernel,
        [((cells, mid), f32), ((cells, chan), f32), ((count, duo), f32), ((all_images, inter), f32),
         ((all_images, inter), f32), ((count, inter), f32), ((1, inter), f32), pay16],
        [g3, a_two, own, row(gain_fc), row(shift_fc), w_excite, row(excite_bias), weh, wel],
        [tile16, pltpu.VMEM((all_images, inter), f32)],
    )
    g4 = share(pay)
    steps = 4
    block = pl.BlockSpec((cells // steps, chan), lambda i: (i, 0))
    whole = lambda *shape: pl.BlockSpec(shape, lambda i: (0,) * len(shape))
    block_out, grad_pre, stat3, pay = call(
        output_kernel,
        [((cells, chan), f32), ((cells, chan), f32), ((16, 128), f32), pay16],
        [g1, g4, row(gain_three), row(shift_three), z_three, x, cot, own],
        [tile16, pltpu.VMEM((8, chan), f32)],
        grid=(steps,),
        in_specs=[whole(devices, 8, 128), whole(devices, 16, 128), whole(1, chan), whole(1, chan), block, block, block,
                  pl.BlockSpec((cells // steps, 128), lambda i: (i, 0))],
        out_specs=[block, block, whole(16, 128), whole(devices, 16, 128)],
    )
    g5 = share(pay)
    dzh, dzl, grad_mixed, first, last, dsum, grads_three, pay = call(
        mixed_kernel,
        [((cells, chan), bf16), ((cells, chan), bf16), ((cells, mid), f32), ((edge, mid), f32), ((edge, mid), f32),
         ((count, mid), f32), ((16, 128), f32), pay16],
        [g5, stat1, stat3, row(gain_three), z_three, grad_pre, own, weh, wel, a_two, slope_two, normed_two, weights,
         w_excite],
        [tile16],
    )
    g6 = share(pay)
    above, below = halos(first, last)
    expand_term, excite_term, bias_term = call(
        expand_grad_kernel,
        [((mid, chan), f32), ((inter, mid), f32), ((1, mid), f32)],
        [mixed, dzh, dzl, fc_act, dsum],
    )
    taps = 3
    piece = 9 * mid // 2 // taps
    dzh, dzl, group_term, grads_two, grads_fc, squeeze_term = call(
        group_kernel,
        [((longer, duo), bf16), ((longer, duo), bf16), ((9 * mid // 2, duo), f32), ((8, 128), f32), ((2, inter), f32),
         ((mid, inter), f32)],
        [g6, gs, fc_pre, fc_normed, fc_inv, row(gain_fc), w_squeeze, pooled, grad_mixed, above, below, slope_two,
         normed_two, ext, weights, stat1, stat2, row(gain_two), valid_rows, valid_cols, tph, tpl],
        [pltpu.VMEM((count, tall + 2, broad, mid), f32), pltpu.VMEM((all_images, inter), f32),
         pltpu.VMEM((all_images, mid), f32)],
        grid=(taps,),
        in_specs=[whole(devices, 16, 128), whole(devices, count, 2 * duo), whole(all_images, inter),
                  whole(all_images, inter), whole(1, inter), whole(1, inter), whole(mid, inter), whole(count, mid),
                  whole(cells, mid), whole(edge, mid), whole(edge, mid), whole(longer, duo), whole(longer, duo),
                  whole(longer, 128), whole(count, duo), whole(8, 128), whole(8, 128), whole(1, duo),
                  whole(count, broad), whole(count, broad),
                  pl.BlockSpec((2, piece, cells), lambda i: (0, i, 0)), pl.BlockSpec((2, piece, cells), lambda i: (0, i, 0))],
        out_specs=[whole(longer, duo), whole(longer, duo), pl.BlockSpec((piece, duo), lambda i: (i, 0)), whole(8, 128),
                   whole(2, inter), whole(mid, inter)],
        limit=56,
    )
    dy_one, pay = call(
        input_grad_kernel,
        [((cells, mid), f32), pay8],
        [dzh, dzl, wgh, wgl, z_one, stat1, own, row(gain_one), row(shift_one)],
        [tile8],
    )
    g7 = share(pay)
    grad_images, reduce_term, grads_one = call(
        final_kernel,
        [((cells, chan), f32), ((chan, mid), f32), ((8, 128), f32)],
        [g7, dy_one, z_one, stat1, row(gain_one), own, wrh, wrl, xth, xtl, grad_pre],
    )
    grad_w_reduce, grad_w_group, grad_w_expand, grad_w_squeeze, grad_excite, grad_bias = lax.psum(
        (reduce_term, group_term, expand_term, squeeze_term, excite_term, bias_term), both
    )
    grads_one = grads_one.reshape(-1)
    grads_two = grads_two.reshape(-1)
    grads_three = grads_three.reshape(-1)
    grad_bias = grad_bias.reshape(-1)
    return (
        block_out.reshape(images.shape),
        grad_images.reshape(images.shape),
        grad_w_reduce,
        grads_one[:mid],
        grads_one[mid:duo],
        grad_w_group.reshape(w_group.shape),
        grads_two[:duo],
        grads_two[duo:],
        grad_w_squeeze,
        grads_fc[0],
        grads_fc[1],
        jnp.concatenate([grad_excite, -grad_excite], axis=1),
        jnp.concatenate([grad_bias, -grad_bias]),
        grad_w_expand,
        grads_three[chan:],
        grads_three[:chan],
    )


def solution(mesh):
    maps = P("batch", "rows", None, None)
    return jax.shard_map(
        on_device,
        mesh=mesh,
        in_specs=(maps,) + (P(),) * 14 + (P("batch", None), P("batch", None), maps),
        out_specs=(maps, maps) + (P(),) * 14,
        check_vma=False,
    )
```

```python
import functools

import jax
import jax.numpy as jnp
from jax import lax
from jax.experimental import pallas as pl
from jax.experimental.pallas import tpu as pltpu
from jax.sharding import PartitionSpec as P

epsilon = 1e-05
f32 = jnp.float32
bf16 = jnp.bfloat16
highest = lax.Precision.HIGHEST
both = ("rows", "batch")
NN = ((1,), (0,))
NT = ((1,), (1,))
TN = ((0,), (0,))


def split(values):
    high = values.astype(bf16)
    return high, (values - high.astype(f32)).astype(bf16)


def dot(left, right, dims):
    return lax.dot_general(left, right, (dims, ((), ())), preferred_element_type=f32)


def product(left, right, dims):
    return dot(left[0], right[0], dims) + (
        dot(left[0], right[1], dims) + dot(left[1], right[0], dims)
    )


def exact(left, right, dims):
    return lax.dot_general(
        left, right, (dims, ((), ())), preferred_element_type=f32, precision=highest
    )


def put(tile, row, vector):
    for j in range(vector.shape[1] // 128):
        tile[row + j : row + j + 1, :] = vector[:, j * 128 : (j + 1) * 128]


def get(tile, row, count):
    return jnp.concatenate([tile[row + j : row + j + 1, :] for j in range(count)], axis=1)


def wide(mask, width):
    return jnp.concatenate([mask] * (width // 128), axis=1)


def column_sum(values):
    return jnp.sum(values, axis=0, keepdims=True)


def image_sum(values, images):
    return jnp.sum(values.reshape(images, values.shape[0] // images, values.shape[1]), axis=1)


def per_image(vector, values):
    count, width = vector.shape
    each = values.shape[0] // count
    return jnp.broadcast_to(vector[:, None, :], (count, each, width)).reshape(values.shape[0], width)


def merge_stats(gathered, counts, width):
    groups = width // 128
    own = jnp.maximum(counts, 1.0)
    total = jnp.sum(counts, axis=0)
    means, inverses = [], []
    for j in range(groups):
        sums = gathered[:, j, :]
        squares = gathered[:, groups + j, :]
        mean = jnp.sum(sums, axis=0, keepdims=True) / total
        shift = sums / own - mean
        spread = jnp.sum(squares + counts * shift * shift, axis=0, keepdims=True) / total
        means.append(mean)
        inverses.append(lax.rsqrt(spread + epsilon))
    return jnp.concatenate(means, axis=1), jnp.concatenate(inverses, axis=1), total


def local_stats(values, mask, count):
    sums = column_sum(values * mask)
    centered = values - sums / jnp.maximum(count, 1.0)
    return sums, column_sum(centered * centered * mask)


def own_rows(extended, images):
    rows, width = extended.shape
    tall = rows // images // 16
    return extended.reshape(images, tall, 16, width)[:, 1 : tall - 1].reshape(-1, width)


class In:
    def __init__(self, source, target, sems, chunks):
        self.ref, self.shape, self.dtype = target, target.shape, target.dtype
        rows = self.shape[0] // chunks
        self.parts = [pl.ds(i * rows, rows) for i in range(chunks)]
        self.copies = [
            pltpu.make_async_copy(source.at[part], target.at[part], sems.at[i])
            for i, part in enumerate(self.parts)
        ]
        self.due = list(range(chunks))

    def start(self):
        for copy in self.copies:
            copy.start()

    def ready(self):
        while self.due:
            self.copies[self.due.pop(0)].wait()
        return self.ref

    def chunk(self, i):
        if i in self.due:
            self.due.remove(i)
            self.copies[i].wait()
        return self.ref[self.parts[i]]

    def __getitem__(self, index):
        return self.ready()[index]


class Out:
    def __init__(self, source, target, sems, chunks):
        self.ref, self.shape, self.dtype = source, source.shape, source.dtype
        rows = self.shape[0] // chunks
        self.parts = [pl.ds(i * rows, rows) for i in range(chunks)]
        self.copies = [
            pltpu.make_async_copy(source.at[part], target.at[part], sems.at[i])
            for i, part in enumerate(self.parts)
        ]
        self.sent = set()

    def send(self, i=None):
        for k in range(len(self.copies)) if i is None else [i]:
            if k not in self.sent:
                self.sent.add(k)
                self.copies[k].start()

    def finish(self):
        self.send()
        for copy in self.copies:
            copy.wait()

    def put(self, i, value):
        self.ref[self.parts[i]] = value
        self.send(i)

    def __getitem__(self, index):
        return self.ref[index]

    def __setitem__(self, index, value):
        self.ref[index] = value


def call(body, outs, ins, scratch=(), limit=60, chunks=None, out_chunks=None, after=()):
    chunks, out_chunks = chunks or {}, out_chunks or {}
    n, m, k = len(ins), len(outs), len(after)
    in_parts = [chunks.get(i, 1) for i in range(n)]
    out_parts = [out_chunks.get(i, 1) for i in range(m)]

    def inner(*refs):
        sources, targets, local = refs[:n], refs[n + k : n + k + m], refs[n + k + m :]
        in_sems, out_sems = local[n + m : n + m + n], local[n + m + n : n + m + n + m]
        given = [In(sources[i], local[i], in_sems[i], in_parts[i]) for i in range(n)]
        made = [Out(local[n + i], targets[i], out_sems[i], out_parts[i]) for i in range(m)]
        for each in given:
            each.start()
        body(*given, *made, *local[n + m + n + m :])
        for each in given:
            each.ready()
        for each in made:
            each.send()
        for each in made:
            each.finish()

    return pl.pallas_call(
        inner,
        out_shape=[jax.ShapeDtypeStruct(shape, kind) for shape, kind in outs],
        in_specs=[pl.BlockSpec(memory_space=pltpu.HBM)] * (n + k),
        out_specs=[pl.BlockSpec(memory_space=pltpu.HBM)] * m,
        scratch_shapes=[
            *[pltpu.VMEM(a.shape, a.dtype) for a in ins],
            *[pltpu.VMEM(shape, kind) for shape, kind in outs],
            *[pltpu.SemaphoreType.DMA((k,)) for k in in_parts + out_parts],
            *scratch,
        ],
        compiler_params=pltpu.CompilerParams(vmem_limit_bytes=limit * 2**20),
        cost_estimate=pl.CostEstimate(flops=1, bytes_accessed=1, transcendentals=0),
    )(*ins, *after)


def local_call(body, outs, ins, scratch=(), limit=16, after=()):
    n, k = len(ins), len(after)

    def inner(*refs):
        body(*refs[:n], *refs[n + k :])

    return pl.pallas_call(
        inner,
        out_shape=[jax.ShapeDtypeStruct(shape, kind) for shape, kind in outs],
        in_specs=[pl.BlockSpec(memory_space=pltpu.VMEM)] * n + [pl.BlockSpec(memory_space=pl.ANY)] * k,
        out_specs=[pl.BlockSpec(memory_space=pltpu.VMEM)] * len(outs),
        scratch_shapes=list(scratch),
        compiler_params=pltpu.CompilerParams(vmem_limit_bytes=limit * 2**20),
        cost_estimate=pl.CostEstimate(flops=1, bytes_accessed=1, transcendentals=0),
    )(*ins, *after)


def share(tile):
    return lax.all_to_all(tile, both, 0, 0)


def halos(first, last):
    count = lax.axis_size("rows")
    above = lax.ppermute(last, "rows", [(i, i + 1) for i in range(count - 1)])
    below = lax.ppermute(first, "rows", [(i + 1, i) for i in range(count - 1)])
    return above, below


def flip(values, axis, bits):
    return lax.ppermute(values, axis, [(i, i ^ bits) for i in range(lax.axis_size(axis))])


class Digit:
    def __init__(self, axis, unit, size):
        self.axis, self.unit, self.size = axis, unit, size

    def own(self):
        return lax.axis_index(self.axis) // self.unit % self.size

    def send(self, pieces):
        return [pieces[0]] + [flip(pieces[j], self.axis, j * self.unit) for j in range(1, self.size)]

    def bits(self):
        return [Digit(self.axis, self.unit << i, 2) for i in range(self.size.bit_length() - 1)]

    def scatter(self, parts, outs):
        size = outs[0].shape[0]
        own = self.own()
        for j, out in enumerate(outs):
            at = pl.ds(pl.multiple_of((own ^ j) * size, 8), size)
            total = parts[0][at, :]
            for part in parts[1:]:
                total = total + part[at, :]
            out[...] = total

    def gather(self, pieces, out):
        size = pieces[0].shape[0]
        own = self.own()
        for j, piece in enumerate(pieces):
            out[pl.ds(pl.multiple_of((own ^ j) * size, 8), size), :] = piece[...]

    def outs(self, rows, width):
        return [((rows // self.size, width), f32)] * self.size


def digits():
    rows, batch = lax.axis_size("rows"), lax.axis_size("batch")
    depth = min(4, batch // 2)
    return Digit("batch", 1, 2), Digit("rows", 1, rows), Digit("batch", 2, depth), Digit("batch", 2 * depth, batch // (2 * depth))


def gate(value, after):
    return pl.pallas_call(
        lambda *refs: None,
        out_shape=jax.ShapeDtypeStruct(value.shape, value.dtype),
        in_specs=[pl.BlockSpec(memory_space=pl.ANY)] * (1 + len(after)),
        out_specs=pl.BlockSpec(memory_space=pl.ANY),
        input_output_aliases={0: 0},
    )(value, *after)


def scatter_kernel(digit, count, *refs):
    digit.scatter(refs[:count], refs[count:])


def sum_kernel(*refs):
    total = refs[0][...]
    for ref in refs[1:-1]:
        total = total + ref[...]
    refs[-1][...] = total


def gather_kernel(digit, *refs):
    digit.gather(refs[:-1], refs[-1])


def scatter_more(digit, pieces, after=()):
    rows, width = pieces[0].shape
    body = functools.partial(scatter_kernel, digit, len(pieces))
    return local_call(body, digit.outs(rows, width), pieces, after=after)


def add_up(pieces, after=()):
    return local_call(sum_kernel, [(pieces[0].shape, f32)], pieces, after=after)[0]


def finish_sum(pieces, extra, after=()):
    total = add_up(pieces, after)
    if extra.size > 1:
        total = add_up(extra.send([total] * extra.size))
    return total


def gather_more(digit, pieces, after=()):
    rows, width = pieces[0].shape
    return local_call(functools.partial(gather_kernel, digit), [((rows * digit.size, width), f32)], pieces, after=after)[0]


def reduce_kernel(rows_ref, cols_ref, w_ref, x_ref, z_ref, ext_ref, own_ref, first_ref, last_ref, wrh_ref, wrl_ref, pay_ref,
                  tile):
    images = rows_ref.shape[0]
    tall = x_ref.shape[0] // images // 16
    shape = (images, tall + 2, 16, 16)
    start = lax.axis_index("rows") * tall - 1
    lane = lax.broadcasted_iota(jnp.int32, shape, 3).reshape(-1, 16)
    at_row = lax.broadcasted_iota(jnp.int32, shape, 1).reshape(-1, 16) + start
    at_col = lax.broadcasted_iota(jnp.int32, shape, 2).reshape(-1, 16)
    row_valid = per_image(rows_ref[...].astype(f32), lane)
    col_valid = per_image(cols_ref[...].astype(f32), lane)
    in_row = jnp.sum(jnp.where(lane == at_row, row_valid, 0.0), axis=1, keepdims=True)
    in_col = jnp.sum(jnp.where(lane == at_col, col_valid, 0.0), axis=1, keepdims=True)
    mask = jnp.broadcast_to(in_row * in_col, (in_row.shape[0], 128)).reshape(ext_ref.shape)
    ext_ref[...] = mask
    own = mask[:, 1 : tall + 1].reshape(-1, 128)
    own_ref[...] = own
    wrh_ref[...], wrl_ref[...] = split(w_ref[...])
    weight = (wrh_ref[...], wrl_ref[...])
    for i in range(len(x_ref.parts)):
        z_ref[x_ref.parts[i]] = product(split(x_ref.chunk(i)), weight, NN)
    z = z_ref[...]
    edges = z.reshape(images, tall, 16, -1)
    first_ref[...] = edges[:, 0].reshape(first_ref.shape)
    last_ref[...] = edges[:, tall - 1].reshape(last_ref.shape)
    for each in (first_ref, last_ref, z_ref, ext_ref, own_ref, wrh_ref, wrl_ref):
        each.send()
    count = column_sum(own)
    sums, squares = local_stats(z, wide(own, z.shape[1]), wide(count, z.shape[1]))
    tile[...] = jnp.zeros_like(tile)
    put(tile, 0, sums)
    put(tile, 2, squares)
    put(tile, 4, count)
    pay_ref[...] = jnp.broadcast_to(tile[...][None], pay_ref.shape)


def parts_kernel(wg_ref, we_ref, *refs):
    vectors, (wgh_ref, wgl_ref, weh_ref, wel_ref, par_ref) = refs[:-5], refs[-5:]
    row = 0
    for vector in vectors:
        put(par_ref, row, vector[...])
        row += vector.shape[1] // 128
    for source, high_ref, low_ref in ((wg_ref, wgh_ref, wgl_ref), (we_ref, weh_ref, wel_ref)):
        for i in range(len(source.parts)):
            high, low = split(source.chunk(i))
            high_ref.put(i, high)
            low_ref.put(i, low)


def turned_kernel(x_ref, high_ref, low_ref):
    high_ref[...], low_ref[...] = split(x_ref[...].T)


def moved(values, step):
    count = values.shape[0]
    at = lax.broadcasted_iota(jnp.int32, values.shape, 0) & 15
    if step == 0:
        return values
    if step > 0:
        return jnp.where(at < 15, pltpu.roll(values, count - 1, 0), 0.0)
    return jnp.where(at > 0, pltpu.roll(values, 1, 0), 0.0)


def window(extended, images, row, width):
    tall = extended.shape[0] // images // 16
    cells = extended.reshape(images, tall, 16, extended.shape[1])
    return cells[:, row : row + tall - 2, :, width].reshape(images * (tall - 2) * 16, -1)


def extend(place, cells, above, below):
    images, tall, broad, width = place.shape
    place[:, 1 : tall - 1] = cells[...].reshape(images, tall - 2, broad, width)
    place[:, 0] = above[...].reshape(images, broad, width)
    place[:, tall - 1] = below[...].reshape(images, broad, width)
    return place[...].reshape(-1, width)


def conv_kernel(g1_ref, par_ref, z_ref, ext_ref, above_ref, below_ref, own_ref, wh_ref, wl_ref,
                z2_ref, a_ref, stat_ref, counts_ref, pay_ref, tile, zext):
    images = zext.shape[0]
    tall = zext.shape[1] - 2
    width = z_ref.shape[1]
    group = width // 2
    gathered = g1_ref[...]
    counts = gathered[:, 4, :]
    counts_ref[...] = counts
    mean, inv, total = merge_stats(gathered, counts, width)
    tile[...] = jnp.zeros_like(tile)
    put(tile, 0, mean)
    put(tile, 2, inv)
    put(tile, 4, total[None])
    stat_ref[...] = tile[...]
    y = (extend(zext, z_ref, above_ref, below_ref) - mean) * inv * get(par_ref, 0, 2) + get(par_ref, 2, 2)
    a = y * jax.nn.sigmoid(y) * wide(ext_ref[...].reshape(-1, 128), width)
    a_ref[...] = a
    a_ref.send()
    shifted = [split(moved(a, step)) for step in (-1, 0, 1)]
    half = z2_ref.shape[1] // 2
    for g in range(2):
        cols = slice(g * group, (g + 1) * group)
        left = [
            jnp.concatenate(
                [window(shifted[tap % 3][part], images, tap // 3, cols) for tap in range(9)], axis=1
            )
            for part in range(2)
        ]
        outs = slice(g * half, (g + 1) * half)
        z2_ref[:, outs] = product(left, (wh_ref[:, outs], wl_ref[:, outs]), NN)
    z2_ref.send()
    z2 = z2_ref[...]
    own = own_ref[...]
    sums, squares = local_stats(z2, wide(own, z2.shape[1]), wide(column_sum(own), z2.shape[1]))
    put(tile, 0, sums)
    put(tile, 4, squares)
    pay_ref[...] = jnp.broadcast_to(tile[...][None], pay_ref.shape)


def taps_kernel(images, a_ref, high_ref, low_ref):
    group = a_ref.shape[1] // 2
    a = a_ref[...]
    shifted = [moved(a, step) for step in (-1, 0, 1)]
    for g in range(2):
        cols = slice(g * group, (g + 1) * group)
        for tap in range(9):
            high, low = split(window(shifted[tap % 3], images, tap // 3, cols).T)
            high_ref[g, tap * group : (tap + 1) * group, :] = high
            low_ref[g, tap * group : (tap + 1) * group, :] = low
        high_ref.send(g)
        low_ref.send(g)


def pixel_count(rows_ref, cols_ref):
    rows = jnp.sum(rows_ref[...].astype(f32), axis=1, keepdims=True)
    return rows * jnp.sum(cols_ref[...].astype(f32), axis=1, keepdims=True)


def pool_kernel(g2_ref, counts_ref, par_ref, rows_ref, cols_ref, z_ref, own_ref, w_ref, a_ref, stat_ref, pooled_ref, pay_ref):
    images = rows_ref.shape[0]
    width = z_ref.shape[1]
    mid = width // 2
    mean, inv, total = merge_stats(g2_ref[...], counts_ref[...], width)
    put(stat_ref, 0, mean)
    put(stat_ref, 4, inv)
    gain, shift = get(par_ref, 4, 4), get(par_ref, 8, 4)
    pieces = len(z_ref.parts)
    sums = []
    for i in range(pieces):
        y = (z_ref.chunk(i) - mean) * inv * gain + shift
        a = y * jax.nn.sigmoid(y) * wide(own_ref.chunk(i), width)
        a_ref.put(i, a)
        sums.append(image_sum(a, images // pieces))
    sums = jnp.concatenate(sums, axis=0)
    pooled = (sums[:, :mid] + sums[:, mid:]) / pixel_count(rows_ref, cols_ref)
    pooled_ref[...] = pooled
    pay_ref[...] = jnp.broadcast_to(exact(pooled, w_ref[...], NN)[None], pay_ref.shape)


def slope_of(values, mean, inv, gain, shift):
    normed = (values - mean) * inv
    y = normed * gain + shift
    sigma = jax.nn.sigmoid(y)
    return sigma * (1.0 + y * (1.0 - sigma)), normed


def slope_kernel(stat_ref, par_ref, rows_ref, cols_ref, own_ref, z_ref, slope_ref, normed_ref, sums_ref):
    images = rows_ref.shape[0]
    width = z_ref.shape[1]
    mean, inv = get(stat_ref, 0, 4), get(stat_ref, 4, 4)
    gain, shift = get(par_ref, 4, 4), get(par_ref, 8, 4)
    pieces = len(z_ref.parts)
    sums, cross = [], []
    for i in range(pieces):
        slope, normed = slope_of(z_ref.chunk(i), mean, inv, gain, shift)
        slope = slope * wide(own_ref.chunk(i), width)
        normed_ref.put(i, normed)
        slope_ref.put(i, slope)
        sums.append(image_sum(slope, images // pieces))
        cross.append(image_sum(slope * normed, images // pieces))
    pixels = pixel_count(rows_ref, cols_ref)
    sums_ref[:, :width] = jnp.concatenate(sums, axis=0) / pixels
    sums_ref[:, width:] = jnp.concatenate(cross, axis=0) / pixels


def expand_kernel(g3_ref, par_ref, w_ref, a_ref, wh_ref, wl_ref, own_ref,
                  mixed_ref, z_ref, weights_ref, normed_ref, pre_ref, act_ref, inv_ref, pay_ref, tile, acts):
    own_images = weights_ref.shape[0]
    mid = mixed_ref.shape[1]
    devices = g3_ref.shape[0]
    rows = lax.axis_size("rows")
    f_one = jnp.sum(g3_ref[...].reshape(rows, devices // rows * own_images, -1), axis=0)
    mean = jnp.mean(f_one, axis=0, keepdims=True)
    centered = f_one - mean
    inv = lax.rsqrt(jnp.mean(centered * centered, axis=0, keepdims=True) + epsilon)
    normed = centered * inv
    pre = normed * par_ref[12:13, :] + par_ref[13:14, :]
    normed_ref[...] = normed
    pre_ref[...] = pre
    inv_ref[...] = inv
    acts[...] = pre * jax.nn.sigmoid(pre)
    at = pl.multiple_of(lax.axis_index("batch") * own_images, own_images)
    act = acts[pl.ds(at, own_images), :]
    act_ref[...] = act
    logits = exact(act, w_ref[...], NN) + get(par_ref, 14, 4)
    lead = logits[:, :mid] - logits[:, mid:]
    first, second = jax.nn.sigmoid(lead), jax.nn.sigmoid(-lead)
    weights_ref[:, :mid] = first
    weights_ref[:, mid:] = second
    a = a_ref[...]
    mixed = per_image(first, a) * a[:, :mid] + per_image(second, a) * a[:, mid:]
    mixed_ref[...] = mixed
    mixed_ref.send()
    left, right = split(mixed), (wh_ref[...], wl_ref[...])
    for i, part in enumerate(z_ref.parts):
        rows = slice(part.start, part.start + part.size)
        z_ref.put(i, product([each[rows] for each in left], right, NN))
    z = z_ref[...]
    width = z.shape[1]
    own = wide(own_ref[...], width)
    sums, squares = local_stats(z, own, wide(column_sum(own_ref[...]), width))
    put(tile, 0, sums)
    put(tile, width // 128, squares)
    pay_ref[...] = jnp.broadcast_to(tile[...][None], pay_ref.shape)


def output_kernel(g4_ref, counts_ref, par_ref, own_ref, z_ref, x_ref, cot_ref, *refs):
    slope_refs, (out_ref, grad_ref, stat_ref, slopes_ref, pay_ref, tile) = refs[:-6], refs[-6:]
    width = z_ref.shape[1]
    groups = width // 128
    mean, inv, total = merge_stats(g4_ref[...], counts_ref[...], width)
    put(stat_ref, 0, mean)
    put(stat_ref, groups, inv)
    gain, shift = get(par_ref, 18, groups), get(par_ref, 26, groups)
    flat, cross = 0.0, 0.0
    for i in range(len(z_ref.parts)):
        own = wide(own_ref.chunk(i), width)
        normed = (z_ref.chunk(i) - mean) * inv
        pre = normed * gain + shift + x_ref.chunk(i)
        sigma = jax.nn.sigmoid(pre)
        out_ref.put(i, pre * sigma * own)
        grad = cot_ref.chunk(i) * own * (sigma * (1.0 + pre * (1.0 - sigma)))
        grad_ref.put(i, grad)
        flat = flat + column_sum(grad)
        cross = cross + column_sum(grad * normed)
    put(tile, 0, flat)
    put(tile, groups, cross)
    pay_ref[...] = jnp.broadcast_to(tile[...][None], pay_ref.shape)
    sum_kernel(*slope_refs, slopes_ref)


def mixed_kernel(digit, g5_ref, stat1_ref, stat3_ref, par_ref, own_ref, grad_ref, z_ref, wh_ref, wl_ref, a_ref, weights_ref,
                 w_ref, slope_ref, normed_ref, *refs):
    shares, (dzh_ref, dzl_ref, gm_ref, dsum_ref, grads_ref, slopes_ref, pay_ref, tile) = refs[: digit.size], refs[digit.size :]
    width = z_ref.shape[1]
    mid = gm_ref.shape[1]
    images = weights_ref.shape[0]
    groups = width // 128
    grads_ref[...] = jnp.sum(g5_ref[...], axis=0)
    count = wide(stat1_ref[4:5, :], width)
    mean, inv = get(stat3_ref, 0, groups), get(stat3_ref, groups, groups)
    flat = get(grads_ref, 0, groups) / count
    cross = get(grads_ref, groups, groups) / count
    scale = get(par_ref, 18, groups) * inv
    for i in range(len(z_ref.parts)):
        normed = (z_ref.chunk(i) - mean) * inv
        dz = scale * (grad_ref.chunk(i) - flat - normed * cross) * wide(own_ref.chunk(i), width)
        high, low = split(dz)
        dzh_ref.put(i, high)
        dzl_ref.put(i, low)
        gm_ref[z_ref.parts[i]] = product((high, low), (wh_ref[...], wl_ref[...]), NT)
    gm = gm_ref[...]
    gm_ref.send()
    a = a_ref[...]
    weights = weights_ref[...]
    gate = image_sum(gm * (a[:, :mid] - a[:, mid:]), images)
    dsum = weights[:, :mid] * weights[:, mid:] * gate
    dsum_ref[...] = dsum
    tile[...] = jnp.zeros_like(tile)
    tile[:images, :] = exact(dsum, w_ref[:, :mid] - w_ref[:, mid:], NT)
    slope = slope_ref[...] * jnp.concatenate([gm, gm], axis=1)
    put(tile, 8, column_sum(weights * image_sum(slope, images)))
    put(tile, 12, column_sum(weights * image_sum(slope * normed_ref[...], images)))
    pay_ref[...] = jnp.broadcast_to(tile[...][None], pay_ref.shape)
    digit.gather(shares, slopes_ref)


def expand_grad_kernel(core, mixed_ref, act_ref, dsum_ref, dzh_ref, dzl_ref, keep_ref, send_ref, excite_ref, term):
    left = split(mixed_ref[...].T)
    rows, width = left[0].shape[0], term.shape[1]
    for j in range(term.shape[0] // rows):
        cols = slice(j * width, (j + 1) * width)
        term[j * rows : (j + 1) * rows, :] = product(left, (dzh_ref[:, cols], dzl_ref[:, cols]), NN)
    core.scatter([term], [keep_ref, send_ref])
    excite_ref[...] = exact(act_ref[...], dsum_ref[...], TN)


def turned_rows(left, wh_ref, wl_ref, outs, row, taps):
    return product(left, [ref[row * taps : (row + 1) * taps, outs] for ref in (wh_ref, wl_ref)], NT)


def fold(total, group):
    return moved(total[:, :group], 1) + total[:, group : 2 * group] + moved(total[:, 2 * group :], -1)


def back_kernel(digit, g6_ref, pre_ref, fcn_ref, inv_ref, par_ref, wsq_ref, pooled_ref, stat1_ref, stat2_ref, rows_ref,
                cols_ref, weights_ref, mine_ref, other_ref, own_ref, gm_ref, slope_ref, normed_ref, wh_ref, wl_ref,
                up_ref, down_ref, dzh_ref, dzl_ref, squeeze_ref, gains_ref, fc_ref, gf, owned, slopes):
    images = rows_ref.shape[0]
    tall = dzh_ref.shape[1] - 2
    width = normed_ref.shape[1]
    mid = width // 2
    groups = width // 128
    rows = lax.axis_size("rows")
    shared = g6_ref[...]
    pre = pre_ref[...]
    fcn = fcn_ref[...]
    sigma = jax.nn.sigmoid(pre)
    total = pre.shape[0]
    grad = jnp.sum(shared[:, :images].reshape(rows, total, -1), axis=0) * (sigma * (1.0 + pre * (1.0 - sigma)))
    flat, cross = column_sum(grad), column_sum(grad * fcn)
    fc_ref[0:1, :] = cross
    fc_ref[1:2, :] = flat
    gf[...] = par_ref[12:13, :] * inv_ref[...] * (grad - flat / total - fcn * cross / total)
    at = pl.multiple_of(lax.axis_index("batch") * images, images)
    mine = gf[pl.ds(at, images), :]
    squeeze = exact(pooled_ref[...], mine, TN)
    half_rows = squeeze.shape[0] // 2
    squeeze_ref[:, : squeeze.shape[1]] = squeeze[:half_rows]
    squeeze_ref[:, squeeze.shape[1] :] = squeeze[half_rows:]
    spread = exact(gf[...], wsq_ref[...], NT)
    owned[...] = spread
    own_spread = owned[pl.ds(at, images), :] / pixel_count(rows_ref, cols_ref)
    for flipped, half in enumerate((mine_ref, other_ref)):
        for block in range(half.shape[0] // images):
            here = pl.multiple_of((2 * block + (digit.own() ^ flipped)) * images, images)
            slopes[pl.ds(here, images), :] = half[block * images : (block + 1) * images, :]
    base = jnp.sum(shared[:, 8:], axis=0)
    count = wide(stat1_ref[4:5, :], mid)
    weights = weights_ref[...]
    gm = gm_ref[...]
    shared_part = per_image(own_spread, gm)
    mask = wide(own_ref[...], mid)
    zero = jnp.zeros((images, 16, width), bf16)
    for ref in (dzh_ref, dzl_ref):
        ref[:, 0] = zero
        ref[:, tall + 1] = zero
    for g in range(2):
        outs = slice(g * mid, (g + 1) * mid)
        crosses = slice(width + g * mid, width + (g + 1) * mid)
        half = groups // 2
        flat_two = get(base, g * half, half) + column_sum(spread * slopes[:, outs])
        cross_two = get(base, groups + g * half, half) + column_sum(spread * slopes[:, crosses])
        put(gains_ref, g * half, cross_two)
        put(gains_ref, groups + g * half, flat_two)
        scale = get(par_ref, 4 + g * half, half) * get(stat2_ref, groups + g * half, half)
        upstream = per_image(weights[:, outs], gm) * gm + shared_part
        dz = scale * (upstream * slope_ref[:, outs] - flat_two / count - normed_ref[:, outs] * (cross_two / count)) * mask
        for ref, part in zip((dzh_ref, dzl_ref), split(dz)):
            ref[:, 1 : tall + 1, :, outs] = part.reshape(images, tall, 16, mid)
    dzh_ref.send()
    dzl_ref.send()
    group = up_ref.shape[1] // 2
    for g in range(2):
        outs = slice(g * mid, (g + 1) * mid)
        cols = slice(g * group, (g + 1) * group)
        for side, row, tap in ((up_ref, 1, 0), (down_ref, tall, 2)):
            left = [ref[:, row, :, outs].reshape(-1, mid) for ref in (dzh_ref, dzl_ref)]
            side[:, cols] = fold(turned_rows(left, wh_ref, wl_ref, outs, tap, 3 * group), group)


def group_kernel(core, dzh_ref, dzl_ref, squeeze_ref, excite_ref, th_ref, tl_ref, keep_ref, send_ref, out_ref):
    tall = dzh_ref.shape[1] - 2
    mid = dzh_ref.shape[3] // 2
    taps = th_ref.shape[1]
    for g in range(2):
        outs = slice(g * mid, (g + 1) * mid)
        right = [ref[:, 1 : tall + 1, :, outs].reshape(-1, mid) for ref in (dzh_ref, dzl_ref)]
        out_ref[g * taps : (g + 1) * taps, :] = product((th_ref.chunk(g)[0], tl_ref.chunk(g)[0]), right, NN)
    inter = excite_ref.shape[0]
    out_ref[2 * taps : 2 * taps + inter, :] = excite_ref[...]
    out_ref[2 * taps + inter :, :] = squeeze_ref[...]
    core.scatter([out_ref], [keep_ref, send_ref])


def input_grad_kernel(par_ref, stat_ref, dsum_ref, z_ref, own_ref, above_ref, below_ref, dzh_ref, dzl_ref, wh_ref, wl_ref,
                      dy_ref, pay_ref, tile, place):
    images = dsum_ref.shape[0]
    width = z_ref.shape[1]
    group = width // 2
    tall = dzh_ref.shape[1] - 2
    half = dzh_ref.shape[3] // 2
    grads = []
    for g in range(2):
        outs = slice(g * half, (g + 1) * half)
        total = None
        for row in range(3):
            left = [ref[:, 2 - row : 2 - row + tall, :, outs].reshape(-1, half) for ref in (dzh_ref, dzl_ref)]
            term = turned_rows(left, wh_ref, wl_ref, outs, row, 3 * group)
            total = term if total is None else total + term
        grads.append(fold(total, group))
    place[...] = jnp.concatenate(grads, axis=1).reshape(place.shape)
    place[:, 0] += above_ref[...].reshape(images, 16, width)
    place[:, tall - 1] += below_ref[...].reshape(images, 16, width)
    grad = place[...].reshape(-1, width)
    mean, inv = get(stat_ref, 0, 2), get(stat_ref, 2, 2)
    normed = (z_ref[...] - mean) * inv
    y = normed * get(par_ref, 0, 2) + get(par_ref, 2, 2)
    sigma = jax.nn.sigmoid(y)
    dy = grad * wide(own_ref[...], width) * (sigma * (1.0 + y * (1.0 - sigma)))
    dy_ref[...] = dy
    dy_ref.send()
    tile[...] = jnp.zeros_like(tile)
    put(tile, 0, column_sum(dy * normed))
    put(tile, 2, column_sum(dy))
    put(tile, 4, column_sum(dsum_ref[...]))
    pay_ref[...] = jnp.broadcast_to(tile[...][None], pay_ref.shape)


def final_kernel(core, g7_ref, par_ref, stat_ref, dy_ref, z_ref, own_ref, th_ref, tl_ref, wh_ref, wl_ref, grad_ref,
                 keep_ref, send_ref, out_ref, gains_ref, term):
    width = z_ref.shape[1]
    gains_ref[...] = jnp.sum(g7_ref[...], axis=0)
    cross, flat = get(gains_ref, 0, 2), get(gains_ref, 2, 2)
    count = wide(stat_ref[4:5, :], width)
    mean, inv = get(stat_ref, 0, 2), get(stat_ref, 2, 2)
    normed = (z_ref[...] - mean) * inv
    scale = get(par_ref, 0, 2) * inv
    dz = scale * (dy_ref[...] - flat / count - normed * (cross / count)) * wide(own_ref[...], width)
    parts = split(dz)
    term[...] = product((th_ref[...], tl_ref[...]), parts, NN)
    core.scatter([term], [keep_ref, send_ref])
    keep_ref.send()
    send_ref.send()
    for i in range(len(grad_ref.parts)):
        rows = slice(grad_ref.parts[i].start, grad_ref.parts[i].start + grad_ref.parts[i].size)
        out_ref.put(i, product([part[rows] for part in parts], (wh_ref[...], wl_ref[...]), NT) + grad_ref.chunk(i))


def deal_kernel(plan, count, *refs):
    outs = list(refs[count:])
    for digit, stretches in plan:
        own = digit.own()
        for j in range(digit.size):
            out, at = outs.pop(0), 0
            for inputs, first, rows in stretches:
                each = rows // digit.size
                here = pl.ds(pl.multiple_of(first + (own ^ j) * each, 8), each)
                total = refs[inputs[0]][here, :]
                for k in inputs[1:]:
                    total = total + refs[k][here, :]
                out[at : at + each, :] = total
                at += each


def deal(plan, ins, after=()):
    width = ins[0].shape[1]
    outs = []
    for digit, stretches in plan:
        rows = sum(rows for _, _, rows in stretches) // digit.size
        outs += [((rows, width), f32)] * digit.size
    return local_call(functools.partial(deal_kernel, plan, len(ins)), outs, ins, after=after)


def halve_kernel(blocks, whole_ref, *outs):
    each = whole_ref.shape[0] // blocks
    half = each // 2
    for k in range(blocks):
        for i, out in enumerate(outs):
            out[k * half : (k + 1) * half, :] = whole_ref[k * each + i * half : k * each + (i + 1) * half, :]


def pair_kernel(digits, *refs):
    outs = refs[4:]
    for i, digit in enumerate(digits):
        digit.gather(refs[2 * i : 2 * i + 2], outs[i] if len(outs) == 2 else outs[0].at[pl.ds(i * 2 * refs[0].shape[0], 2 * refs[0].shape[0])])


def last_kernel(core, expand_map, group_map, mine_ref, other_ref, expand_ref, group_ref, excite_ref, squeeze_ref, whole):
    core.gather([mine_ref, other_ref], whole)
    taps, mid = group_ref.shape[0], whole.shape[1]
    inter = squeeze_ref.shape[1]
    tall = expand_ref.shape[0]
    places = [
        (taps, lambda rows, value: group_ref.__setitem__((rows, slice(0, mid)), value)),
        (taps, lambda rows, value: group_ref.__setitem__((rows, slice(mid, 2 * mid)), value)),
        (inter, lambda rows, value: excite_ref.__setitem__((rows, slice(0, mid)), value)),
        (inter, lambda rows, value: squeeze_put(squeeze_ref, rows, value)),
    ]
    for at, first, rows in expand_map:
        j, m = first // tall, first % tall
        expand_ref[m : m + rows, j * mid : (j + 1) * mid] = whole[at : at + rows, :]
    for at, first, rows in group_map:
        base = 0
        for length, store in places:
            low, high = max(first, base), min(first + rows, base + length)
            if low < high:
                store(slice(low - base, high - base), whole[at + low - first : at + high - first, :])
            base += length
    excite_ref[:, mid:] = -excite_ref[:, :mid]


def squeeze_put(squeeze_ref, rows, value):
    half = squeeze_ref.shape[0] // 2
    width = squeeze_ref.shape[1]
    squeeze_ref[rows, :] = value[:, :width]
    squeeze_ref[slice(half + rows.start, half + rows.stop), :] = value[:, width:]


def on_device(
    images,
    w_reduce,
    gain_one,
    shift_one,
    w_group,
    gain_two,
    shift_two,
    w_squeeze,
    gain_fc,
    shift_fc,
    w_excite,
    excite_bias,
    w_expand,
    gain_three,
    shift_three,
    valid_rows,
    valid_cols,
    cotangent,
):
    count, tall, broad, chan = images.shape
    mid = w_reduce.shape[1]
    inter = w_squeeze.shape[1]
    duo = 2 * mid
    taps = 9 * mid // 2
    cells = count * tall * broad
    longer = count * (tall + 2) * broad
    edge = count * broad
    devices = lax.axis_size("rows") * lax.axis_size("batch")
    all_images = count * lax.axis_size("batch")
    x = images.reshape(cells, chan)
    cot = cotangent.reshape(cells, chan)
    pay8 = ((devices, 8, 128), f32)
    pay16 = ((devices, 16, 128), f32)
    tile8 = pltpu.VMEM((8, 128), f32)
    tile16 = pltpu.VMEM((16, 128), f32)
    twice = lambda *shape: [(shape, bf16)] * 2
    flat_w = w_group.reshape(taps, duo)
    vectors = (gain_one, shift_one, gain_two, shift_two, gain_fc, shift_fc, excite_bias, gain_three, shift_three)
    core, line, depth, extra = digits()

    z_one, ext, own, first, last, wrh, wrl, pay = call(
        reduce_kernel,
        [((cells, mid), f32), ((count, tall + 2, broad, 128), f32), ((cells, 128), f32), ((edge, mid), f32),
         ((edge, mid), f32), *twice(chan, mid), pay8],
        [valid_rows, valid_cols, w_reduce, x],
        [tile8],
        chunks={3: 2},
    )
    g1 = share(pay)
    above, below = halos(first, last)
    wgh, wgl, weh, wel, par = call(
        parts_kernel,
        [*twice(taps, duo), *twice(mid, chan), ((40, 128), f32)],
        [flat_w, w_expand, *[v.reshape(1, -1) for v in vectors]],
        chunks={0: 4, 1: 2},
        out_chunks={0: 4, 1: 4, 2: 2, 3: 2},
        after=[z_one],
    )
    z_two, a_one, stat1, counts, pay = call(
        conv_kernel,
        [((cells, duo), f32), ((longer, mid), f32), ((8, 128), f32), ((devices, 128), f32), pay8],
        [g1, par, z_one, ext, above, below, own, wgh, wgl],
        [tile8, pltpu.VMEM((count, tall + 2, broad, mid), f32)],
    )
    g2 = share(pay)
    xth, xtl = call(turned_kernel, twice(chan, cells), [x], after=[stat1])
    a_two, stat2, pooled, pay = call(
        pool_kernel,
        [((cells, duo), f32), ((8, 128), f32), ((count, mid), f32), ((devices, count, inter), f32)],
        [g2, counts, par, valid_rows, valid_cols, z_two, own, w_squeeze],
        chunks={5: 2, 6: 2},
        out_chunks={0: 2},
        after=[xth],
    )
    g3 = share(pay)
    slope_two, normed_two, slopes = call(
        slope_kernel,
        [((cells, duo), f32), ((cells, duo), f32), ((count, 2 * duo), f32)],
        [stat2, par, valid_rows, valid_cols, own, z_two],
        chunks={4: 2, 5: 2},
        out_chunks={0: 2, 1: 2},
    )
    mixed, z_three, weights, fc_normed, fc_pre, fc_act, fc_inv, pay = call(
        expand_kernel,
        [((cells, mid), f32), ((cells, chan), f32), ((count, duo), f32), ((all_images, inter), f32),
         ((all_images, inter), f32), ((count, inter), f32), ((1, inter), f32), pay16],
        [g3, par, w_excite, a_two, weh, wel, own],
        [tile16, pltpu.VMEM((all_images, inter), f32)],
        out_chunks={1: 2},
        after=[slopes],
    )
    g4 = share(pay)
    slopes = line.send([slopes] * line.size)
    block_out, grad_pre, stat3, slopes, pay = call(
        output_kernel,
        [((cells, chan), f32), ((cells, chan), f32), ((16, 128), f32), ((count, 2 * duo), f32), pay16],
        [g4, counts, par, own, z_three, x, cot, *slopes],
        [tile16],
        chunks={3: 4, 4: 4, 5: 4, 6: 4},
        out_chunks={0: 4, 1: 4},
    )
    g5 = share(pay)
    slopes = depth.send([slopes] * depth.size)
    tph, tpl = call(functools.partial(taps_kernel, count), twice(2, taps, cells), [a_one], out_chunks={0: 2, 1: 2}, after=[stat3])
    dzh, dzl, grad_mixed, dsum, grads_three, slopes, pay = call(
        functools.partial(mixed_kernel, depth),
        [*twice(cells, chan), ((cells, mid), f32), ((count, mid), f32),
         ((16, 128), f32), ((depth.size * count, 2 * duo), f32), pay16],
        [g5, stat1, stat3, par, own, grad_pre, z_three, weh, wel, a_two, weights, w_excite, slope_two, normed_two, *slopes],
        [tile16],
        chunks={4: 2, 5: 2, 6: 2},
        out_chunks={0: 2, 1: 2},
        after=[tph],
    )
    g6 = share(pay)
    *expand_sum, excite_term = call(
        functools.partial(expand_grad_kernel, core),
        [*core.outs(mid * chan // mid, mid), ((inter, mid), f32)],
        [mixed, fc_act, dsum, dzh, dzl],
        [pltpu.VMEM((chan, mid), f32)],
    )
    if extra.size > 1:
        slopes = gather_more(extra, extra.send([slopes] * extra.size))
    slopes = core.send([slopes] * 2)
    packed = 2 * taps + 2 * inter
    up, down, dzh, dzl, squeeze_term, grads_two, grads_fc = call(
        functools.partial(back_kernel, core),
        [((edge, mid), f32), ((edge, mid), f32), *twice(count, tall + 2, broad, duo), ((inter, mid), f32),
         ((8, 128), f32), ((2, inter), f32)],
        [g6, fc_pre, fc_normed, fc_inv, par, w_squeeze, pooled, stat1, stat2, valid_rows, valid_cols, weights, *slopes, own,
         grad_mixed, slope_two, normed_two, wgh, wgl],
        [pltpu.VMEM((all_images, inter), f32), pltpu.VMEM((all_images, mid), f32), pltpu.VMEM((all_images, 2 * duo), f32)],
        after=[excite_term],
    )
    above, below = halos(up, down)
    group_sum = call(
        functools.partial(group_kernel, core),
        core.outs(packed, mid),
        [dzh, dzl, squeeze_term, excite_term, tph, tpl],
        [pltpu.VMEM((packed, mid), f32)],
        chunks={4: 2, 5: 2},
    )
    expand_sum = core.send(expand_sum)
    group_sum = core.send([group_sum[0], gate(group_sum[1], [above, below])])
    dy_one, pay = call(
        input_grad_kernel,
        [((cells, mid), f32), pay8],
        [par, stat1, dsum, z_one, own, above, below, dzh, dzl, wgh, wgl],
        [tile8, pltpu.VMEM((count, tall, broad, mid), f32)],
    )
    first_bit, second_bit = line.bits()
    some, more = expand_sum[0].shape[0] // 2, group_sum[0].shape[0] // 2
    both_of = lambda start, a, b: [((0, 1), start * a, a), ((2, 3), start * b, b)]
    first_half = lambda digit: (digit, both_of(0, some, more))
    second_half = lambda digit: (digit, both_of(1, some, more))
    keep_a, send_a, keep_b, send_b = deal(
        [first_half(first_bit), second_half(second_bit)], [*expand_sum, *group_sum], after=[dy_one]
    )
    g7 = share(pay)
    come_a, come_b = first_bit.send([keep_a, send_a]), second_bit.send([keep_b, send_b])
    some, more = some // 2, more // 2
    turn = lambda k: [((k, k + 1), 0, some), ((k, k + 1), some, more)]
    keep_a, send_a, keep_b, send_b = deal([(second_bit, turn(0)), (first_bit, turn(2))], [*come_a, *come_b])
    *reduce_sum, grad_images, grads_one = call(
        functools.partial(final_kernel, core),
        [*core.outs(chan, mid), ((cells, chan), f32), ((8, 128), f32)],
        [g7, par, stat1, dy_one, z_one, own, xth, xtl, wrh, wrl, grad_pre],
        [pltpu.VMEM((chan, mid), f32)],
        chunks={10: 2},
        out_chunks={2: 2},
        after=[keep_a],
    )
    come_a, come_b = second_bit.send([keep_a, send_a]), first_bit.send([keep_b, send_b])
    some, more = some // 2, more // 2
    joined = deal([(depth, turn(0) + turn(2))], [*come_a, *come_b], after=[grad_images])
    reduce_sum[1] = gate(reduce_sum[1], [joined[1]])
    bits = [core, *line.bits(), *depth.bits()]
    reduce_sum = scatter_more(bits[1], bits[0].send(reduce_sum))
    joined = finish_sum(depth.send(joined), extra, after=[reduce_sum[0]])
    reduce_sum = scatter_more(bits[2], bits[1].send(reduce_sum), after=[joined])
    joined = gather_more(depth, depth.send([joined] * depth.size), after=[reduce_sum[0]])
    rows_in = joined.shape[0]
    half_a, half_b = local_call(
        functools.partial(halve_kernel, depth.size), [((rows_in // 2, mid), f32)] * 2, [joined]
    )
    for here, there in zip(bits[2:-1], bits[3:]):
        reduce_sum = scatter_more(there, here.send(reduce_sum), after=[half_a])
    half_a, half_b = local_call(
        functools.partial(pair_kernel, [second_bit, first_bit]),
        [((rows_in, mid), f32)] * 2,
        [*second_bit.send([half_a] * 2), *first_bit.send([half_b] * 2)],
        after=[reduce_sum[0]],
    )
    reduce_sum = finish_sum(bits[-1].send(reduce_sum), extra, after=[half_a])
    reduce_sum = gather_more(bits[-1], bits[-1].send([reduce_sum] * 2))
    (joined,) = local_call(
        functools.partial(pair_kernel, [first_bit, second_bit]),
        [((4 * rows_in, mid), f32)],
        [*first_bit.send([half_a] * 2), *second_bit.send([half_b] * 2)],
        after=[reduce_sum],
    )
    for here in bits[-2:0:-1]:
        reduce_sum = gather_more(here, here.send([reduce_sum] * 2), after=[joined])
    expand_map, group_map = [], []
    at = 0
    some, more = some // depth.size, more // depth.size
    for half in range(core.size):
        for part in range(2):
            for outer in range(2):
                for inner in range(2):
                    for deep in range(depth.size):
                        block = (((half * 2 + part) * 2 + outer) * 2 + inner) * depth.size + deep
                        expand_map.append((at, block * some, some))
                        group_map.append((at + some, block * more, more))
                        at += some + more
    grad_w_expand, grad_w_group, grad_w_excite, grad_w_squeeze = local_call(
        functools.partial(last_kernel, core, expand_map, group_map),
        [((mid, chan), f32), ((taps, duo), f32), ((inter, duo), f32), ((mid, inter), f32)],
        core.send([joined] * 2),
        [pltpu.VMEM((chan + packed, mid), f32)],
    )
    grad_w_reduce = gather_more(core, core.send([reduce_sum] * 2))
    grads_one = grads_one.reshape(-1)
    grads_two = grads_two.reshape(-1)
    grads_three = grads_three.reshape(-1)
    grad_bias = grads_one[duo : duo + mid]
    return (
        block_out.reshape(images.shape),
        grad_images.reshape(images.shape),
        grad_w_reduce,
        grads_one[:mid],
        grads_one[mid:duo],
        grad_w_group.reshape(w_group.shape),
        grads_two[:duo],
        grads_two[duo:],
        grad_w_squeeze,
        grads_fc[0],
        grads_fc[1],
        grad_w_excite,
        jnp.concatenate([grad_bias, -grad_bias]),
        grad_w_expand,
        grads_three[chan:],
        grads_three[:chan],
    )


def solution(mesh):
    maps = P("batch", "rows", None, None)
    return jax.shard_map(
        on_device,
        mesh=mesh,
        in_specs=(maps,) + (P(),) * 14 + (P("batch", None), P("batch", None), maps),
        out_specs=(maps, maps) + (P(),) * 14,
        check_vma=False,
    )
```

```python
import functools

import jax
import jax.numpy as jnp
from jax import lax
from jax.experimental import pallas as pl
from jax.experimental.pallas import tpu as pltpu
from jax.sharding import PartitionSpec as P

epsilon = 1e-05
f32 = jnp.float32
bf16 = jnp.bfloat16
highest = lax.Precision.HIGHEST
both = ("rows", "batch")
NN = ((1,), (0,))
NT = ((1,), (1,))
TN = ((0,), (0,))


def split(values):
    high = values.astype(bf16)
    return high, (values - high.astype(f32)).astype(bf16)


def dot(left, right, dims):
    return lax.dot_general(left, right, (dims, ((), ())), preferred_element_type=f32)


def product(left, right, dims):
    return dot(left[0], right[0], dims) + (
        dot(left[0], right[1], dims) + dot(left[1], right[0], dims)
    )


def exact(left, right, dims):
    return lax.dot_general(
        left, right, (dims, ((), ())), preferred_element_type=f32, precision=highest
    )


def put(tile, row, vector):
    for j in range(vector.shape[1] // 128):
        tile[row + j : row + j + 1, :] = vector[:, j * 128 : (j + 1) * 128]


def get(tile, row, count):
    return jnp.concatenate([tile[row + j : row + j + 1, :] for j in range(count)], axis=1)


def wide(mask, width):
    return jnp.concatenate([mask] * (width // 128), axis=1)


def column_sum(values):
    return jnp.sum(values, axis=0, keepdims=True)


def image_sum(values, images):
    return jnp.sum(values.reshape(images, values.shape[0] // images, values.shape[1]), axis=1)


def per_image(vector, values):
    count, width = vector.shape
    each = values.shape[0] // count
    return jnp.broadcast_to(vector[:, None, :], (count, each, width)).reshape(values.shape[0], width)


def merge_stats(gathered, counts, width):
    groups = width // 128
    own = jnp.maximum(counts, 1.0)
    total = jnp.sum(counts, axis=0)
    means, inverses = [], []
    for j in range(groups):
        sums = gathered[:, j, :]
        squares = gathered[:, groups + j, :]
        mean = jnp.sum(sums, axis=0, keepdims=True) / total
        shift = sums / own - mean
        spread = jnp.sum(squares + counts * shift * shift, axis=0, keepdims=True) / total
        means.append(mean)
        inverses.append(lax.rsqrt(spread + epsilon))
    return jnp.concatenate(means, axis=1), jnp.concatenate(inverses, axis=1), total


def local_stats(values, mask, count):
    sums = column_sum(values * mask)
    centered = values - sums / jnp.maximum(count, 1.0)
    return sums, column_sum(centered * centered * mask)


def own_rows(extended, images):
    rows, width = extended.shape
    tall = rows // images // 16
    return extended.reshape(images, tall, 16, width)[:, 1 : tall - 1].reshape(-1, width)


class In:
    def __init__(self, source, target, sems, chunks):
        self.ref, self.shape, self.dtype = target, target.shape, target.dtype
        rows = self.shape[0] // chunks
        self.parts = [pl.ds(i * rows, rows) for i in range(chunks)]
        self.copies = [
            pltpu.make_async_copy(source.at[part], target.at[part], sems.at[i])
            for i, part in enumerate(self.parts)
        ]
        self.due = list(range(chunks))

    def start(self):
        for copy in self.copies:
            copy.start()

    def ready(self):
        while self.due:
            self.copies[self.due.pop(0)].wait()
        return self.ref

    def chunk(self, i):
        if i in self.due:
            self.due.remove(i)
            self.copies[i].wait()
        return self.ref[self.parts[i]]

    def __getitem__(self, index):
        return self.ready()[index]


class Near:
    def __init__(self, ref):
        self.ref, self.shape, self.dtype = ref, ref.shape, ref.dtype

    def start(self, i=None):
        pass

    ready = send = start

    def finish(self):
        pass

    def __getitem__(self, index):
        return self.ref[index]

    def __setitem__(self, index, value):
        self.ref[index] = value


class Out:
    def __init__(self, source, target, sems, chunks):
        self.ref, self.shape, self.dtype = source, source.shape, source.dtype
        rows = self.shape[0] // chunks
        self.parts = [pl.ds(i * rows, rows) for i in range(chunks)]
        self.copies = [
            pltpu.make_async_copy(source.at[part], target.at[part], sems.at[i])
            for i, part in enumerate(self.parts)
        ]
        self.sent = set()

    def send(self, i=None):
        for k in range(len(self.copies)) if i is None else [i]:
            if k not in self.sent:
                self.sent.add(k)
                self.copies[k].start()

    def finish(self):
        self.send()
        for copy in self.copies:
            copy.wait()

    def put(self, i, value):
        self.ref[self.parts[i]] = value
        self.send(i)

    def __getitem__(self, index):
        return self.ref[index]

    def __setitem__(self, index, value):
        self.ref[index] = value


def call(body, outs, ins, scratch=(), limit=54, chunks=None, out_chunks=None, after=(), near=(), near_outs=()):
    chunks, out_chunks = chunks or {}, out_chunks or {}
    n, m, k = len(ins), len(outs), len(after)
    far = [i for i in range(n) if i not in near]
    far_outs = [i for i in range(m) if i not in near_outs]
    parts = [chunks.get(i, 1) for i in far] + [out_chunks.get(i, 1) for i in far_outs]

    def inner(*refs):
        sources, targets, local = refs[:n], refs[n + k : n + k + m], refs[n + k + m :]
        held, sems, rest = local[: len(parts)], local[len(parts) : 2 * len(parts)], local[2 * len(parts) :]
        given = [Near(ref) for ref in sources]
        for at, i in enumerate(far):
            given[i] = In(sources[i], held[at], sems[at], parts[at])
        made = [Near(ref) for ref in targets]
        for at, i in enumerate(far_outs, len(far)):
            made[i] = Out(held[at], targets[i], sems[at], parts[at])
        for each in given:
            each.start()
        body(*given, *made, *rest)
        for each in given:
            each.ready()
        for each in made:
            each.send()
        for each in made:
            each.finish()

    space = lambda count, places: [pl.BlockSpec(memory_space=pltpu.VMEM if i in places else pltpu.HBM) for i in range(count)]
    return pl.pallas_call(
        inner,
        out_shape=[(pltpu.VMEM if i in near_outs else pltpu.HBM)(*out) for i, out in enumerate(outs)],
        in_specs=space(n, near) + space(k, ()),
        out_specs=space(m, near_outs),
        scratch_shapes=[
            *[pltpu.VMEM(ins[i].shape, ins[i].dtype) for i in far],
            *[pltpu.VMEM(*outs[i]) for i in far_outs],
            *[pltpu.SemaphoreType.DMA((k,)) for k in parts],
            *scratch,
        ],
        compiler_params=pltpu.CompilerParams(vmem_limit_bytes=limit * 2**20),
        cost_estimate=pl.CostEstimate(flops=1, bytes_accessed=1, transcendentals=0),
    )(
        *[pltpu.with_memory_space_constraint(a, pltpu.VMEM if i in near else pltpu.HBM) for i, a in enumerate(ins)],
        *[pltpu.with_memory_space_constraint(a, pltpu.HBM) for a in after],
    )


def local_call(body, outs, ins, scratch=(), limit=16, after=()):
    n, k = len(ins), len(after)

    def inner(*refs):
        body(*refs[:n], *refs[n + k :])

    return pl.pallas_call(
        inner,
        out_shape=[jax.ShapeDtypeStruct(shape, kind) for shape, kind in outs],
        in_specs=[pl.BlockSpec(memory_space=pltpu.VMEM)] * n + [pl.BlockSpec(memory_space=pl.ANY)] * k,
        out_specs=[pl.BlockSpec(memory_space=pltpu.VMEM)] * len(outs),
        scratch_shapes=list(scratch),
        compiler_params=pltpu.CompilerParams(vmem_limit_bytes=limit * 2**20),
        cost_estimate=pl.CostEstimate(flops=1, bytes_accessed=1, transcendentals=0),
    )(*ins, *after)


def share(tile):
    return lax.all_to_all(tile, both, 0, 0)


def halos(first, last):
    count = lax.axis_size("rows")
    above = lax.ppermute(last, "rows", [(i, i + 1) for i in range(count - 1)])
    below = lax.ppermute(first, "rows", [(i + 1, i) for i in range(count - 1)])
    return above, below


def flip(values, axis, bits):
    return lax.ppermute(values, axis, [(i, i ^ bits) for i in range(lax.axis_size(axis))])


class Digit:
    def __init__(self, axis, unit, size):
        self.axis, self.unit, self.size = axis, unit, size

    def own(self):
        return lax.axis_index(self.axis) // self.unit % self.size

    def send(self, pieces):
        return [pieces[0]] + [flip(pieces[j], self.axis, j * self.unit) for j in range(1, self.size)]

    def bits(self):
        return [Digit(self.axis, self.unit << i, 2) for i in range(self.size.bit_length() - 1)]

    def trade(self, stacked):
        count = lax.axis_size(self.axis)
        span = self.unit * self.size
        starts = [high + low for high in range(0, count, span) for low in range(self.unit)]
        groups = [[start + self.unit * d for d in range(self.size)] for start in starts]
        return lax.all_to_all(stacked, self.axis, 0, 0, axis_index_groups=groups)

    def scatter(self, parts, outs):
        size = outs[0].shape[0]
        own = self.own()
        for j, out in enumerate(outs):
            at = pl.ds(pl.multiple_of((own ^ j) * size, 8), size)
            total = parts[0][at, :]
            for part in parts[1:]:
                total = total + part[at, :]
            out[...] = total

    def gather(self, pieces, out):
        size = pieces[0].shape[0]
        own = self.own()
        for j, piece in enumerate(pieces):
            out[pl.ds(pl.multiple_of((own ^ j) * size, 8), size), :] = piece[...]

    def outs(self, rows, width):
        return [((rows // self.size, width), f32)] * self.size


def digits():
    rows, batch = lax.axis_size("rows"), lax.axis_size("batch")
    depth = min(4, batch // 2)
    return Digit("batch", 1, 2), Digit("rows", 1, rows), Digit("batch", 2, depth), Digit("batch", 2 * depth, batch // (2 * depth))


def gate(value, after):
    return pl.pallas_call(
        lambda *refs: None,
        out_shape=jax.ShapeDtypeStruct(value.shape, value.dtype),
        in_specs=[pl.BlockSpec(memory_space=pl.ANY)] * (1 + len(after)),
        out_specs=pl.BlockSpec(memory_space=pl.ANY),
        input_output_aliases={0: 0},
    )(value, *after)


def scatter_kernel(digit, count, *refs):
    digit.scatter(refs[:count], refs[count:])


def sum_kernel(*refs):
    total = refs[0][...]
    for ref in refs[1:-1]:
        total = total + ref[...]
    refs[-1][...] = total


def gather_kernel(digit, *refs):
    digit.gather(refs[:-1], refs[-1])


def scatter_more(digit, pieces, after=()):
    rows, width = pieces[0].shape
    body = functools.partial(scatter_kernel, digit, len(pieces))
    return local_call(body, digit.outs(rows, width), pieces, after=after)


def add_up(pieces, after=()):
    return local_call(sum_kernel, [(pieces[0].shape, f32)], pieces, after=after)[0]


def finish_sum(pieces, extra, after=()):
    total = add_up(pieces, after)
    if extra.size > 1:
        total = add_up(extra.send([total] * extra.size))
    return total


def gather_more(digit, pieces, after=()):
    rows, width = pieces[0].shape
    return local_call(functools.partial(gather_kernel, digit), [((rows * digit.size, width), f32)], pieces, after=after)[0]


def reduce_kernel(rows_ref, cols_ref, w_ref, x_ref, z_ref, ext_ref, own_ref, first_ref, last_ref, wrh_ref, wrl_ref, pay_ref,
                  tile):
    images = rows_ref.shape[0]
    tall = x_ref.shape[0] // images // 16
    shape = (images, tall + 2, 16, 16)
    start = lax.axis_index("rows") * tall - 1
    lane = lax.broadcasted_iota(jnp.int32, shape, 3).reshape(-1, 16)
    at_row = lax.broadcasted_iota(jnp.int32, shape, 1).reshape(-1, 16) + start
    at_col = lax.broadcasted_iota(jnp.int32, shape, 2).reshape(-1, 16)
    row_valid = per_image(rows_ref[...].astype(f32), lane)
    col_valid = per_image(cols_ref[...].astype(f32), lane)
    in_row = jnp.sum(jnp.where(lane == at_row, row_valid, 0.0), axis=1, keepdims=True)
    in_col = jnp.sum(jnp.where(lane == at_col, col_valid, 0.0), axis=1, keepdims=True)
    mask = jnp.broadcast_to(in_row * in_col, (in_row.shape[0], 128)).reshape(ext_ref.shape)
    ext_ref[...] = mask
    own = mask[:, 1 : tall + 1].reshape(-1, 128)
    own_ref[...] = own
    wrh_ref[...], wrl_ref[...] = split(w_ref[...])
    weight = (wrh_ref[...], wrl_ref[...])
    for i in range(len(x_ref.parts)):
        z_ref[x_ref.parts[i]] = product(split(x_ref.chunk(i)), weight, NN)
    z = z_ref[...]
    edges = z.reshape(images, tall, 16, -1)
    first_ref[...] = edges[:, 0].reshape(first_ref.shape)
    last_ref[...] = edges[:, tall - 1].reshape(last_ref.shape)
    for each in (first_ref, last_ref, z_ref, ext_ref, own_ref, wrh_ref, wrl_ref):
        each.send()
    count = column_sum(own)
    sums, squares = local_stats(z, wide(own, z.shape[1]), wide(count, z.shape[1]))
    tile[...] = jnp.zeros_like(tile)
    put(tile, 0, sums)
    put(tile, 2, squares)
    put(tile, 4, count)
    pay_ref[...] = jnp.broadcast_to(tile[...][None], pay_ref.shape)


def parts_kernel(wg_ref, we_ref, *refs):
    vectors, (wgh_ref, wgl_ref, weh_ref, wel_ref, par_ref) = refs[:-5], refs[-5:]
    row = 0
    for vector in vectors:
        put(par_ref, row, vector[...])
        row += vector.shape[1] // 128
    for source, high_ref, low_ref in ((wg_ref, wgh_ref, wgl_ref), (we_ref, weh_ref, wel_ref)):
        for i in range(len(source.parts)):
            high, low = split(source.chunk(i))
            high_ref.put(i, high)
            low_ref.put(i, low)


def turned_kernel(x_ref, high_ref, low_ref):
    high_ref[...], low_ref[...] = split(x_ref[...].T)


def moved(values, step):
    count = values.shape[0]
    at = lax.broadcasted_iota(jnp.int32, values.shape, 0) & 15
    if step == 0:
        return values
    if step > 0:
        return jnp.where(at < 15, pltpu.roll(values, count - 1, 0), 0.0)
    return jnp.where(at > 0, pltpu.roll(values, 1, 0), 0.0)


def window(extended, images, row, width):
    tall = extended.shape[0] // images // 16
    cells = extended.reshape(images, tall, 16, extended.shape[1])
    return cells[:, row : row + tall - 2, :, width].reshape(images * (tall - 2) * 16, -1)


def extend(place, cells, above, below):
    images, tall, broad, width = place.shape
    place[:, 1 : tall - 1] = cells[...].reshape(images, tall - 2, broad, width)
    place[:, 0] = above[...].reshape(images, broad, width)
    place[:, tall - 1] = below[...].reshape(images, broad, width)
    return place[...].reshape(-1, width)


def conv_kernel(g1_ref, par_ref, z_ref, ext_ref, above_ref, below_ref, own_ref, wh_ref, wl_ref,
                z2_ref, a_ref, stat_ref, counts_ref, pay_ref, tile, zext):
    images = zext.shape[0]
    tall = zext.shape[1] - 2
    width = z_ref.shape[1]
    group = width // 2
    gathered = g1_ref[...]
    counts = gathered[:, 4, :]
    counts_ref[...] = counts
    mean, inv, total = merge_stats(gathered, counts, width)
    tile[...] = jnp.zeros_like(tile)
    put(tile, 0, mean)
    put(tile, 2, inv)
    put(tile, 4, total[None])
    stat_ref[...] = tile[...]
    y = (extend(zext, z_ref, above_ref, below_ref) - mean) * inv * get(par_ref, 0, 2) + get(par_ref, 2, 2)
    a = y * jax.nn.sigmoid(y) * wide(ext_ref[...].reshape(-1, 128), width)
    a_ref[...] = a
    a_ref.send()
    shifted = [split(moved(a, step)) for step in (-1, 0, 1)]
    half = z2_ref.shape[1] // 2
    for g in range(2):
        cols = slice(g * group, (g + 1) * group)
        left = [
            jnp.concatenate(
                [window(shifted[tap % 3][part], images, tap // 3, cols) for tap in range(9)], axis=1
            )
            for part in range(2)
        ]
        outs = slice(g * half, (g + 1) * half)
        z2_ref[:, outs] = product(left, (wh_ref[:, outs], wl_ref[:, outs]), NN)
    z2_ref.send()
    z2 = z2_ref[...]
    own = own_ref[...]
    sums, squares = local_stats(z2, wide(own, z2.shape[1]), wide(column_sum(own), z2.shape[1]))
    put(tile, 0, sums)
    put(tile, 4, squares)
    pay_ref[...] = jnp.broadcast_to(tile[...][None], pay_ref.shape)


def taps_kernel(images, a_ref, high_ref, low_ref):
    group = a_ref.shape[1] // 2
    a = a_ref[...]
    shifted = [moved(a, step) for step in (-1, 0, 1)]
    for g in range(2):
        cols = slice(g * group, (g + 1) * group)
        for tap in range(9):
            high, low = split(window(shifted[tap % 3], images, tap // 3, cols).T)
            high_ref[g, tap * group : (tap + 1) * group, :] = high
            low_ref[g, tap * group : (tap + 1) * group, :] = low
        high_ref.send(g)
        low_ref.send(g)


def pixel_count(rows_ref, cols_ref):
    rows = jnp.sum(rows_ref[...].astype(f32), axis=1, keepdims=True)
    return rows * jnp.sum(cols_ref[...].astype(f32), axis=1, keepdims=True)


def pool_kernel(g2_ref, counts_ref, par_ref, rows_ref, cols_ref, z_ref, own_ref, w_ref, a_ref, stat_ref, pooled_ref, pay_ref):
    images = rows_ref.shape[0]
    width = z_ref.shape[1]
    mid = width // 2
    mean, inv, total = merge_stats(g2_ref[...], counts_ref[...], width)
    put(stat_ref, 0, mean)
    put(stat_ref, 4, inv)
    gain, shift = get(par_ref, 4, 4), get(par_ref, 8, 4)
    pieces = len(z_ref.parts)
    sums = []
    for i in range(pieces):
        y = (z_ref.chunk(i) - mean) * inv * gain + shift
        a = y * jax.nn.sigmoid(y) * wide(own_ref.chunk(i), width)
        a_ref.put(i, a)
        sums.append(image_sum(a, images // pieces))
    sums = jnp.concatenate(sums, axis=0)
    pooled = (sums[:, :mid] + sums[:, mid:]) / pixel_count(rows_ref, cols_ref)
    pooled_ref[...] = pooled
    pay_ref[...] = jnp.broadcast_to(exact(pooled, w_ref[...], NN)[None], pay_ref.shape)


def slope_of(values, mean, inv, gain, shift):
    normed = (values - mean) * inv
    y = normed * gain + shift
    sigma = jax.nn.sigmoid(y)
    return sigma * (1.0 + y * (1.0 - sigma)), normed


def slope_kernel(stat_ref, par_ref, rows_ref, cols_ref, own_ref, z_ref, slope_ref, normed_ref, sums_ref):
    images = rows_ref.shape[0]
    width = z_ref.shape[1]
    mean, inv = get(stat_ref, 0, 4), get(stat_ref, 4, 4)
    gain, shift = get(par_ref, 4, 4), get(par_ref, 8, 4)
    pieces = len(z_ref.parts)
    sums, cross = [], []
    for i in range(pieces):
        slope, normed = slope_of(z_ref.chunk(i), mean, inv, gain, shift)
        slope = slope * wide(own_ref.chunk(i), width)
        normed_ref.put(i, normed)
        slope_ref.put(i, slope)
        sums.append(image_sum(slope, images // pieces))
        cross.append(image_sum(slope * normed, images // pieces))
    pixels = pixel_count(rows_ref, cols_ref)
    sums_ref[:, :width] = jnp.concatenate(sums, axis=0) / pixels
    sums_ref[:, width:] = jnp.concatenate(cross, axis=0) / pixels


def expand_kernel(g3_ref, par_ref, w_ref, a_ref, wh_ref, wl_ref, own_ref,
                  mixed_ref, z_ref, weights_ref, normed_ref, pre_ref, act_ref, inv_ref, pay_ref, tile, acts):
    own_images = weights_ref.shape[0]
    mid = mixed_ref.shape[1]
    devices = g3_ref.shape[0]
    rows = lax.axis_size("rows")
    f_one = jnp.sum(g3_ref[...].reshape(rows, devices // rows * own_images, -1), axis=0)
    mean = jnp.mean(f_one, axis=0, keepdims=True)
    centered = f_one - mean
    inv = lax.rsqrt(jnp.mean(centered * centered, axis=0, keepdims=True) + epsilon)
    normed = centered * inv
    pre = normed * par_ref[12:13, :] + par_ref[13:14, :]
    normed_ref[...] = normed
    pre_ref[...] = pre
    inv_ref[...] = inv
    acts[...] = pre * jax.nn.sigmoid(pre)
    at = pl.multiple_of(lax.axis_index("batch") * own_images, own_images)
    act = acts[pl.ds(at, own_images), :]
    act_ref[...] = act
    logits = exact(act, w_ref[...], NN) + get(par_ref, 14, 4)
    lead = logits[:, :mid] - logits[:, mid:]
    first, second = jax.nn.sigmoid(lead), jax.nn.sigmoid(-lead)
    weights_ref[:, :mid] = first
    weights_ref[:, mid:] = second
    a = a_ref[...]
    mixed = per_image(first, a) * a[:, :mid] + per_image(second, a) * a[:, mid:]
    mixed_ref[...] = mixed
    mixed_ref.send()
    left, right = split(mixed), (wh_ref[...], wl_ref[...])
    for i, part in enumerate(z_ref.parts):
        rows = slice(part.start, part.start + part.size)
        z_ref.put(i, product([each[rows] for each in left], right, NN))
    z = z_ref[...]
    width = z.shape[1]
    own = wide(own_ref[...], width)
    sums, squares = local_stats(z, own, wide(column_sum(own_ref[...]), width))
    put(tile, 0, sums)
    put(tile, width // 128, squares)
    pay_ref[...] = jnp.broadcast_to(tile[...][None], pay_ref.shape)


def output_kernel(g4_ref, counts_ref, par_ref, own_ref, z_ref, x_ref, cot_ref, *refs):
    slope_refs, (out_ref, grad_ref, stat_ref, slopes_ref, pay_ref, tile) = refs[:-6], refs[-6:]
    width = z_ref.shape[1]
    groups = width // 128
    mean, inv, total = merge_stats(g4_ref[...], counts_ref[...], width)
    put(stat_ref, 0, mean)
    put(stat_ref, groups, inv)
    gain, shift = get(par_ref, 18, groups), get(par_ref, 26, groups)
    flat, cross = 0.0, 0.0
    for i in range(len(z_ref.parts)):
        own = wide(own_ref.chunk(i), width)
        normed = (z_ref.chunk(i) - mean) * inv
        pre = normed * gain + shift + x_ref.chunk(i)
        sigma = jax.nn.sigmoid(pre)
        out_ref.put(i, pre * sigma * own)
        grad = cot_ref.chunk(i) * own * (sigma * (1.0 + pre * (1.0 - sigma)))
        grad_ref.put(i, grad)
        flat = flat + column_sum(grad)
        cross = cross + column_sum(grad * normed)
    put(tile, 0, flat)
    put(tile, groups, cross)
    pay_ref[...] = jnp.broadcast_to(tile[...][None], pay_ref.shape)
    sum_kernel(*slope_refs, slopes_ref)


def mixed_kernel(digit, g5_ref, stat1_ref, stat3_ref, par_ref, own_ref, grad_ref, z_ref, wh_ref, wl_ref, a_ref, weights_ref,
                 w_ref, slope_ref, normed_ref, *refs):
    shares, (dzh_ref, dzl_ref, gm_ref, dsum_ref, grads_ref, slopes_ref, pay_ref, tile) = refs[: digit.size], refs[digit.size :]
    width = z_ref.shape[1]
    mid = gm_ref.shape[1]
    images = weights_ref.shape[0]
    groups = width // 128
    grads_ref[...] = jnp.sum(g5_ref[...], axis=0)
    count = wide(stat1_ref[4:5, :], width)
    mean, inv = get(stat3_ref, 0, groups), get(stat3_ref, groups, groups)
    flat = get(grads_ref, 0, groups) / count
    cross = get(grads_ref, groups, groups) / count
    scale = get(par_ref, 18, groups) * inv
    for i in range(len(z_ref.parts)):
        normed = (z_ref.chunk(i) - mean) * inv
        dz = scale * (grad_ref.chunk(i) - flat - normed * cross) * wide(own_ref.chunk(i), width)
        high, low = split(dz)
        dzh_ref.put(i, high)
        dzl_ref.put(i, low)
        gm_ref[z_ref.parts[i]] = product((high, low), (wh_ref[...], wl_ref[...]), NT)
    gm = gm_ref[...]
    gm_ref.send()
    a = a_ref[...]
    weights = weights_ref[...]
    gate = image_sum(gm * (a[:, :mid] - a[:, mid:]), images)
    dsum = weights[:, :mid] * weights[:, mid:] * gate
    dsum_ref[...] = dsum
    tile[...] = jnp.zeros_like(tile)
    tile[:images, :] = exact(dsum, w_ref[:, :mid] - w_ref[:, mid:], NT)
    slope = slope_ref[...] * jnp.concatenate([gm, gm], axis=1)
    put(tile, 8, column_sum(weights * image_sum(slope, images)))
    put(tile, 12, column_sum(weights * image_sum(slope * normed_ref[...], images)))
    pay_ref[...] = jnp.broadcast_to(tile[...][None], pay_ref.shape)
    digit.gather(shares, slopes_ref)


def expand_grad_kernel(core, mixed_ref, act_ref, dsum_ref, dzh_ref, dzl_ref, keep_ref, send_ref, excite_ref, term):
    left = split(mixed_ref[...].T)
    rows, width = left[0].shape[0], term.shape[1]
    for j in range(term.shape[0] // rows):
        cols = slice(j * width, (j + 1) * width)
        term[j * rows : (j + 1) * rows, :] = product(left, (dzh_ref[:, cols], dzl_ref[:, cols]), NN)
    core.scatter([term], [keep_ref, send_ref])
    excite_ref[...] = exact(act_ref[...], dsum_ref[...], TN)


def turned_rows(left, wh_ref, wl_ref, outs, row, taps):
    return product(left, [ref[row * taps : (row + 1) * taps, outs] for ref in (wh_ref, wl_ref)], NT)


def fold(total, group):
    return moved(total[:, :group], 1) + total[:, group : 2 * group] + moved(total[:, 2 * group :], -1)


def back_kernel(digit, g6_ref, pre_ref, fcn_ref, inv_ref, par_ref, wsq_ref, pooled_ref, stat1_ref, stat2_ref, rows_ref,
                cols_ref, weights_ref, mine_ref, other_ref, own_ref, gm_ref, slope_ref, normed_ref, wh_ref, wl_ref,
                up_ref, down_ref, dzh_ref, dzl_ref, squeeze_ref, gains_ref, fc_ref, gf, owned, slopes):
    images = rows_ref.shape[0]
    tall = dzh_ref.shape[1] - 2
    width = normed_ref.shape[1]
    mid = width // 2
    groups = width // 128
    rows = lax.axis_size("rows")
    shared = g6_ref[...]
    pre = pre_ref[...]
    fcn = fcn_ref[...]
    sigma = jax.nn.sigmoid(pre)
    total = pre.shape[0]
    grad = jnp.sum(shared[:, :images].reshape(rows, total, -1), axis=0) * (sigma * (1.0 + pre * (1.0 - sigma)))
    flat, cross = column_sum(grad), column_sum(grad * fcn)
    fc_ref[0:1, :] = cross
    fc_ref[1:2, :] = flat
    gf[...] = par_ref[12:13, :] * inv_ref[...] * (grad - flat / total - fcn * cross / total)
    at = pl.multiple_of(lax.axis_index("batch") * images, images)
    mine = gf[pl.ds(at, images), :]
    squeeze = exact(pooled_ref[...], mine, TN)
    half_rows = squeeze.shape[0] // 2
    squeeze_ref[:, : squeeze.shape[1]] = squeeze[:half_rows]
    squeeze_ref[:, squeeze.shape[1] :] = squeeze[half_rows:]
    spread = exact(gf[...], wsq_ref[...], NT)
    owned[...] = spread
    own_spread = owned[pl.ds(at, images), :] / pixel_count(rows_ref, cols_ref)
    for flipped, half in enumerate((mine_ref, other_ref)):
        for block in range(half.shape[0] // images):
            here = pl.multiple_of((2 * block + (digit.own() ^ flipped)) * images, images)
            slopes[pl.ds(here, images), :] = half[block * images : (block + 1) * images, :]
    base = jnp.sum(shared[:, 8:], axis=0)
    count = wide(stat1_ref[4:5, :], mid)
    weights = weights_ref[...]
    gm = gm_ref[...]
    shared_part = per_image(own_spread, gm)
    mask = wide(own_ref[...], mid)
    zero = jnp.zeros((images, 16, width), bf16)
    for ref in (dzh_ref, dzl_ref):
        ref[:, 0] = zero
        ref[:, tall + 1] = zero
    for g in range(2):
        outs = slice(g * mid, (g + 1) * mid)
        crosses = slice(width + g * mid, width + (g + 1) * mid)
        half = groups // 2
        flat_two = get(base, g * half, half) + column_sum(spread * slopes[:, outs])
        cross_two = get(base, groups + g * half, half) + column_sum(spread * slopes[:, crosses])
        put(gains_ref, g * half, cross_two)
        put(gains_ref, groups + g * half, flat_two)
        scale = get(par_ref, 4 + g * half, half) * get(stat2_ref, groups + g * half, half)
        upstream = per_image(weights[:, outs], gm) * gm + shared_part
        dz = scale * (upstream * slope_ref[:, outs] - flat_two / count - normed_ref[:, outs] * (cross_two / count)) * mask
        for ref, part in zip((dzh_ref, dzl_ref), split(dz)):
            ref[:, 1 : tall + 1, :, outs] = part.reshape(images, tall, 16, mid)
    dzh_ref.send()
    dzl_ref.send()
    group = up_ref.shape[1] // 2
    for g in range(2):
        outs = slice(g * mid, (g + 1) * mid)
        cols = slice(g * group, (g + 1) * group)
        for side, row, tap in ((up_ref, 1, 0), (down_ref, tall, 2)):
            left = [ref[:, row, :, outs].reshape(-1, mid) for ref in (dzh_ref, dzl_ref)]
            side[:, cols] = fold(turned_rows(left, wh_ref, wl_ref, outs, tap, 3 * group), group)


def group_kernel(core, dzh_ref, dzl_ref, squeeze_ref, excite_ref, th_ref, tl_ref, keep_ref, send_ref, out_ref):
    tall = dzh_ref.shape[1] - 2
    mid = dzh_ref.shape[3] // 2
    taps = th_ref.shape[1]
    for g in range(2):
        outs = slice(g * mid, (g + 1) * mid)
        right = [ref[:, 1 : tall + 1, :, outs].reshape(-1, mid) for ref in (dzh_ref, dzl_ref)]
        out_ref[g * taps : (g + 1) * taps, :] = product((th_ref.chunk(g)[0], tl_ref.chunk(g)[0]), right, NN)
    inter = excite_ref.shape[0]
    out_ref[2 * taps : 2 * taps + inter, :] = excite_ref[...]
    out_ref[2 * taps + inter :, :] = squeeze_ref[...]
    core.scatter([out_ref], [keep_ref, send_ref])


def input_grad_kernel(par_ref, stat_ref, dsum_ref, z_ref, own_ref, above_ref, below_ref, dzh_ref, dzl_ref, wh_ref, wl_ref,
                      dy_ref, pay_ref, tile, place):
    images = dsum_ref.shape[0]
    width = z_ref.shape[1]
    group = width // 2
    tall = dzh_ref.shape[1] - 2
    half = dzh_ref.shape[3] // 2
    grads = []
    for g in range(2):
        outs = slice(g * half, (g + 1) * half)
        total = None
        for row in range(3):
            left = [ref[:, 2 - row : 2 - row + tall, :, outs].reshape(-1, half) for ref in (dzh_ref, dzl_ref)]
            term = turned_rows(left, wh_ref, wl_ref, outs, row, 3 * group)
            total = term if total is None else total + term
        grads.append(fold(total, group))
    place[...] = jnp.concatenate(grads, axis=1).reshape(place.shape)
    place[:, 0] += above_ref[...].reshape(images, 16, width)
    place[:, tall - 1] += below_ref[...].reshape(images, 16, width)
    grad = place[...].reshape(-1, width)
    mean, inv = get(stat_ref, 0, 2), get(stat_ref, 2, 2)
    normed = (z_ref[...] - mean) * inv
    y = normed * get(par_ref, 0, 2) + get(par_ref, 2, 2)
    sigma = jax.nn.sigmoid(y)
    dy = grad * wide(own_ref[...], width) * (sigma * (1.0 + y * (1.0 - sigma)))
    dy_ref[...] = dy
    dy_ref.send()
    tile[...] = jnp.zeros_like(tile)
    put(tile, 0, column_sum(dy * normed))
    put(tile, 2, column_sum(dy))
    put(tile, 4, column_sum(dsum_ref[...]))
    pay_ref[...] = jnp.broadcast_to(tile[...][None], pay_ref.shape)


def final_kernel(core, g7_ref, par_ref, stat_ref, dy_ref, z_ref, own_ref, th_ref, tl_ref,
                 keep_ref, send_ref, dzh_ref, dzl_ref, gains_ref, term):
    width = z_ref.shape[1]
    gains_ref[...] = jnp.sum(g7_ref[...], axis=0)
    cross, flat = get(gains_ref, 0, 2), get(gains_ref, 2, 2)
    count = wide(stat_ref[4:5, :], width)
    mean, inv = get(stat_ref, 0, 2), get(stat_ref, 2, 2)
    normed = (z_ref[...] - mean) * inv
    scale = get(par_ref, 0, 2) * inv
    dz = scale * (dy_ref[...] - flat / count - normed * (cross / count)) * wide(own_ref[...], width)
    high, low = split(dz)
    dzh_ref[...] = high
    dzl_ref[...] = low
    term[...] = product((th_ref[...], tl_ref[...]), (high, low), NN)
    core.scatter([term], [keep_ref, send_ref])


def images_kernel(dzh_ref, dzl_ref, wh_ref, wl_ref, grad_ref, out_ref):
    for i in range(len(grad_ref.parts)):
        left = [ref.chunk(i) for ref in (dzh_ref, dzl_ref)]
        out_ref.put(i, product(left, (wh_ref[...], wl_ref[...]), NT) + grad_ref.chunk(i))


def deal_kernel(plan, count, *refs):
    outs = list(refs[count:])
    for digit, stretches in plan:
        own = digit.own()
        for j in range(digit.size):
            out, at = outs.pop(0), 0
            for inputs, first, rows in stretches:
                each = rows // digit.size
                here = pl.ds(pl.multiple_of(first + (own ^ j) * each, 8), each)
                total = refs[inputs[0]][here, :]
                for k in inputs[1:]:
                    total = total + refs[k][here, :]
                out[at : at + each, :] = total
                at += each


def deal(plan, ins, after=()):
    width = ins[0].shape[1]
    outs = []
    for digit, stretches in plan:
        rows = sum(rows for _, _, rows in stretches) // digit.size
        outs += [((rows, width), f32)] * digit.size
    return local_call(functools.partial(deal_kernel, plan, len(ins)), outs, ins, after=after)


def stack_kernel(stretches, *refs):
    refs, out = refs[:-1], refs[-1]
    at = 0
    for inputs, first, rows in stretches:
        each = rows // out.shape[0]
        for d in range(out.shape[0]):
            here = slice(first + d * each, first + (d + 1) * each)
            total = refs[inputs[0]][here, :]
            for k in inputs[1:]:
                total = total + refs[k][here, :]
            out[d, at : at + each, :] = total
        at += each


def extra_pieces(extra, stacked):
    if extra.size == 1:
        return [stacked]
    total = local_call(lambda ref, out: out.__setitem__(Ellipsis, jnp.sum(ref[...], axis=0)), [(stacked.shape[1:], f32)], [stacked])[0]
    return extra.send([total] * extra.size)


def spread_kernel(count, *refs):
    if count == 1:
        total = jnp.sum(refs[0][...], axis=0)
    else:
        total = refs[0][...]
        for ref in refs[1:-1]:
            total = total + ref[...]
    refs[-1][...] = jnp.broadcast_to(total[None], refs[-1].shape)


def halve_kernel(blocks, whole_ref, *outs):
    each = whole_ref.shape[0] // blocks
    half = each // 2
    for k in range(blocks):
        for i, out in enumerate(outs):
            out[k * half : (k + 1) * half, :] = whole_ref[k * each + i * half : k * each + (i + 1) * half, :]


def pair_kernel(digits, *refs):
    outs = refs[4:]
    for i, digit in enumerate(digits):
        digit.gather(refs[2 * i : 2 * i + 2], outs[i] if len(outs) == 2 else outs[0].at[pl.ds(i * 2 * refs[0].shape[0], 2 * refs[0].shape[0])])


def last_kernel(core, expand_map, group_map, mine_ref, other_ref, expand_ref, group_ref, excite_ref, squeeze_ref, whole):
    core.gather([mine_ref, other_ref], whole)
    taps, mid = group_ref.shape[0], whole.shape[1]
    inter = squeeze_ref.shape[1]
    tall = expand_ref.shape[0]
    places = [
        (taps, lambda rows, value: group_ref.__setitem__((rows, slice(0, mid)), value)),
        (taps, lambda rows, value: group_ref.__setitem__((rows, slice(mid, 2 * mid)), value)),
        (inter, lambda rows, value: excite_ref.__setitem__((rows, slice(0, mid)), value)),
        (inter, lambda rows, value: squeeze_put(squeeze_ref, rows, value)),
    ]
    for at, first, rows in expand_map:
        j, m = first // tall, first % tall
        expand_ref[m : m + rows, j * mid : (j + 1) * mid] = whole[at : at + rows, :]
    for at, first, rows in group_map:
        base = 0
        for length, store in places:
            low, high = max(first, base), min(first + rows, base + length)
            if low < high:
                store(slice(low - base, high - base), whole[at + low - first : at + high - first, :])
            base += length
    excite_ref[:, mid:] = -excite_ref[:, :mid]


def squeeze_put(squeeze_ref, rows, value):
    half = squeeze_ref.shape[0] // 2
    width = squeeze_ref.shape[1]
    squeeze_ref[rows, :] = value[:, :width]
    squeeze_ref[slice(half + rows.start, half + rows.stop), :] = value[:, width:]


def on_device(
    images,
    w_reduce,
    gain_one,
    shift_one,
    w_group,
    gain_two,
    shift_two,
    w_squeeze,
    gain_fc,
    shift_fc,
    w_excite,
    excite_bias,
    w_expand,
    gain_three,
    shift_three,
    valid_rows,
    valid_cols,
    cotangent,
):
    count, tall, broad, chan = images.shape
    mid = w_reduce.shape[1]
    inter = w_squeeze.shape[1]
    duo = 2 * mid
    taps = 9 * mid // 2
    cells = count * tall * broad
    longer = count * (tall + 2) * broad
    edge = count * broad
    devices = lax.axis_size("rows") * lax.axis_size("batch")
    all_images = count * lax.axis_size("batch")
    x = images.reshape(cells, chan)
    cot = cotangent.reshape(cells, chan)
    pay8 = ((devices, 8, 128), f32)
    pay16 = ((devices, 16, 128), f32)
    tile8 = pltpu.VMEM((8, 128), f32)
    tile16 = pltpu.VMEM((16, 128), f32)
    twice = lambda *shape: [(shape, bf16)] * 2
    flat_w = w_group.reshape(taps, duo)
    vectors = (gain_one, shift_one, gain_two, shift_two, gain_fc, shift_fc, excite_bias, gain_three, shift_three)
    core, line, depth, extra = digits()

    z_one, ext, own, first, last, wrh, wrl, pay = call(
        reduce_kernel,
        [((cells, mid), f32), ((count, tall + 2, broad, 128), f32), ((cells, 128), f32), ((edge, mid), f32),
         ((edge, mid), f32), *twice(chan, mid), pay8],
        [valid_rows, valid_cols, w_reduce, x],
        [tile8],
        chunks={3: 2},
        near_outs=(3, 4, 7),
    )
    g1 = share(pay)
    above, below = halos(first, last)
    wgh, wgl, weh, wel, par = call(
        parts_kernel,
        [*twice(taps, duo), *twice(mid, chan), ((40, 128), f32)],
        [flat_w, w_expand, *[v.reshape(1, -1) for v in vectors]],
        chunks={0: 4, 1: 2},
        out_chunks={0: 4, 1: 4, 2: 2, 3: 2},
        after=[z_one],
    )
    z_two, a_one, stat1, counts, pay = call(
        conv_kernel,
        [((cells, duo), f32), ((longer, mid), f32), ((8, 128), f32), ((devices, 128), f32), pay8],
        [g1, par, z_one, ext, above, below, own, wgh, wgl],
        [tile8, pltpu.VMEM((count, tall + 2, broad, mid), f32)],
        near=(0, 4, 5),
        near_outs=(4,),
    )
    g2 = share(pay)
    xth, xtl = call(turned_kernel, twice(chan, cells), [x], after=[stat1])
    a_two, stat2, pooled, pay = call(
        pool_kernel,
        [((cells, duo), f32), ((8, 128), f32), ((count, mid), f32), ((devices, count, inter), f32)],
        [g2, counts, par, valid_rows, valid_cols, z_two, own, w_squeeze],
        chunks={5: 2, 6: 2},
        out_chunks={0: 2},
        after=[xth],
        near=(0,),
        near_outs=(3,),
    )
    g3 = share(pay)
    slope_two, normed_two, slopes = call(
        slope_kernel,
        [((cells, duo), f32), ((cells, duo), f32), ((count, 2 * duo), f32)],
        [stat2, par, valid_rows, valid_cols, own, z_two],
        chunks={4: 2, 5: 2},
        out_chunks={0: 2, 1: 2},
        near_outs=(2,),
    )
    mixed, z_three, weights, fc_normed, fc_pre, fc_act, fc_inv, pay = call(
        expand_kernel,
        [((cells, mid), f32), ((cells, chan), f32), ((count, duo), f32), ((all_images, inter), f32),
         ((all_images, inter), f32), ((count, inter), f32), ((1, inter), f32), pay16],
        [g3, par, w_excite, a_two, weh, wel, own],
        [tile16, pltpu.VMEM((all_images, inter), f32)],
        out_chunks={1: 2},
        after=[slopes],
        near=(0,),
        near_outs=(7,),
    )
    g4 = share(pay)
    slopes = line.send([slopes] * line.size)
    block_out, grad_pre, stat3, slopes, pay = call(
        output_kernel,
        [((cells, chan), f32), ((cells, chan), f32), ((16, 128), f32), ((count, 2 * duo), f32), pay16],
        [g4, counts, par, own, z_three, x, cot, *slopes],
        [tile16],
        chunks={3: 4, 4: 4, 5: 4, 6: 4},
        out_chunks={0: 4, 1: 4},
        near=(0, *range(7, 7 + line.size)),
        near_outs=(3, 4),
    )
    g5 = share(pay)
    slopes = depth.send([slopes] * depth.size)
    tph, tpl = call(functools.partial(taps_kernel, count), twice(2, taps, cells), [a_one], out_chunks={0: 2, 1: 2}, after=[stat3])
    dzh, dzl, grad_mixed, dsum, grads_three, slopes, pay = call(
        functools.partial(mixed_kernel, depth),
        [*twice(cells, chan), ((cells, mid), f32), ((count, mid), f32),
         ((16, 128), f32), ((depth.size * count, 2 * duo), f32), pay16],
        [g5, stat1, stat3, par, own, grad_pre, z_three, weh, wel, a_two, weights, w_excite, slope_two, normed_two, *slopes],
        [tile16],
        chunks={4: 2, 5: 2, 6: 2},
        out_chunks={0: 2, 1: 2},
        after=[tph],
        near=(0, *range(14, 14 + depth.size)),
        near_outs=(5, 6),
    )
    g6 = share(pay)
    *expand_sum, excite_term = call(
        functools.partial(expand_grad_kernel, core),
        [*core.outs(mid * chan // mid, mid), ((inter, mid), f32)],
        [mixed, fc_act, dsum, dzh, dzl],
        [pltpu.VMEM((chan, mid), f32)],
    )
    if extra.size > 1:
        slopes = gather_more(extra, extra.send([slopes] * extra.size))
    slopes = core.send([slopes] * 2)
    packed = 2 * taps + 2 * inter
    up, down, dzh, dzl, squeeze_term, grads_two, grads_fc = call(
        functools.partial(back_kernel, core),
        [((edge, mid), f32), ((edge, mid), f32), *twice(count, tall + 2, broad, duo), ((inter, mid), f32),
         ((8, 128), f32), ((2, inter), f32)],
        [g6, fc_pre, fc_normed, fc_inv, par, w_squeeze, pooled, stat1, stat2, valid_rows, valid_cols, weights, *slopes, own,
         grad_mixed, slope_two, normed_two, wgh, wgl],
        [pltpu.VMEM((all_images, inter), f32), pltpu.VMEM((all_images, mid), f32), pltpu.VMEM((all_images, 2 * duo), f32)],
        after=[excite_term],
        near=(0, 12, 13),
        near_outs=(0, 1),
    )
    above, below = halos(up, down)
    group_sum = call(
        functools.partial(group_kernel, core),
        core.outs(packed, mid),
        [dzh, dzl, squeeze_term, excite_term, tph, tpl],
        [pltpu.VMEM((packed, mid), f32)],
        chunks={4: 2, 5: 2},
        near_outs=(0, 1),
    )
    expand_sum = core.send(expand_sum)
    group_sum = core.send([group_sum[0], gate(group_sum[1], [above, below])])
    first_bit, second_bit = line.bits()
    some, more = expand_sum[0].shape[0] // 2, group_sum[0].shape[0] // 2
    both_of = lambda start, a, b: [((0, 1), start * a, a), ((2, 3), start * b, b)]
    first_half = lambda digit: (digit, both_of(0, some, more))
    second_half = lambda digit: (digit, both_of(1, some, more))
    keep_a, send_a, keep_b, send_b = deal(
        [first_half(first_bit), second_half(second_bit)], [*expand_sum, *group_sum]
    )
    come_a, come_b = first_bit.send([keep_a, send_a]), second_bit.send([keep_b, send_b])
    dy_one, pay = call(
        input_grad_kernel,
        [((cells, mid), f32), pay8],
        [par, stat1, dsum, z_one, own, above, below, dzh, dzl, wgh, wgl],
        [tile8, pltpu.VMEM((count, tall, broad, mid), f32)],
        after=[keep_a],
        near=(5, 6),
        near_outs=(1,),
    )
    g7 = share(pay)
    some, more = some // 2, more // 2
    turn = lambda k: [((k, k + 1), 0, some), ((k, k + 1), some, more)]
    keep_a, send_a, keep_b, send_b = deal([(second_bit, turn(0)), (first_bit, turn(2))], [*come_a, *come_b], after=[dy_one])
    *reduce_sum, dzh, dzl, grads_one = call(
        functools.partial(final_kernel, core),
        [*core.outs(chan, mid), *twice(cells, mid), ((8, 128), f32)],
        [g7, par, stat1, dy_one, z_one, own, xth, xtl],
        [pltpu.VMEM((chan, mid), f32)],
        after=[keep_a],
        near=(0,),
        near_outs=(0, 1),
    )
    come_a, come_b = second_bit.send([keep_a, send_a]), first_bit.send([keep_b, send_b])
    some, more = some // 2, more // 2
    stretches = turn(0) + turn(2)
    (joined,) = local_call(
        functools.partial(stack_kernel, stretches),
        [((depth.size, (some + more) * 2 // depth.size, mid), f32)],
        [*come_a, *come_b],
        after=[dzh],
    )
    reduce_sum[1] = gate(reduce_sum[1], [joined])
    joined = depth.trade(joined)
    low_bit, high_bit = depth.bits()
    reduce_sum = scatter_more(second_bit, core.send(reduce_sum))
    (grad_images,) = call(
        images_kernel,
        [((cells, chan), f32)],
        [dzh, dzl, wrh, wrl, grad_pre],
        chunks={0: 2, 1: 2, 4: 2},
        out_chunks={0: 2},
        after=[reduce_sum[0]],
    )
    reduce_sum = scatter_more(first_bit, second_bit.send(reduce_sum), after=[grad_images])
    (joined,) = local_call(
        functools.partial(spread_kernel, extra.size), [(joined.shape, f32)], extra_pieces(extra, joined), after=[reduce_sum[0]]
    )
    joined = depth.trade(joined)
    reduce_sum = scatter_more(high_bit, first_bit.send(reduce_sum))
    rows_in = joined.shape[0] * joined.shape[1]
    half_a, half_b = local_call(
        functools.partial(halve_kernel, depth.size), [((rows_in // 2, mid), f32)] * 2, [joined.reshape(-1, mid)], after=[reduce_sum[0]]
    )
    reduce_sum = scatter_more(low_bit, high_bit.send(reduce_sum), after=[half_a])
    half_a, half_b = local_call(
        functools.partial(pair_kernel, [second_bit, first_bit]),
        [((rows_in, mid), f32)] * 2,
        [*second_bit.send([half_a] * 2), *first_bit.send([half_b] * 2)],
        after=[reduce_sum[0]],
    )
    reduce_sum = finish_sum(low_bit.send(reduce_sum), extra, after=[half_a])
    reduce_sum = gather_more(depth, depth.send([reduce_sum] * depth.size))
    (joined,) = local_call(
        functools.partial(pair_kernel, [first_bit, second_bit]),
        [((4 * rows_in, mid), f32)],
        [*first_bit.send([half_a] * 2), *second_bit.send([half_b] * 2)],
        after=[reduce_sum],
    )
    reduce_sum = gather_more(line, line.send([reduce_sum] * line.size), after=[joined])
    expand_map, group_map = [], []
    at = 0
    some, more = some // depth.size, more // depth.size
    for half in range(core.size):
        for part in range(2):
            for outer in range(2):
                for inner in range(2):
                    for deep in range(depth.size):
                        block = (((half * 2 + part) * 2 + outer) * 2 + inner) * depth.size + deep
                        expand_map.append((at, block * some, some))
                        group_map.append((at + some, block * more, more))
                        at += some + more
    grad_w_expand, grad_w_group, grad_w_excite, grad_w_squeeze = local_call(
        functools.partial(last_kernel, core, expand_map, group_map),
        [((mid, chan), f32), ((taps, duo), f32), ((inter, duo), f32), ((mid, inter), f32)],
        core.send([joined] * 2),
        [pltpu.VMEM((chan + packed, mid), f32)],
    )
    grad_w_reduce = gather_more(core, core.send([reduce_sum] * 2))
    grads_one = grads_one.reshape(-1)
    grads_two = grads_two.reshape(-1)
    grads_three = grads_three.reshape(-1)
    grad_bias = grads_one[duo : duo + mid]
    return (
        block_out.reshape(images.shape),
        grad_images.reshape(images.shape),
        grad_w_reduce,
        grads_one[:mid],
        grads_one[mid:duo],
        grad_w_group.reshape(w_group.shape),
        grads_two[:duo],
        grads_two[duo:],
        grad_w_squeeze,
        grads_fc[0],
        grads_fc[1],
        grad_w_excite,
        jnp.concatenate([grad_bias, -grad_bias]),
        grad_w_expand,
        grads_three[chan:],
        grads_three[:chan],
    )


def solution(mesh):
    maps = P("batch", "rows", None, None)
    return jax.shard_map(
        on_device,
        mesh=mesh,
        in_specs=(maps,) + (P(),) * 14 + (P("batch", None), P("batch", None), maps),
        out_specs=(maps, maps) + (P(),) * 14,
        check_vma=False,
    )
```

```python
import functools

import jax
import jax.numpy as jnp
from jax import lax
from jax.experimental import pallas as pl
from jax.experimental.pallas import tpu as pltpu
from jax.sharding import PartitionSpec as P

epsilon = 1e-05
f32 = jnp.float32
bf16 = jnp.bfloat16
highest = lax.Precision.HIGHEST
both = ("rows", "batch")
NN = ((1,), (0,))
NT = ((1,), (1,))
TN = ((0,), (0,))


def split(values):
    high = values.astype(bf16)
    return high, (values - high.astype(f32)).astype(bf16)


def dot(left, right, dims):
    return lax.dot_general(left, right, (dims, ((), ())), preferred_element_type=f32)


def product(left, right, dims):
    return dot(left[0], right[0], dims) + (
        dot(left[0], right[1], dims) + dot(left[1], right[0], dims)
    )


def exact(left, right, dims):
    return lax.dot_general(
        left, right, (dims, ((), ())), preferred_element_type=f32, precision=highest
    )


def put(tile, row, vector):
    for j in range(vector.shape[1] // 128):
        tile[row + j : row + j + 1, :] = vector[:, j * 128 : (j + 1) * 128]


def get(tile, row, count):
    return jnp.concatenate([tile[row + j : row + j + 1, :] for j in range(count)], axis=1)


def wide(mask, width):
    return jnp.concatenate([mask] * (width // 128), axis=1)


def column_sum(values):
    return jnp.sum(values, axis=0, keepdims=True)


def image_sum(values, images):
    return jnp.sum(values.reshape(images, values.shape[0] // images, values.shape[1]), axis=1)


def per_image(vector, values):
    count, width = vector.shape
    each = values.shape[0] // count
    return jnp.broadcast_to(vector[:, None, :], (count, each, width)).reshape(values.shape[0], width)


def merge_stats(gathered, counts, width):
    groups = width // 128
    own = jnp.maximum(counts, 1.0)
    total = jnp.sum(counts, axis=0)
    means, inverses = [], []
    for j in range(groups):
        sums = gathered[:, j, :]
        squares = gathered[:, groups + j, :]
        mean = jnp.sum(sums, axis=0, keepdims=True) / total
        shift = sums / own - mean
        spread = jnp.sum(squares + counts * shift * shift, axis=0, keepdims=True) / total
        means.append(mean)
        inverses.append(lax.rsqrt(spread + epsilon))
    return jnp.concatenate(means, axis=1), jnp.concatenate(inverses, axis=1), total


def local_stats(values, mask, count):
    sums = column_sum(values * mask)
    centered = values - sums / jnp.maximum(count, 1.0)
    return sums, column_sum(centered * centered * mask)


def own_rows(extended, images):
    rows, width = extended.shape
    tall = rows // images // 16
    return extended.reshape(images, tall, 16, width)[:, 1 : tall - 1].reshape(-1, width)


class In:
    def __init__(self, source, target, sems, chunks):
        self.ref, self.shape, self.dtype = target, target.shape, target.dtype
        rows = self.shape[0] // chunks
        self.parts = [pl.ds(i * rows, rows) for i in range(chunks)]
        self.copies = [
            pltpu.make_async_copy(source.at[part], target.at[part], sems.at[i])
            for i, part in enumerate(self.parts)
        ]
        self.due = list(range(chunks))

    def start(self):
        for copy in self.copies:
            copy.start()

    def ready(self):
        while self.due:
            self.copies[self.due.pop(0)].wait()
        return self.ref

    def chunk(self, i):
        if i in self.due:
            self.due.remove(i)
            self.copies[i].wait()
        return self.ref[self.parts[i]]

    def __getitem__(self, index):
        return self.ready()[index]


class Near:
    def __init__(self, ref):
        self.ref, self.shape, self.dtype = ref, ref.shape, ref.dtype

    def start(self, i=None):
        pass

    ready = send = start

    def finish(self):
        pass

    def __getitem__(self, index):
        return self.ref[index]

    def __setitem__(self, index, value):
        self.ref[index] = value


class Out:
    def __init__(self, source, target, sems, chunks):
        self.ref, self.shape, self.dtype = source, source.shape, source.dtype
        rows = self.shape[0] // chunks
        self.parts = [pl.ds(i * rows, rows) for i in range(chunks)]
        self.copies = [
            pltpu.make_async_copy(source.at[part], target.at[part], sems.at[i])
            for i, part in enumerate(self.parts)
        ]
        self.sent = set()

    def send(self, i=None):
        for k in range(len(self.copies)) if i is None else [i]:
            if k not in self.sent:
                self.sent.add(k)
                self.copies[k].start()

    def finish(self):
        self.send()
        for copy in self.copies:
            copy.wait()

    def put(self, i, value):
        self.ref[self.parts[i]] = value
        self.send(i)

    def __getitem__(self, index):
        return self.ref[index]

    def __setitem__(self, index, value):
        self.ref[index] = value


def call(body, outs, ins, scratch=(), limit=54, chunks=None, out_chunks=None, after=(), beside=(), near=(), near_outs=()):
    chunks, out_chunks = chunks or {}, out_chunks or {}
    n, m, k = len(ins), len(outs), len(after) + len(beside)
    far = [i for i in range(n) if i not in near]
    far_outs = [i for i in range(m) if i not in near_outs]
    parts = [chunks.get(i, 1) for i in far] + [out_chunks.get(i, 1) for i in far_outs]

    def inner(*refs):
        sources, targets, local = refs[:n], refs[n + k : n + k + m], refs[n + k + m :]
        held, sems, rest = local[: len(parts)], local[len(parts) : 2 * len(parts)], local[2 * len(parts) :]
        given = [Near(ref) for ref in sources]
        for at, i in enumerate(far):
            given[i] = In(sources[i], held[at], sems[at], parts[at])
        made = [Near(ref) for ref in targets]
        for at, i in enumerate(far_outs, len(far)):
            made[i] = Out(held[at], targets[i], sems[at], parts[at])
        for each in given:
            each.start()
        body(*given, *made, *rest)
        for each in given:
            each.ready()
        for each in made:
            each.send()
        for each in made:
            each.finish()

    space = lambda count, places: [pl.BlockSpec(memory_space=pltpu.VMEM if i in places else pltpu.HBM) for i in range(count)]
    return pl.pallas_call(
        inner,
        out_shape=[(pltpu.VMEM if i in near_outs else pltpu.HBM)(*out) for i, out in enumerate(outs)],
        in_specs=space(n, near) + space(len(after), ()) + space(len(beside), range(len(beside))),
        out_specs=space(m, near_outs),
        scratch_shapes=[
            *[pltpu.VMEM(ins[i].shape, ins[i].dtype) for i in far],
            *[pltpu.VMEM(*outs[i]) for i in far_outs],
            *[pltpu.SemaphoreType.DMA((k,)) for k in parts],
            *scratch,
        ],
        compiler_params=pltpu.CompilerParams(vmem_limit_bytes=limit * 2**20),
        cost_estimate=pl.CostEstimate(flops=1, bytes_accessed=1, transcendentals=0),
    )(
        *[pltpu.with_memory_space_constraint(a, pltpu.VMEM if i in near else pltpu.HBM) for i, a in enumerate(ins)],
        *[pltpu.with_memory_space_constraint(a, pltpu.HBM) for a in after],
        *[pltpu.with_memory_space_constraint(a, pltpu.VMEM) for a in beside],
    )


def local_call(body, outs, ins, scratch=(), limit=16, after=(), beside=()):
    n, k = len(ins), len(after) + len(beside)

    def inner(*refs):
        body(*refs[:n], *refs[n + k :])

    spec = lambda space, count: [pl.BlockSpec(memory_space=space)] * count
    return pl.pallas_call(
        inner,
        out_shape=[pltpu.VMEM(*out) for out in outs],
        in_specs=spec(pltpu.VMEM, n) + spec(pltpu.HBM, len(after)) + spec(pltpu.VMEM, len(beside)),
        out_specs=spec(pltpu.VMEM, len(outs)),
        scratch_shapes=list(scratch),
        compiler_params=pltpu.CompilerParams(vmem_limit_bytes=limit * 2**20),
        cost_estimate=pl.CostEstimate(flops=1, bytes_accessed=1, transcendentals=0),
    )(
        *[pltpu.with_memory_space_constraint(a, pltpu.VMEM) for a in ins],
        *[pltpu.with_memory_space_constraint(a, pltpu.HBM) for a in after],
        *[pltpu.with_memory_space_constraint(a, pltpu.VMEM) for a in beside],
    )


def share(tile):
    return lax.all_to_all(tile, both, 0, 0)


def halos(first, last):
    count = lax.axis_size("rows")
    above = lax.ppermute(last, "rows", [(i, i + 1) for i in range(count - 1)])
    below = lax.ppermute(first, "rows", [(i + 1, i) for i in range(count - 1)])
    return above, below


def flip(values, axis, bits):
    return lax.ppermute(values, axis, [(i, i ^ bits) for i in range(lax.axis_size(axis))])


class Digit:
    def __init__(self, axis, unit, size):
        self.axis, self.unit, self.size = axis, unit, size

    def own(self):
        return lax.axis_index(self.axis) // self.unit % self.size

    def send(self, pieces):
        return [pieces[0]] + [flip(pieces[j], self.axis, j * self.unit) for j in range(1, self.size)]

    def bits(self):
        return [Digit(self.axis, self.unit << i, 2) for i in range(self.size.bit_length() - 1)]

    def trade(self, stacked):
        count = lax.axis_size(self.axis)
        span = self.unit * self.size
        starts = [high + low for high in range(0, count, span) for low in range(self.unit)]
        groups = [[start + self.unit * d for d in range(self.size)] for start in starts]
        return lax.all_to_all(stacked, self.axis, 0, 0, axis_index_groups=groups)

    def scatter(self, parts, outs):
        size = outs[0].shape[0]
        own = self.own()
        for j, out in enumerate(outs):
            at = pl.ds(pl.multiple_of((own ^ j) * size, 8), size)
            total = parts[0][at, :]
            for part in parts[1:]:
                total = total + part[at, :]
            out[...] = total

    def gather(self, pieces, out):
        size = pieces[0].shape[0]
        own = self.own()
        for j, piece in enumerate(pieces):
            out[pl.ds(pl.multiple_of((own ^ j) * size, 8), size), :] = piece[...]

    def outs(self, rows, width):
        return [((rows // self.size, width), f32)] * self.size


def digits():
    rows, batch = lax.axis_size("rows"), lax.axis_size("batch")
    depth = min(4, batch // 2)
    return Digit("batch", 1, 2), Digit("rows", 1, rows), Digit("batch", 2, depth), Digit("batch", 2 * depth, batch // (2 * depth))


def gate(value, beside):
    return pl.pallas_call(
        lambda *refs: None,
        out_shape=pltpu.VMEM(value.shape, value.dtype),
        in_specs=[pl.BlockSpec(memory_space=pltpu.VMEM)] * (1 + len(beside)),
        out_specs=pl.BlockSpec(memory_space=pltpu.VMEM),
        input_output_aliases={0: 0},
        cost_estimate=pl.CostEstimate(flops=1, bytes_accessed=1, transcendentals=0),
    )(*[pltpu.with_memory_space_constraint(a, pltpu.VMEM) for a in (value, *beside)])


def scatter_kernel(digit, count, *refs):
    digit.scatter(refs[:count], refs[count:])


def sum_kernel(*refs):
    total = refs[0][...]
    for ref in refs[1:-1]:
        total = total + ref[...]
    refs[-1][...] = total


def gather_kernel(digit, *refs):
    digit.gather(refs[:-1], refs[-1])


def scatter_more(digit, pieces, **order):
    rows, width = pieces[0].shape
    body = functools.partial(scatter_kernel, digit, len(pieces))
    return local_call(body, digit.outs(rows, width), pieces, **order)


def add_up(pieces, **order):
    return local_call(sum_kernel, [(pieces[0].shape, f32)], pieces, **order)[0]


def finish_sum(pieces, extra, **order):
    total = add_up(pieces, **order)
    if extra.size > 1:
        total = add_up(extra.send([total] * extra.size))
    return total


def gather_more(digit, pieces, **order):
    rows, width = pieces[0].shape
    return local_call(functools.partial(gather_kernel, digit), [((rows * digit.size, width), f32)], pieces, **order)[0]


def reduce_kernel(rows_ref, cols_ref, w_ref, x_ref, z_ref, ext_ref, own_ref, first_ref, last_ref, pay_ref,
                  tile):
    images = rows_ref.shape[0]
    tall = x_ref.shape[0] // images // 16
    shape = (images, tall + 2, 16, 16)
    start = lax.axis_index("rows") * tall - 1
    lane = lax.broadcasted_iota(jnp.int32, shape, 3).reshape(-1, 16)
    at_row = lax.broadcasted_iota(jnp.int32, shape, 1).reshape(-1, 16) + start
    at_col = lax.broadcasted_iota(jnp.int32, shape, 2).reshape(-1, 16)
    row_valid = per_image(rows_ref[...].astype(f32), lane)
    col_valid = per_image(cols_ref[...].astype(f32), lane)
    in_row = jnp.sum(jnp.where(lane == at_row, row_valid, 0.0), axis=1, keepdims=True)
    in_col = jnp.sum(jnp.where(lane == at_col, col_valid, 0.0), axis=1, keepdims=True)
    mask = jnp.broadcast_to(in_row * in_col, (in_row.shape[0], 128)).reshape(ext_ref.shape)
    ext_ref[...] = mask
    own = mask[:, 1 : tall + 1].reshape(-1, 128)
    own_ref[...] = own
    weight = split(w_ref[...])
    for i in range(len(x_ref.parts)):
        z_ref[x_ref.parts[i]] = product(split(x_ref.chunk(i)), weight, NN)
    z = z_ref[...]
    edges = z.reshape(images, tall, 16, -1)
    first_ref[...] = edges[:, 0].reshape(first_ref.shape)
    last_ref[...] = edges[:, tall - 1].reshape(last_ref.shape)
    for each in (first_ref, last_ref, z_ref, ext_ref, own_ref):
        each.send()
    count = column_sum(own)
    sums, squares = local_stats(z, wide(own, z.shape[1]), wide(count, z.shape[1]))
    tile[...] = jnp.zeros_like(tile)
    put(tile, 0, sums)
    put(tile, 2, squares)
    put(tile, 4, count)
    pay_ref[...] = jnp.broadcast_to(tile[...][None], pay_ref.shape)


def parts_kernel(wg_ref, we_ref, wr_ref, *refs):
    vectors, (wgh_ref, wgl_ref, weh_ref, wel_ref, wrh_ref, wrl_ref, par_ref) = refs[:-7], refs[-7:]
    row = 0
    for vector in vectors:
        put(par_ref, row, vector[...])
        row += vector.shape[1] // 128
    for source, high_ref, low_ref in ((wg_ref, wgh_ref, wgl_ref), (we_ref, weh_ref, wel_ref), (wr_ref, wrh_ref, wrl_ref)):
        for i in range(len(source.parts)):
            high, low = split(source.chunk(i))
            high_ref.put(i, high)
            low_ref.put(i, low)


def turned_kernel(x_ref, high_ref, low_ref):
    high_ref[...], low_ref[...] = split(x_ref[...].T)


def moved(values, step):
    count = values.shape[0]
    at = lax.broadcasted_iota(jnp.int32, values.shape, 0) & 15
    if step == 0:
        return values
    if step > 0:
        return jnp.where(at < 15, pltpu.roll(values, count - 1, 0), 0.0)
    return jnp.where(at > 0, pltpu.roll(values, 1, 0), 0.0)


def window(extended, images, row, width):
    tall = extended.shape[0] // images // 16
    cells = extended.reshape(images, tall, 16, extended.shape[1])
    return cells[:, row : row + tall - 2, :, width].reshape(images * (tall - 2) * 16, -1)


def extend(place, cells, above, below):
    images, tall, broad, width = place.shape
    place[:, 1 : tall - 1] = cells[...].reshape(images, tall - 2, broad, width)
    place[:, 0] = above[...].reshape(images, broad, width)
    place[:, tall - 1] = below[...].reshape(images, broad, width)
    return place[...].reshape(-1, width)


def conv_kernel(g1_ref, par_ref, z_ref, ext_ref, above_ref, below_ref, own_ref, wh_ref, wl_ref,
                z2_ref, a_ref, stat_ref, counts_ref, pay_ref, tile, zext):
    images = zext.shape[0]
    tall = zext.shape[1] - 2
    width = z_ref.shape[1]
    group = width // 2
    gathered = g1_ref[...]
    counts = gathered[:, 4, :]
    counts_ref[...] = counts
    mean, inv, total = merge_stats(gathered, counts, width)
    tile[...] = jnp.zeros_like(tile)
    put(tile, 0, mean)
    put(tile, 2, inv)
    put(tile, 4, total[None])
    stat_ref[...] = tile[...]
    y = (extend(zext, z_ref, above_ref, below_ref) - mean) * inv * get(par_ref, 0, 2) + get(par_ref, 2, 2)
    a = y * jax.nn.sigmoid(y) * wide(ext_ref[...].reshape(-1, 128), width)
    a_ref[...] = a
    a_ref.send()
    shifted = [split(moved(a, step)) for step in (-1, 0, 1)]
    half = z2_ref.shape[1] // 2
    for g in range(2):
        cols = slice(g * group, (g + 1) * group)
        left = [
            jnp.concatenate(
                [window(shifted[tap % 3][part], images, tap // 3, cols) for tap in range(9)], axis=1
            )
            for part in range(2)
        ]
        outs = slice(g * half, (g + 1) * half)
        z2_ref[:, outs] = product(left, (wh_ref[:, outs], wl_ref[:, outs]), NN)
    z2_ref.send()
    z2 = z2_ref[...]
    own = own_ref[...]
    sums, squares = local_stats(z2, wide(own, z2.shape[1]), wide(column_sum(own), z2.shape[1]))
    put(tile, 0, sums)
    put(tile, 4, squares)
    pay_ref[...] = jnp.broadcast_to(tile[...][None], pay_ref.shape)


def taps_kernel(images, a_ref, high_ref, low_ref):
    group = a_ref.shape[1] // 2
    a = a_ref[...]
    shifted = [moved(a, step) for step in (-1, 0, 1)]
    for g in range(2):
        cols = slice(g * group, (g + 1) * group)
        for tap in range(9):
            high, low = split(window(shifted[tap % 3], images, tap // 3, cols).T)
            high_ref[g, tap * group : (tap + 1) * group, :] = high
            low_ref[g, tap * group : (tap + 1) * group, :] = low
        high_ref.send(g)
        low_ref.send(g)


def pixel_count(rows_ref, cols_ref):
    rows = jnp.sum(rows_ref[...].astype(f32), axis=1, keepdims=True)
    return rows * jnp.sum(cols_ref[...].astype(f32), axis=1, keepdims=True)


def pool_kernel(g2_ref, counts_ref, par_ref, rows_ref, cols_ref, z_ref, own_ref, w_ref, a_ref, stat_ref, pooled_ref, pay_ref):
    images = rows_ref.shape[0]
    width = z_ref.shape[1]
    mid = width // 2
    mean, inv, total = merge_stats(g2_ref[...], counts_ref[...], width)
    put(stat_ref, 0, mean)
    put(stat_ref, 4, inv)
    gain, shift = get(par_ref, 4, 4), get(par_ref, 8, 4)
    pieces = len(z_ref.parts)
    sums = []
    for i in range(pieces):
        y = (z_ref.chunk(i) - mean) * inv * gain + shift
        a = y * jax.nn.sigmoid(y) * wide(own_ref.chunk(i), width)
        a_ref.put(i, a)
        sums.append(image_sum(a, images // pieces))
    sums = jnp.concatenate(sums, axis=0)
    pooled = (sums[:, :mid] + sums[:, mid:]) / pixel_count(rows_ref, cols_ref)
    pooled_ref[...] = pooled
    pay_ref[...] = jnp.broadcast_to(exact(pooled, w_ref[...], NN)[None], pay_ref.shape)


def slope_of(values, mean, inv, gain, shift):
    normed = (values - mean) * inv
    y = normed * gain + shift
    sigma = jax.nn.sigmoid(y)
    return sigma * (1.0 + y * (1.0 - sigma)), normed


def slope_kernel(stat_ref, par_ref, rows_ref, cols_ref, own_ref, z_ref, slope_ref, normed_ref, sums_ref):
    images = rows_ref.shape[0]
    width = z_ref.shape[1]
    mean, inv = get(stat_ref, 0, 4), get(stat_ref, 4, 4)
    gain, shift = get(par_ref, 4, 4), get(par_ref, 8, 4)
    pieces = len(z_ref.parts)
    sums, cross = [], []
    for i in range(pieces):
        slope, normed = slope_of(z_ref.chunk(i), mean, inv, gain, shift)
        slope = slope * wide(own_ref.chunk(i), width)
        normed_ref.put(i, normed)
        slope_ref.put(i, slope)
        sums.append(image_sum(slope, images // pieces))
        cross.append(image_sum(slope * normed, images // pieces))
    pixels = pixel_count(rows_ref, cols_ref)
    sums_ref[:, :width] = jnp.concatenate(sums, axis=0) / pixels
    sums_ref[:, width:] = jnp.concatenate(cross, axis=0) / pixels


def expand_kernel(g3_ref, par_ref, w_ref, a_ref, wh_ref, wl_ref, own_ref,
                  mixed_ref, z_ref, weights_ref, normed_ref, pre_ref, act_ref, inv_ref, pay_ref, tile, acts):
    own_images = weights_ref.shape[0]
    mid = mixed_ref.shape[1]
    devices = g3_ref.shape[0]
    rows = lax.axis_size("rows")
    f_one = jnp.sum(g3_ref[...].reshape(rows, devices // rows * own_images, -1), axis=0)
    mean = jnp.mean(f_one, axis=0, keepdims=True)
    centered = f_one - mean
    inv = lax.rsqrt(jnp.mean(centered * centered, axis=0, keepdims=True) + epsilon)
    normed = centered * inv
    pre = normed * par_ref[12:13, :] + par_ref[13:14, :]
    normed_ref[...] = normed
    pre_ref[...] = pre
    inv_ref[...] = inv
    acts[...] = pre * jax.nn.sigmoid(pre)
    at = pl.multiple_of(lax.axis_index("batch") * own_images, own_images)
    act = acts[pl.ds(at, own_images), :]
    act_ref[...] = act
    logits = exact(act, w_ref[...], NN) + get(par_ref, 14, 4)
    lead = logits[:, :mid] - logits[:, mid:]
    first, second = jax.nn.sigmoid(lead), jax.nn.sigmoid(-lead)
    weights_ref[:, :mid] = first
    weights_ref[:, mid:] = second
    a = a_ref[...]
    mixed = per_image(first, a) * a[:, :mid] + per_image(second, a) * a[:, mid:]
    mixed_ref[...] = mixed
    mixed_ref.send()
    left, right = split(mixed), (wh_ref[...], wl_ref[...])
    for i, part in enumerate(z_ref.parts):
        rows = slice(part.start, part.start + part.size)
        z_ref.put(i, product([each[rows] for each in left], right, NN))
    z = z_ref[...]
    width = z.shape[1]
    own = wide(own_ref[...], width)
    sums, squares = local_stats(z, own, wide(column_sum(own_ref[...]), width))
    put(tile, 0, sums)
    put(tile, width // 128, squares)
    pay_ref[...] = jnp.broadcast_to(tile[...][None], pay_ref.shape)


def output_kernel(g4_ref, counts_ref, par_ref, own_ref, z_ref, x_ref, cot_ref, *refs):
    slope_refs, (grad_ref, stat_ref, slopes_ref, pay_ref, tile) = refs[:-5], refs[-5:]
    width = z_ref.shape[1]
    groups = width // 128
    mean, inv, total = merge_stats(g4_ref[...], counts_ref[...], width)
    put(stat_ref, 0, mean)
    put(stat_ref, groups, inv)
    gain, shift = get(par_ref, 18, groups), get(par_ref, 26, groups)
    flat, cross = 0.0, 0.0
    for i in range(len(z_ref.parts)):
        own = wide(own_ref.chunk(i), width)
        normed = (z_ref.chunk(i) - mean) * inv
        pre = normed * gain + shift + x_ref.chunk(i)
        sigma = jax.nn.sigmoid(pre)
        grad = cot_ref.chunk(i) * own * (sigma * (1.0 + pre * (1.0 - sigma)))
        grad_ref.put(i, grad)
        flat = flat + column_sum(grad)
        cross = cross + column_sum(grad * normed)
    put(tile, 0, flat)
    put(tile, groups, cross)
    pay_ref[...] = jnp.broadcast_to(tile[...][None], pay_ref.shape)
    sum_kernel(*slope_refs, slopes_ref)


def result_kernel(stat_ref, par_ref, own_ref, z_ref, x_ref, out_ref, mark_ref):
    width = z_ref.shape[1]
    groups = width // 128
    mean, inv = get(stat_ref, 0, groups), get(stat_ref, groups, groups)
    gain, shift = get(par_ref, 18, groups), get(par_ref, 26, groups)
    for i in range(len(z_ref.parts)):
        pre = (z_ref.chunk(i) - mean) * inv * gain + shift + x_ref.chunk(i)
        out_ref.put(i, pre * jax.nn.sigmoid(pre) * wide(own_ref.chunk(i), width))
    mark_ref[...] = own_ref[:8, :]


def mixed_kernel(digit, g5_ref, stat1_ref, stat3_ref, par_ref, own_ref, grad_ref, z_ref, wh_ref, wl_ref, a_ref, weights_ref,
                 w_ref, slope_ref, normed_ref, *refs):
    shares, (gm_ref, dsum_ref, grads_ref, slopes_ref, pay_ref, tile) = refs[: digit.size], refs[digit.size :]
    width = z_ref.shape[1]
    mid = gm_ref.shape[1]
    images = weights_ref.shape[0]
    groups = width // 128
    grads_ref[...] = jnp.sum(g5_ref[...], axis=0)
    count = wide(stat1_ref[4:5, :], width)
    mean, inv = get(stat3_ref, 0, groups), get(stat3_ref, groups, groups)
    flat = get(grads_ref, 0, groups) / count
    cross = get(grads_ref, groups, groups) / count
    scale = get(par_ref, 18, groups) * inv
    for i in range(len(z_ref.parts)):
        normed = (z_ref.chunk(i) - mean) * inv
        dz = scale * (grad_ref.chunk(i) - flat - normed * cross) * wide(own_ref.chunk(i), width)
        gm_ref[z_ref.parts[i]] = product(split(dz), (wh_ref[...], wl_ref[...]), NT)
    gm = gm_ref[...]
    gm_ref.send()
    a = a_ref[...]
    weights = weights_ref[...]
    gate = image_sum(gm * (a[:, :mid] - a[:, mid:]), images)
    dsum = weights[:, :mid] * weights[:, mid:] * gate
    dsum_ref[...] = dsum
    tile[...] = jnp.zeros_like(tile)
    tile[:images, :] = exact(dsum, w_ref[:, :mid] - w_ref[:, mid:], NT)
    slope = slope_ref[...] * jnp.concatenate([gm, gm], axis=1)
    put(tile, 8, column_sum(weights * image_sum(slope, images)))
    put(tile, 12, column_sum(weights * image_sum(slope * normed_ref[...], images)))
    pay_ref[...] = jnp.broadcast_to(tile[...][None], pay_ref.shape)
    digit.gather(shares, slopes_ref)


def expand_grad_kernel(core, grads_ref, stat1_ref, stat3_ref, par_ref, mixed_ref, act_ref, dsum_ref, own_ref, grad_ref, z_ref,
                       keep_ref, send_ref, excite_ref, term):
    width = z_ref.shape[1]
    groups = width // 128
    count = wide(stat1_ref[4:5, :], width)
    mean, inv = get(stat3_ref, 0, groups), get(stat3_ref, groups, groups)
    flat = get(grads_ref, 0, groups) / count
    cross = get(grads_ref, groups, groups) / count
    scale = get(par_ref, 18, groups) * inv
    left = split(mixed_ref[...].T)
    rows, span = left[0].shape[0], term.shape[1]
    for i, part in enumerate(z_ref.parts):
        normed = (z_ref.chunk(i) - mean) * inv
        dz = scale * (grad_ref.chunk(i) - flat - normed * cross) * wide(own_ref.chunk(i), width)
        right = split(dz)
        some = [each[:, part.start : part.start + part.size] for each in left]
        for j in range(term.shape[0] // rows):
            value = product(some, [each[:, j * span : (j + 1) * span] for each in right], NN)
            if i:
                value = value + term[j * rows : (j + 1) * rows, :]
            term[j * rows : (j + 1) * rows, :] = value
    core.scatter([term], [keep_ref, send_ref])
    excite_ref[...] = exact(act_ref[...], dsum_ref[...], TN)


def turned_rows(left, wh_ref, wl_ref, outs, row, taps):
    return product(left, [ref[row * taps : (row + 1) * taps, outs] for ref in (wh_ref, wl_ref)], NT)


def fold(total, group):
    return moved(total[:, :group], 1) + total[:, group : 2 * group] + moved(total[:, 2 * group :], -1)


def back_kernel(digit, g6_ref, pre_ref, fcn_ref, inv_ref, par_ref, wsq_ref, pooled_ref, stat1_ref, stat2_ref, rows_ref,
                cols_ref, weights_ref, mine_ref, other_ref, own_ref, gm_ref, slope_ref, normed_ref, wh_ref, wl_ref,
                up_ref, down_ref, dzh_ref, dzl_ref, squeeze_ref, gains_ref, fc_ref, gf, owned, slopes):
    images = rows_ref.shape[0]
    tall = dzh_ref.shape[1] - 2
    width = normed_ref.shape[1]
    mid = width // 2
    groups = width // 128
    rows = lax.axis_size("rows")
    shared = g6_ref[...]
    pre = pre_ref[...]
    fcn = fcn_ref[...]
    sigma = jax.nn.sigmoid(pre)
    total = pre.shape[0]
    grad = jnp.sum(shared[:, :images].reshape(rows, total, -1), axis=0) * (sigma * (1.0 + pre * (1.0 - sigma)))
    flat, cross = column_sum(grad), column_sum(grad * fcn)
    fc_ref[0:1, :] = cross
    fc_ref[1:2, :] = flat
    gf[...] = par_ref[12:13, :] * inv_ref[...] * (grad - flat / total - fcn * cross / total)
    at = pl.multiple_of(lax.axis_index("batch") * images, images)
    mine = gf[pl.ds(at, images), :]
    squeeze = exact(pooled_ref[...], mine, TN)
    half_rows = squeeze.shape[0] // 2
    squeeze_ref[:, : squeeze.shape[1]] = squeeze[:half_rows]
    squeeze_ref[:, squeeze.shape[1] :] = squeeze[half_rows:]
    spread = exact(gf[...], wsq_ref[...], NT)
    owned[...] = spread
    own_spread = owned[pl.ds(at, images), :] / pixel_count(rows_ref, cols_ref)
    for flipped, half in enumerate((mine_ref, other_ref)):
        for block in range(half.shape[0] // images):
            here = pl.multiple_of((2 * block + (digit.own() ^ flipped)) * images, images)
            slopes[pl.ds(here, images), :] = half[block * images : (block + 1) * images, :]
    base = jnp.sum(shared[:, 8:], axis=0)
    count = wide(stat1_ref[4:5, :], mid)
    weights = weights_ref[...]
    gm = gm_ref[...]
    shared_part = per_image(own_spread, gm)
    mask = wide(own_ref[...], mid)
    zero = jnp.zeros((images, 16, width), bf16)
    for ref in (dzh_ref, dzl_ref):
        ref[:, 0] = zero
        ref[:, tall + 1] = zero
    for g in range(2):
        outs = slice(g * mid, (g + 1) * mid)
        crosses = slice(width + g * mid, width + (g + 1) * mid)
        half = groups // 2
        flat_two = get(base, g * half, half) + column_sum(spread * slopes[:, outs])
        cross_two = get(base, groups + g * half, half) + column_sum(spread * slopes[:, crosses])
        put(gains_ref, g * half, cross_two)
        put(gains_ref, groups + g * half, flat_two)
        scale = get(par_ref, 4 + g * half, half) * get(stat2_ref, groups + g * half, half)
        upstream = per_image(weights[:, outs], gm) * gm + shared_part
        dz = scale * (upstream * slope_ref[:, outs] - flat_two / count - normed_ref[:, outs] * (cross_two / count)) * mask
        for ref, part in zip((dzh_ref, dzl_ref), split(dz)):
            ref[:, 1 : tall + 1, :, outs] = part.reshape(images, tall, 16, mid)
    dzh_ref.send()
    dzl_ref.send()
    group = up_ref.shape[1] // 2
    for g in range(2):
        outs = slice(g * mid, (g + 1) * mid)
        cols = slice(g * group, (g + 1) * group)
        for side, row, tap in ((up_ref, 1, 0), (down_ref, tall, 2)):
            left = [ref[:, row, :, outs].reshape(-1, mid) for ref in (dzh_ref, dzl_ref)]
            side[:, cols] = fold(turned_rows(left, wh_ref, wl_ref, outs, tap, 3 * group), group)


def group_kernel(core, dzh_ref, dzl_ref, squeeze_ref, excite_ref, th_ref, tl_ref, keep_ref, send_ref, out_ref):
    tall = dzh_ref.shape[1] - 2
    mid = dzh_ref.shape[3] // 2
    taps = th_ref.shape[1]
    for g in range(2):
        outs = slice(g * mid, (g + 1) * mid)
        right = [ref[:, 1 : tall + 1, :, outs].reshape(-1, mid) for ref in (dzh_ref, dzl_ref)]
        out_ref[g * taps : (g + 1) * taps, :] = product((th_ref.chunk(g)[0], tl_ref.chunk(g)[0]), right, NN)
    inter = excite_ref.shape[0]
    out_ref[2 * taps : 2 * taps + inter, :] = excite_ref[...]
    out_ref[2 * taps + inter :, :] = squeeze_ref[...]
    core.scatter([out_ref], [keep_ref, send_ref])


def input_grad_kernel(par_ref, stat_ref, dsum_ref, z_ref, own_ref, above_ref, below_ref, dzh_ref, dzl_ref, wh_ref, wl_ref,
                      dy_ref, pay_ref, tile, place):
    images = dsum_ref.shape[0]
    width = z_ref.shape[1]
    group = width // 2
    tall = dzh_ref.shape[1] - 2
    half = dzh_ref.shape[3] // 2
    grads = []
    for g in range(2):
        outs = slice(g * half, (g + 1) * half)
        total = None
        for row in range(3):
            left = [ref[:, 2 - row : 2 - row + tall, :, outs].reshape(-1, half) for ref in (dzh_ref, dzl_ref)]
            term = turned_rows(left, wh_ref, wl_ref, outs, row, 3 * group)
            total = term if total is None else total + term
        grads.append(fold(total, group))
    place[...] = jnp.concatenate(grads, axis=1).reshape(place.shape)
    place[:, 0] += above_ref[...].reshape(images, 16, width)
    place[:, tall - 1] += below_ref[...].reshape(images, 16, width)
    grad = place[...].reshape(-1, width)
    mean, inv = get(stat_ref, 0, 2), get(stat_ref, 2, 2)
    normed = (z_ref[...] - mean) * inv
    y = normed * get(par_ref, 0, 2) + get(par_ref, 2, 2)
    sigma = jax.nn.sigmoid(y)
    dy = grad * wide(own_ref[...], width) * (sigma * (1.0 + y * (1.0 - sigma)))
    dy_ref[...] = dy
    dy_ref.send()
    tile[...] = jnp.zeros_like(tile)
    put(tile, 0, column_sum(dy * normed))
    put(tile, 2, column_sum(dy))
    put(tile, 4, column_sum(dsum_ref[...]))
    pay_ref[...] = jnp.broadcast_to(tile[...][None], pay_ref.shape)


def final_kernel(core, g7_ref, par_ref, stat_ref, dy_ref, z_ref, own_ref, th_ref, tl_ref,
                 keep_ref, send_ref, dzh_ref, dzl_ref, gains_ref, term):
    width = z_ref.shape[1]
    gains_ref[...] = jnp.sum(g7_ref[...], axis=0)
    cross, flat = get(gains_ref, 0, 2), get(gains_ref, 2, 2)
    count = wide(stat_ref[4:5, :], width)
    mean, inv = get(stat_ref, 0, 2), get(stat_ref, 2, 2)
    normed = (z_ref[...] - mean) * inv
    scale = get(par_ref, 0, 2) * inv
    dz = scale * (dy_ref[...] - flat / count - normed * (cross / count)) * wide(own_ref[...], width)
    high, low = split(dz)
    dzh_ref[...] = high
    dzl_ref[...] = low
    term[...] = product((th_ref[...], tl_ref[...]), (high, low), NN)
    core.scatter([term], [keep_ref, send_ref])


def images_kernel(dzh_ref, dzl_ref, wh_ref, wl_ref, grad_ref, out_ref):
    for i in range(len(grad_ref.parts)):
        left = [ref.chunk(i) for ref in (dzh_ref, dzl_ref)]
        out_ref.put(i, product(left, (wh_ref[...], wl_ref[...]), NT) + grad_ref.chunk(i))


def deal_kernel(plan, count, *refs):
    outs = list(refs[count:])
    for digit, stretches in plan:
        own = digit.own()
        for j in range(digit.size):
            out, at = outs.pop(0), 0
            for inputs, first, rows in stretches:
                each = rows // digit.size
                here = pl.ds(pl.multiple_of(first + (own ^ j) * each, 8), each)
                total = refs[inputs[0]][here, :]
                for k in inputs[1:]:
                    total = total + refs[k][here, :]
                out[at : at + each, :] = total
                at += each


def deal(plan, ins, **order):
    width = ins[0].shape[1]
    outs = []
    for digit, stretches in plan:
        rows = sum(rows for _, _, rows in stretches) // digit.size
        outs += [((rows, width), f32)] * digit.size
    return local_call(functools.partial(deal_kernel, plan, len(ins)), outs, ins, **order)


def stack_kernel(stretches, *refs):
    refs, out = refs[:-1], refs[-1]
    at = 0
    for inputs, first, rows in stretches:
        each = rows // out.shape[0]
        for d in range(out.shape[0]):
            here = slice(first + d * each, first + (d + 1) * each)
            total = refs[inputs[0]][here, :]
            for k in inputs[1:]:
                total = total + refs[k][here, :]
            out[d, at : at + each, :] = total
        at += each


def extra_pieces(extra, stacked):
    if extra.size == 1:
        return [stacked]
    total = local_call(lambda ref, out: out.__setitem__(Ellipsis, jnp.sum(ref[...], axis=0)), [(stacked.shape[1:], f32)], [stacked])[0]
    return extra.send([total] * extra.size)


def stacked_kernel(count, *refs):
    if count == 1:
        refs[-1][...] = jnp.sum(refs[0][...], axis=0)
    else:
        sum_kernel(*refs)


def halves_kernel(digit, *refs):
    pieces, outs = refs[: digit.size], refs[digit.size :]
    half = pieces[0].shape[0] // 2
    own = digit.own()
    for j, piece in enumerate(pieces):
        at = pl.ds(pl.multiple_of((own ^ j) * half, 8), half)
        for i, out in enumerate(outs):
            out[at, :] = piece[i * half : (i + 1) * half, :]


def pair_kernel(digits, *refs):
    outs = refs[4:]
    for i, digit in enumerate(digits):
        digit.gather(refs[2 * i : 2 * i + 2], outs[i] if len(outs) == 2 else outs[0].at[pl.ds(i * 2 * refs[0].shape[0], 2 * refs[0].shape[0])])


def last_kernel(core, expand_map, group_map, mine_ref, other_ref, expand_ref, group_ref, excite_ref, squeeze_ref, whole):
    core.gather([mine_ref, other_ref], whole)
    taps, mid = group_ref.shape[0], whole.shape[1]
    inter = squeeze_ref.shape[1]
    tall = expand_ref.shape[0]
    places = [
        (taps, lambda rows, value: group_ref.__setitem__((rows, slice(0, mid)), value)),
        (taps, lambda rows, value: group_ref.__setitem__((rows, slice(mid, 2 * mid)), value)),
        (inter, lambda rows, value: excite_ref.__setitem__((rows, slice(0, mid)), value)),
        (inter, lambda rows, value: squeeze_put(squeeze_ref, rows, value)),
    ]
    for at, first, rows in expand_map:
        j, m = first // tall, first % tall
        expand_ref[m : m + rows, j * mid : (j + 1) * mid] = whole[at : at + rows, :]
    for at, first, rows in group_map:
        base = 0
        for length, store in places:
            low, high = max(first, base), min(first + rows, base + length)
            if low < high:
                store(slice(low - base, high - base), whole[at + low - first : at + high - first, :])
            base += length
    excite_ref[:, mid:] = -excite_ref[:, :mid]


def squeeze_put(squeeze_ref, rows, value):
    half = squeeze_ref.shape[0] // 2
    width = squeeze_ref.shape[1]
    squeeze_ref[rows, :] = value[:, :width]
    squeeze_ref[slice(half + rows.start, half + rows.stop), :] = value[:, width:]


def on_device(
    images,
    w_reduce,
    gain_one,
    shift_one,
    w_group,
    gain_two,
    shift_two,
    w_squeeze,
    gain_fc,
    shift_fc,
    w_excite,
    excite_bias,
    w_expand,
    gain_three,
    shift_three,
    valid_rows,
    valid_cols,
    cotangent,
):
    count, tall, broad, chan = images.shape
    mid = w_reduce.shape[1]
    inter = w_squeeze.shape[1]
    duo = 2 * mid
    taps = 9 * mid // 2
    cells = count * tall * broad
    longer = count * (tall + 2) * broad
    edge = count * broad
    devices = lax.axis_size("rows") * lax.axis_size("batch")
    all_images = count * lax.axis_size("batch")
    x = images.reshape(cells, chan)
    cot = cotangent.reshape(cells, chan)
    pay8 = ((devices, 8, 128), f32)
    pay16 = ((devices, 16, 128), f32)
    tile8 = pltpu.VMEM((8, 128), f32)
    tile16 = pltpu.VMEM((16, 128), f32)
    twice = lambda *shape: [(shape, bf16)] * 2
    flat_w = w_group.reshape(taps, duo)
    vectors = (gain_one, shift_one, gain_two, shift_two, gain_fc, shift_fc, excite_bias, gain_three, shift_three)
    core, line, depth, extra = digits()

    z_one, ext, own, first, last, pay = call(
        reduce_kernel,
        [((cells, mid), f32), ((count, tall + 2, broad, 128), f32), ((cells, 128), f32), ((edge, mid), f32),
         ((edge, mid), f32), pay8],
        [valid_rows, valid_cols, w_reduce, x],
        [tile8],
        chunks={3: 2},
        near_outs=(3, 4, 5),
    )
    g1 = share(pay)
    above, below = halos(first, last)
    wgh, wgl, weh, wel, wrh, wrl, par = call(
        parts_kernel,
        [*twice(taps, duo), *twice(mid, chan), *twice(chan, mid), ((40, 128), f32)],
        [flat_w, w_expand, w_reduce, *[v.reshape(1, -1) for v in vectors]],
        chunks={0: 4, 1: 2, 2: 2},
        out_chunks={0: 4, 1: 4, 2: 2, 3: 2, 4: 2, 5: 2},
        after=[z_one],
    )
    z_two, a_one, stat1, counts, pay = call(
        conv_kernel,
        [((cells, duo), f32), ((longer, mid), f32), ((8, 128), f32), ((devices, 128), f32), pay8],
        [g1, par, z_one, ext, above, below, own, wgh, wgl],
        [tile8, pltpu.VMEM((count, tall + 2, broad, mid), f32)],
        near=(0, 4, 5),
        near_outs=(4,),
    )
    g2 = share(pay)
    xth, xtl = call(turned_kernel, twice(chan, cells), [x], after=[stat1])
    a_two, stat2, pooled, pay = call(
        pool_kernel,
        [((cells, duo), f32), ((8, 128), f32), ((count, mid), f32), ((devices, count, inter), f32)],
        [g2, counts, par, valid_rows, valid_cols, z_two, own, w_squeeze],
        chunks={5: 2, 6: 2},
        out_chunks={0: 2},
        after=[xth],
        near=(0,),
        near_outs=(3,),
    )
    g3 = share(pay)
    slope_two, normed_two, slopes = call(
        slope_kernel,
        [((cells, duo), f32), ((cells, duo), f32), ((count, 2 * duo), f32)],
        [stat2, par, valid_rows, valid_cols, own, z_two],
        chunks={4: 2, 5: 2},
        out_chunks={0: 2, 1: 2},
    )
    mixed, z_three, weights, fc_normed, fc_pre, fc_act, fc_inv, pay = call(
        expand_kernel,
        [((cells, mid), f32), ((cells, chan), f32), ((count, duo), f32), ((all_images, inter), f32),
         ((all_images, inter), f32), ((count, inter), f32), ((1, inter), f32), pay16],
        [g3, par, w_excite, a_two, weh, wel, own],
        [tile16, pltpu.VMEM((all_images, inter), f32)],
        out_chunks={1: 2},
        after=[slopes],
        near=(0,),
        near_outs=(7,),
    )
    g4 = share(pay)
    slopes = line.send([slopes] * line.size)
    grad_pre, stat3, slopes, pay = call(
        output_kernel,
        [((cells, chan), f32), ((16, 128), f32), ((count, 2 * duo), f32), pay16],
        [g4, counts, par, own, z_three, x, cot, *slopes],
        [tile16],
        chunks={3: 4, 4: 4, 5: 4, 6: 4},
        out_chunks={0: 4},
        near=(0, *range(7, 7 + line.size)),
        near_outs=(2, 3),
    )
    g5 = share(pay)
    slopes = depth.send([slopes] * depth.size)
    tph, tpl = call(functools.partial(taps_kernel, count), twice(2, taps, cells), [a_one], out_chunks={0: 2, 1: 2}, after=[stat3])
    grad_mixed, dsum, grads_three, slopes, pay = call(
        functools.partial(mixed_kernel, depth),
        [((cells, mid), f32), ((count, mid), f32),
         ((16, 128), f32), ((depth.size * count, 2 * duo), f32), pay16],
        [g5, stat1, stat3, par, own, grad_pre, z_three, weh, wel, a_two, weights, w_excite, slope_two, normed_two, *slopes],
        [tile16],
        after=[tph],
        near=(0, *range(14, 14 + depth.size)),
        near_outs=(3, 4),
    )
    g6 = share(pay)
    *expand_sum, excite_term = call(
        functools.partial(expand_grad_kernel, core),
        [*core.outs(mid * chan // mid, mid), ((inter, mid), f32)],
        [grads_three, stat1, stat3, par, mixed, fc_act, dsum, own, grad_pre, z_three],
        [pltpu.VMEM((chan, mid), f32)],
        chunks={7: 2, 8: 2, 9: 2},
    )
    if extra.size > 1:
        slopes = gather_more(extra, extra.send([slopes] * extra.size))
    slopes = core.send([slopes] * 2)
    packed = 2 * taps + 2 * inter
    up, down, dzh, dzl, squeeze_term, grads_two, grads_fc = call(
        functools.partial(back_kernel, core),
        [((edge, mid), f32), ((edge, mid), f32), *twice(count, tall + 2, broad, duo), ((inter, mid), f32),
         ((8, 128), f32), ((2, inter), f32)],
        [g6, fc_pre, fc_normed, fc_inv, par, w_squeeze, pooled, stat1, stat2, valid_rows, valid_cols, weights, *slopes, own,
         grad_mixed, slope_two, normed_two, wgh, wgl],
        [pltpu.VMEM((all_images, inter), f32), pltpu.VMEM((all_images, mid), f32), pltpu.VMEM((all_images, 2 * duo), f32)],
        after=[excite_term],
        near=(0, 12, 13),
        near_outs=(0, 1),
    )
    above, below = halos(up, down)
    group_sum = call(
        functools.partial(group_kernel, core),
        core.outs(packed, mid),
        [dzh, dzl, squeeze_term, excite_term, tph, tpl],
        [pltpu.VMEM((packed, mid), f32)],
        chunks={4: 2, 5: 2},
        near_outs=(0, 1),
    )
    expand_sum = core.send(expand_sum)
    group_sum = core.send([group_sum[0], gate(group_sum[1], [above, below])])
    first_bit, second_bit = line.bits()
    some, more = expand_sum[0].shape[0] // 2, group_sum[0].shape[0] // 2
    both_of = lambda start, a, b: [((0, 1), start * a, a), ((2, 3), start * b, b)]
    first_half = lambda digit: (digit, both_of(0, some, more))
    second_half = lambda digit: (digit, both_of(1, some, more))
    keep_a, send_a, keep_b, send_b = deal(
        [first_half(first_bit), second_half(second_bit)], [*expand_sum, *group_sum]
    )
    come_a, come_b = first_bit.send([keep_a, send_a]), second_bit.send([keep_b, send_b])
    dy_one, pay = call(
        input_grad_kernel,
        [((cells, mid), f32), pay8],
        [par, stat1, dsum, z_one, own, above, below, dzh, dzl, wgh, wgl],
        [tile8, pltpu.VMEM((count, tall, broad, mid), f32)],
        beside=[keep_a],
        near=(5, 6),
        near_outs=(1,),
    )
    g7 = share(pay)
    some, more = some // 2, more // 2
    turn = lambda k: [((k, k + 1), 0, some), ((k, k + 1), some, more)]
    keep_a, send_a, keep_b, send_b = deal([(second_bit, turn(0)), (first_bit, turn(2))], [*come_a, *come_b], after=[dy_one])
    *reduce_sum, dzh, dzl, grads_one = call(
        functools.partial(final_kernel, core),
        [*core.outs(chan, mid), *twice(cells, mid), ((8, 128), f32)],
        [g7, par, stat1, dy_one, z_one, own, xth, xtl],
        [pltpu.VMEM((chan, mid), f32)],
        beside=[keep_a],
        near=(0,),
        near_outs=(0, 1),
    )
    come_a, come_b = second_bit.send([keep_a, send_a]), first_bit.send([keep_b, send_b])
    some, more = some // 2, more // 2
    stretches = turn(0) + turn(2)
    (joined,) = local_call(
        functools.partial(stack_kernel, stretches),
        [((depth.size, (some + more) * 2 // depth.size, mid), f32)],
        [*come_a, *come_b],
        after=[grads_one],
    )
    reduce_sum[1] = gate(reduce_sum[1], [joined])
    joined = depth.trade(joined)
    reduce_sum = scatter_more(line, core.send(reduce_sum))
    (grad_images,) = call(
        images_kernel,
        [((cells, chan), f32)],
        [dzh, dzl, wrh, wrl, grad_pre],
        chunks={0: 2, 1: 2, 4: 2},
        out_chunks={0: 2},
        beside=[reduce_sum[0]],
    )
    reduce_sum = scatter_more(depth, line.send(reduce_sum), after=[grad_images])
    (joined,) = local_call(
        functools.partial(stacked_kernel, extra.size), [(joined.shape[1:], f32)], extra_pieces(extra, joined), beside=[reduce_sum[0]]
    )
    rows_in = depth.size * joined.shape[0]
    block_out, mark = call(
        result_kernel,
        [((cells, chan), f32), ((8, 128), f32)],
        [stat3, par, own, z_three, x],
        chunks={2: 4, 3: 4, 4: 4},
        out_chunks={0: 4},
        beside=[joined],
    )
    half_a, half_b = local_call(
        functools.partial(halves_kernel, depth),
        [((rows_in // 2, mid), f32)] * 2,
        depth.send([joined] * depth.size),
        after=[mark],
    )
    reduce_sum = finish_sum(depth.send(reduce_sum), extra, beside=[half_a])
    half_a, half_b = local_call(
        functools.partial(pair_kernel, [second_bit, first_bit]),
        [((rows_in, mid), f32)] * 2,
        [*second_bit.send([half_a] * 2), *first_bit.send([half_b] * 2)],
        beside=[reduce_sum],
    )
    reduce_sum = gather_more(depth, depth.send([reduce_sum] * depth.size), beside=[half_a])
    (joined,) = local_call(
        functools.partial(pair_kernel, [first_bit, second_bit]),
        [((4 * rows_in, mid), f32)],
        [*first_bit.send([half_a] * 2), *second_bit.send([half_b] * 2)],
        beside=[reduce_sum],
    )
    reduce_sum = gather_more(line, line.send([reduce_sum] * line.size), beside=[joined])
    expand_map, group_map = [], []
    at = 0
    some, more = some // depth.size, more // depth.size
    for half in range(core.size):
        for part in range(2):
            for outer in range(2):
                for inner in range(2):
                    for deep in range(depth.size):
                        block = (((half * 2 + part) * 2 + outer) * 2 + inner) * depth.size + deep
                        expand_map.append((at, block * some, some))
                        group_map.append((at + some, block * more, more))
                        at += some + more
    grad_w_expand, grad_w_group, grad_w_excite, grad_w_squeeze = call(
        functools.partial(last_kernel, core, expand_map, group_map),
        [((mid, chan), f32), ((taps, duo), f32), ((inter, duo), f32), ((mid, inter), f32)],
        core.send([joined] * 2),
        [pltpu.VMEM((chan + packed, mid), f32)],
        near=(0, 1),
    )
    (grad_w_reduce,) = call(
        functools.partial(gather_kernel, core), [((chan, mid), f32)], core.send([reduce_sum] * 2), near=(0, 1)
    )
    grads_one = grads_one.reshape(-1)
    grads_two = grads_two.reshape(-1)
    grads_three = grads_three.reshape(-1)
    grad_bias = grads_one[duo : duo + mid]
    return (
        block_out.reshape(images.shape),
        grad_images.reshape(images.shape),
        grad_w_reduce,
        grads_one[:mid],
        grads_one[mid:duo],
        grad_w_group.reshape(w_group.shape),
        grads_two[:duo],
        grads_two[duo:],
        grad_w_squeeze,
        grads_fc[0],
        grads_fc[1],
        grad_w_excite,
        jnp.concatenate([grad_bias, -grad_bias]),
        grad_w_expand,
        grads_three[chan:],
        grads_three[:chan],
    )


def solution(mesh):
    maps = P("batch", "rows", None, None)
    return jax.shard_map(
        on_device,
        mesh=mesh,
        in_specs=(maps,) + (P(),) * 14 + (P("batch", None), P("batch", None), maps),
        out_specs=(maps, maps) + (P(),) * 14,
        check_vma=False,
    )
```

```python
import functools

import jax
import jax.numpy as jnp
from jax import lax
from jax.experimental import pallas as pl
from jax.experimental.pallas import tpu as pltpu
from jax.sharding import PartitionSpec as P

epsilon = 1e-05
f32 = jnp.float32
bf16 = jnp.bfloat16
highest = lax.Precision.HIGHEST
both = ("rows", "batch")
NN = ((1,), (0,))
NT = ((1,), (1,))
TN = ((0,), (0,))


def split(values):
    high = values.astype(bf16)
    return high, (values - high.astype(f32)).astype(bf16)


def dot(left, right, dims):
    return lax.dot_general(left, right, (dims, ((), ())), preferred_element_type=f32)


def product(left, right, dims):
    return dot(left[0], right[0], dims) + (
        dot(left[0], right[1], dims) + dot(left[1], right[0], dims)
    )


def exact(left, right, dims):
    return lax.dot_general(
        left, right, (dims, ((), ())), preferred_element_type=f32, precision=highest
    )


def put(tile, row, vector):
    for j in range(vector.shape[1] // 128):
        tile[row + j : row + j + 1, :] = vector[:, j * 128 : (j + 1) * 128]


def get(tile, row, count):
    return jnp.concatenate([tile[row + j : row + j + 1, :] for j in range(count)], axis=1)


def wide(mask, width):
    return jnp.concatenate([mask] * (width // 128), axis=1)


def column_sum(values):
    return jnp.sum(values, axis=0, keepdims=True)


def image_sum(values, images):
    return jnp.sum(values.reshape(images, values.shape[0] // images, values.shape[1]), axis=1)


def per_image(vector, values):
    count, width = vector.shape
    each = values.shape[0] // count
    return jnp.broadcast_to(vector[:, None, :], (count, each, width)).reshape(values.shape[0], width)


def merge_stats(gathered, counts, width):
    groups = width // 128
    own = jnp.maximum(counts, 1.0)
    total = jnp.sum(counts, axis=0)
    means, inverses = [], []
    for j in range(groups):
        sums = gathered[:, j, :]
        squares = gathered[:, groups + j, :]
        mean = jnp.sum(sums, axis=0, keepdims=True) / total
        shift = sums / own - mean
        spread = jnp.sum(squares + counts * shift * shift, axis=0, keepdims=True) / total
        means.append(mean)
        inverses.append(lax.rsqrt(spread + epsilon))
    return jnp.concatenate(means, axis=1), jnp.concatenate(inverses, axis=1), total


def local_stats(values, mask, count):
    sums = column_sum(values * mask)
    centered = values - sums / jnp.maximum(count, 1.0)
    return sums, column_sum(centered * centered * mask)


def own_rows(extended, images):
    rows, width = extended.shape
    tall = rows // images // 16
    return extended.reshape(images, tall, 16, width)[:, 1 : tall - 1].reshape(-1, width)


class In:
    def __init__(self, source, target, sems, chunks):
        self.ref, self.shape, self.dtype = target, target.shape, target.dtype
        rows = self.shape[0] // chunks
        self.parts = [pl.ds(i * rows, rows) for i in range(chunks)]
        self.copies = [
            pltpu.make_async_copy(source.at[part], target.at[part], sems.at[i])
            for i, part in enumerate(self.parts)
        ]
        self.due = list(range(chunks))

    def start(self):
        for copy in self.copies:
            copy.start()

    def ready(self):
        while self.due:
            self.copies[self.due.pop(0)].wait()
        return self.ref

    def chunk(self, i):
        if i in self.due:
            self.due.remove(i)
            self.copies[i].wait()
        return self.ref[self.parts[i]]

    def __getitem__(self, index):
        return self.ready()[index]


class Near:
    def __init__(self, ref):
        self.ref, self.shape, self.dtype = ref, ref.shape, ref.dtype

    def start(self, i=None):
        pass

    ready = send = start

    def finish(self):
        pass

    def __getitem__(self, index):
        return self.ref[index]

    def __setitem__(self, index, value):
        self.ref[index] = value


class Out:
    def __init__(self, source, target, sems, chunks):
        self.ref, self.shape, self.dtype = source, source.shape, source.dtype
        rows = self.shape[0] // chunks
        self.parts = [pl.ds(i * rows, rows) for i in range(chunks)]
        self.copies = [
            pltpu.make_async_copy(source.at[part], target.at[part], sems.at[i])
            for i, part in enumerate(self.parts)
        ]
        self.sent = set()

    def send(self, i=None):
        for k in range(len(self.copies)) if i is None else [i]:
            if k not in self.sent:
                self.sent.add(k)
                self.copies[k].start()

    def finish(self):
        self.send()
        for copy in self.copies:
            copy.wait()

    def put(self, i, value):
        self.ref[self.parts[i]] = value
        self.send(i)

    def __getitem__(self, index):
        return self.ref[index]

    def __setitem__(self, index, value):
        self.ref[index] = value


def call(body, outs, ins, scratch=(), limit=54, chunks=None, out_chunks=None, after=(), beside=(), near=(), near_outs=()):
    chunks, out_chunks = chunks or {}, out_chunks or {}
    n, m, k = len(ins), len(outs), len(after) + len(beside)
    far = [i for i in range(n) if i not in near]
    far_outs = [i for i in range(m) if i not in near_outs]
    parts = [chunks.get(i, 1) for i in far] + [out_chunks.get(i, 1) for i in far_outs]

    def inner(*refs):
        sources, targets, local = refs[:n], refs[n + k : n + k + m], refs[n + k + m :]
        held, sems, rest = local[: len(parts)], local[len(parts) : 2 * len(parts)], local[2 * len(parts) :]
        given = [Near(ref) for ref in sources]
        for at, i in enumerate(far):
            given[i] = In(sources[i], held[at], sems[at], parts[at])
        made = [Near(ref) for ref in targets]
        for at, i in enumerate(far_outs, len(far)):
            made[i] = Out(held[at], targets[i], sems[at], parts[at])
        for each in given:
            each.start()
        body(*given, *made, *rest)
        for each in given:
            each.ready()
        for each in made:
            each.send()
        for each in made:
            each.finish()

    space = lambda count, places: [pl.BlockSpec(memory_space=pltpu.VMEM if i in places else pltpu.HBM) for i in range(count)]
    return pl.pallas_call(
        inner,
        out_shape=[(pltpu.VMEM if i in near_outs else pltpu.HBM)(*out) for i, out in enumerate(outs)],
        in_specs=space(n, near) + space(len(after), ()) + space(len(beside), range(len(beside))),
        out_specs=space(m, near_outs),
        scratch_shapes=[
            *[pltpu.VMEM(ins[i].shape, ins[i].dtype) for i in far],
            *[pltpu.VMEM(*outs[i]) for i in far_outs],
            *[pltpu.SemaphoreType.DMA((k,)) for k in parts],
            *scratch,
        ],
        compiler_params=pltpu.CompilerParams(vmem_limit_bytes=limit * 2**20),
        cost_estimate=pl.CostEstimate(flops=1, bytes_accessed=1, transcendentals=0),
    )(
        *[pltpu.with_memory_space_constraint(a, pltpu.VMEM if i in near else pltpu.HBM) for i, a in enumerate(ins)],
        *[pltpu.with_memory_space_constraint(a, pltpu.HBM) for a in after],
        *[pltpu.with_memory_space_constraint(a, pltpu.VMEM) for a in beside],
    )


def local_call(body, outs, ins, scratch=(), limit=16, after=(), beside=()):
    n, k = len(ins), len(after) + len(beside)

    def inner(*refs):
        body(*refs[:n], *refs[n + k :])

    spec = lambda space, count: [pl.BlockSpec(memory_space=space)] * count
    return pl.pallas_call(
        inner,
        out_shape=[pltpu.VMEM(*out) for out in outs],
        in_specs=spec(pltpu.VMEM, n) + spec(pltpu.HBM, len(after)) + spec(pltpu.VMEM, len(beside)),
        out_specs=spec(pltpu.VMEM, len(outs)),
        scratch_shapes=list(scratch),
        compiler_params=pltpu.CompilerParams(vmem_limit_bytes=limit * 2**20),
        cost_estimate=pl.CostEstimate(flops=1, bytes_accessed=1, transcendentals=0),
    )(
        *[pltpu.with_memory_space_constraint(a, pltpu.VMEM) for a in ins],
        *[pltpu.with_memory_space_constraint(a, pltpu.HBM) for a in after],
        *[pltpu.with_memory_space_constraint(a, pltpu.VMEM) for a in beside],
    )


def share(tile):
    return lax.all_to_all(tile, both, 0, 0)


def halos(first, last):
    count = lax.axis_size("rows")
    above = lax.ppermute(last, "rows", [(i, i + 1) for i in range(count - 1)])
    below = lax.ppermute(first, "rows", [(i + 1, i) for i in range(count - 1)])
    return above, below


def flip(values, axis, bits):
    return lax.ppermute(values, axis, [(i, i ^ bits) for i in range(lax.axis_size(axis))])


class Digit:
    def __init__(self, axis, unit, size):
        self.axis, self.unit, self.size = axis, unit, size

    def own(self):
        return lax.axis_index(self.axis) // self.unit % self.size

    def send(self, pieces):
        return [pieces[0]] + [flip(pieces[j], self.axis, j * self.unit) for j in range(1, self.size)]

    def bits(self):
        return [Digit(self.axis, self.unit << i, 2) for i in range(self.size.bit_length() - 1)]

    def trade(self, stacked):
        count = lax.axis_size(self.axis)
        span = self.unit * self.size
        starts = [high + low for high in range(0, count, span) for low in range(self.unit)]
        groups = [[start + self.unit * d for d in range(self.size)] for start in starts]
        return lax.all_to_all(stacked, self.axis, 0, 0, axis_index_groups=groups)

    def scatter(self, parts, outs):
        size = outs[0].shape[0]
        own = self.own()
        for j, out in enumerate(outs):
            at = pl.ds(pl.multiple_of((own ^ j) * size, 8), size)
            total = parts[0][at, :]
            for part in parts[1:]:
                total = total + part[at, :]
            out[...] = total

    def gather(self, pieces, out):
        size = pieces[0].shape[0]
        own = self.own()
        for j, piece in enumerate(pieces):
            out[pl.ds(pl.multiple_of((own ^ j) * size, 8), size), :] = piece[...]

    def outs(self, rows, width):
        return [((rows // self.size, width), f32)] * self.size


def digits():
    rows, batch = lax.axis_size("rows"), lax.axis_size("batch")
    depth = min(4, batch // 2)
    return Digit("batch", 1, 2), Digit("rows", 1, rows), Digit("batch", 2, depth), Digit("batch", 2 * depth, batch // (2 * depth))


def gate(value, beside):
    return pl.pallas_call(
        lambda *refs: None,
        out_shape=pltpu.VMEM(value.shape, value.dtype),
        in_specs=[pl.BlockSpec(memory_space=pltpu.VMEM)] * (1 + len(beside)),
        out_specs=pl.BlockSpec(memory_space=pltpu.VMEM),
        input_output_aliases={0: 0},
        cost_estimate=pl.CostEstimate(flops=1, bytes_accessed=1, transcendentals=0),
    )(*[pltpu.with_memory_space_constraint(a, pltpu.VMEM) for a in (value, *beside)])


def scatter_kernel(digit, count, *refs):
    digit.scatter(refs[:count], refs[count:])


def sum_kernel(*refs):
    total = refs[0][...]
    for ref in refs[1:-1]:
        total = total + ref[...]
    refs[-1][...] = total


def gather_kernel(digit, *refs):
    digit.gather(refs[:-1], refs[-1])


def scatter_more(digit, pieces, **order):
    rows, width = pieces[0].shape
    body = functools.partial(scatter_kernel, digit, len(pieces))
    return local_call(body, digit.outs(rows, width), pieces, **order)


def add_up(pieces, **order):
    return local_call(sum_kernel, [(pieces[0].shape, f32)], pieces, **order)[0]


def finish_sum(pieces, extra, **order):
    total = add_up(pieces, **order)
    if extra.size > 1:
        total = add_up(extra.send([total] * extra.size))
    return total


def gather_more(digit, pieces, **order):
    rows, width = pieces[0].shape
    return local_call(functools.partial(gather_kernel, digit), [((rows * digit.size, width), f32)], pieces, **order)[0]


def reduce_kernel(rows_ref, cols_ref, w_ref, x_ref, z_ref, ext_ref, own_ref, first_ref, last_ref, pay_ref,
                  tile):
    images = rows_ref.shape[0]
    tall = x_ref.shape[0] // images // 16
    shape = (images, tall + 2, 16, 16)
    start = lax.axis_index("rows") * tall - 1
    lane = lax.broadcasted_iota(jnp.int32, shape, 3).reshape(-1, 16)
    at_row = lax.broadcasted_iota(jnp.int32, shape, 1).reshape(-1, 16) + start
    at_col = lax.broadcasted_iota(jnp.int32, shape, 2).reshape(-1, 16)
    row_valid = per_image(rows_ref[...].astype(f32), lane)
    col_valid = per_image(cols_ref[...].astype(f32), lane)
    in_row = jnp.sum(jnp.where(lane == at_row, row_valid, 0.0), axis=1, keepdims=True)
    in_col = jnp.sum(jnp.where(lane == at_col, col_valid, 0.0), axis=1, keepdims=True)
    mask = jnp.broadcast_to(in_row * in_col, (in_row.shape[0], 128)).reshape(ext_ref.shape)
    ext_ref[...] = mask
    own = mask[:, 1 : tall + 1].reshape(-1, 128)
    own_ref[...] = own
    weight = split(w_ref[...])
    for i in range(len(x_ref.parts)):
        z_ref[x_ref.parts[i]] = product(split(x_ref.chunk(i)), weight, NN)
    z = z_ref[...]
    edges = z.reshape(images, tall, 16, -1)
    first_ref[...] = edges[:, 0].reshape(first_ref.shape)
    last_ref[...] = edges[:, tall - 1].reshape(last_ref.shape)
    for each in (first_ref, last_ref, z_ref, ext_ref, own_ref):
        each.send()
    count = column_sum(own)
    sums, squares = local_stats(z, wide(own, z.shape[1]), wide(count, z.shape[1]))
    tile[...] = jnp.zeros_like(tile)
    put(tile, 0, sums)
    put(tile, 2, squares)
    put(tile, 4, count)
    pay_ref[...] = jnp.broadcast_to(tile[...][None], pay_ref.shape)


def parts_kernel(wg_ref, we_ref, wr_ref, *refs):
    vectors, wg_refs, (weh_ref, wel_ref, wrh_ref, wrl_ref, par_ref) = refs[:-9], refs[-9:-5], refs[-5:]
    row = 0
    for vector in vectors:
        put(par_ref, row, vector[...])
        row += vector.shape[1] // 128
    half = wg_ref.shape[1] // 2
    for i in range(len(wg_ref.parts)):
        for j, part in enumerate(split(wg_ref.chunk(i))):
            for g in range(2):
                wg_refs[2 * g + j].put(i, part[:, g * half : (g + 1) * half])
    for source, high_ref, low_ref in ((we_ref, weh_ref, wel_ref), (wr_ref, wrh_ref, wrl_ref)):
        for i in range(len(source.parts)):
            high, low = split(source.chunk(i))
            high_ref.put(i, high)
            low_ref.put(i, low)


def turned_kernel(x_ref, high_ref, low_ref):
    high_ref[...], low_ref[...] = split(x_ref[...].T)


def moved(values, step):
    count = values.shape[0]
    at = lax.broadcasted_iota(jnp.int32, values.shape, 0) & 15
    if step == 0:
        return values
    if step > 0:
        return jnp.where(at < 15, pltpu.roll(values, count - 1, 0), 0.0)
    return jnp.where(at > 0, pltpu.roll(values, 1, 0), 0.0)


def window(extended, images, row, width):
    tall = extended.shape[0] // images // 16
    cells = extended.reshape(images, tall, 16, extended.shape[1])
    return cells[:, row : row + tall - 2, :, width].reshape(images * (tall - 2) * 16, -1)


def extend(place, cells, above, below):
    images, tall, broad, width = place.shape
    place[:, 1 : tall - 1] = cells[...].reshape(images, tall - 2, broad, width)
    place[:, 0] = above[...].reshape(images, broad, width)
    place[:, tall - 1] = below[...].reshape(images, broad, width)
    return place[...].reshape(-1, width)


def conv_kernel(g1_ref, par_ref, z_ref, ext_ref, above_ref, below_ref, own_ref, first_high, first_low, second_high, second_low,
                z2_ref, a_ref, stat_ref, counts_ref, pay_ref, tile, zext):
    images = zext.shape[0]
    tall = zext.shape[1] - 2
    width = z_ref.shape[1]
    group = width // 2
    gathered = g1_ref[...]
    counts = gathered[:, 4, :]
    counts_ref[...] = counts
    mean, inv, total = merge_stats(gathered, counts, width)
    tile[...] = jnp.zeros_like(tile)
    put(tile, 0, mean)
    put(tile, 2, inv)
    put(tile, 4, total[None])
    stat_ref[...] = tile[...]
    y = (extend(zext, z_ref, above_ref, below_ref) - mean) * inv * get(par_ref, 0, 2) + get(par_ref, 2, 2)
    a = y * jax.nn.sigmoid(y) * wide(ext_ref[...].reshape(-1, 128), width)
    a_ref[...] = a
    a_ref.send()
    shifted = [split(moved(a, step)) for step in (-1, 0, 1)]
    half = z2_ref.shape[1] // 2
    for ref in (first_high, first_low, second_high, second_low):
        ref.ready()
    for g in range(2):
        cols = slice(g * group, (g + 1) * group)
        left = [
            jnp.concatenate(
                [window(shifted[tap % 3][part], images, tap // 3, cols) for tap in range(9)], axis=1
            )
            for part in range(2)
        ]
        outs = slice(g * half, (g + 1) * half)
        right = [ref[...] for ref in ((first_high, first_low), (second_high, second_low))[g]]
        z2_ref[:, outs] = product(left, right, NN)
    z2_ref.send()
    z2 = z2_ref[...]
    own = own_ref[...]
    sums, squares = local_stats(z2, wide(own, z2.shape[1]), wide(column_sum(own), z2.shape[1]))
    put(tile, 0, sums)
    put(tile, 4, squares)
    pay_ref[...] = jnp.broadcast_to(tile[...][None], pay_ref.shape)


def taps_kernel(images, a_ref, high_ref, low_ref):
    group = a_ref.shape[1] // 2
    a = a_ref[...]
    shifted = [moved(a, step) for step in (-1, 0, 1)]
    for g in range(2):
        cols = slice(g * group, (g + 1) * group)
        for tap in range(9):
            high, low = split(window(shifted[tap % 3], images, tap // 3, cols).T)
            high_ref[g, tap * group : (tap + 1) * group, :] = high
            low_ref[g, tap * group : (tap + 1) * group, :] = low
        high_ref.send(g)
        low_ref.send(g)


def pixel_count(rows_ref, cols_ref):
    rows = jnp.sum(rows_ref[...].astype(f32), axis=1, keepdims=True)
    return rows * jnp.sum(cols_ref[...].astype(f32), axis=1, keepdims=True)


def pool_kernel(g2_ref, counts_ref, par_ref, rows_ref, cols_ref, z_ref, own_ref, w_ref, a_ref, stat_ref, pooled_ref, pay_ref):
    images = rows_ref.shape[0]
    width = z_ref.shape[1]
    mid = width // 2
    mean, inv, total = merge_stats(g2_ref[...], counts_ref[...], width)
    put(stat_ref, 0, mean)
    put(stat_ref, 4, inv)
    gain, shift = get(par_ref, 4, 4), get(par_ref, 8, 4)
    pieces = len(z_ref.parts)
    sums = []
    for i in range(pieces):
        y = (z_ref.chunk(i) - mean) * inv * gain + shift
        a = y * jax.nn.sigmoid(y) * wide(own_ref.chunk(i), width)
        a_ref.put(i, a)
        sums.append(image_sum(a, images // pieces))
    sums = jnp.concatenate(sums, axis=0)
    pooled = (sums[:, :mid] + sums[:, mid:]) / pixel_count(rows_ref, cols_ref)
    pooled_ref[...] = pooled
    pay_ref[...] = jnp.broadcast_to(exact(pooled, w_ref[...], NN)[None], pay_ref.shape)


def slope_of(values, mean, inv, gain, shift):
    normed = (values - mean) * inv
    y = normed * gain + shift
    sigma = jax.nn.sigmoid(y)
    return sigma * (1.0 + y * (1.0 - sigma)), normed


def slope_kernel(stat_ref, par_ref, rows_ref, cols_ref, own_ref, z_ref, slope_ref, normed_ref, sums_ref):
    images = rows_ref.shape[0]
    width = z_ref.shape[1]
    mean, inv = get(stat_ref, 0, 4), get(stat_ref, 4, 4)
    gain, shift = get(par_ref, 4, 4), get(par_ref, 8, 4)
    pieces = len(z_ref.parts)
    sums, cross = [], []
    for i in range(pieces):
        slope, normed = slope_of(z_ref.chunk(i), mean, inv, gain, shift)
        slope = slope * wide(own_ref.chunk(i), width)
        normed_ref.put(i, normed)
        slope_ref.put(i, slope)
        sums.append(image_sum(slope, images // pieces))
        cross.append(image_sum(slope * normed, images // pieces))
    pixels = pixel_count(rows_ref, cols_ref)
    sums_ref[:, :width] = jnp.concatenate(sums, axis=0) / pixels
    sums_ref[:, width:] = jnp.concatenate(cross, axis=0) / pixels


def expand_kernel(g3_ref, par_ref, w_ref, a_ref, wh_ref, wl_ref, own_ref,
                  mixed_ref, z_ref, weights_ref, normed_ref, pre_ref, act_ref, inv_ref, pay_ref, tile, acts):
    own_images = weights_ref.shape[0]
    mid = mixed_ref.shape[1]
    devices = g3_ref.shape[0]
    rows = lax.axis_size("rows")
    f_one = jnp.sum(g3_ref[...].reshape(rows, devices // rows * own_images, -1), axis=0)
    mean = jnp.mean(f_one, axis=0, keepdims=True)
    centered = f_one - mean
    inv = lax.rsqrt(jnp.mean(centered * centered, axis=0, keepdims=True) + epsilon)
    normed = centered * inv
    pre = normed * par_ref[12:13, :] + par_ref[13:14, :]
    normed_ref[...] = normed
    pre_ref[...] = pre
    inv_ref[...] = inv
    acts[...] = pre * jax.nn.sigmoid(pre)
    at = pl.multiple_of(lax.axis_index("batch") * own_images, own_images)
    act = acts[pl.ds(at, own_images), :]
    act_ref[...] = act
    logits = exact(act, w_ref[...], NN) + get(par_ref, 14, 4)
    lead = logits[:, :mid] - logits[:, mid:]
    first, second = jax.nn.sigmoid(lead), jax.nn.sigmoid(-lead)
    weights_ref[:, :mid] = first
    weights_ref[:, mid:] = second
    a = a_ref[...]
    mixed = per_image(first, a) * a[:, :mid] + per_image(second, a) * a[:, mid:]
    mixed_ref[...] = mixed
    mixed_ref.send()
    left, right = split(mixed), (wh_ref[...], wl_ref[...])
    for i, part in enumerate(z_ref.parts):
        rows = slice(part.start, part.start + part.size)
        z_ref.put(i, product([each[rows] for each in left], right, NN))
    z = z_ref[...]
    width = z.shape[1]
    own = wide(own_ref[...], width)
    sums, squares = local_stats(z, own, wide(column_sum(own_ref[...]), width))
    put(tile, 0, sums)
    put(tile, width // 128, squares)
    pay_ref[...] = jnp.broadcast_to(tile[...][None], pay_ref.shape)


def output_kernel(g4_ref, counts_ref, par_ref, own_ref, z_ref, x_ref, cot_ref, *refs):
    slope_refs, (grad_ref, stat_ref, slopes_ref, pay_ref, tile) = refs[:-5], refs[-5:]
    width = z_ref.shape[1]
    groups = width // 128
    mean, inv, total = merge_stats(g4_ref[...], counts_ref[...], width)
    put(stat_ref, 0, mean)
    put(stat_ref, groups, inv)
    gain, shift = get(par_ref, 18, groups), get(par_ref, 26, groups)
    flat, cross = 0.0, 0.0
    for i in range(len(z_ref.parts)):
        own = wide(own_ref.chunk(i), width)
        normed = (z_ref.chunk(i) - mean) * inv
        pre = normed * gain + shift + x_ref.chunk(i)
        sigma = jax.nn.sigmoid(pre)
        grad = cot_ref.chunk(i) * own * (sigma * (1.0 + pre * (1.0 - sigma)))
        grad_ref.put(i, grad)
        flat = flat + column_sum(grad)
        cross = cross + column_sum(grad * normed)
    put(tile, 0, flat)
    put(tile, groups, cross)
    pay_ref[...] = jnp.broadcast_to(tile[...][None], pay_ref.shape)
    sum_kernel(*slope_refs, slopes_ref)


def result_kernel(stat_ref, par_ref, own_ref, z_ref, x_ref, out_ref, mark_ref):
    width = z_ref.shape[1]
    groups = width // 128
    mean, inv = get(stat_ref, 0, groups), get(stat_ref, groups, groups)
    gain, shift = get(par_ref, 18, groups), get(par_ref, 26, groups)
    for i in range(len(z_ref.parts)):
        pre = (z_ref.chunk(i) - mean) * inv * gain + shift + x_ref.chunk(i)
        out_ref.put(i, pre * jax.nn.sigmoid(pre) * wide(own_ref.chunk(i), width))
    mark_ref[...] = own_ref[:8, :]


def mixed_kernel(digit, g5_ref, stat1_ref, stat3_ref, par_ref, own_ref, grad_ref, z_ref, wh_ref, wl_ref, a_ref, weights_ref,
                 w_ref, slope_ref, normed_ref, *refs):
    shares, (gm_ref, dsum_ref, grads_ref, gain_ref, shift_ref, slopes_ref, pay_ref, tile) = refs[: digit.size], refs[digit.size :]
    width = z_ref.shape[1]
    mid = gm_ref.shape[1]
    images = weights_ref.shape[0]
    groups = width // 128
    grads_ref[...] = jnp.sum(g5_ref[...], axis=0)
    shift_ref[...] = grads_ref[:groups, :]
    gain_ref[...] = grads_ref[groups:, :]
    count = wide(stat1_ref[4:5, :], width)
    mean, inv = get(stat3_ref, 0, groups), get(stat3_ref, groups, groups)
    flat = get(grads_ref, 0, groups) / count
    cross = get(grads_ref, groups, groups) / count
    scale = get(par_ref, 18, groups) * inv
    for i in range(len(z_ref.parts)):
        normed = (z_ref.chunk(i) - mean) * inv
        dz = scale * (grad_ref.chunk(i) - flat - normed * cross) * wide(own_ref.chunk(i), width)
        gm_ref[z_ref.parts[i]] = product(split(dz), (wh_ref[...], wl_ref[...]), NT)
    gm = gm_ref[...]
    gm_ref.send()
    a = a_ref[...]
    weights = weights_ref[...]
    gate = image_sum(gm * (a[:, :mid] - a[:, mid:]), images)
    dsum = weights[:, :mid] * weights[:, mid:] * gate
    dsum_ref[...] = dsum
    tile[...] = jnp.zeros_like(tile)
    tile[:images, :] = exact(dsum, w_ref[:, :mid] - w_ref[:, mid:], NT)
    slope = slope_ref[...] * jnp.concatenate([gm, gm], axis=1)
    put(tile, 8, column_sum(weights * image_sum(slope, images)))
    put(tile, 12, column_sum(weights * image_sum(slope * normed_ref[...], images)))
    pay_ref[...] = jnp.broadcast_to(tile[...][None], pay_ref.shape)
    digit.gather(shares, slopes_ref)


def expand_grad_kernel(core, grads_ref, stat1_ref, stat3_ref, par_ref, mixed_ref, act_ref, dsum_ref, own_ref, grad_ref, z_ref,
                       keep_ref, send_ref, excite_ref, term):
    width = z_ref.shape[1]
    groups = width // 128
    count = wide(stat1_ref[4:5, :], width)
    mean, inv = get(stat3_ref, 0, groups), get(stat3_ref, groups, groups)
    flat = get(grads_ref, 0, groups) / count
    cross = get(grads_ref, groups, groups) / count
    scale = get(par_ref, 18, groups) * inv
    left = split(mixed_ref[...].T)
    rows, span = left[0].shape[0], term.shape[1]
    for i, part in enumerate(z_ref.parts):
        normed = (z_ref.chunk(i) - mean) * inv
        dz = scale * (grad_ref.chunk(i) - flat - normed * cross) * wide(own_ref.chunk(i), width)
        right = split(dz)
        some = [each[:, part.start : part.start + part.size] for each in left]
        for j in range(term.shape[0] // rows):
            value = product(some, [each[:, j * span : (j + 1) * span] for each in right], NN)
            if i:
                value = value + term[j * rows : (j + 1) * rows, :]
            term[j * rows : (j + 1) * rows, :] = value
    core.scatter([term], [keep_ref, send_ref])
    excite_ref[...] = exact(act_ref[...], dsum_ref[...], TN)


def turned_rows(left, refs, row, taps):
    return product(left, [ref[row * taps : (row + 1) * taps, :] for ref in refs], NT)


def fold(total, group):
    return moved(total[:, :group], 1) + total[:, group : 2 * group] + moved(total[:, 2 * group :], -1)


def back_kernel(digit, g6_ref, pre_ref, fcn_ref, inv_ref, par_ref, wsq_ref, pooled_ref, stat1_ref, stat2_ref, rows_ref,
                cols_ref, weights_ref, mine_ref, other_ref, own_ref, gm_ref, slope_ref, normed_ref, *refs):
    w_refs, (up_ref, down_ref), dz_refs, (squeeze_ref, gain_ref, flat_ref, fc_gain_ref, fc_flat_ref, gf, owned, slopes) = (
        refs[:4], refs[4:6], refs[6:10], refs[10:]
    )
    images = rows_ref.shape[0]
    tall = dz_refs[0].shape[1] - 2
    width = normed_ref.shape[1]
    mid = width // 2
    groups = width // 128
    rows = lax.axis_size("rows")
    shared = g6_ref[...]
    pre = pre_ref[...]
    fcn = fcn_ref[...]
    sigma = jax.nn.sigmoid(pre)
    total = pre.shape[0]
    grad = jnp.sum(shared[:, :images].reshape(rows, total, -1), axis=0) * (sigma * (1.0 + pre * (1.0 - sigma)))
    flat, cross = column_sum(grad), column_sum(grad * fcn)
    fc_gain_ref[...] = cross
    fc_flat_ref[...] = flat
    gf[...] = par_ref[12:13, :] * inv_ref[...] * (grad - flat / total - fcn * cross / total)
    at = pl.multiple_of(lax.axis_index("batch") * images, images)
    mine = gf[pl.ds(at, images), :]
    squeeze = exact(pooled_ref[...], mine, TN)
    half_rows = squeeze.shape[0] // 2
    squeeze_ref[:, : squeeze.shape[1]] = squeeze[:half_rows]
    squeeze_ref[:, squeeze.shape[1] :] = squeeze[half_rows:]
    spread = exact(gf[...], wsq_ref[...], NT)
    owned[...] = spread
    own_spread = owned[pl.ds(at, images), :] / pixel_count(rows_ref, cols_ref)
    for flipped, half in enumerate((mine_ref, other_ref)):
        for block in range(half.shape[0] // images):
            here = pl.multiple_of((2 * block + (digit.own() ^ flipped)) * images, images)
            slopes[pl.ds(here, images), :] = half[block * images : (block + 1) * images, :]
    base = jnp.sum(shared[:, 8:], axis=0)
    count = wide(stat1_ref[4:5, :], mid)
    weights = weights_ref[...]
    gm = gm_ref[...]
    shared_part = per_image(own_spread, gm)
    mask = wide(own_ref[...], mid)
    zero = jnp.zeros((images, 16, mid), bf16)
    for ref in dz_refs:
        ref[:, 0] = zero
        ref[:, tall + 1] = zero
    for g in range(2):
        outs = slice(g * mid, (g + 1) * mid)
        crosses = slice(width + g * mid, width + (g + 1) * mid)
        half = groups // 2
        flat_two = get(base, g * half, half) + column_sum(spread * slopes[:, outs])
        cross_two = get(base, groups + g * half, half) + column_sum(spread * slopes[:, crosses])
        put(gain_ref, g * half, cross_two)
        put(flat_ref, g * half, flat_two)
        scale = get(par_ref, 4 + g * half, half) * get(stat2_ref, groups + g * half, half)
        upstream = per_image(weights[:, outs], gm) * gm + shared_part
        dz = scale * (upstream * slope_ref[:, outs] - flat_two / count - normed_ref[:, outs] * (cross_two / count)) * mask
        for ref, part in zip(dz_refs[2 * g : 2 * g + 2], split(dz)):
            ref[:, 1 : tall + 1] = part.reshape(images, tall, 16, mid)
            ref.send()
    group = up_ref.shape[1] // 2
    for g in range(2):
        cols = slice(g * group, (g + 1) * group)
        for side, row, tap in ((up_ref, 1, 0), (down_ref, tall, 2)):
            left = [ref[:, row].reshape(-1, mid) for ref in dz_refs[2 * g : 2 * g + 2]]
            side[:, cols] = fold(turned_rows(left, w_refs[2 * g : 2 * g + 2], tap, 3 * group), group)


def group_kernel(core, *refs):
    dz_refs, (squeeze_ref, excite_ref, th_ref, tl_ref, keep_ref, send_ref, out_ref) = refs[:4], refs[4:]
    tall = dz_refs[0].shape[1] - 2
    taps = th_ref.shape[1]
    for g in range(2):
        right = [ref[:, 1 : tall + 1].reshape(-1, ref.shape[3]) for ref in dz_refs[2 * g : 2 * g + 2]]
        out_ref[g * taps : (g + 1) * taps, :] = product((th_ref.chunk(g)[0], tl_ref.chunk(g)[0]), right, NN)
    inter = excite_ref.shape[0]
    out_ref[2 * taps : 2 * taps + inter, :] = excite_ref[...]
    out_ref[2 * taps + inter :, :] = squeeze_ref[...]
    core.scatter([out_ref], [keep_ref, send_ref])


def input_grad_kernel(g, par_ref, stat_ref, z_ref, own_ref, above_ref, below_ref, dzh_ref, dzl_ref, wh_ref, wl_ref, *refs):
    images, tall = dzh_ref.shape[0], dzh_ref.shape[1] - 2
    group = z_ref.shape[1] // 2
    cols = slice(g * group, (g + 1) * group)
    total = None
    for row in range(3):
        left = [ref[:, 2 - row : 2 - row + tall].reshape(-1, ref.shape[3]) for ref in (dzh_ref, dzl_ref)]
        term = turned_rows(left, (wh_ref, wl_ref), row, 3 * group)
        total = term if total is None else total + term
    place = refs[-1]
    place[...] = fold(total, group).reshape(place.shape)
    place[:, 0] += above_ref[:, cols].reshape(images, 16, group)
    place[:, tall - 1] += below_ref[:, cols].reshape(images, 16, group)
    grad = place[...].reshape(-1, group)
    mean, inv, gain, shift = [ref[row + g : row + g + 1, :] for ref, row in ((stat_ref, 0), (stat_ref, 2), (par_ref, 0), (par_ref, 2))]
    normed = (z_ref[:, cols] - mean) * inv
    y = normed * gain + shift
    sigma = jax.nn.sigmoid(y)
    dy = grad * wide(own_ref[...], group) * (sigma * (1.0 + y * (1.0 - sigma)))
    if g == 0:
        dy_ref, tile = refs[:2]
        tile[...] = jnp.zeros(tile.shape, f32)
    else:
        dsum_ref, before_ref, dy_ref, pay_ref, tile = refs[:5]
        tile[...] = before_ref[...]
        put(tile, 4, column_sum(dsum_ref[...]))
    dy_ref[...] = dy
    dy_ref.send()
    put(tile, g, column_sum(dy * normed))
    put(tile, 2 + g, column_sum(dy))
    if g:
        pay_ref[...] = jnp.broadcast_to(tile[...][None], pay_ref.shape)


def final_kernel(core, g7_ref, par_ref, stat_ref, first_ref, second_ref, z_ref, own_ref, th_ref, tl_ref,
                 keep_ref, send_ref, dzh_ref, dzl_ref, mark_ref, gain_ref, flat_ref, bias_ref, gains_ref, term):
    width = z_ref.shape[1]
    gains_ref[...] = jnp.sum(g7_ref[...], axis=0)
    mark_ref[...] = gains_ref[...]
    gain_ref[...] = gains_ref[0:2, :]
    flat_ref[...] = gains_ref[2:4, :]
    bias_ref[0:2, :] = gains_ref[4:6, :]
    bias_ref[2:4, :] = -gains_ref[4:6, :]
    cross, flat = get(gains_ref, 0, 2), get(gains_ref, 2, 2)
    count = wide(stat_ref[4:5, :], width)
    mean, inv = get(stat_ref, 0, 2), get(stat_ref, 2, 2)
    normed = (z_ref[...] - mean) * inv
    scale = get(par_ref, 0, 2) * inv
    dy = jnp.concatenate([first_ref[...], second_ref[...]], axis=1)
    dz = scale * (dy - flat / count - normed * (cross / count)) * wide(own_ref[...], width)
    high, low = split(dz)
    dzh_ref[...] = high
    dzl_ref[...] = low
    term[...] = product((th_ref[...], tl_ref[...]), (high, low), NN)
    core.scatter([term], [keep_ref, send_ref])


def images_kernel(dzh_ref, dzl_ref, wh_ref, wl_ref, grad_ref, out_ref):
    for i in range(len(grad_ref.parts)):
        left = [ref.chunk(i) for ref in (dzh_ref, dzl_ref)]
        out_ref.put(i, product(left, (wh_ref[...], wl_ref[...]), NT) + grad_ref.chunk(i))


def deal_kernel(plan, count, *refs):
    outs = list(refs[count:])
    for digit, stretches in plan:
        own = digit.own()
        for j in range(digit.size):
            out, at = outs.pop(0), 0
            for inputs, first, rows in stretches:
                each = rows // digit.size
                here = pl.ds(pl.multiple_of(first + (own ^ j) * each, 8), each)
                total = refs[inputs[0]][here, :]
                for k in inputs[1:]:
                    total = total + refs[k][here, :]
                out[at : at + each, :] = total
                at += each


def deal(plan, ins, **order):
    width = ins[0].shape[1]
    outs = []
    for digit, stretches in plan:
        rows = sum(rows for _, _, rows in stretches) // digit.size
        outs += [((rows, width), f32)] * digit.size
    return local_call(functools.partial(deal_kernel, plan, len(ins)), outs, ins, **order)


def stack_kernel(stretches, *refs):
    refs, out = refs[:-1], refs[-1]
    at = 0
    for inputs, first, rows in stretches:
        each = rows // out.shape[0]
        for d in range(out.shape[0]):
            here = slice(first + d * each, first + (d + 1) * each)
            total = refs[inputs[0]][here, :]
            for k in inputs[1:]:
                total = total + refs[k][here, :]
            out[d, at : at + each, :] = total
        at += each


def extra_pieces(extra, stacked):
    if extra.size == 1:
        return [stacked]
    total = local_call(lambda ref, out: out.__setitem__(Ellipsis, jnp.sum(ref[...], axis=0)), [(stacked.shape[1:], f32)], [stacked])[0]
    return extra.send([total] * extra.size)


def stacked_kernel(count, *refs):
    if count == 1:
        refs[-1][...] = jnp.sum(refs[0][...], axis=0)
    else:
        sum_kernel(*refs)


def halves_kernel(digit, *refs):
    pieces, outs = refs[: digit.size], refs[digit.size :]
    half = pieces[0].shape[0] // 2
    own = digit.own()
    for j, piece in enumerate(pieces):
        at = pl.ds(pl.multiple_of((own ^ j) * half, 8), half)
        for i, out in enumerate(outs):
            out[at, :] = piece[i * half : (i + 1) * half, :]


def pair_kernel(digits, *refs):
    outs = refs[4:]
    for i, digit in enumerate(digits):
        digit.gather(refs[2 * i : 2 * i + 2], outs[i] if len(outs) == 2 else outs[0].at[pl.ds(i * 2 * refs[0].shape[0], 2 * refs[0].shape[0])])


def last_kernel(core, expand_map, group_map, mine_ref, other_ref, expand_ref, group_ref, excite_ref, squeeze_ref, whole):
    core.gather([mine_ref, other_ref], whole)
    taps, mid = group_ref.shape[0], whole.shape[1]
    inter = squeeze_ref.shape[1]
    tall = expand_ref.shape[0]
    places = [
        (taps, lambda rows, value: group_ref.__setitem__((rows, slice(0, mid)), value)),
        (taps, lambda rows, value: group_ref.__setitem__((rows, slice(mid, 2 * mid)), value)),
        (inter, lambda rows, value: excite_ref.__setitem__((rows, slice(0, mid)), value)),
        (inter, lambda rows, value: squeeze_put(squeeze_ref, rows, value)),
    ]
    for at, first, rows in expand_map:
        j, m = first // tall, first % tall
        expand_ref[m : m + rows, j * mid : (j + 1) * mid] = whole[at : at + rows, :]
    for at, first, rows in group_map:
        base = 0
        for length, store in places:
            low, high = max(first, base), min(first + rows, base + length)
            if low < high:
                store(slice(low - base, high - base), whole[at + low - first : at + high - first, :])
            base += length
    excite_ref[:, mid:] = -excite_ref[:, :mid]


def squeeze_put(squeeze_ref, rows, value):
    half = squeeze_ref.shape[0] // 2
    width = squeeze_ref.shape[1]
    squeeze_ref[rows, :] = value[:, :width]
    squeeze_ref[slice(half + rows.start, half + rows.stop), :] = value[:, width:]


def on_device(
    images,
    w_reduce,
    gain_one,
    shift_one,
    w_group,
    gain_two,
    shift_two,
    w_squeeze,
    gain_fc,
    shift_fc,
    w_excite,
    excite_bias,
    w_expand,
    gain_three,
    shift_three,
    valid_rows,
    valid_cols,
    cotangent,
):
    count, tall, broad, chan = images.shape
    mid = w_reduce.shape[1]
    inter = w_squeeze.shape[1]
    duo = 2 * mid
    taps = 9 * mid // 2
    cells = count * tall * broad
    longer = count * (tall + 2) * broad
    edge = count * broad
    devices = lax.axis_size("rows") * lax.axis_size("batch")
    all_images = count * lax.axis_size("batch")
    x = images.reshape(cells, chan)
    cot = cotangent.reshape(cells, chan)
    pay8 = ((devices, 8, 128), f32)
    pay16 = ((devices, 16, 128), f32)
    tile8 = pltpu.VMEM((8, 128), f32)
    tile16 = pltpu.VMEM((16, 128), f32)
    twice = lambda *shape: [(shape, bf16)] * 2
    flat_w = w_group.reshape(taps, duo)
    vectors = (gain_one, shift_one, gain_two, shift_two, gain_fc, shift_fc, excite_bias, gain_three, shift_three)
    core, line, depth, extra = digits()

    z_one, ext, own, first, last, pay = call(
        reduce_kernel,
        [((cells, mid), f32), ((count, tall + 2, broad, 128), f32), ((cells, 128), f32), ((edge, mid), f32),
         ((edge, mid), f32), pay8],
        [valid_rows, valid_cols, w_reduce, x],
        [tile8],
        chunks={3: 2},
        near_outs=(3, 4, 5),
    )
    g1 = share(pay)
    above, below = halos(first, last)
    *group_parts, weh, wel, wrh, wrl, par = call(
        parts_kernel,
        [*twice(taps, mid), *twice(taps, mid), *twice(mid, chan), *twice(chan, mid), ((40, 128), f32)],
        [flat_w, w_expand, w_reduce, *[v.reshape(1, -1) for v in vectors]],
        chunks={0: 4, 1: 2, 2: 2},
        out_chunks={0: 4, 1: 4, 2: 4, 3: 4, 4: 2, 5: 2, 6: 2, 7: 2},
        after=[z_one],
    )
    z_two, a_one, stat1, counts, pay = call(
        conv_kernel,
        [((cells, duo), f32), ((longer, mid), f32), ((8, 128), f32), ((devices, 128), f32), pay8],
        [g1, par, z_one, ext, above, below, own, *group_parts],
        [tile8, pltpu.VMEM((count, tall + 2, broad, mid), f32)],
        near=(0, 4, 5),
        near_outs=(4,),
    )
    g2 = share(pay)
    xth, xtl = call(turned_kernel, twice(chan, cells), [x], after=[stat1])
    a_two, stat2, pooled, pay = call(
        pool_kernel,
        [((cells, duo), f32), ((8, 128), f32), ((count, mid), f32), ((devices, count, inter), f32)],
        [g2, counts, par, valid_rows, valid_cols, z_two, own, w_squeeze],
        chunks={5: 2, 6: 2},
        out_chunks={0: 2},
        after=[xth],
        near=(0,),
        near_outs=(3,),
    )
    g3 = share(pay)
    slope_two, normed_two, slopes = call(
        slope_kernel,
        [((cells, duo), f32), ((cells, duo), f32), ((count, 2 * duo), f32)],
        [stat2, par, valid_rows, valid_cols, own, z_two],
        chunks={4: 2, 5: 2},
        out_chunks={0: 2, 1: 2},
    )
    mixed, z_three, weights, fc_normed, fc_pre, fc_act, fc_inv, pay = call(
        expand_kernel,
        [((cells, mid), f32), ((cells, chan), f32), ((count, duo), f32), ((all_images, inter), f32),
         ((all_images, inter), f32), ((count, inter), f32), ((1, inter), f32), pay16],
        [g3, par, w_excite, a_two, weh, wel, own],
        [tile16, pltpu.VMEM((all_images, inter), f32)],
        out_chunks={1: 2},
        after=[slopes],
        near=(0,),
        near_outs=(7,),
    )
    g4 = share(pay)
    slopes = line.send([slopes] * line.size)
    grad_pre, stat3, slopes, pay = call(
        output_kernel,
        [((cells, chan), f32), ((16, 128), f32), ((count, 2 * duo), f32), pay16],
        [g4, counts, par, own, z_three, x, cot, *slopes],
        [tile16],
        chunks={3: 4, 4: 4, 5: 4, 6: 4},
        out_chunks={0: 4},
        near=(0, *range(7, 7 + line.size)),
        near_outs=(2, 3),
    )
    g5 = share(pay)
    slopes = depth.send([slopes] * depth.size)
    tph, tpl = call(functools.partial(taps_kernel, count), twice(2, taps, cells), [a_one], out_chunks={0: 2, 1: 2}, after=[stat3])
    grad_mixed, dsum, grads_three, grad_gain_three, grad_shift_three, slopes, pay = call(
        functools.partial(mixed_kernel, depth),
        [((cells, mid), f32), ((count, mid), f32),
         ((16, 128), f32), ((8, 128), f32), ((8, 128), f32), ((depth.size * count, 2 * duo), f32), pay16],
        [g5, stat1, stat3, par, own, grad_pre, z_three, weh, wel, a_two, weights, w_excite, slope_two, normed_two, *slopes],
        [tile16],
        after=[tph],
        near=(0, *range(14, 14 + depth.size)),
        near_outs=(5, 6),
    )
    g6 = share(pay)
    *expand_sum, excite_term = call(
        functools.partial(expand_grad_kernel, core),
        [*core.outs(mid * chan // mid, mid), ((inter, mid), f32)],
        [grads_three, stat1, stat3, par, mixed, fc_act, dsum, own, grad_pre, z_three],
        [pltpu.VMEM((chan, mid), f32)],
        chunks={7: 2, 8: 2, 9: 2},
    )
    if extra.size > 1:
        slopes = gather_more(extra, extra.send([slopes] * extra.size))
    slopes = core.send([slopes] * 2)
    packed = 2 * taps + 2 * inter
    up, down, *dz_parts, squeeze_term, grad_gain_two, grad_shift_two, grad_gain_fc, grad_shift_fc = call(
        functools.partial(back_kernel, core),
        [((edge, mid), f32), ((edge, mid), f32), *twice(count, tall + 2, broad, mid), *twice(count, tall + 2, broad, mid), ((inter, mid), f32),
         ((duo // 128, 128), f32), ((duo // 128, 128), f32), ((1, inter), f32), ((1, inter), f32)],
        [g6, fc_pre, fc_normed, fc_inv, par, w_squeeze, pooled, stat1, stat2, valid_rows, valid_cols, weights, *slopes, own,
         grad_mixed, slope_two, normed_two, *group_parts],
        [pltpu.VMEM((all_images, inter), f32), pltpu.VMEM((all_images, mid), f32), pltpu.VMEM((all_images, 2 * duo), f32)],
        after=[excite_term],
        near=(0, 12, 13),
        near_outs=(0, 1),
    )
    above, below = halos(up, down)
    group_sum = call(
        functools.partial(group_kernel, core),
        core.outs(packed, mid),
        [*dz_parts, squeeze_term, excite_term, tph, tpl],
        [pltpu.VMEM((packed, mid), f32)],
        chunks={6: 2, 7: 2},
        near_outs=(0, 1),
    )
    expand_sum = core.send(expand_sum)
    group_sum = core.send([group_sum[0], gate(group_sum[1], [above, below])])
    dy_first, tile = call(
        functools.partial(input_grad_kernel, 0),
        [((cells, mid // 2), f32), ((8, 128), f32)],
        [par, stat1, z_one, own, above, below, *dz_parts[:2], *group_parts[:2]],
        [pltpu.VMEM((count, tall, broad, mid // 2), f32)],
        near=(4, 5),
    )
    first_bit, second_bit = line.bits()
    some, more = expand_sum[0].shape[0] // 2, group_sum[0].shape[0] // 2
    both_of = lambda start, a, b: [((0, 1), start * a, a), ((2, 3), start * b, b)]
    first_half = lambda digit: (digit, both_of(0, some, more))
    second_half = lambda digit: (digit, both_of(1, some, more))
    keep_a, send_a, keep_b, send_b = deal(
        [first_half(first_bit), second_half(second_bit)], [*expand_sum, *group_sum], after=[tile]
    )
    come_a, come_b = first_bit.send([keep_a, send_a]), second_bit.send([keep_b, send_b])
    place = pltpu.VMEM((count, tall, broad, mid // 2), f32)
    dy_second, pay = call(
        functools.partial(input_grad_kernel, 1),
        [((cells, mid // 2), f32), pay8],
        [par, stat1, z_one, own, above, below, *dz_parts[2:], *group_parts[2:], dsum, tile],
        [tile8, place],
        beside=[keep_a],
        near=(4, 5),
        near_outs=(1,),
    )
    g7 = share(pay)
    some, more = some // 2, more // 2
    turn = lambda k: [((k, k + 1), 0, some), ((k, k + 1), some, more)]
    keep_a, send_a, keep_b, send_b = deal([(second_bit, turn(0)), (first_bit, turn(2))], [*come_a, *come_b], after=[dy_second])
    *reduce_sum, dzh, dzl, mark_one, grad_gain_one, grad_shift_one, grad_bias = call(
        functools.partial(final_kernel, core),
        [*core.outs(chan, mid), *twice(cells, mid), ((8, 128), f32), *[((mid // 128, 128), f32)] * 2, ((duo // 128, 128), f32)],
        [g7, par, stat1, dy_first, dy_second, z_one, own, xth, xtl],
        [tile8, pltpu.VMEM((chan, mid), f32)],
        beside=[keep_a],
        near=(0,),
        near_outs=(0, 1),
    )
    come_a, come_b = second_bit.send([keep_a, send_a]), first_bit.send([keep_b, send_b])
    some, more = some // 2, more // 2
    stretches = turn(0) + turn(2)
    (joined,) = local_call(
        functools.partial(stack_kernel, stretches),
        [((depth.size, (some + more) * 2 // depth.size, mid), f32)],
        [*come_a, *come_b],
        after=[mark_one],
    )
    reduce_sum[1] = gate(reduce_sum[1], [joined])
    joined = depth.trade(joined)
    reduce_sum = scatter_more(line, core.send(reduce_sum))
    (grad_images,) = call(
        images_kernel,
        [((cells, chan), f32)],
        [dzh, dzl, wrh, wrl, grad_pre],
        chunks={0: 2, 1: 2, 4: 2},
        out_chunks={0: 2},
        beside=[reduce_sum[0]],
    )
    reduce_sum = scatter_more(depth, line.send(reduce_sum), after=[grad_images])
    (joined,) = local_call(
        functools.partial(stacked_kernel, extra.size), [(joined.shape[1:], f32)], extra_pieces(extra, joined), beside=[reduce_sum[0]]
    )
    rows_in = depth.size * joined.shape[0]
    block_out, mark = call(
        result_kernel,
        [((cells, chan), f32), ((8, 128), f32)],
        [stat3, par, own, z_three, x],
        chunks={2: 4, 3: 4, 4: 4},
        out_chunks={0: 4},
        beside=[joined],
    )
    half_a, half_b = local_call(
        functools.partial(halves_kernel, depth),
        [((rows_in // 2, mid), f32)] * 2,
        depth.send([joined] * depth.size),
        after=[mark],
    )
    reduce_sum = finish_sum(depth.send(reduce_sum), extra, beside=[half_a])
    half_a, half_b = local_call(
        functools.partial(pair_kernel, [second_bit, first_bit]),
        [((rows_in, mid), f32)] * 2,
        [*second_bit.send([half_a] * 2), *first_bit.send([half_b] * 2)],
        beside=[reduce_sum],
    )
    reduce_sum = gather_more(depth, depth.send([reduce_sum] * depth.size), beside=[half_a])
    (joined,) = local_call(
        functools.partial(pair_kernel, [first_bit, second_bit]),
        [((4 * rows_in, mid), f32)],
        [*first_bit.send([half_a] * 2), *second_bit.send([half_b] * 2)],
        beside=[reduce_sum],
    )
    expand_map, group_map = [], []
    at = 0
    some, more = some // depth.size, more // depth.size
    for half in range(core.size):
        for part in range(2):
            for outer in range(2):
                for inner in range(2):
                    for deep in range(depth.size):
                        block = (((half * 2 + part) * 2 + outer) * 2 + inner) * depth.size + deep
                        expand_map.append((at, block * some, some))
                        group_map.append((at + some, block * more, more))
                        at += some + more
    grad_w_expand, grad_w_group, grad_w_excite, grad_w_squeeze = call(
        functools.partial(last_kernel, core, expand_map, group_map),
        [((mid, chan), f32), ((taps, duo), f32), ((inter, duo), f32), ((mid, inter), f32)],
        core.send([joined] * 2),
        [pltpu.VMEM((chan + packed, mid), f32)],
        near=(0, 1),
    )
    reduce_sum = gather_more(line, line.send([reduce_sum] * line.size), after=[grad_w_squeeze])
    (grad_w_reduce,) = call(
        functools.partial(gather_kernel, core), [((chan, mid), f32)], core.send([reduce_sum] * 2), near=(0, 1)
    )
    return (
        block_out.reshape(images.shape),
        grad_images.reshape(images.shape),
        grad_w_reduce,
        grad_gain_one.reshape(-1),
        grad_shift_one.reshape(-1),
        grad_w_group.reshape(w_group.shape),
        grad_gain_two.reshape(-1),
        grad_shift_two.reshape(-1),
        grad_w_squeeze,
        grad_gain_fc.reshape(-1),
        grad_shift_fc.reshape(-1),
        grad_w_excite,
        grad_bias.reshape(-1),
        grad_w_expand,
        grad_gain_three.reshape(-1),
        grad_shift_three.reshape(-1),
    )


def solution(mesh):
    maps = P("batch", "rows", None, None)
    return jax.shard_map(
        on_device,
        mesh=mesh,
        in_specs=(maps,) + (P(),) * 14 + (P("batch", None), P("batch", None), maps),
        out_specs=(maps, maps) + (P(),) * 14,
        check_vma=False,
    )
```

```python
import functools

import jax
import jax.numpy as jnp
from jax import lax
from jax.experimental import pallas as pl
from jax.experimental.pallas import tpu as pltpu
from jax.sharding import PartitionSpec as P

epsilon = 1e-05
f32 = jnp.float32
bf16 = jnp.bfloat16
highest = lax.Precision.HIGHEST
both = ("rows", "batch")
NN = ((1,), (0,))
NT = ((1,), (1,))
TN = ((0,), (0,))


def split(values):
    high = values.astype(bf16)
    return high, (values - high.astype(f32)).astype(bf16)


def dot(left, right, dims):
    return lax.dot_general(left, right, (dims, ((), ())), preferred_element_type=f32)


def product(left, right, dims):
    return dot(left[0], right[0], dims) + (
        dot(left[0], right[1], dims) + dot(left[1], right[0], dims)
    )


def exact(left, right, dims):
    return lax.dot_general(
        left, right, (dims, ((), ())), preferred_element_type=f32, precision=highest
    )


def put(tile, row, vector):
    for j in range(vector.shape[1] // 128):
        tile[row + j : row + j + 1, :] = vector[:, j * 128 : (j + 1) * 128]


def get(tile, row, count):
    return jnp.concatenate([tile[row + j : row + j + 1, :] for j in range(count)], axis=1)


def wide(mask, width):
    return jnp.concatenate([mask] * (width // 128), axis=1)


def column_sum(values):
    return jnp.sum(values, axis=0, keepdims=True)


def image_sum(values, images):
    return jnp.sum(values.reshape(images, values.shape[0] // images, values.shape[1]), axis=1)


def per_image(vector, values):
    count, width = vector.shape
    each = values.shape[0] // count
    return jnp.broadcast_to(vector[:, None, :], (count, each, width)).reshape(values.shape[0], width)


def merge_stats(gathered, counts, width):
    groups = width // 128
    own = jnp.maximum(counts, 1.0)
    total = jnp.sum(counts, axis=0)
    means, inverses = [], []
    for j in range(groups):
        sums = gathered[:, j, :]
        squares = gathered[:, groups + j, :]
        mean = jnp.sum(sums, axis=0, keepdims=True) / total
        shift = sums / own - mean
        spread = jnp.sum(squares + counts * shift * shift, axis=0, keepdims=True) / total
        means.append(mean)
        inverses.append(lax.rsqrt(spread + epsilon))
    return jnp.concatenate(means, axis=1), jnp.concatenate(inverses, axis=1), total


def local_stats(values, mask, count):
    sums = column_sum(values * mask)
    centered = values - sums / jnp.maximum(count, 1.0)
    return sums, column_sum(centered * centered * mask)


def own_rows(extended, images):
    rows, width = extended.shape
    tall = rows // images // 16
    return extended.reshape(images, tall, 16, width)[:, 1 : tall - 1].reshape(-1, width)


class In:
    def __init__(self, source, target, sems, chunks):
        self.ref, self.shape, self.dtype = target, target.shape, target.dtype
        rows = self.shape[0] // chunks
        self.parts = [pl.ds(i * rows, rows) for i in range(chunks)]
        self.copies = [
            pltpu.make_async_copy(source.at[part], target.at[part], sems.at[i])
            for i, part in enumerate(self.parts)
        ]
        self.due = list(range(chunks))

    def start(self):
        for copy in self.copies:
            copy.start()

    def ready(self):
        while self.due:
            self.copies[self.due.pop(0)].wait()
        return self.ref

    def chunk(self, i):
        if i in self.due:
            self.due.remove(i)
            self.copies[i].wait()
        return self.ref[self.parts[i]]

    def __getitem__(self, index):
        return self.ready()[index]


class Near:
    def __init__(self, ref):
        self.ref, self.shape, self.dtype = ref, ref.shape, ref.dtype

    def start(self, i=None):
        pass

    ready = send = start

    def finish(self):
        pass

    def __getitem__(self, index):
        return self.ref[index]

    def __setitem__(self, index, value):
        self.ref[index] = value


class Out:
    def __init__(self, source, target, sems, chunks):
        self.ref, self.shape, self.dtype = source, source.shape, source.dtype
        rows = self.shape[0] // chunks
        self.parts = [pl.ds(i * rows, rows) for i in range(chunks)]
        self.copies = [
            pltpu.make_async_copy(source.at[part], target.at[part], sems.at[i])
            for i, part in enumerate(self.parts)
        ]
        self.sent = set()

    def send(self, i=None):
        for k in range(len(self.copies)) if i is None else [i]:
            if k not in self.sent:
                self.sent.add(k)
                self.copies[k].start()

    def finish(self):
        self.send()
        for copy in self.copies:
            copy.wait()

    def put(self, i, value):
        self.ref[self.parts[i]] = value
        self.send(i)

    def __getitem__(self, index):
        return self.ref[index]

    def __setitem__(self, index, value):
        self.ref[index] = value


def call(body, outs, ins, scratch=(), limit=54, chunks=None, out_chunks=None, after=(), beside=(), near=(), near_outs=()):
    chunks, out_chunks = chunks or {}, out_chunks or {}
    n, m, k = len(ins), len(outs), len(after) + len(beside)
    far = [i for i in range(n) if i not in near]
    far_outs = [i for i in range(m) if i not in near_outs]
    parts = [chunks.get(i, 1) for i in far] + [out_chunks.get(i, 1) for i in far_outs]

    def inner(*refs):
        sources, targets, local = refs[:n], refs[n + k : n + k + m], refs[n + k + m :]
        held, sems, rest = local[: len(parts)], local[len(parts) : 2 * len(parts)], local[2 * len(parts) :]
        given = [Near(ref) for ref in sources]
        for at, i in enumerate(far):
            given[i] = In(sources[i], held[at], sems[at], parts[at])
        made = [Near(ref) for ref in targets]
        for at, i in enumerate(far_outs, len(far)):
            made[i] = Out(held[at], targets[i], sems[at], parts[at])
        for each in given:
            each.start()
        body(*given, *made, *rest)
        for each in given:
            each.ready()
        for each in made:
            each.send()
        for each in made:
            each.finish()

    space = lambda count, places: [pl.BlockSpec(memory_space=pltpu.VMEM if i in places else pltpu.HBM) for i in range(count)]
    return pl.pallas_call(
        inner,
        out_shape=[(pltpu.VMEM if i in near_outs else pltpu.HBM)(*out) for i, out in enumerate(outs)],
        in_specs=space(n, near) + space(len(after), ()) + space(len(beside), range(len(beside))),
        out_specs=space(m, near_outs),
        scratch_shapes=[
            *[pltpu.VMEM(ins[i].shape, ins[i].dtype) for i in far],
            *[pltpu.VMEM(*outs[i]) for i in far_outs],
            *[pltpu.SemaphoreType.DMA((k,)) for k in parts],
            *scratch,
        ],
        compiler_params=pltpu.CompilerParams(vmem_limit_bytes=limit * 2**20),
        cost_estimate=pl.CostEstimate(flops=1, bytes_accessed=1, transcendentals=0),
    )(
        *[pltpu.with_memory_space_constraint(a, pltpu.VMEM if i in near else pltpu.HBM) for i, a in enumerate(ins)],
        *[pltpu.with_memory_space_constraint(a, pltpu.HBM) for a in after],
        *[pltpu.with_memory_space_constraint(a, pltpu.VMEM) for a in beside],
    )


def local_call(body, outs, ins, scratch=(), limit=16, after=(), beside=()):
    n, k = len(ins), len(after) + len(beside)

    def inner(*refs):
        body(*refs[:n], *refs[n + k :])

    spec = lambda space, count: [pl.BlockSpec(memory_space=space)] * count
    return pl.pallas_call(
        inner,
        out_shape=[pltpu.VMEM(*out) for out in outs],
        in_specs=spec(pltpu.VMEM, n) + spec(pltpu.HBM, len(after)) + spec(pltpu.VMEM, len(beside)),
        out_specs=spec(pltpu.VMEM, len(outs)),
        scratch_shapes=list(scratch),
        compiler_params=pltpu.CompilerParams(vmem_limit_bytes=limit * 2**20),
        cost_estimate=pl.CostEstimate(flops=1, bytes_accessed=1, transcendentals=0),
    )(
        *[pltpu.with_memory_space_constraint(a, pltpu.VMEM) for a in ins],
        *[pltpu.with_memory_space_constraint(a, pltpu.HBM) for a in after],
        *[pltpu.with_memory_space_constraint(a, pltpu.VMEM) for a in beside],
    )


def share(tile):
    return lax.all_to_all(tile, both, 0, 0)


def halos(first, last):
    count = lax.axis_size("rows")
    above = lax.ppermute(last, "rows", [(i, i + 1) for i in range(count - 1)])
    below = lax.ppermute(first, "rows", [(i + 1, i) for i in range(count - 1)])
    return above, below


def flip(values, axis, bits):
    return lax.ppermute(values, axis, [(i, i ^ bits) for i in range(lax.axis_size(axis))])


class Digit:
    def __init__(self, axis, unit, size):
        self.axis, self.unit, self.size = axis, unit, size

    def own(self):
        return lax.axis_index(self.axis) // self.unit % self.size

    def send(self, pieces):
        return [pieces[0]] + [flip(pieces[j], self.axis, j * self.unit) for j in range(1, self.size)]

    def bits(self):
        return [Digit(self.axis, self.unit << i, 2) for i in range(self.size.bit_length() - 1)]

    def trade(self, stacked):
        count = lax.axis_size(self.axis)
        span = self.unit * self.size
        starts = [high + low for high in range(0, count, span) for low in range(self.unit)]
        groups = [[start + self.unit * d for d in range(self.size)] for start in starts]
        return lax.all_to_all(stacked, self.axis, 0, 0, axis_index_groups=groups)

    def scatter(self, parts, outs):
        size = outs[0].shape[0]
        own = self.own()
        for j, out in enumerate(outs):
            at = pl.ds(pl.multiple_of((own ^ j) * size, 8), size)
            total = parts[0][at, :]
            for part in parts[1:]:
                total = total + part[at, :]
            out[...] = total

    def gather(self, pieces, out):
        size = pieces[0].shape[0]
        own = self.own()
        for j, piece in enumerate(pieces):
            out[pl.ds(pl.multiple_of((own ^ j) * size, 8), size), :] = piece[...]

    def outs(self, rows, width):
        return [((rows // self.size, width), f32)] * self.size


def digits():
    rows, batch = lax.axis_size("rows"), lax.axis_size("batch")
    depth = min(4, batch // 2)
    return Digit("batch", 1, 2), Digit("rows", 1, rows), Digit("batch", 2, depth), Digit("batch", 2 * depth, batch // (2 * depth))


def gate(value, beside):
    return pl.pallas_call(
        lambda *refs: None,
        out_shape=pltpu.VMEM(value.shape, value.dtype),
        in_specs=[pl.BlockSpec(memory_space=pltpu.VMEM)] * (1 + len(beside)),
        out_specs=pl.BlockSpec(memory_space=pltpu.VMEM),
        input_output_aliases={0: 0},
        cost_estimate=pl.CostEstimate(flops=1, bytes_accessed=1, transcendentals=0),
    )(*[pltpu.with_memory_space_constraint(a, pltpu.VMEM) for a in (value, *beside)])


def scatter_kernel(digit, count, *refs):
    digit.scatter(refs[:count], refs[count:])


def sum_kernel(*refs):
    total = refs[0][...]
    for ref in refs[1:-1]:
        total = total + ref[...]
    refs[-1][...] = total


def gather_kernel(digit, *refs):
    digit.gather(refs[:-1], refs[-1])


def scatter_more(digit, pieces, **order):
    rows, width = pieces[0].shape
    body = functools.partial(scatter_kernel, digit, len(pieces))
    return local_call(body, digit.outs(rows, width), pieces, **order)


def add_up(pieces, **order):
    return local_call(sum_kernel, [(pieces[0].shape, f32)], pieces, **order)[0]


def finish_sum(pieces, extra, **order):
    total = add_up(pieces, **order)
    if extra.size > 1:
        total = add_up(extra.send([total] * extra.size))
    return total


def gather_more(digit, pieces, **order):
    rows, width = pieces[0].shape
    return local_call(functools.partial(gather_kernel, digit), [((rows * digit.size, width), f32)], pieces, **order)[0]


def reduce_kernel(rows_ref, cols_ref, w_ref, x_ref, z_ref, ext_ref, own_ref, first_ref, last_ref, pay_ref,
                  tile):
    images = rows_ref.shape[0]
    tall = x_ref.shape[0] // images // 16
    shape = (images, tall + 2, 16, 16)
    start = lax.axis_index("rows") * tall - 1
    lane = lax.broadcasted_iota(jnp.int32, shape, 3).reshape(-1, 16)
    at_row = lax.broadcasted_iota(jnp.int32, shape, 1).reshape(-1, 16) + start
    at_col = lax.broadcasted_iota(jnp.int32, shape, 2).reshape(-1, 16)
    row_valid = per_image(rows_ref[...].astype(f32), lane)
    col_valid = per_image(cols_ref[...].astype(f32), lane)
    in_row = jnp.sum(jnp.where(lane == at_row, row_valid, 0.0), axis=1, keepdims=True)
    in_col = jnp.sum(jnp.where(lane == at_col, col_valid, 0.0), axis=1, keepdims=True)
    mask = jnp.broadcast_to(in_row * in_col, (in_row.shape[0], 128)).reshape(ext_ref.shape)
    ext_ref[...] = mask
    own = mask[:, 1 : tall + 1].reshape(-1, 128)
    own_ref[...] = own
    weight = split(w_ref[...])
    for i in range(len(x_ref.parts)):
        z_ref[x_ref.parts[i]] = product(split(x_ref.chunk(i)), weight, NN)
    z = z_ref[...]
    edges = z.reshape(images, tall, 16, -1)
    first_ref[...] = edges[:, 0].reshape(first_ref.shape)
    last_ref[...] = edges[:, tall - 1].reshape(last_ref.shape)
    for each in (first_ref, last_ref, z_ref, ext_ref, own_ref):
        each.send()
    count = column_sum(own)
    sums, squares = local_stats(z, wide(own, z.shape[1]), wide(count, z.shape[1]))
    tile[...] = jnp.zeros_like(tile)
    put(tile, 0, sums)
    put(tile, 2, squares)
    put(tile, 4, count)
    pay_ref[...] = jnp.broadcast_to(tile[...][None], pay_ref.shape)


def parts_kernel(wg_ref, we_ref, wr_ref, *refs):
    vectors, wg_refs, (weh_ref, wel_ref, wrh_ref, wrl_ref, par_ref) = refs[:-9], refs[-9:-5], refs[-5:]
    row = 0
    for vector in vectors:
        put(par_ref, row, vector[...])
        row += vector.shape[1] // 128
    half = wg_ref.shape[1] // 2
    for i in range(len(wg_ref.parts)):
        for j, part in enumerate(split(wg_ref.chunk(i))):
            for g in range(2):
                wg_refs[2 * g + j].put(i, part[:, g * half : (g + 1) * half])
    for source, high_ref, low_ref in ((we_ref, weh_ref, wel_ref), (wr_ref, wrh_ref, wrl_ref)):
        for i in range(len(source.parts)):
            high, low = split(source.chunk(i))
            high_ref.put(i, high)
            low_ref.put(i, low)


def turned_kernel(x_ref, high_ref, low_ref):
    high_ref[...], low_ref[...] = split(x_ref[...].T)


def moved(values, step):
    count = values.shape[0]
    at = lax.broadcasted_iota(jnp.int32, values.shape, 0) & 15
    if step == 0:
        return values
    if step > 0:
        return jnp.where(at < 15, pltpu.roll(values, count - 1, 0), 0.0)
    return jnp.where(at > 0, pltpu.roll(values, 1, 0), 0.0)


def window(extended, images, row, width):
    tall = extended.shape[0] // images // 16
    cells = extended.reshape(images, tall, 16, extended.shape[1])
    return cells[:, row : row + tall - 2, :, width].reshape(images * (tall - 2) * 16, -1)


def extend(place, cells, above, below):
    images, tall, broad, width = place.shape
    place[:, 1 : tall - 1] = cells[...].reshape(images, tall - 2, broad, width)
    place[:, 0] = above[...].reshape(images, broad, width)
    place[:, tall - 1] = below[...].reshape(images, broad, width)
    return place[...].reshape(-1, width)


def conv_kernel(g1_ref, par_ref, z_ref, ext_ref, above_ref, below_ref, own_ref, first_high, first_low, second_high, second_low,
                z2_ref, a_ref, stat_ref, counts_ref, pay_ref, tile, zext):
    images = zext.shape[0]
    tall = zext.shape[1] - 2
    width = z_ref.shape[1]
    group = width // 2
    gathered = g1_ref[...]
    counts = gathered[:, 4, :]
    counts_ref[...] = counts
    mean, inv, total = merge_stats(gathered, counts, width)
    tile[...] = jnp.zeros_like(tile)
    put(tile, 0, mean)
    put(tile, 2, inv)
    put(tile, 4, total[None])
    stat_ref[...] = tile[...]
    y = (extend(zext, z_ref, above_ref, below_ref) - mean) * inv * get(par_ref, 0, 2) + get(par_ref, 2, 2)
    a = y * jax.nn.sigmoid(y) * wide(ext_ref[...].reshape(-1, 128), width)
    a_ref[...] = a
    a_ref.send()
    shifted = [split(moved(a, step)) for step in (-1, 0, 1)]
    half = z2_ref.shape[1] // 2
    for ref in (first_high, first_low, second_high, second_low):
        ref.ready()
    for g in range(2):
        cols = slice(g * group, (g + 1) * group)
        left = [
            jnp.concatenate(
                [window(shifted[tap % 3][part], images, tap // 3, cols) for tap in range(9)], axis=1
            )
            for part in range(2)
        ]
        outs = slice(g * half, (g + 1) * half)
        right = [ref[...] for ref in ((first_high, first_low), (second_high, second_low))[g]]
        z2_ref[:, outs] = product(left, right, NN)
    z2_ref.send()
    z2 = z2_ref[...]
    own = own_ref[...]
    sums, squares = local_stats(z2, wide(own, z2.shape[1]), wide(column_sum(own), z2.shape[1]))
    put(tile, 0, sums)
    put(tile, 4, squares)
    pay_ref[...] = jnp.broadcast_to(tile[...][None], pay_ref.shape)


def taps_kernel(images, a_ref, high_ref, low_ref):
    group = a_ref.shape[1] // 2
    a = a_ref[...]
    shifted = [moved(a, step) for step in (-1, 0, 1)]
    for g in range(2):
        cols = slice(g * group, (g + 1) * group)
        for tap in range(9):
            high, low = split(window(shifted[tap % 3], images, tap // 3, cols).T)
            high_ref[g, tap * group : (tap + 1) * group, :] = high
            low_ref[g, tap * group : (tap + 1) * group, :] = low
        high_ref.send(g)
        low_ref.send(g)


def pixel_count(rows_ref, cols_ref):
    rows = jnp.sum(rows_ref[...].astype(f32), axis=1, keepdims=True)
    return rows * jnp.sum(cols_ref[...].astype(f32), axis=1, keepdims=True)


def pool_kernel(g2_ref, counts_ref, par_ref, rows_ref, cols_ref, z_ref, own_ref, w_ref, a_ref, stat_ref, pooled_ref, pay_ref):
    images = rows_ref.shape[0]
    width = z_ref.shape[1]
    mid = width // 2
    mean, inv, total = merge_stats(g2_ref[...], counts_ref[...], width)
    put(stat_ref, 0, mean)
    put(stat_ref, 4, inv)
    gain, shift = get(par_ref, 4, 4), get(par_ref, 8, 4)
    pieces = len(z_ref.parts)
    sums = []
    for i in range(pieces):
        y = (z_ref.chunk(i) - mean) * inv * gain + shift
        a = y * jax.nn.sigmoid(y) * wide(own_ref.chunk(i), width)
        a_ref.put(i, a)
        sums.append(image_sum(a, images // pieces))
    sums = jnp.concatenate(sums, axis=0)
    pooled = (sums[:, :mid] + sums[:, mid:]) / pixel_count(rows_ref, cols_ref)
    pooled_ref[...] = pooled
    pay_ref[...] = jnp.broadcast_to(exact(pooled, w_ref[...], NN)[None], pay_ref.shape)


def slope_of(values, mean, inv, gain, shift):
    normed = (values - mean) * inv
    y = normed * gain + shift
    sigma = jax.nn.sigmoid(y)
    return sigma * (1.0 + y * (1.0 - sigma)), normed


def slope_kernel(stat_ref, par_ref, rows_ref, cols_ref, own_ref, z_ref, slope_ref, normed_ref, sums_ref):
    images = rows_ref.shape[0]
    width = z_ref.shape[1]
    mean, inv = get(stat_ref, 0, 4), get(stat_ref, 4, 4)
    gain, shift = get(par_ref, 4, 4), get(par_ref, 8, 4)
    pieces = len(z_ref.parts)
    sums, cross = [], []
    for i in range(pieces):
        slope, normed = slope_of(z_ref.chunk(i), mean, inv, gain, shift)
        slope = slope * wide(own_ref.chunk(i), width)
        normed_ref.put(i, normed)
        slope_ref.put(i, slope)
        sums.append(image_sum(slope, images // pieces))
        cross.append(image_sum(slope * normed, images // pieces))
    pixels = pixel_count(rows_ref, cols_ref)
    sums_ref[:, :width] = jnp.concatenate(sums, axis=0) / pixels
    sums_ref[:, width:] = jnp.concatenate(cross, axis=0) / pixels


def expand_kernel(g3_ref, par_ref, w_ref, a_ref, wh_ref, wl_ref, own_ref,
                  mixed_ref, z_ref, weights_ref, normed_ref, pre_ref, act_ref, inv_ref, pay_ref, tile, acts):
    own_images = weights_ref.shape[0]
    mid = mixed_ref.shape[1]
    devices = g3_ref.shape[0]
    rows = lax.axis_size("rows")
    f_one = jnp.sum(g3_ref[...].reshape(rows, devices // rows * own_images, -1), axis=0)
    mean = jnp.mean(f_one, axis=0, keepdims=True)
    centered = f_one - mean
    inv = lax.rsqrt(jnp.mean(centered * centered, axis=0, keepdims=True) + epsilon)
    normed = centered * inv
    pre = normed * par_ref[12:13, :] + par_ref[13:14, :]
    normed_ref[...] = normed
    pre_ref[...] = pre
    inv_ref[...] = inv
    acts[...] = pre * jax.nn.sigmoid(pre)
    at = pl.multiple_of(lax.axis_index("batch") * own_images, own_images)
    act = acts[pl.ds(at, own_images), :]
    act_ref[...] = act
    logits = exact(act, w_ref[...], NN) + get(par_ref, 14, 4)
    lead = logits[:, :mid] - logits[:, mid:]
    first, second = jax.nn.sigmoid(lead), jax.nn.sigmoid(-lead)
    weights_ref[:, :mid] = first
    weights_ref[:, mid:] = second
    a = a_ref[...]
    mixed = per_image(first, a) * a[:, :mid] + per_image(second, a) * a[:, mid:]
    mixed_ref[...] = mixed
    mixed_ref.send()
    left, right = split(mixed), (wh_ref[...], wl_ref[...])
    for i, part in enumerate(z_ref.parts):
        rows = slice(part.start, part.start + part.size)
        z_ref.put(i, product([each[rows] for each in left], right, NN))
    z = z_ref[...]
    width = z.shape[1]
    own = wide(own_ref[...], width)
    sums, squares = local_stats(z, own, wide(column_sum(own_ref[...]), width))
    put(tile, 0, sums)
    put(tile, width // 128, squares)
    pay_ref[...] = jnp.broadcast_to(tile[...][None], pay_ref.shape)


def output_kernel(g4_ref, counts_ref, par_ref, own_ref, z_ref, x_ref, cot_ref, *refs):
    slope_refs, (grad_ref, stat_ref, slopes_ref, pay_ref, tile) = refs[:-5], refs[-5:]
    width = z_ref.shape[1]
    groups = width // 128
    mean, inv, total = merge_stats(g4_ref[...], counts_ref[...], width)
    put(stat_ref, 0, mean)
    put(stat_ref, groups, inv)
    gain, shift = get(par_ref, 18, groups), get(par_ref, 26, groups)
    flat, cross = 0.0, 0.0
    for i in range(len(z_ref.parts)):
        own = wide(own_ref.chunk(i), width)
        normed = (z_ref.chunk(i) - mean) * inv
        pre = normed * gain + shift + x_ref.chunk(i)
        sigma = jax.nn.sigmoid(pre)
        grad = cot_ref.chunk(i) * own * (sigma * (1.0 + pre * (1.0 - sigma)))
        grad_ref.put(i, grad)
        flat = flat + column_sum(grad)
        cross = cross + column_sum(grad * normed)
    put(tile, 0, flat)
    put(tile, groups, cross)
    pay_ref[...] = jnp.broadcast_to(tile[...][None], pay_ref.shape)
    sum_kernel(*slope_refs, slopes_ref)


def result_kernel(stat_ref, par_ref, own_ref, z_ref, x_ref, out_ref, mark_ref):
    width = z_ref.shape[1]
    groups = width // 128
    mean, inv = get(stat_ref, 0, groups), get(stat_ref, groups, groups)
    gain, shift = get(par_ref, 18, groups), get(par_ref, 26, groups)
    for i in range(len(z_ref.parts)):
        pre = (z_ref.chunk(i) - mean) * inv * gain + shift + x_ref.chunk(i)
        out_ref.put(i, pre * jax.nn.sigmoid(pre) * wide(own_ref.chunk(i), width))
    mark_ref[...] = own_ref[:8, :]


def mixed_kernel(digit, g5_ref, stat1_ref, stat3_ref, par_ref, own_ref, grad_ref, z_ref, wh_ref, wl_ref, a_ref, weights_ref,
                 w_ref, slope_ref, normed_ref, *refs):
    shares, (gm_ref, dsum_ref, grads_ref, gain_ref, shift_ref, slopes_ref, pay_ref, tile) = refs[: digit.size], refs[digit.size :]
    width = z_ref.shape[1]
    mid = gm_ref.shape[1]
    images = weights_ref.shape[0]
    groups = width // 128
    grads_ref[...] = jnp.sum(g5_ref[...], axis=0)
    shift_ref[...] = grads_ref[:groups, :]
    gain_ref[...] = grads_ref[groups:, :]
    count = wide(stat1_ref[4:5, :], width)
    mean, inv = get(stat3_ref, 0, groups), get(stat3_ref, groups, groups)
    flat = get(grads_ref, 0, groups) / count
    cross = get(grads_ref, groups, groups) / count
    scale = get(par_ref, 18, groups) * inv
    for i in range(len(z_ref.parts)):
        normed = (z_ref.chunk(i) - mean) * inv
        dz = scale * (grad_ref.chunk(i) - flat - normed * cross) * wide(own_ref.chunk(i), width)
        gm_ref[z_ref.parts[i]] = product(split(dz), (wh_ref[...], wl_ref[...]), NT)
    gm = gm_ref[...]
    gm_ref.send()
    a = a_ref[...]
    weights = weights_ref[...]
    gate = image_sum(gm * (a[:, :mid] - a[:, mid:]), images)
    dsum = weights[:, :mid] * weights[:, mid:] * gate
    dsum_ref[...] = dsum
    tile[...] = jnp.zeros_like(tile)
    tile[:images, :] = exact(dsum, w_ref[:, :mid] - w_ref[:, mid:], NT)
    slope = slope_ref[...] * jnp.concatenate([gm, gm], axis=1)
    put(tile, 8, column_sum(weights * image_sum(slope, images)))
    put(tile, 12, column_sum(weights * image_sum(slope * normed_ref[...], images)))
    pay_ref[...] = jnp.broadcast_to(tile[...][None], pay_ref.shape)
    digit.gather(shares, slopes_ref)


def expand_grad_kernel(core, grads_ref, stat1_ref, stat3_ref, par_ref, mixed_ref, act_ref, dsum_ref, own_ref, grad_ref, z_ref,
                       keep_ref, send_ref, excite_ref, term):
    width = z_ref.shape[1]
    groups = width // 128
    count = wide(stat1_ref[4:5, :], width)
    mean, inv = get(stat3_ref, 0, groups), get(stat3_ref, groups, groups)
    flat = get(grads_ref, 0, groups) / count
    cross = get(grads_ref, groups, groups) / count
    scale = get(par_ref, 18, groups) * inv
    left = split(mixed_ref[...].T)
    rows, span = left[0].shape[0], term.shape[1]
    for i, part in enumerate(z_ref.parts):
        normed = (z_ref.chunk(i) - mean) * inv
        dz = scale * (grad_ref.chunk(i) - flat - normed * cross) * wide(own_ref.chunk(i), width)
        right = split(dz)
        some = [each[:, part.start : part.start + part.size] for each in left]
        for j in range(term.shape[0] // rows):
            value = product(some, [each[:, j * span : (j + 1) * span] for each in right], NN)
            if i:
                value = value + term[j * rows : (j + 1) * rows, :]
            term[j * rows : (j + 1) * rows, :] = value
    core.scatter([term], [keep_ref, send_ref])
    excite_ref[...] = exact(act_ref[...], dsum_ref[...], TN)


def turned_rows(left, refs, row, taps):
    return product(left, [ref[row * taps : (row + 1) * taps, :] for ref in refs], NT)


def fold(total, group):
    return moved(total[:, :group], 1) + total[:, group : 2 * group] + moved(total[:, 2 * group :], -1)


def back_kernel(digit, g6_ref, pre_ref, fcn_ref, inv_ref, par_ref, wsq_ref, pooled_ref, stat1_ref, stat2_ref, rows_ref,
                cols_ref, weights_ref, mine_ref, other_ref, own_ref, gm_ref, slope_ref, normed_ref, *refs):
    w_refs, (up_ref, down_ref), dz_refs, (squeeze_ref, gain_ref, flat_ref, fc_gain_ref, fc_flat_ref, gf, owned, slopes) = (
        refs[:4], refs[4:6], refs[6:10], refs[10:]
    )
    images = rows_ref.shape[0]
    tall = dz_refs[0].shape[1] - 2
    width = normed_ref.shape[1]
    mid = width // 2
    groups = width // 128
    rows = lax.axis_size("rows")
    shared = g6_ref[...]
    pre = pre_ref[...]
    fcn = fcn_ref[...]
    sigma = jax.nn.sigmoid(pre)
    total = pre.shape[0]
    grad = jnp.sum(shared[:, :images].reshape(rows, total, -1), axis=0) * (sigma * (1.0 + pre * (1.0 - sigma)))
    flat, cross = column_sum(grad), column_sum(grad * fcn)
    fc_gain_ref[...] = cross
    fc_flat_ref[...] = flat
    gf[...] = par_ref[12:13, :] * inv_ref[...] * (grad - flat / total - fcn * cross / total)
    at = pl.multiple_of(lax.axis_index("batch") * images, images)
    mine = gf[pl.ds(at, images), :]
    squeeze = exact(pooled_ref[...], mine, TN)
    half_rows = squeeze.shape[0] // 2
    squeeze_ref[:, : squeeze.shape[1]] = squeeze[:half_rows]
    squeeze_ref[:, squeeze.shape[1] :] = squeeze[half_rows:]
    spread = exact(gf[...], wsq_ref[...], NT)
    owned[...] = spread
    own_spread = owned[pl.ds(at, images), :] / pixel_count(rows_ref, cols_ref)
    for flipped, half in enumerate((mine_ref, other_ref)):
        for block in range(half.shape[0] // images):
            here = pl.multiple_of((2 * block + (digit.own() ^ flipped)) * images, images)
            slopes[pl.ds(here, images), :] = half[block * images : (block + 1) * images, :]
    base = jnp.sum(shared[:, 8:], axis=0)
    count = wide(stat1_ref[4:5, :], mid)
    weights = weights_ref[...]
    gm = gm_ref[...]
    shared_part = per_image(own_spread, gm)
    mask = wide(own_ref[...], mid)
    zero = jnp.zeros((images, 16, mid), bf16)
    for ref in dz_refs:
        ref[:, 0] = zero
        ref[:, tall + 1] = zero
    for g in range(2):
        outs = slice(g * mid, (g + 1) * mid)
        crosses = slice(width + g * mid, width + (g + 1) * mid)
        half = groups // 2
        flat_two = get(base, g * half, half) + column_sum(spread * slopes[:, outs])
        cross_two = get(base, groups + g * half, half) + column_sum(spread * slopes[:, crosses])
        put(gain_ref, g * half, cross_two)
        put(flat_ref, g * half, flat_two)
        scale = get(par_ref, 4 + g * half, half) * get(stat2_ref, groups + g * half, half)
        upstream = per_image(weights[:, outs], gm) * gm + shared_part
        dz = scale * (upstream * slope_ref[:, outs] - flat_two / count - normed_ref[:, outs] * (cross_two / count)) * mask
        for ref, part in zip(dz_refs[2 * g : 2 * g + 2], split(dz)):
            ref[:, 1 : tall + 1] = part.reshape(images, tall, 16, mid)
            ref.send()
    group = up_ref.shape[1] // 2
    for g in range(2):
        cols = slice(g * group, (g + 1) * group)
        for side, row, tap in ((up_ref, 1, 0), (down_ref, tall, 2)):
            left = [ref[:, row].reshape(-1, mid) for ref in dz_refs[2 * g : 2 * g + 2]]
            side[:, cols] = fold(turned_rows(left, w_refs[2 * g : 2 * g + 2], tap, 3 * group), group)


def group_kernel(core, *refs):
    dz_refs, (squeeze_ref, excite_ref, th_ref, tl_ref, keep_ref, send_ref, out_ref) = refs[:4], refs[4:]
    for ref in (*dz_refs, squeeze_ref, excite_ref, th_ref, tl_ref):
        ref.ready()
    tall = dz_refs[0].shape[1] - 2
    taps = th_ref.shape[1]
    for g in range(2):
        right = [ref[:, 1 : tall + 1].reshape(-1, ref.shape[3]) for ref in dz_refs[2 * g : 2 * g + 2]]
        out_ref[g * taps : (g + 1) * taps, :] = product((th_ref.chunk(g)[0], tl_ref.chunk(g)[0]), right, NN)
    inter = excite_ref.shape[0]
    out_ref[2 * taps : 2 * taps + inter, :] = excite_ref[...]
    out_ref[2 * taps + inter :, :] = squeeze_ref[...]
    core.scatter([out_ref], [keep_ref, send_ref])


def input_grad_kernel(g, par_ref, stat_ref, z_ref, own_ref, above_ref, below_ref, dzh_ref, dzl_ref, wh_ref, wl_ref, *refs):
    images, tall = dzh_ref.shape[0], dzh_ref.shape[1] - 2
    group = z_ref.shape[1] // 2
    cols = slice(g * group, (g + 1) * group)
    total = None
    for row in range(3):
        left = [ref[:, 2 - row : 2 - row + tall].reshape(-1, ref.shape[3]) for ref in (dzh_ref, dzl_ref)]
        term = turned_rows(left, (wh_ref, wl_ref), row, 3 * group)
        total = term if total is None else total + term
    place = refs[-1]
    place[...] = fold(total, group).reshape(place.shape)
    place[:, 0] += above_ref[:, cols].reshape(images, 16, group)
    place[:, tall - 1] += below_ref[:, cols].reshape(images, 16, group)
    grad = place[...].reshape(-1, group)
    mean, inv, gain, shift = [ref[row + g : row + g + 1, :] for ref, row in ((stat_ref, 0), (stat_ref, 2), (par_ref, 0), (par_ref, 2))]
    normed = (z_ref[:, cols] - mean) * inv
    y = normed * gain + shift
    sigma = jax.nn.sigmoid(y)
    dy = grad * wide(own_ref[...], group) * (sigma * (1.0 + y * (1.0 - sigma)))
    if g == 0:
        dy_ref, tile = refs[:2]
        tile[...] = jnp.zeros(tile.shape, f32)
    else:
        dsum_ref, before_ref, dy_ref, pay_ref, tile = refs[:5]
        tile[...] = before_ref[...]
        put(tile, 4, column_sum(dsum_ref[...]))
    dy_ref[...] = dy
    dy_ref.send()
    put(tile, g, column_sum(dy * normed))
    put(tile, 2 + g, column_sum(dy))
    if g:
        pay_ref[...] = jnp.broadcast_to(tile[...][None], pay_ref.shape)


def final_kernel(core, g7_ref, par_ref, stat_ref, first_ref, second_ref, z_ref, own_ref, th_ref, tl_ref,
                 keep_ref, send_ref, dzh_ref, dzl_ref, mark_ref, gain_ref, flat_ref, bias_ref, gains_ref, term):
    width = z_ref.shape[1]
    gains_ref[...] = jnp.sum(g7_ref[...], axis=0)
    mark_ref[...] = gains_ref[...]
    gain_ref[...] = gains_ref[0:2, :]
    flat_ref[...] = gains_ref[2:4, :]
    bias_ref[0:2, :] = gains_ref[4:6, :]
    bias_ref[2:4, :] = -gains_ref[4:6, :]
    cross, flat = get(gains_ref, 0, 2), get(gains_ref, 2, 2)
    count = wide(stat_ref[4:5, :], width)
    mean, inv = get(stat_ref, 0, 2), get(stat_ref, 2, 2)
    normed = (z_ref[...] - mean) * inv
    scale = get(par_ref, 0, 2) * inv
    dy = jnp.concatenate([first_ref[...], second_ref[...]], axis=1)
    dz = scale * (dy - flat / count - normed * (cross / count)) * wide(own_ref[...], width)
    high, low = split(dz)
    dzh_ref[...] = high
    dzl_ref[...] = low
    term[...] = product((th_ref[...], tl_ref[...]), (high, low), NN)
    core.scatter([term], [keep_ref, send_ref])


def images_kernel(dzh_ref, dzl_ref, wh_ref, wl_ref, grad_ref, out_ref):
    for i in range(len(grad_ref.parts)):
        left = [ref.chunk(i) for ref in (dzh_ref, dzl_ref)]
        out_ref.put(i, product(left, (wh_ref[...], wl_ref[...]), NT) + grad_ref.chunk(i))


def deal_kernel(plan, count, *refs):
    outs = list(refs[count:])
    for digit, stretches in plan:
        own = digit.own()
        for j in range(digit.size):
            out, at = outs.pop(0), 0
            for inputs, first, rows in stretches:
                each = rows // digit.size
                here = pl.ds(pl.multiple_of(first + (own ^ j) * each, 8), each)
                total = refs[inputs[0]][here, :]
                for k in inputs[1:]:
                    total = total + refs[k][here, :]
                out[at : at + each, :] = total
                at += each


def deal(plan, ins, **order):
    width = ins[0].shape[1]
    outs = []
    for digit, stretches in plan:
        rows = sum(rows for _, _, rows in stretches) // digit.size
        outs += [((rows, width), f32)] * digit.size
    return local_call(functools.partial(deal_kernel, plan, len(ins)), outs, ins, **order)


def stack_kernel(stretches, *refs):
    refs, out = refs[:-1], refs[-1]
    at = 0
    for inputs, first, rows in stretches:
        each = rows // out.shape[0]
        for d in range(out.shape[0]):
            here = slice(first + d * each, first + (d + 1) * each)
            total = refs[inputs[0]][here, :]
            for k in inputs[1:]:
                total = total + refs[k][here, :]
            out[d, at : at + each, :] = total
        at += each


def extra_pieces(extra, stacked):
    if extra.size == 1:
        return [stacked]
    total = local_call(lambda ref, out: out.__setitem__(Ellipsis, jnp.sum(ref[...], axis=0)), [(stacked.shape[1:], f32)], [stacked])[0]
    return extra.send([total] * extra.size)


def stacked_kernel(count, *refs):
    if count == 1:
        refs[-1][...] = jnp.sum(refs[0][...], axis=0)
    else:
        sum_kernel(*refs)


def halves_kernel(digit, *refs):
    pieces, outs = refs[: digit.size], refs[digit.size :]
    half = pieces[0].shape[0] // 2
    own = digit.own()
    for j, piece in enumerate(pieces):
        at = pl.ds(pl.multiple_of((own ^ j) * half, 8), half)
        for i, out in enumerate(outs):
            out[at, :] = piece[i * half : (i + 1) * half, :]


def pair_kernel(digits, *refs):
    outs = refs[4:]
    for i, digit in enumerate(digits):
        digit.gather(refs[2 * i : 2 * i + 2], outs[i] if len(outs) == 2 else outs[0].at[pl.ds(i * 2 * refs[0].shape[0], 2 * refs[0].shape[0])])


def last_kernel(core, expand_map, group_map, mine_ref, other_ref, expand_ref, group_ref, excite_ref, squeeze_ref, whole):
    core.gather([mine_ref, other_ref], whole)
    taps, mid = group_ref.shape[0], whole.shape[1]
    inter = squeeze_ref.shape[1]
    tall = expand_ref.shape[0]
    places = [
        (taps, lambda rows, value: group_ref.__setitem__((rows, slice(0, mid)), value)),
        (taps, lambda rows, value: group_ref.__setitem__((rows, slice(mid, 2 * mid)), value)),
        (inter, lambda rows, value: excite_ref.__setitem__((rows, slice(0, mid)), value)),
        (inter, lambda rows, value: squeeze_put(squeeze_ref, rows, value)),
    ]
    for at, first, rows in expand_map:
        j, m = first // tall, first % tall
        expand_ref[m : m + rows, j * mid : (j + 1) * mid] = whole[at : at + rows, :]
    for at, first, rows in group_map:
        base = 0
        for length, store in places:
            low, high = max(first, base), min(first + rows, base + length)
            if low < high:
                store(slice(low - base, high - base), whole[at + low - first : at + high - first, :])
            base += length
    excite_ref[:, mid:] = -excite_ref[:, :mid]


def squeeze_put(squeeze_ref, rows, value):
    half = squeeze_ref.shape[0] // 2
    width = squeeze_ref.shape[1]
    squeeze_ref[rows, :] = value[:, :width]
    squeeze_ref[slice(half + rows.start, half + rows.stop), :] = value[:, width:]


def on_device(
    images,
    w_reduce,
    gain_one,
    shift_one,
    w_group,
    gain_two,
    shift_two,
    w_squeeze,
    gain_fc,
    shift_fc,
    w_excite,
    excite_bias,
    w_expand,
    gain_three,
    shift_three,
    valid_rows,
    valid_cols,
    cotangent,
):
    count, tall, broad, chan = images.shape
    mid = w_reduce.shape[1]
    inter = w_squeeze.shape[1]
    duo = 2 * mid
    taps = 9 * mid // 2
    cells = count * tall * broad
    longer = count * (tall + 2) * broad
    edge = count * broad
    devices = lax.axis_size("rows") * lax.axis_size("batch")
    all_images = count * lax.axis_size("batch")
    x = images.reshape(cells, chan)
    cot = cotangent.reshape(cells, chan)
    pay8 = ((devices, 8, 128), f32)
    pay16 = ((devices, 16, 128), f32)
    tile8 = pltpu.VMEM((8, 128), f32)
    tile16 = pltpu.VMEM((16, 128), f32)
    twice = lambda *shape: [(shape, bf16)] * 2
    flat_w = w_group.reshape(taps, duo)
    vectors = (gain_one, shift_one, gain_two, shift_two, gain_fc, shift_fc, excite_bias, gain_three, shift_three)
    core, line, depth, extra = digits()

    z_one, ext, own, first, last, pay = call(
        reduce_kernel,
        [((cells, mid), f32), ((count, tall + 2, broad, 128), f32), ((cells, 128), f32), ((edge, mid), f32),
         ((edge, mid), f32), pay8],
        [valid_rows, valid_cols, w_reduce, x],
        [tile8],
        near_outs=(3, 4, 5),
    )
    g1 = share(pay)
    above, below = halos(first, last)
    *group_parts, weh, wel, wrh, wrl, par = call(
        parts_kernel,
        [*twice(taps, mid), *twice(taps, mid), *twice(mid, chan), *twice(chan, mid), ((40, 128), f32)],
        [flat_w, w_expand, w_reduce, *[v.reshape(1, -1) for v in vectors]],
        chunks={0: 4, 1: 2, 2: 2},
        out_chunks={0: 4, 1: 4, 2: 4, 3: 4, 4: 2, 5: 2, 6: 2, 7: 2},
        after=[z_one],
    )
    z_two, a_one, stat1, counts, pay = call(
        conv_kernel,
        [((cells, duo), f32), ((longer, mid), f32), ((8, 128), f32), ((devices, 128), f32), pay8],
        [g1, par, z_one, ext, above, below, own, *group_parts],
        [tile8, pltpu.VMEM((count, tall + 2, broad, mid), f32)],
        near=(0, 4, 5),
        near_outs=(4,),
    )
    g2 = share(pay)
    xth, xtl = call(turned_kernel, twice(chan, cells), [x], after=[stat1])
    a_two, stat2, pooled, pay = call(
        pool_kernel,
        [((cells, duo), f32), ((8, 128), f32), ((count, mid), f32), ((devices, count, inter), f32)],
        [g2, counts, par, valid_rows, valid_cols, z_two, own, w_squeeze],
        chunks={5: 2, 6: 2},
        out_chunks={0: 2},
        after=[xth],
        near=(0,),
        near_outs=(3,),
    )
    g3 = share(pay)
    slope_two, normed_two, slopes = call(
        slope_kernel,
        [((cells, duo), f32), ((cells, duo), f32), ((count, 2 * duo), f32)],
        [stat2, par, valid_rows, valid_cols, own, z_two],
        chunks={4: 2, 5: 2},
        out_chunks={0: 2, 1: 2},
    )
    mixed, z_three, weights, fc_normed, fc_pre, fc_act, fc_inv, pay = call(
        expand_kernel,
        [((cells, mid), f32), ((cells, chan), f32), ((count, duo), f32), ((all_images, inter), f32),
         ((all_images, inter), f32), ((count, inter), f32), ((1, inter), f32), pay16],
        [g3, par, w_excite, a_two, weh, wel, own],
        [tile16, pltpu.VMEM((all_images, inter), f32)],
        out_chunks={1: 2},
        after=[slopes],
        near=(0,),
        near_outs=(7,),
    )
    g4 = share(pay)
    slopes = line.send([slopes] * line.size)
    grad_pre, stat3, slopes, pay = call(
        output_kernel,
        [((cells, chan), f32), ((16, 128), f32), ((count, 2 * duo), f32), pay16],
        [g4, counts, par, own, z_three, x, cot, *slopes],
        [tile16],
        chunks={3: 4, 4: 4, 5: 4, 6: 4},
        out_chunks={0: 4},
        near=(0, *range(7, 7 + line.size)),
        near_outs=(2, 3),
    )
    g5 = share(pay)
    slopes = depth.send([slopes] * depth.size)
    tph, tpl = call(functools.partial(taps_kernel, count), twice(2, taps, cells), [a_one], out_chunks={0: 2, 1: 2}, after=[stat3])
    grad_mixed, dsum, grads_three, grad_gain_three, grad_shift_three, slopes, pay = call(
        functools.partial(mixed_kernel, depth),
        [((cells, mid), f32), ((count, mid), f32),
         ((16, 128), f32), ((8, 128), f32), ((8, 128), f32), ((depth.size * count, 2 * duo), f32), pay16],
        [g5, stat1, stat3, par, own, grad_pre, z_three, weh, wel, a_two, weights, w_excite, slope_two, normed_two, *slopes],
        [tile16],
        after=[tph],
        near=(0, *range(14, 14 + depth.size)),
        near_outs=(5, 6),
    )
    g6 = share(pay)
    *expand_sum, excite_term = call(
        functools.partial(expand_grad_kernel, core),
        [*core.outs(mid * chan // mid, mid), ((inter, mid), f32)],
        [grads_three, stat1, stat3, par, mixed, fc_act, dsum, own, grad_pre, z_three],
        [pltpu.VMEM((chan, mid), f32)],
        chunks={7: 2, 8: 2, 9: 2},
    )
    if extra.size > 1:
        slopes = gather_more(extra, extra.send([slopes] * extra.size))
    slopes = core.send([slopes] * 2)
    packed = 2 * taps + 2 * inter
    up, down, *dz_parts, squeeze_term, grad_gain_two, grad_shift_two, grad_gain_fc, grad_shift_fc = call(
        functools.partial(back_kernel, core),
        [((edge, mid), f32), ((edge, mid), f32), *twice(count, tall + 2, broad, mid), *twice(count, tall + 2, broad, mid), ((inter, mid), f32),
         ((duo // 128, 128), f32), ((duo // 128, 128), f32), ((1, inter), f32), ((1, inter), f32)],
        [g6, fc_pre, fc_normed, fc_inv, par, w_squeeze, pooled, stat1, stat2, valid_rows, valid_cols, weights, *slopes, own,
         grad_mixed, slope_two, normed_two, *group_parts],
        [pltpu.VMEM((all_images, inter), f32), pltpu.VMEM((all_images, mid), f32), pltpu.VMEM((all_images, 2 * duo), f32)],
        after=[excite_term],
        near=(0, 12, 13),
        near_outs=(0, 1),
    )
    above, below = halos(up, down)
    group_sum = call(
        functools.partial(group_kernel, core),
        core.outs(packed, mid),
        [*dz_parts, squeeze_term, excite_term, tph, tpl],
        [pltpu.VMEM((packed, mid), f32)],
        chunks={6: 2, 7: 2},
        near_outs=(0, 1),
    )
    expand_sum = core.send(expand_sum)
    group_sum = core.send([group_sum[0], gate(group_sum[1], [above, below])])
    dy_first, tile = call(
        functools.partial(input_grad_kernel, 0),
        [((cells, mid // 2), f32), ((8, 128), f32)],
        [par, stat1, z_one, own, above, below, *dz_parts[:2], *group_parts[:2]],
        [pltpu.VMEM((count, tall, broad, mid // 2), f32)],
        near=(4, 5),
    )
    first_bit, second_bit = line.bits()
    some, more = expand_sum[0].shape[0] // 2, group_sum[0].shape[0] // 2
    both_of = lambda start, a, b: [((0, 1), start * a, a), ((2, 3), start * b, b)]
    first_half = lambda digit: (digit, both_of(0, some, more))
    second_half = lambda digit: (digit, both_of(1, some, more))
    keep_a, send_a, keep_b, send_b = deal(
        [first_half(first_bit), second_half(second_bit)], [*expand_sum, *group_sum], after=[tile]
    )
    come_a, come_b = first_bit.send([keep_a, send_a]), second_bit.send([keep_b, send_b])
    place = pltpu.VMEM((count, tall, broad, mid // 2), f32)
    dy_second, pay = call(
        functools.partial(input_grad_kernel, 1),
        [((cells, mid // 2), f32), pay8],
        [par, stat1, z_one, own, above, below, *dz_parts[2:], *group_parts[2:], dsum, tile],
        [tile8, place],
        beside=[keep_a],
        near=(4, 5),
        near_outs=(1,),
    )
    g7 = share(pay)
    some, more = some // 2, more // 2
    turn = lambda k: [((k, k + 1), 0, some), ((k, k + 1), some, more)]
    keep_a, send_a, keep_b, send_b = deal([(second_bit, turn(0)), (first_bit, turn(2))], [*come_a, *come_b], after=[dy_second])
    *reduce_sum, dzh, dzl, mark_one, grad_gain_one, grad_shift_one, grad_bias = call(
        functools.partial(final_kernel, core),
        [*core.outs(chan, mid), *twice(cells, mid), ((8, 128), f32), *[((mid // 128, 128), f32)] * 2, ((duo // 128, 128), f32)],
        [g7, par, stat1, dy_first, dy_second, z_one, own, xth, xtl],
        [tile8, pltpu.VMEM((chan, mid), f32)],
        beside=[keep_a],
        near=(0,),
        near_outs=(0, 1),
    )
    come_a, come_b = second_bit.send([keep_a, send_a]), first_bit.send([keep_b, send_b])
    some, more = some // 2, more // 2
    stretches = turn(0) + turn(2)
    (joined,) = local_call(
        functools.partial(stack_kernel, stretches),
        [((depth.size, (some + more) * 2 // depth.size, mid), f32)],
        [*come_a, *come_b],
        after=[mark_one],
    )
    joined = depth.trade(joined)
    reduce_sum = scatter_more(line, core.send(reduce_sum))
    (grad_images,) = call(
        images_kernel,
        [((cells, chan), f32)],
        [dzh, dzl, wrh, wrl, grad_pre],
        chunks={0: 2, 1: 2, 4: 2},
        out_chunks={0: 2},
        beside=[reduce_sum[0]],
    )
    reduce_sum = scatter_more(depth, line.send(reduce_sum), after=[grad_images])
    (joined,) = local_call(
        functools.partial(stacked_kernel, extra.size), [(joined.shape[1:], f32)], extra_pieces(extra, joined), beside=[reduce_sum[0]]
    )
    rows_in = depth.size * joined.shape[0]
    block_out, mark = call(
        result_kernel,
        [((cells, chan), f32), ((8, 128), f32)],
        [stat3, par, own, z_three, x],
        chunks={2: 4, 3: 4, 4: 4},
        out_chunks={0: 4},
        beside=[joined],
    )
    half_a, half_b = local_call(
        functools.partial(halves_kernel, depth),
        [((rows_in // 2, mid), f32)] * 2,
        depth.send([joined] * depth.size),
        after=[mark],
    )
    reduce_sum = finish_sum(depth.send(reduce_sum), extra, beside=[half_a])
    half_a, half_b = local_call(
        functools.partial(pair_kernel, [second_bit, first_bit]),
        [((rows_in, mid), f32)] * 2,
        [*second_bit.send([half_a] * 2), *first_bit.send([half_b] * 2)],
        beside=[reduce_sum],
    )
    reduce_sum = gather_more(depth, depth.send([reduce_sum] * depth.size), beside=[half_a])
    (joined,) = local_call(
        functools.partial(pair_kernel, [first_bit, second_bit]),
        [((4 * rows_in, mid), f32)],
        [*first_bit.send([half_a] * 2), *second_bit.send([half_b] * 2)],
        beside=[reduce_sum],
    )
    expand_map, group_map = [], []
    at = 0
    some, more = some // depth.size, more // depth.size
    for half in range(core.size):
        for part in range(2):
            for outer in range(2):
                for inner in range(2):
                    for deep in range(depth.size):
                        block = (((half * 2 + part) * 2 + outer) * 2 + inner) * depth.size + deep
                        expand_map.append((at, block * some, some))
                        group_map.append((at + some, block * more, more))
                        at += some + more
    grad_w_expand, grad_w_group, grad_w_excite, grad_w_squeeze = call(
        functools.partial(last_kernel, core, expand_map, group_map),
        [((mid, chan), f32), ((taps, duo), f32), ((inter, duo), f32), ((mid, inter), f32)],
        core.send([joined] * 2),
        [pltpu.VMEM((chan + packed, mid), f32)],
        near=(0, 1),
    )
    reduce_sum = gather_more(line, line.send([reduce_sum] * line.size), after=[grad_w_squeeze])
    (grad_w_reduce,) = call(
        functools.partial(gather_kernel, core), [((chan, mid), f32)], core.send([reduce_sum] * 2), near=(0, 1)
    )
    return (
        block_out.reshape(images.shape),
        grad_images.reshape(images.shape),
        grad_w_reduce,
        grad_gain_one.reshape(-1),
        grad_shift_one.reshape(-1),
        grad_w_group.reshape(w_group.shape),
        grad_gain_two.reshape(-1),
        grad_shift_two.reshape(-1),
        grad_w_squeeze,
        grad_gain_fc.reshape(-1),
        grad_shift_fc.reshape(-1),
        grad_w_excite,
        grad_bias.reshape(-1),
        grad_w_expand,
        grad_gain_three.reshape(-1),
        grad_shift_three.reshape(-1),
    )


def solution(mesh):
    maps = P("batch", "rows", None, None)
    return jax.shard_map(
        on_device,
        mesh=mesh,
        in_specs=(maps,) + (P(),) * 14 + (P("batch", None), P("batch", None), maps),
        out_specs=(maps, maps) + (P(),) * 14,
        check_vma=False,
    )
```

```python
import functools

import jax
import jax.numpy as jnp
from jax import lax
from jax.experimental import pallas as pl
from jax.experimental.pallas import tpu as pltpu
from jax.sharding import PartitionSpec as P

epsilon = 1e-05
f32 = jnp.float32
bf16 = jnp.bfloat16
highest = lax.Precision.HIGHEST
both = ("rows", "batch")
NN = ((1,), (0,))
NT = ((1,), (1,))
TN = ((0,), (0,))


def split(values):
    high = values.astype(bf16)
    return high, (values - high.astype(f32)).astype(bf16)


def dot(left, right, dims):
    return lax.dot_general(left, right, (dims, ((), ())), preferred_element_type=f32)


def product(left, right, dims):
    return dot(left[0], right[0], dims) + (
        dot(left[0], right[1], dims) + dot(left[1], right[0], dims)
    )


def exact(left, right, dims):
    return lax.dot_general(
        left, right, (dims, ((), ())), preferred_element_type=f32, precision=highest
    )


def put(tile, row, vector):
    for j in range(vector.shape[1] // 128):
        tile[row + j : row + j + 1, :] = vector[:, j * 128 : (j + 1) * 128]


def get(tile, row, count):
    return jnp.concatenate([tile[row + j : row + j + 1, :] for j in range(count)], axis=1)


def wide(mask, width):
    return jnp.concatenate([mask] * (width // 128), axis=1)


def column_sum(values):
    return jnp.sum(values, axis=0, keepdims=True)


def image_sum(values, images):
    return jnp.sum(values.reshape(images, values.shape[0] // images, values.shape[1]), axis=1)


def per_image(vector, values):
    count, width = vector.shape
    each = values.shape[0] // count
    return jnp.broadcast_to(vector[:, None, :], (count, each, width)).reshape(values.shape[0], width)


def merge_stats(gathered, counts, width):
    groups = width // 128
    own = jnp.maximum(counts, 1.0)
    total = jnp.sum(counts, axis=0)
    means, inverses = [], []
    for j in range(groups):
        sums = gathered[:, j, :]
        squares = gathered[:, groups + j, :]
        mean = jnp.sum(sums, axis=0, keepdims=True) / total
        shift = sums / own - mean
        spread = jnp.sum(squares + counts * shift * shift, axis=0, keepdims=True) / total
        means.append(mean)
        inverses.append(lax.rsqrt(spread + epsilon))
    return jnp.concatenate(means, axis=1), jnp.concatenate(inverses, axis=1), total


def local_stats(values, mask, count):
    sums = column_sum(values * mask)
    centered = values - sums / jnp.maximum(count, 1.0)
    return sums, column_sum(centered * centered * mask)


def own_rows(extended, images):
    rows, width = extended.shape
    tall = rows // images // 16
    return extended.reshape(images, tall, 16, width)[:, 1 : tall - 1].reshape(-1, width)


class In:
    def __init__(self, source, target, sems, chunks):
        self.ref, self.shape, self.dtype = target, target.shape, target.dtype
        rows = self.shape[0] // chunks
        self.parts = [pl.ds(i * rows, rows) for i in range(chunks)]
        self.copies = [
            pltpu.make_async_copy(source.at[part], target.at[part], sems.at[i])
            for i, part in enumerate(self.parts)
        ]
        self.due = list(range(chunks))

    def start(self):
        for copy in self.copies:
            copy.start()

    def ready(self):
        while self.due:
            self.copies[self.due.pop(0)].wait()
        return self.ref

    def chunk(self, i):
        if i in self.due:
            self.due.remove(i)
            self.copies[i].wait()
        return self.ref[self.parts[i]]

    def __getitem__(self, index):
        return self.ready()[index]


class Near:
    def __init__(self, ref):
        self.ref, self.shape, self.dtype = ref, ref.shape, ref.dtype

    def start(self, i=None):
        pass

    ready = send = start

    def finish(self):
        pass

    def __getitem__(self, index):
        return self.ref[index]

    def __setitem__(self, index, value):
        self.ref[index] = value


class Out:
    def __init__(self, source, target, sems, chunks):
        self.ref, self.shape, self.dtype = source, source.shape, source.dtype
        rows = self.shape[0] // chunks
        self.parts = [pl.ds(i * rows, rows) for i in range(chunks)]
        self.copies = [
            pltpu.make_async_copy(source.at[part], target.at[part], sems.at[i])
            for i, part in enumerate(self.parts)
        ]
        self.sent = set()

    def send(self, i=None):
        for k in range(len(self.copies)) if i is None else [i]:
            if k not in self.sent:
                self.sent.add(k)
                self.copies[k].start()

    def finish(self):
        self.send()
        for copy in self.copies:
            copy.wait()

    def put(self, i, value):
        self.ref[self.parts[i]] = value
        self.send(i)

    def __getitem__(self, index):
        return self.ref[index]

    def __setitem__(self, index, value):
        self.ref[index] = value


def call(body, outs, ins, scratch=(), limit=54, chunks=None, out_chunks=None, after=(), beside=(), near=(), near_outs=()):
    chunks, out_chunks = chunks or {}, out_chunks or {}
    n, m, k = len(ins), len(outs), len(after) + len(beside)
    far = [i for i in range(n) if i not in near]
    far_outs = [i for i in range(m) if i not in near_outs]
    parts = [chunks.get(i, 1) for i in far] + [out_chunks.get(i, 1) for i in far_outs]

    def inner(*refs):
        sources, targets, local = refs[:n], refs[n + k : n + k + m], refs[n + k + m :]
        held, sems, rest = local[: len(parts)], local[len(parts) : 2 * len(parts)], local[2 * len(parts) :]
        given = [Near(ref) for ref in sources]
        for at, i in enumerate(far):
            given[i] = In(sources[i], held[at], sems[at], parts[at])
        made = [Near(ref) for ref in targets]
        for at, i in enumerate(far_outs, len(far)):
            made[i] = Out(held[at], targets[i], sems[at], parts[at])
        for each in given:
            each.start()
        body(*given, *made, *rest)
        for each in given:
            each.ready()
        for each in made:
            each.send()
        for each in made:
            each.finish()

    space = lambda count, places: [pl.BlockSpec(memory_space=pltpu.VMEM if i in places else pltpu.HBM) for i in range(count)]
    return pl.pallas_call(
        inner,
        out_shape=[(pltpu.VMEM if i in near_outs else pltpu.HBM)(*out) for i, out in enumerate(outs)],
        in_specs=space(n, near) + space(len(after), ()) + space(len(beside), range(len(beside))),
        out_specs=space(m, near_outs),
        scratch_shapes=[
            *[pltpu.VMEM(ins[i].shape, ins[i].dtype) for i in far],
            *[pltpu.VMEM(*outs[i]) for i in far_outs],
            *[pltpu.SemaphoreType.DMA((k,)) for k in parts],
            *scratch,
        ],
        compiler_params=pltpu.CompilerParams(vmem_limit_bytes=limit * 2**20),
        cost_estimate=pl.CostEstimate(flops=1, bytes_accessed=1, transcendentals=0),
    )(
        *[pltpu.with_memory_space_constraint(a, pltpu.VMEM if i in near else pltpu.HBM) for i, a in enumerate(ins)],
        *[pltpu.with_memory_space_constraint(a, pltpu.HBM) for a in after],
        *[pltpu.with_memory_space_constraint(a, pltpu.VMEM) for a in beside],
    )


def local_call(body, outs, ins, scratch=(), limit=16, after=(), beside=()):
    n, k = len(ins), len(after) + len(beside)

    def inner(*refs):
        body(*refs[:n], *refs[n + k :])

    spec = lambda space, count: [pl.BlockSpec(memory_space=space)] * count
    return pl.pallas_call(
        inner,
        out_shape=[pltpu.VMEM(*out) for out in outs],
        in_specs=spec(pltpu.VMEM, n) + spec(pltpu.HBM, len(after)) + spec(pltpu.VMEM, len(beside)),
        out_specs=spec(pltpu.VMEM, len(outs)),
        scratch_shapes=list(scratch),
        compiler_params=pltpu.CompilerParams(vmem_limit_bytes=limit * 2**20),
        cost_estimate=pl.CostEstimate(flops=1, bytes_accessed=1, transcendentals=0),
    )(
        *[pltpu.with_memory_space_constraint(a, pltpu.VMEM) for a in ins],
        *[pltpu.with_memory_space_constraint(a, pltpu.HBM) for a in after],
        *[pltpu.with_memory_space_constraint(a, pltpu.VMEM) for a in beside],
    )


def share(tile):
    return lax.all_to_all(tile, both, 0, 0)


def halos(first, last):
    count = lax.axis_size("rows")
    above = lax.ppermute(last, "rows", [(i, i + 1) for i in range(count - 1)])
    below = lax.ppermute(first, "rows", [(i + 1, i) for i in range(count - 1)])
    return above, below


def flip(values, axis, bits):
    return lax.ppermute(values, axis, [(i, i ^ bits) for i in range(lax.axis_size(axis))])


class Digit:
    def __init__(self, axis, unit, size):
        self.axis, self.unit, self.size = axis, unit, size

    def own(self):
        return lax.axis_index(self.axis) // self.unit % self.size

    def send(self, pieces):
        return [pieces[0]] + [flip(pieces[j], self.axis, j * self.unit) for j in range(1, self.size)]

    def bits(self):
        return [Digit(self.axis, self.unit << i, 2) for i in range(self.size.bit_length() - 1)]

    def trade(self, stacked):
        count = lax.axis_size(self.axis)
        span = self.unit * self.size
        starts = [high + low for high in range(0, count, span) for low in range(self.unit)]
        groups = [[start + self.unit * d for d in range(self.size)] for start in starts]
        return lax.all_to_all(stacked, self.axis, 0, 0, axis_index_groups=groups)

    def scatter(self, parts, outs):
        size = outs[0].shape[0]
        own = self.own()
        for j, out in enumerate(outs):
            at = pl.ds(pl.multiple_of((own ^ j) * size, 8), size)
            total = parts[0][at, :]
            for part in parts[1:]:
                total = total + part[at, :]
            out[...] = total

    def gather(self, pieces, out):
        size = pieces[0].shape[0]
        own = self.own()
        for j, piece in enumerate(pieces):
            out[pl.ds(pl.multiple_of((own ^ j) * size, 8), size), :] = piece[...]

    def outs(self, rows, width):
        return [((rows // self.size, width), f32)] * self.size


def digits():
    rows, batch = lax.axis_size("rows"), lax.axis_size("batch")
    depth = min(4, batch // 2)
    return Digit("batch", 1, 2), Digit("rows", 1, rows), Digit("batch", 2, depth), Digit("batch", 2 * depth, batch // (2 * depth))


def gate(value, beside):
    return pl.pallas_call(
        lambda *refs: None,
        out_shape=pltpu.VMEM(value.shape, value.dtype),
        in_specs=[pl.BlockSpec(memory_space=pltpu.VMEM)] * (1 + len(beside)),
        out_specs=pl.BlockSpec(memory_space=pltpu.VMEM),
        input_output_aliases={0: 0},
        cost_estimate=pl.CostEstimate(flops=1, bytes_accessed=1, transcendentals=0),
    )(*[pltpu.with_memory_space_constraint(a, pltpu.VMEM) for a in (value, *beside)])


def scatter_kernel(digit, count, *refs):
    digit.scatter(refs[:count], refs[count:])


def sum_kernel(*refs):
    total = refs[0][...]
    for ref in refs[1:-1]:
        total = total + ref[...]
    refs[-1][...] = total


def gather_kernel(digit, *refs):
    digit.gather(refs[:-1], refs[-1])


def scatter_more(digit, pieces, **order):
    rows, width = pieces[0].shape
    body = functools.partial(scatter_kernel, digit, len(pieces))
    return local_call(body, digit.outs(rows, width), pieces, **order)


def add_up(pieces, **order):
    return local_call(sum_kernel, [(pieces[0].shape, f32)], pieces, **order)[0]


def finish_sum(pieces, extra, **order):
    total = add_up(pieces, **order)
    if extra.size > 1:
        total = add_up(extra.send([total] * extra.size))
    return total


def gather_more(digit, pieces, **order):
    rows, width = pieces[0].shape
    return local_call(functools.partial(gather_kernel, digit), [((rows * digit.size, width), f32)], pieces, **order)[0]


def reduce_kernel(rows_ref, cols_ref, w_ref, x_ref, z_ref, ext_ref, own_ref, first_ref, last_ref, pay_ref,
                  tile):
    images = rows_ref.shape[0]
    tall = x_ref.shape[0] // images // 16
    shape = (images, tall + 2, 16, 16)
    start = lax.axis_index("rows") * tall - 1
    lane = lax.broadcasted_iota(jnp.int32, shape, 3).reshape(-1, 16)
    at_row = lax.broadcasted_iota(jnp.int32, shape, 1).reshape(-1, 16) + start
    at_col = lax.broadcasted_iota(jnp.int32, shape, 2).reshape(-1, 16)
    row_valid = per_image(rows_ref[...].astype(f32), lane)
    col_valid = per_image(cols_ref[...].astype(f32), lane)
    in_row = jnp.sum(jnp.where(lane == at_row, row_valid, 0.0), axis=1, keepdims=True)
    in_col = jnp.sum(jnp.where(lane == at_col, col_valid, 0.0), axis=1, keepdims=True)
    mask = jnp.broadcast_to(in_row * in_col, (in_row.shape[0], 128)).reshape(ext_ref.shape)
    ext_ref[...] = mask
    own = mask[:, 1 : tall + 1].reshape(-1, 128)
    own_ref[...] = own
    weight = split(w_ref[...])
    for i in range(len(x_ref.parts)):
        z_ref[x_ref.parts[i]] = product(split(x_ref.chunk(i)), weight, NN)
    z = z_ref[...]
    edges = z.reshape(images, tall, 16, -1)
    first_ref[...] = edges[:, 0].reshape(first_ref.shape)
    last_ref[...] = edges[:, tall - 1].reshape(last_ref.shape)
    for each in (first_ref, last_ref, z_ref, ext_ref, own_ref):
        each.send()
    count = column_sum(own)
    sums, squares = local_stats(z, wide(own, z.shape[1]), wide(count, z.shape[1]))
    tile[...] = jnp.zeros_like(tile)
    put(tile, 0, sums)
    put(tile, 2, squares)
    put(tile, 4, count)
    pay_ref[...] = jnp.broadcast_to(tile[...][None], pay_ref.shape)


def parts_kernel(wg_ref, we_ref, wr_ref, *refs):
    vectors, wg_refs, (weh_ref, wel_ref, wrh_ref, wrl_ref, par_ref) = refs[:-9], refs[-9:-5], refs[-5:]
    row = 0
    for vector in vectors:
        put(par_ref, row, vector[...])
        row += vector.shape[1] // 128
    half = wg_ref.shape[1] // 2
    for i in range(len(wg_ref.parts)):
        for j, part in enumerate(split(wg_ref.chunk(i))):
            for g in range(2):
                wg_refs[2 * g + j].put(i, part[:, g * half : (g + 1) * half])
    for source, high_ref, low_ref in ((we_ref, weh_ref, wel_ref), (wr_ref, wrh_ref, wrl_ref)):
        for i in range(len(source.parts)):
            high, low = split(source.chunk(i))
            high_ref.put(i, high)
            low_ref.put(i, low)


def turned_kernel(x_ref, high_ref, low_ref):
    high_ref[...], low_ref[...] = split(x_ref[...].T)


def moved(values, step):
    count = values.shape[0]
    at = lax.broadcasted_iota(jnp.int32, values.shape, 0) & 15
    if step == 0:
        return values
    if step > 0:
        return jnp.where(at < 15, pltpu.roll(values, count - 1, 0), 0.0)
    return jnp.where(at > 0, pltpu.roll(values, 1, 0), 0.0)


def window(extended, images, row, width):
    tall = extended.shape[0] // images // 16
    cells = extended.reshape(images, tall, 16, extended.shape[1])
    return cells[:, row : row + tall - 2, :, width].reshape(images * (tall - 2) * 16, -1)


def extend(place, cells, above, below):
    images, tall, broad, width = place.shape
    place[:, 1 : tall - 1] = cells[...].reshape(images, tall - 2, broad, width)
    place[:, 0] = above[...].reshape(images, broad, width)
    place[:, tall - 1] = below[...].reshape(images, broad, width)
    return place[...].reshape(-1, width)


def conv_kernel(g1_ref, par_ref, z_ref, ext_ref, above_ref, below_ref, own_ref, first_high, first_low, second_high, second_low,
                z2_ref, a_ref, stat_ref, counts_ref, pay_ref, tile, zext):
    images = zext.shape[0]
    tall = zext.shape[1] - 2
    width = z_ref.shape[1]
    group = width // 2
    gathered = g1_ref[...]
    counts = gathered[:, 4, :]
    counts_ref[...] = counts
    mean, inv, total = merge_stats(gathered, counts, width)
    tile[...] = jnp.zeros_like(tile)
    put(tile, 0, mean)
    put(tile, 2, inv)
    put(tile, 4, total[None])
    stat_ref[...] = tile[...]
    y = (extend(zext, z_ref, above_ref, below_ref) - mean) * inv * get(par_ref, 0, 2) + get(par_ref, 2, 2)
    a = y * jax.nn.sigmoid(y) * wide(ext_ref[...].reshape(-1, 128), width)
    a_ref[...] = a
    a_ref.send()
    shifted = [split(moved(a, step)) for step in (-1, 0, 1)]
    half = z2_ref.shape[1] // 2
    for ref in (first_high, first_low, second_high, second_low):
        ref.ready()
    for g in range(2):
        cols = slice(g * group, (g + 1) * group)
        left = [
            jnp.concatenate(
                [window(shifted[tap % 3][part], images, tap // 3, cols) for tap in range(9)], axis=1
            )
            for part in range(2)
        ]
        outs = slice(g * half, (g + 1) * half)
        right = [ref[...] for ref in ((first_high, first_low), (second_high, second_low))[g]]
        z2_ref[:, outs] = product(left, right, NN)
    z2_ref.send()
    z2 = z2_ref[...]
    own = own_ref[...]
    sums, squares = local_stats(z2, wide(own, z2.shape[1]), wide(column_sum(own), z2.shape[1]))
    put(tile, 0, sums)
    put(tile, 4, squares)
    pay_ref[...] = jnp.broadcast_to(tile[...][None], pay_ref.shape)


def taps_kernel(images, a_ref, high_ref, low_ref):
    group = a_ref.shape[1] // 2
    a = a_ref[...]
    shifted = [moved(a, step) for step in (-1, 0, 1)]
    for g in range(2):
        cols = slice(g * group, (g + 1) * group)
        for tap in range(9):
            high, low = split(window(shifted[tap % 3], images, tap // 3, cols).T)
            high_ref[g, tap * group : (tap + 1) * group, :] = high
            low_ref[g, tap * group : (tap + 1) * group, :] = low
        high_ref.send(g)
        low_ref.send(g)


def pixel_count(rows_ref, cols_ref):
    rows = jnp.sum(rows_ref[...].astype(f32), axis=1, keepdims=True)
    return rows * jnp.sum(cols_ref[...].astype(f32), axis=1, keepdims=True)


def pool_kernel(g2_ref, counts_ref, par_ref, rows_ref, cols_ref, z_ref, own_ref, w_ref, a_ref, stat_ref, pooled_ref, pay_ref):
    images = rows_ref.shape[0]
    width = z_ref.shape[1]
    mid = width // 2
    mean, inv, total = merge_stats(g2_ref[...], counts_ref[...], width)
    put(stat_ref, 0, mean)
    put(stat_ref, 4, inv)
    gain, shift = get(par_ref, 4, 4), get(par_ref, 8, 4)
    pieces = len(z_ref.parts)
    sums = []
    for i in range(pieces):
        y = (z_ref.chunk(i) - mean) * inv * gain + shift
        a = y * jax.nn.sigmoid(y) * wide(own_ref.chunk(i), width)
        a_ref.put(i, a)
        sums.append(image_sum(a, images // pieces))
    sums = jnp.concatenate(sums, axis=0)
    pooled = (sums[:, :mid] + sums[:, mid:]) / pixel_count(rows_ref, cols_ref)
    pooled_ref[...] = pooled
    pay_ref[...] = jnp.broadcast_to(exact(pooled, w_ref[...], NN)[None], pay_ref.shape)


def slope_of(values, mean, inv, gain, shift):
    normed = (values - mean) * inv
    y = normed * gain + shift
    sigma = jax.nn.sigmoid(y)
    return sigma * (1.0 + y * (1.0 - sigma)), normed


def slope_kernel(stat_ref, par_ref, rows_ref, cols_ref, own_ref, z_ref, slope_ref, normed_ref, sums_ref):
    images = rows_ref.shape[0]
    width = z_ref.shape[1]
    mean, inv = get(stat_ref, 0, 4), get(stat_ref, 4, 4)
    gain, shift = get(par_ref, 4, 4), get(par_ref, 8, 4)
    pieces = len(z_ref.parts)
    sums, cross = [], []
    for i in range(pieces):
        slope, normed = slope_of(z_ref.chunk(i), mean, inv, gain, shift)
        slope = slope * wide(own_ref.chunk(i), width)
        normed_ref.put(i, normed)
        slope_ref.put(i, slope)
        sums.append(image_sum(slope, images // pieces))
        cross.append(image_sum(slope * normed, images // pieces))
    pixels = pixel_count(rows_ref, cols_ref)
    sums_ref[:, :width] = jnp.concatenate(sums, axis=0) / pixels
    sums_ref[:, width:] = jnp.concatenate(cross, axis=0) / pixels


def expand_kernel(g3_ref, par_ref, w_ref, a_ref, wh_ref, wl_ref, own_ref,
                  mixed_ref, z_ref, weights_ref, normed_ref, pre_ref, act_ref, inv_ref, pay_ref, tile, acts):
    own_images = weights_ref.shape[0]
    mid = mixed_ref.shape[1]
    devices = g3_ref.shape[0]
    rows = lax.axis_size("rows")
    f_one = jnp.sum(g3_ref[...].reshape(rows, devices // rows * own_images, -1), axis=0)
    mean = jnp.mean(f_one, axis=0, keepdims=True)
    centered = f_one - mean
    inv = lax.rsqrt(jnp.mean(centered * centered, axis=0, keepdims=True) + epsilon)
    normed = centered * inv
    pre = normed * par_ref[12:13, :] + par_ref[13:14, :]
    normed_ref[...] = normed
    pre_ref[...] = pre
    inv_ref[...] = inv
    acts[...] = pre * jax.nn.sigmoid(pre)
    at = pl.multiple_of(lax.axis_index("batch") * own_images, own_images)
    act = acts[pl.ds(at, own_images), :]
    act_ref[...] = act
    logits = exact(act, w_ref[...], NN) + get(par_ref, 14, 4)
    lead = logits[:, :mid] - logits[:, mid:]
    first, second = jax.nn.sigmoid(lead), jax.nn.sigmoid(-lead)
    weights_ref[:, :mid] = first
    weights_ref[:, mid:] = second
    a = a_ref[...]
    mixed = per_image(first, a) * a[:, :mid] + per_image(second, a) * a[:, mid:]
    mixed_ref[...] = mixed
    mixed_ref.send()
    left, right = split(mixed), (wh_ref[...], wl_ref[...])
    for i, part in enumerate(z_ref.parts):
        rows = slice(part.start, part.start + part.size)
        z_ref.put(i, product([each[rows] for each in left], right, NN))
    z = z_ref[...]
    width = z.shape[1]
    own = wide(own_ref[...], width)
    sums, squares = local_stats(z, own, wide(column_sum(own_ref[...]), width))
    put(tile, 0, sums)
    put(tile, width // 128, squares)
    pay_ref[...] = jnp.broadcast_to(tile[...][None], pay_ref.shape)


def output_kernel(g4_ref, counts_ref, par_ref, own_ref, z_ref, x_ref, cot_ref, *refs):
    slope_refs, (grad_ref, stat_ref, slopes_ref, pay_ref, tile) = refs[:-5], refs[-5:]
    width = z_ref.shape[1]
    groups = width // 128
    mean, inv, total = merge_stats(g4_ref[...], counts_ref[...], width)
    put(stat_ref, 0, mean)
    put(stat_ref, groups, inv)
    gain, shift = get(par_ref, 18, groups), get(par_ref, 26, groups)
    flat, cross = 0.0, 0.0
    for i in range(len(z_ref.parts)):
        own = wide(own_ref.chunk(i), width)
        normed = (z_ref.chunk(i) - mean) * inv
        pre = normed * gain + shift + x_ref.chunk(i)
        sigma = jax.nn.sigmoid(pre)
        grad = cot_ref.chunk(i) * own * (sigma * (1.0 + pre * (1.0 - sigma)))
        grad_ref.put(i, grad)
        flat = flat + column_sum(grad)
        cross = cross + column_sum(grad * normed)
    put(tile, 0, flat)
    put(tile, groups, cross)
    pay_ref[...] = jnp.broadcast_to(tile[...][None], pay_ref.shape)
    sum_kernel(*slope_refs, slopes_ref)


def result_kernel(stat_ref, par_ref, own_ref, z_ref, x_ref, out_ref, mark_ref):
    width = z_ref.shape[1]
    groups = width // 128
    mean, inv = get(stat_ref, 0, groups), get(stat_ref, groups, groups)
    gain, shift = get(par_ref, 18, groups), get(par_ref, 26, groups)
    for i in range(len(z_ref.parts)):
        pre = (z_ref.chunk(i) - mean) * inv * gain + shift + x_ref.chunk(i)
        out_ref.put(i, pre * jax.nn.sigmoid(pre) * wide(own_ref.chunk(i), width))
    mark_ref[...] = own_ref[:8, :]


def mixed_kernel(digit, g5_ref, stat1_ref, stat3_ref, par_ref, own_ref, grad_ref, z_ref, wh_ref, wl_ref, a_ref, weights_ref,
                 w_ref, slope_ref, normed_ref, *refs):
    shares, (gm_ref, dsum_ref, grads_ref, gain_ref, shift_ref, slopes_ref, pay_ref, tile) = refs[: digit.size], refs[digit.size :]
    width = z_ref.shape[1]
    mid = gm_ref.shape[1]
    images = weights_ref.shape[0]
    groups = width // 128
    grads_ref[...] = jnp.sum(g5_ref[...], axis=0)
    shift_ref[...] = grads_ref[:groups, :]
    gain_ref[...] = grads_ref[groups:, :]
    count = wide(stat1_ref[4:5, :], width)
    mean, inv = get(stat3_ref, 0, groups), get(stat3_ref, groups, groups)
    flat = get(grads_ref, 0, groups) / count
    cross = get(grads_ref, groups, groups) / count
    scale = get(par_ref, 18, groups) * inv
    for i in range(len(z_ref.parts)):
        normed = (z_ref.chunk(i) - mean) * inv
        dz = scale * (grad_ref.chunk(i) - flat - normed * cross) * wide(own_ref.chunk(i), width)
        gm_ref[z_ref.parts[i]] = product(split(dz), (wh_ref[...], wl_ref[...]), NT)
    gm = gm_ref[...]
    gm_ref.send()
    a = a_ref[...]
    weights = weights_ref[...]
    gate = image_sum(gm * (a[:, :mid] - a[:, mid:]), images)
    dsum = weights[:, :mid] * weights[:, mid:] * gate
    dsum_ref[...] = dsum
    tile[...] = jnp.zeros_like(tile)
    tile[:images, :] = exact(dsum, w_ref[:, :mid] - w_ref[:, mid:], NT)
    slope = slope_ref[...] * jnp.concatenate([gm, gm], axis=1)
    put(tile, 8, column_sum(weights * image_sum(slope, images)))
    put(tile, 12, column_sum(weights * image_sum(slope * normed_ref[...], images)))
    pay_ref[...] = jnp.broadcast_to(tile[...][None], pay_ref.shape)
    digit.gather(shares, slopes_ref)


def expand_grad_kernel(core, grads_ref, stat1_ref, stat3_ref, par_ref, mixed_ref, act_ref, dsum_ref, own_ref, grad_ref, z_ref,
                       keep_ref, send_ref, excite_ref, term):
    width = z_ref.shape[1]
    groups = width // 128
    count = wide(stat1_ref[4:5, :], width)
    mean, inv = get(stat3_ref, 0, groups), get(stat3_ref, groups, groups)
    flat = get(grads_ref, 0, groups) / count
    cross = get(grads_ref, groups, groups) / count
    scale = get(par_ref, 18, groups) * inv
    left = split(mixed_ref[...].T)
    rows, span = left[0].shape[0], term.shape[1]
    for i, part in enumerate(z_ref.parts):
        normed = (z_ref.chunk(i) - mean) * inv
        dz = scale * (grad_ref.chunk(i) - flat - normed * cross) * wide(own_ref.chunk(i), width)
        right = split(dz)
        some = [each[:, part.start : part.start + part.size] for each in left]
        for j in range(term.shape[0] // rows):
            value = product(some, [each[:, j * span : (j + 1) * span] for each in right], NN)
            if i:
                value = value + term[j * rows : (j + 1) * rows, :]
            term[j * rows : (j + 1) * rows, :] = value
    core.scatter([term], [keep_ref, send_ref])
    excite_ref[...] = exact(act_ref[...], dsum_ref[...], TN)


def turned_rows(left, refs, row, taps):
    return product(left, [ref[row * taps : (row + 1) * taps, :] for ref in refs], NT)


def fold(total, group):
    return moved(total[:, :group], 1) + total[:, group : 2 * group] + moved(total[:, 2 * group :], -1)


def back_kernel(digit, g6_ref, pre_ref, fcn_ref, inv_ref, par_ref, wsq_ref, pooled_ref, stat1_ref, stat2_ref, rows_ref,
                cols_ref, weights_ref, mine_ref, other_ref, own_ref, gm_ref, slope_ref, normed_ref, *refs):
    w_refs, (up_ref, down_ref), dz_refs, (squeeze_ref, gain_ref, flat_ref, fc_gain_ref, fc_flat_ref, gf, owned, slopes) = (
        refs[:4], refs[4:6], refs[6:10], refs[10:]
    )
    images = rows_ref.shape[0]
    tall = dz_refs[0].shape[1] - 2
    width = normed_ref.shape[1]
    mid = width // 2
    groups = width // 128
    rows = lax.axis_size("rows")
    shared = g6_ref[...]
    pre = pre_ref[...]
    fcn = fcn_ref[...]
    sigma = jax.nn.sigmoid(pre)
    total = pre.shape[0]
    grad = jnp.sum(shared[:, :images].reshape(rows, total, -1), axis=0) * (sigma * (1.0 + pre * (1.0 - sigma)))
    flat, cross = column_sum(grad), column_sum(grad * fcn)
    fc_gain_ref[...] = cross
    fc_flat_ref[...] = flat
    gf[...] = par_ref[12:13, :] * inv_ref[...] * (grad - flat / total - fcn * cross / total)
    at = pl.multiple_of(lax.axis_index("batch") * images, images)
    mine = gf[pl.ds(at, images), :]
    squeeze = exact(pooled_ref[...], mine, TN)
    half_rows = squeeze.shape[0] // 2
    squeeze_ref[:, : squeeze.shape[1]] = squeeze[:half_rows]
    squeeze_ref[:, squeeze.shape[1] :] = squeeze[half_rows:]
    spread = exact(gf[...], wsq_ref[...], NT)
    owned[...] = spread
    own_spread = owned[pl.ds(at, images), :] / pixel_count(rows_ref, cols_ref)
    for flipped, half in enumerate((mine_ref, other_ref)):
        for block in range(half.shape[0] // images):
            here = pl.multiple_of((2 * block + (digit.own() ^ flipped)) * images, images)
            slopes[pl.ds(here, images), :] = half[block * images : (block + 1) * images, :]
    base = jnp.sum(shared[:, 8:], axis=0)
    count = wide(stat1_ref[4:5, :], mid)
    weights = weights_ref[...]
    gm = gm_ref[...]
    shared_part = per_image(own_spread, gm)
    mask = wide(own_ref[...], mid)
    zero = jnp.zeros((images, 16, mid), bf16)
    for ref in dz_refs:
        ref[:, 0] = zero
        ref[:, tall + 1] = zero
    for g in range(2):
        outs = slice(g * mid, (g + 1) * mid)
        crosses = slice(width + g * mid, width + (g + 1) * mid)
        half = groups // 2
        flat_two = get(base, g * half, half) + column_sum(spread * slopes[:, outs])
        cross_two = get(base, groups + g * half, half) + column_sum(spread * slopes[:, crosses])
        put(gain_ref, g * half, cross_two)
        put(flat_ref, g * half, flat_two)
        scale = get(par_ref, 4 + g * half, half) * get(stat2_ref, groups + g * half, half)
        upstream = per_image(weights[:, outs], gm) * gm + shared_part
        dz = scale * (upstream * slope_ref[:, outs] - flat_two / count - normed_ref[:, outs] * (cross_two / count)) * mask
        for ref, part in zip(dz_refs[2 * g : 2 * g + 2], split(dz)):
            ref[:, 1 : tall + 1] = part.reshape(images, tall, 16, mid)
            ref.send()
    group = up_ref.shape[1] // 2
    for g in range(2):
        cols = slice(g * group, (g + 1) * group)
        for side, row, tap in ((up_ref, 1, 0), (down_ref, tall, 2)):
            left = [ref[:, row].reshape(-1, mid) for ref in dz_refs[2 * g : 2 * g + 2]]
            side[:, cols] = fold(turned_rows(left, w_refs[2 * g : 2 * g + 2], tap, 3 * group), group)


def group_kernel(core, *refs):
    dz_refs, (squeeze_ref, excite_ref, th_ref, tl_ref, keep_ref, send_ref, out_ref) = refs[:4], refs[4:]
    for ref in (*dz_refs, squeeze_ref, excite_ref, th_ref, tl_ref):
        ref.ready()
    tall = dz_refs[0].shape[1] - 2
    taps = th_ref.shape[1]
    for g in range(2):
        right = [ref[:, 1 : tall + 1].reshape(-1, ref.shape[3]) for ref in dz_refs[2 * g : 2 * g + 2]]
        out_ref[g * taps : (g + 1) * taps, :] = product((th_ref.chunk(g)[0], tl_ref.chunk(g)[0]), right, NN)
    inter = excite_ref.shape[0]
    out_ref[2 * taps : 2 * taps + inter, :] = excite_ref[...]
    out_ref[2 * taps + inter :, :] = squeeze_ref[...]
    core.scatter([out_ref], [keep_ref, send_ref])


def input_grad_kernel(g, par_ref, stat_ref, z_ref, own_ref, above_ref, below_ref, dzh_ref, dzl_ref, wh_ref, wl_ref, *refs):
    images, tall = dzh_ref.shape[0], dzh_ref.shape[1] - 2
    group = z_ref.shape[1] // 2
    cols = slice(g * group, (g + 1) * group)
    total = None
    for row in range(3):
        left = [ref[:, 2 - row : 2 - row + tall].reshape(-1, ref.shape[3]) for ref in (dzh_ref, dzl_ref)]
        term = turned_rows(left, (wh_ref, wl_ref), row, 3 * group)
        total = term if total is None else total + term
    place = refs[-1]
    place[...] = fold(total, group).reshape(place.shape)
    place[:, 0] += above_ref[:, cols].reshape(images, 16, group)
    place[:, tall - 1] += below_ref[:, cols].reshape(images, 16, group)
    grad = place[...].reshape(-1, group)
    mean, inv, gain, shift = [ref[row + g : row + g + 1, :] for ref, row in ((stat_ref, 0), (stat_ref, 2), (par_ref, 0), (par_ref, 2))]
    normed = (z_ref[:, cols] - mean) * inv
    y = normed * gain + shift
    sigma = jax.nn.sigmoid(y)
    dy = grad * wide(own_ref[...], group) * (sigma * (1.0 + y * (1.0 - sigma)))
    if g == 0:
        dy_ref, tile = refs[:2]
        tile[...] = jnp.zeros(tile.shape, f32)
    else:
        dsum_ref, before_ref, dy_ref, pay_ref, tile = refs[:5]
        tile[...] = before_ref[...]
        put(tile, 4, column_sum(dsum_ref[...]))
    dy_ref[...] = dy
    dy_ref.send()
    put(tile, g, column_sum(dy * normed))
    put(tile, 2 + g, column_sum(dy))
    if g:
        pay_ref[...] = jnp.broadcast_to(tile[...][None], pay_ref.shape)


def final_kernel(core, g7_ref, par_ref, stat_ref, first_ref, second_ref, z_ref, own_ref, th_ref, tl_ref,
                 keep_ref, send_ref, dzh_ref, dzl_ref, mark_ref, gain_ref, flat_ref, bias_ref, gains_ref, term):
    width = z_ref.shape[1]
    gains_ref[...] = jnp.sum(g7_ref[...], axis=0)
    mark_ref[...] = gains_ref[...]
    gain_ref[...] = gains_ref[0:2, :]
    flat_ref[...] = gains_ref[2:4, :]
    bias_ref[0:2, :] = gains_ref[4:6, :]
    bias_ref[2:4, :] = -gains_ref[4:6, :]
    cross, flat = get(gains_ref, 0, 2), get(gains_ref, 2, 2)
    count = wide(stat_ref[4:5, :], width)
    mean, inv = get(stat_ref, 0, 2), get(stat_ref, 2, 2)
    normed = (z_ref[...] - mean) * inv
    scale = get(par_ref, 0, 2) * inv
    dy = jnp.concatenate([first_ref[...], second_ref[...]], axis=1)
    dz = scale * (dy - flat / count - normed * (cross / count)) * wide(own_ref[...], width)
    high, low = split(dz)
    dzh_ref[...] = high
    dzl_ref[...] = low
    term[...] = product((th_ref[...], tl_ref[...]), (high, low), NN)
    core.scatter([term], [keep_ref, send_ref])


def images_kernel(dzh_ref, dzl_ref, wh_ref, wl_ref, grad_ref, out_ref):
    for i in range(len(grad_ref.parts)):
        left = [ref.chunk(i) for ref in (dzh_ref, dzl_ref)]
        out_ref.put(i, product(left, (wh_ref[...], wl_ref[...]), NT) + grad_ref.chunk(i))


def deal_kernel(plan, count, *refs):
    outs = list(refs[count:])
    for digit, stretches in plan:
        own = digit.own()
        for j in range(digit.size):
            out, at = outs.pop(0), 0
            for inputs, first, rows in stretches:
                each = rows // digit.size
                here = pl.ds(pl.multiple_of(first + (own ^ j) * each, 8), each)
                total = refs[inputs[0]][here, :]
                for k in inputs[1:]:
                    total = total + refs[k][here, :]
                out[at : at + each, :] = total
                at += each


def deal(plan, ins, **order):
    width = ins[0].shape[1]
    outs = []
    for digit, stretches in plan:
        rows = sum(rows for _, _, rows in stretches) // digit.size
        outs += [((rows, width), f32)] * digit.size
    return local_call(functools.partial(deal_kernel, plan, len(ins)), outs, ins, **order)


def stack_kernel(stretches, *refs):
    refs, out = refs[:-1], refs[-1]
    at = 0
    for inputs, first, rows in stretches:
        each = rows // out.shape[0]
        for d in range(out.shape[0]):
            here = slice(first + d * each, first + (d + 1) * each)
            total = refs[inputs[0]][here, :]
            for k in inputs[1:]:
                total = total + refs[k][here, :]
            out[d, at : at + each, :] = total
        at += each


def extra_pieces(extra, stacked):
    if extra.size == 1:
        return [stacked]
    total = local_call(lambda ref, out: out.__setitem__(Ellipsis, jnp.sum(ref[...], axis=0)), [(stacked.shape[1:], f32)], [stacked])[0]
    return extra.send([total] * extra.size)


def stacked_kernel(count, *refs):
    if count == 1:
        refs[-1][...] = jnp.sum(refs[0][...], axis=0)
    else:
        sum_kernel(*refs)


def halves_kernel(digit, *refs):
    pieces, outs = refs[: digit.size], refs[digit.size :]
    half = pieces[0].shape[0] // 2
    own = digit.own()
    for j, piece in enumerate(pieces):
        at = pl.ds(pl.multiple_of((own ^ j) * half, 8), half)
        for i, out in enumerate(outs):
            out[at, :] = piece[i * half : (i + 1) * half, :]


def pair_kernel(digits, *refs):
    outs = refs[4:]
    for i, digit in enumerate(digits):
        digit.gather(refs[2 * i : 2 * i + 2], outs[i] if len(outs) == 2 else outs[0].at[pl.ds(i * 2 * refs[0].shape[0], 2 * refs[0].shape[0])])


def last_kernel(core, expand_map, group_map, mine_ref, other_ref, expand_ref, group_ref, excite_ref, squeeze_ref, whole):
    core.gather([mine_ref, other_ref], whole)
    taps, mid = group_ref.shape[0], whole.shape[1]
    inter = squeeze_ref.shape[1]
    tall = expand_ref.shape[0]
    places = [
        (taps, lambda rows, value: group_ref.__setitem__((rows, slice(0, mid)), value)),
        (taps, lambda rows, value: group_ref.__setitem__((rows, slice(mid, 2 * mid)), value)),
        (inter, lambda rows, value: excite_ref.__setitem__((rows, slice(0, mid)), value)),
        (inter, lambda rows, value: squeeze_put(squeeze_ref, rows, value)),
    ]
    for at, first, rows in expand_map:
        j, m = first // tall, first % tall
        expand_ref[m : m + rows, j * mid : (j + 1) * mid] = whole[at : at + rows, :]
    for at, first, rows in group_map:
        base = 0
        for length, store in places:
            low, high = max(first, base), min(first + rows, base + length)
            if low < high:
                store(slice(low - base, high - base), whole[at + low - first : at + high - first, :])
            base += length
    excite_ref[:, mid:] = -excite_ref[:, :mid]


def squeeze_put(squeeze_ref, rows, value):
    half = squeeze_ref.shape[0] // 2
    width = squeeze_ref.shape[1]
    squeeze_ref[rows, :] = value[:, :width]
    squeeze_ref[slice(half + rows.start, half + rows.stop), :] = value[:, width:]


def on_device(
    images,
    w_reduce,
    gain_one,
    shift_one,
    w_group,
    gain_two,
    shift_two,
    w_squeeze,
    gain_fc,
    shift_fc,
    w_excite,
    excite_bias,
    w_expand,
    gain_three,
    shift_three,
    valid_rows,
    valid_cols,
    cotangent,
):
    count, tall, broad, chan = images.shape
    mid = w_reduce.shape[1]
    inter = w_squeeze.shape[1]
    duo = 2 * mid
    taps = 9 * mid // 2
    cells = count * tall * broad
    longer = count * (tall + 2) * broad
    edge = count * broad
    devices = lax.axis_size("rows") * lax.axis_size("batch")
    all_images = count * lax.axis_size("batch")
    x = images.reshape(cells, chan)
    cot = cotangent.reshape(cells, chan)
    pay8 = ((devices, 8, 128), f32)
    pay16 = ((devices, 16, 128), f32)
    tile8 = pltpu.VMEM((8, 128), f32)
    tile16 = pltpu.VMEM((16, 128), f32)
    twice = lambda *shape: [(shape, bf16)] * 2
    flat_w = w_group.reshape(taps, duo)
    vectors = (gain_one, shift_one, gain_two, shift_two, gain_fc, shift_fc, excite_bias, gain_three, shift_three)
    core, line, depth, extra = digits()

    z_one, ext, own, first, last, pay = call(
        reduce_kernel,
        [((cells, mid), f32), ((count, tall + 2, broad, 128), f32), ((cells, 128), f32), ((edge, mid), f32),
         ((edge, mid), f32), pay8],
        [valid_rows, valid_cols, w_reduce, x],
        [tile8],
        near_outs=(3, 4, 5),
    )
    g1 = share(pay)
    above, below = halos(first, last)
    *group_parts, weh, wel, wrh, wrl, par = call(
        parts_kernel,
        [*twice(taps, mid), *twice(taps, mid), *twice(mid, chan), *twice(chan, mid), ((40, 128), f32)],
        [flat_w, w_expand, w_reduce, *[v.reshape(1, -1) for v in vectors]],
        chunks={0: 4, 1: 2, 2: 2},
        out_chunks={0: 4, 1: 4, 2: 4, 3: 4, 4: 2, 5: 2, 6: 2, 7: 2},
        after=[z_one],
    )
    z_two, a_one, stat1, counts, pay = call(
        conv_kernel,
        [((cells, duo), f32), ((longer, mid), f32), ((8, 128), f32), ((devices, 128), f32), pay8],
        [g1, par, z_one, ext, above, below, own, *group_parts],
        [tile8, pltpu.VMEM((count, tall + 2, broad, mid), f32)],
        near=(0, 4, 5),
        near_outs=(4,),
    )
    g2 = share(pay)
    xth, xtl = call(turned_kernel, twice(chan, cells), [x], after=[stat1])
    a_two, stat2, pooled, pay = call(
        pool_kernel,
        [((cells, duo), f32), ((8, 128), f32), ((count, mid), f32), ((devices, count, inter), f32)],
        [g2, counts, par, valid_rows, valid_cols, z_two, own, w_squeeze],
        chunks={5: 2, 6: 2},
        out_chunks={0: 2},
        after=[xth],
        near=(0,),
        near_outs=(3,),
    )
    g3 = share(pay)
    slope_two, normed_two, slopes = call(
        slope_kernel,
        [((cells, duo), f32), ((cells, duo), f32), ((count, 2 * duo), f32)],
        [stat2, par, valid_rows, valid_cols, own, z_two],
        chunks={4: 2, 5: 2},
        out_chunks={0: 2, 1: 2},
    )
    mixed, z_three, weights, fc_normed, fc_pre, fc_act, fc_inv, pay = call(
        expand_kernel,
        [((cells, mid), f32), ((cells, chan), f32), ((count, duo), f32), ((all_images, inter), f32),
         ((all_images, inter), f32), ((count, inter), f32), ((1, inter), f32), pay16],
        [g3, par, w_excite, a_two, weh, wel, own],
        [tile16, pltpu.VMEM((all_images, inter), f32)],
        out_chunks={1: 2},
        after=[slopes],
        near=(0,),
        near_outs=(7,),
    )
    g4 = share(pay)
    slopes = line.send([slopes] * line.size)
    grad_pre, stat3, slopes, pay = call(
        output_kernel,
        [((cells, chan), f32), ((16, 128), f32), ((count, 2 * duo), f32), pay16],
        [g4, counts, par, own, z_three, x, cot, *slopes],
        [tile16],
        chunks={3: 2, 4: 2, 5: 2, 6: 2},
        out_chunks={0: 2},
        near=(0, *range(7, 7 + line.size)),
        near_outs=(2, 3),
    )
    g5 = share(pay)
    slopes = depth.send([slopes] * depth.size)
    tph, tpl = call(functools.partial(taps_kernel, count), twice(2, taps, cells), [a_one], out_chunks={0: 2, 1: 2}, after=[stat3])
    grad_mixed, dsum, grads_three, grad_gain_three, grad_shift_three, slopes, pay = call(
        functools.partial(mixed_kernel, depth),
        [((cells, mid), f32), ((count, mid), f32),
         ((16, 128), f32), ((8, 128), f32), ((8, 128), f32), ((depth.size * count, 2 * duo), f32), pay16],
        [g5, stat1, stat3, par, own, grad_pre, z_three, weh, wel, a_two, weights, w_excite, slope_two, normed_two, *slopes],
        [tile16],
        after=[tph],
        near=(0, *range(14, 14 + depth.size)),
        near_outs=(5, 6),
    )
    g6 = share(pay)
    *expand_sum, excite_term = call(
        functools.partial(expand_grad_kernel, core),
        [*core.outs(mid * chan // mid, mid), ((inter, mid), f32)],
        [grads_three, stat1, stat3, par, mixed, fc_act, dsum, own, grad_pre, z_three],
        [pltpu.VMEM((chan, mid), f32)],
        chunks={7: 2, 8: 2, 9: 2},
    )
    if extra.size > 1:
        slopes = gather_more(extra, extra.send([slopes] * extra.size))
    slopes = core.send([slopes] * 2)
    packed = 2 * taps + 2 * inter
    up, down, *dz_parts, squeeze_term, grad_gain_two, grad_shift_two, grad_gain_fc, grad_shift_fc = call(
        functools.partial(back_kernel, core),
        [((edge, mid), f32), ((edge, mid), f32), *twice(count, tall + 2, broad, mid), *twice(count, tall + 2, broad, mid), ((inter, mid), f32),
         ((duo // 128, 128), f32), ((duo // 128, 128), f32), ((1, inter), f32), ((1, inter), f32)],
        [g6, fc_pre, fc_normed, fc_inv, par, w_squeeze, pooled, stat1, stat2, valid_rows, valid_cols, weights, *slopes, own,
         grad_mixed, slope_two, normed_two, *group_parts],
        [pltpu.VMEM((all_images, inter), f32), pltpu.VMEM((all_images, mid), f32), pltpu.VMEM((all_images, 2 * duo), f32)],
        after=[excite_term],
        near=(0, 12, 13),
        near_outs=(0, 1),
    )
    above, below = halos(up, down)
    group_sum = call(
        functools.partial(group_kernel, core),
        core.outs(packed, mid),
        [*dz_parts, squeeze_term, excite_term, tph, tpl],
        [pltpu.VMEM((packed, mid), f32)],
        chunks={6: 2, 7: 2},
        near_outs=(0, 1),
    )
    expand_sum = core.send(expand_sum)
    group_sum = core.send([group_sum[0], gate(group_sum[1], [above, below])])
    dy_first, tile = call(
        functools.partial(input_grad_kernel, 0),
        [((cells, mid // 2), f32), ((8, 128), f32)],
        [par, stat1, z_one, own, above, below, *dz_parts[:2], *group_parts[:2]],
        [pltpu.VMEM((count, tall, broad, mid // 2), f32)],
        near=(4, 5),
    )
    first_bit, second_bit = line.bits()
    some, more = expand_sum[0].shape[0] // 2, group_sum[0].shape[0] // 2
    both_of = lambda start, a, b: [((0, 1), start * a, a), ((2, 3), start * b, b)]
    first_half = lambda digit: (digit, both_of(0, some, more))
    second_half = lambda digit: (digit, both_of(1, some, more))
    keep_a, send_a, keep_b, send_b = deal(
        [first_half(first_bit), second_half(second_bit)], [*expand_sum, *group_sum], after=[tile]
    )
    come_a, come_b = first_bit.send([keep_a, send_a]), second_bit.send([keep_b, send_b])
    place = pltpu.VMEM((count, tall, broad, mid // 2), f32)
    dy_second, pay = call(
        functools.partial(input_grad_kernel, 1),
        [((cells, mid // 2), f32), pay8],
        [par, stat1, z_one, own, above, below, *dz_parts[2:], *group_parts[2:], dsum, tile],
        [tile8, place],
        beside=[keep_a],
        near=(4, 5),
        near_outs=(1,),
    )
    g7 = share(pay)
    some, more = some // 2, more // 2
    turn = lambda k: [((k, k + 1), 0, some), ((k, k + 1), some, more)]
    keep_a, send_a, keep_b, send_b = deal([(second_bit, turn(0)), (first_bit, turn(2))], [*come_a, *come_b], after=[dy_second])
    *reduce_sum, dzh, dzl, mark_one, grad_gain_one, grad_shift_one, grad_bias = call(
        functools.partial(final_kernel, core),
        [*core.outs(chan, mid), *twice(cells, mid), ((8, 128), f32), *[((mid // 128, 128), f32)] * 2, ((duo // 128, 128), f32)],
        [g7, par, stat1, dy_first, dy_second, z_one, own, xth, xtl],
        [tile8, pltpu.VMEM((chan, mid), f32)],
        beside=[keep_a],
        near=(0,),
        near_outs=(0, 1),
    )
    come_a, come_b = second_bit.send([keep_a, send_a]), first_bit.send([keep_b, send_b])
    some, more = some // 2, more // 2
    stretches = turn(0) + turn(2)
    (joined,) = local_call(
        functools.partial(stack_kernel, stretches),
        [((depth.size, (some + more) * 2 // depth.size, mid), f32)],
        [*come_a, *come_b],
        after=[mark_one],
    )
    joined = depth.trade(joined)
    reduce_sum = scatter_more(line, core.send(reduce_sum))
    (grad_images,) = call(
        images_kernel,
        [((cells, chan), f32)],
        [dzh, dzl, wrh, wrl, grad_pre],
        chunks={0: 2, 1: 2, 4: 2},
        out_chunks={0: 2},
        beside=[reduce_sum[0]],
    )
    reduce_sum = scatter_more(depth, line.send(reduce_sum), after=[grad_images])
    (joined,) = local_call(
        functools.partial(stacked_kernel, extra.size), [(joined.shape[1:], f32)], extra_pieces(extra, joined), beside=[reduce_sum[0]]
    )
    rows_in = depth.size * joined.shape[0]
    block_out, mark = call(
        result_kernel,
        [((cells, chan), f32), ((8, 128), f32)],
        [stat3, par, own, z_three, x],
        chunks={2: 4, 3: 4, 4: 4},
        out_chunks={0: 4},
        beside=[joined],
    )
    half_a, half_b = local_call(
        functools.partial(halves_kernel, depth),
        [((rows_in // 2, mid), f32)] * 2,
        depth.send([joined] * depth.size),
        after=[mark],
    )
    reduce_sum = finish_sum(depth.send(reduce_sum), extra, beside=[half_a])
    half_a, half_b = local_call(
        functools.partial(pair_kernel, [second_bit, first_bit]),
        [((rows_in, mid), f32)] * 2,
        [*second_bit.send([half_a] * 2), *first_bit.send([half_b] * 2)],
        beside=[reduce_sum],
    )
    reduce_sum = gather_more(depth, depth.send([reduce_sum] * depth.size), beside=[half_a])
    (joined,) = local_call(
        functools.partial(pair_kernel, [first_bit, second_bit]),
        [((4 * rows_in, mid), f32)],
        [*first_bit.send([half_a] * 2), *second_bit.send([half_b] * 2)],
        beside=[reduce_sum],
    )
    expand_map, group_map = [], []
    at = 0
    some, more = some // depth.size, more // depth.size
    for half in range(core.size):
        for part in range(2):
            for outer in range(2):
                for inner in range(2):
                    for deep in range(depth.size):
                        block = (((half * 2 + part) * 2 + outer) * 2 + inner) * depth.size + deep
                        expand_map.append((at, block * some, some))
                        group_map.append((at + some, block * more, more))
                        at += some + more
    grad_w_expand, grad_w_group, grad_w_excite, grad_w_squeeze = call(
        functools.partial(last_kernel, core, expand_map, group_map),
        [((mid, chan), f32), ((taps, duo), f32), ((inter, duo), f32), ((mid, inter), f32)],
        core.send([joined] * 2),
        [pltpu.VMEM((chan + packed, mid), f32)],
        near=(0, 1),
    )
    reduce_sum = gather_more(line, line.send([reduce_sum] * line.size), after=[grad_w_squeeze])
    (grad_w_reduce,) = call(
        functools.partial(gather_kernel, core), [((chan, mid), f32)], core.send([reduce_sum] * 2), near=(0, 1)
    )
    return (
        block_out.reshape(images.shape),
        grad_images.reshape(images.shape),
        grad_w_reduce,
        grad_gain_one.reshape(-1),
        grad_shift_one.reshape(-1),
        grad_w_group.reshape(w_group.shape),
        grad_gain_two.reshape(-1),
        grad_shift_two.reshape(-1),
        grad_w_squeeze,
        grad_gain_fc.reshape(-1),
        grad_shift_fc.reshape(-1),
        grad_w_excite,
        grad_bias.reshape(-1),
        grad_w_expand,
        grad_gain_three.reshape(-1),
        grad_shift_three.reshape(-1),
    )


def solution(mesh):
    maps = P("batch", "rows", None, None)
    return jax.shard_map(
        on_device,
        mesh=mesh,
        in_specs=(maps,) + (P(),) * 14 + (P("batch", None), P("batch", None), maps),
        out_specs=(maps, maps) + (P(),) * 14,
        check_vma=False,
    )
```

```python
import functools

import jax
import jax.numpy as jnp
from jax import lax
from jax.experimental import pallas as pl
from jax.experimental.pallas import tpu as pltpu
from jax.sharding import PartitionSpec as P

epsilon = 1e-05
f32 = jnp.float32
bf16 = jnp.bfloat16
highest = lax.Precision.HIGHEST
both = ("rows", "batch")
NN = ((1,), (0,))
NT = ((1,), (1,))
TN = ((0,), (0,))


def split(values):
    high = values.astype(bf16)
    return high, (values - high.astype(f32)).astype(bf16)


def dot(left, right, dims):
    return lax.dot_general(left, right, (dims, ((), ())), preferred_element_type=f32)


def product(left, right, dims):
    return dot(left[0], right[0], dims) + (
        dot(left[0], right[1], dims) + dot(left[1], right[0], dims)
    )


def exact(left, right, dims):
    return lax.dot_general(
        left, right, (dims, ((), ())), preferred_element_type=f32, precision=highest
    )


def put(tile, row, vector):
    for j in range(vector.shape[1] // 128):
        tile[row + j : row + j + 1, :] = vector[:, j * 128 : (j + 1) * 128]


def get(tile, row, count):
    return jnp.concatenate([tile[row + j : row + j + 1, :] for j in range(count)], axis=1)


def wide(mask, width):
    return jnp.concatenate([mask] * (width // 128), axis=1)


def column_sum(values):
    return jnp.sum(values, axis=0, keepdims=True)


def image_sum(values, images):
    return jnp.sum(values.reshape(images, values.shape[0] // images, values.shape[1]), axis=1)


def per_image(vector, values):
    count, width = vector.shape
    each = values.shape[0] // count
    return jnp.broadcast_to(vector[:, None, :], (count, each, width)).reshape(values.shape[0], width)


def merge_stats(gathered, counts, width):
    groups = width // 128
    own = jnp.maximum(counts, 1.0)
    total = jnp.sum(counts, axis=0)
    means, inverses = [], []
    for j in range(groups):
        sums = gathered[:, j, :]
        squares = gathered[:, groups + j, :]
        mean = jnp.sum(sums, axis=0, keepdims=True) / total
        shift = sums / own - mean
        spread = jnp.sum(squares + counts * shift * shift, axis=0, keepdims=True) / total
        means.append(mean)
        inverses.append(lax.rsqrt(spread + epsilon))
    return jnp.concatenate(means, axis=1), jnp.concatenate(inverses, axis=1), total


def local_stats(values, mask, count):
    sums = column_sum(values * mask)
    centered = values - sums / jnp.maximum(count, 1.0)
    return sums, column_sum(centered * centered * mask)


def own_rows(extended, images):
    rows, width = extended.shape
    tall = rows // images // 16
    return extended.reshape(images, tall, 16, width)[:, 1 : tall - 1].reshape(-1, width)


class In:
    def __init__(self, source, target, sems, chunks):
        self.ref, self.shape, self.dtype = target, target.shape, target.dtype
        rows = self.shape[0] // chunks
        self.parts = [pl.ds(i * rows, rows) for i in range(chunks)]
        self.copies = [
            pltpu.make_async_copy(source.at[part], target.at[part], sems.at[i])
            for i, part in enumerate(self.parts)
        ]
        self.due = list(range(chunks))

    def start(self):
        for copy in self.copies:
            copy.start()

    def ready(self):
        while self.due:
            self.copies[self.due.pop(0)].wait()
        return self.ref

    def chunk(self, i):
        if i in self.due:
            self.due.remove(i)
            self.copies[i].wait()
        return self.ref[self.parts[i]]

    def __getitem__(self, index):
        return self.ready()[index]


class Near:
    def __init__(self, ref):
        self.ref, self.shape, self.dtype = ref, ref.shape, ref.dtype

    def start(self, i=None):
        pass

    ready = send = start

    def finish(self):
        pass

    def __getitem__(self, index):
        return self.ref[index]

    def __setitem__(self, index, value):
        self.ref[index] = value


class Out:
    def __init__(self, source, target, sems, chunks):
        self.ref, self.shape, self.dtype = source, source.shape, source.dtype
        rows = self.shape[0] // chunks
        self.parts = [pl.ds(i * rows, rows) for i in range(chunks)]
        self.copies = [
            pltpu.make_async_copy(source.at[part], target.at[part], sems.at[i])
            for i, part in enumerate(self.parts)
        ]
        self.sent = set()

    def send(self, i=None):
        for k in range(len(self.copies)) if i is None else [i]:
            if k not in self.sent:
                self.sent.add(k)
                self.copies[k].start()

    def finish(self):
        self.send()
        for copy in self.copies:
            copy.wait()

    def put(self, i, value):
        self.ref[self.parts[i]] = value
        self.send(i)

    def __getitem__(self, index):
        return self.ref[index]

    def __setitem__(self, index, value):
        self.ref[index] = value


def call(body, outs, ins, scratch=(), limit=54, chunks=None, out_chunks=None, after=(), beside=(), near=(), near_outs=()):
    chunks, out_chunks = chunks or {}, out_chunks or {}
    n, m, k = len(ins), len(outs), len(after) + len(beside)
    far = [i for i in range(n) if i not in near]
    far_outs = [i for i in range(m) if i not in near_outs]
    parts = [chunks.get(i, 1) for i in far] + [out_chunks.get(i, 1) for i in far_outs]

    def inner(*refs):
        sources, targets, local = refs[:n], refs[n + k : n + k + m], refs[n + k + m :]
        held, sems, rest = local[: len(parts)], local[len(parts) : 2 * len(parts)], local[2 * len(parts) :]
        given = [Near(ref) for ref in sources]
        for at, i in enumerate(far):
            given[i] = In(sources[i], held[at], sems[at], parts[at])
        made = [Near(ref) for ref in targets]
        for at, i in enumerate(far_outs, len(far)):
            made[i] = Out(held[at], targets[i], sems[at], parts[at])
        for each in given:
            each.start()
        body(*given, *made, *rest)
        for each in given:
            each.ready()
        for each in made:
            each.send()
        for each in made:
            each.finish()

    space = lambda count, places: [pl.BlockSpec(memory_space=pltpu.VMEM if i in places else pltpu.HBM) for i in range(count)]
    return pl.pallas_call(
        inner,
        out_shape=[(pltpu.VMEM if i in near_outs else pltpu.HBM)(*out) for i, out in enumerate(outs)],
        in_specs=space(n, near) + space(len(after), ()) + space(len(beside), range(len(beside))),
        out_specs=space(m, near_outs),
        scratch_shapes=[
            *[pltpu.VMEM(ins[i].shape, ins[i].dtype) for i in far],
            *[pltpu.VMEM(*outs[i]) for i in far_outs],
            *[pltpu.SemaphoreType.DMA((k,)) for k in parts],
            *scratch,
        ],
        compiler_params=pltpu.CompilerParams(vmem_limit_bytes=limit * 2**20),
        cost_estimate=pl.CostEstimate(flops=1, bytes_accessed=1, transcendentals=0),
    )(
        *[pltpu.with_memory_space_constraint(a, pltpu.VMEM if i in near else pltpu.HBM) for i, a in enumerate(ins)],
        *[pltpu.with_memory_space_constraint(a, pltpu.HBM) for a in after],
        *[pltpu.with_memory_space_constraint(a, pltpu.VMEM) for a in beside],
    )


def local_call(body, outs, ins, scratch=(), limit=16, after=(), beside=()):
    n, k = len(ins), len(after) + len(beside)

    def inner(*refs):
        body(*refs[:n], *refs[n + k :])

    spec = lambda space, count: [pl.BlockSpec(memory_space=space)] * count
    return pl.pallas_call(
        inner,
        out_shape=[pltpu.VMEM(*out) for out in outs],
        in_specs=spec(pltpu.VMEM, n) + spec(pltpu.HBM, len(after)) + spec(pltpu.VMEM, len(beside)),
        out_specs=spec(pltpu.VMEM, len(outs)),
        scratch_shapes=list(scratch),
        compiler_params=pltpu.CompilerParams(vmem_limit_bytes=limit * 2**20),
        cost_estimate=pl.CostEstimate(flops=1, bytes_accessed=1, transcendentals=0),
    )(
        *[pltpu.with_memory_space_constraint(a, pltpu.VMEM) for a in ins],
        *[pltpu.with_memory_space_constraint(a, pltpu.HBM) for a in after],
        *[pltpu.with_memory_space_constraint(a, pltpu.VMEM) for a in beside],
    )


def share(tile):
    return lax.all_to_all(tile, both, 0, 0)


def halos(first, last):
    count = lax.axis_size("rows")
    above = lax.ppermute(last, "rows", [(i, i + 1) for i in range(count - 1)])
    below = lax.ppermute(first, "rows", [(i + 1, i) for i in range(count - 1)])
    return above, below


def flip(values, axis, bits):
    return lax.ppermute(values, axis, [(i, i ^ bits) for i in range(lax.axis_size(axis))])


class Digit:
    def __init__(self, axis, unit, size):
        self.axis, self.unit, self.size = axis, unit, size

    def own(self):
        return lax.axis_index(self.axis) // self.unit % self.size

    def send(self, pieces):
        return [pieces[0]] + [flip(pieces[j], self.axis, j * self.unit) for j in range(1, self.size)]

    def bits(self):
        return [Digit(self.axis, self.unit << i, 2) for i in range(self.size.bit_length() - 1)]

    def trade(self, stacked):
        count = lax.axis_size(self.axis)
        span = self.unit * self.size
        starts = [high + low for high in range(0, count, span) for low in range(self.unit)]
        groups = [[start + self.unit * d for d in range(self.size)] for start in starts]
        return lax.all_to_all(stacked, self.axis, 0, 0, axis_index_groups=groups)

    def scatter(self, parts, outs):
        size = outs[0].shape[0]
        own = self.own()
        for j, out in enumerate(outs):
            at = pl.ds(pl.multiple_of((own ^ j) * size, 8), size)
            total = parts[0][at, :]
            for part in parts[1:]:
                total = total + part[at, :]
            out[...] = total

    def gather(self, pieces, out):
        size = pieces[0].shape[0]
        own = self.own()
        for j, piece in enumerate(pieces):
            out[pl.ds(pl.multiple_of((own ^ j) * size, 8), size), :] = piece[...]

    def outs(self, rows, width):
        return [((rows // self.size, width), f32)] * self.size


def digits():
    rows, batch = lax.axis_size("rows"), lax.axis_size("batch")
    depth = min(4, batch // 2)
    return Digit("batch", 1, 2), Digit("rows", 1, rows), Digit("batch", 2, depth), Digit("batch", 2 * depth, batch // (2 * depth))


def gate(value, beside):
    return pl.pallas_call(
        lambda *refs: None,
        out_shape=pltpu.VMEM(value.shape, value.dtype),
        in_specs=[pl.BlockSpec(memory_space=pltpu.VMEM)] * (1 + len(beside)),
        out_specs=pl.BlockSpec(memory_space=pltpu.VMEM),
        input_output_aliases={0: 0},
        cost_estimate=pl.CostEstimate(flops=1, bytes_accessed=1, transcendentals=0),
    )(*[pltpu.with_memory_space_constraint(a, pltpu.VMEM) for a in (value, *beside)])


def scatter_kernel(digit, count, *refs):
    digit.scatter(refs[:count], refs[count:])


def sum_kernel(*refs):
    total = refs[0][...]
    for ref in refs[1:-1]:
        total = total + ref[...]
    refs[-1][...] = total


def gather_kernel(digit, *refs):
    digit.gather(refs[:-1], refs[-1])


def scatter_more(digit, pieces, **order):
    rows, width = pieces[0].shape
    body = functools.partial(scatter_kernel, digit, len(pieces))
    return local_call(body, digit.outs(rows, width), pieces, **order)


def add_up(pieces, **order):
    return local_call(sum_kernel, [(pieces[0].shape, f32)], pieces, **order)[0]


def finish_sum(pieces, extra, **order):
    total = add_up(pieces, **order)
    if extra.size > 1:
        total = add_up(extra.send([total] * extra.size))
    return total


def gather_more(digit, pieces, **order):
    rows, width = pieces[0].shape
    return local_call(functools.partial(gather_kernel, digit), [((rows * digit.size, width), f32)], pieces, **order)[0]


def reduce_kernel(rows_ref, cols_ref, w_ref, x_ref, z_ref, ext_ref, own_ref, first_ref, last_ref, pay_ref,
                  tile):
    images = rows_ref.shape[0]
    tall = x_ref.shape[0] // images // 16
    shape = (images, tall + 2, 16, 16)
    start = lax.axis_index("rows") * tall - 1
    lane = lax.broadcasted_iota(jnp.int32, shape, 3).reshape(-1, 16)
    at_row = lax.broadcasted_iota(jnp.int32, shape, 1).reshape(-1, 16) + start
    at_col = lax.broadcasted_iota(jnp.int32, shape, 2).reshape(-1, 16)
    row_valid = per_image(rows_ref[...].astype(f32), lane)
    col_valid = per_image(cols_ref[...].astype(f32), lane)
    in_row = jnp.sum(jnp.where(lane == at_row, row_valid, 0.0), axis=1, keepdims=True)
    in_col = jnp.sum(jnp.where(lane == at_col, col_valid, 0.0), axis=1, keepdims=True)
    mask = jnp.broadcast_to(in_row * in_col, (in_row.shape[0], 128)).reshape(ext_ref.shape)
    ext_ref[...] = mask
    own = mask[:, 1 : tall + 1].reshape(-1, 128)
    own_ref[...] = own
    weight = split(w_ref[...])
    for i in range(len(x_ref.parts)):
        z_ref[x_ref.parts[i]] = product(split(x_ref.chunk(i)), weight, NN)
    z = z_ref[...]
    edges = z.reshape(images, tall, 16, -1)
    first_ref[...] = edges[:, 0].reshape(first_ref.shape)
    last_ref[...] = edges[:, tall - 1].reshape(last_ref.shape)
    for each in (first_ref, last_ref, z_ref, ext_ref, own_ref):
        each.send()
    count = column_sum(own)
    sums, squares = local_stats(z, wide(own, z.shape[1]), wide(count, z.shape[1]))
    tile[...] = jnp.zeros_like(tile)
    put(tile, 0, sums)
    put(tile, 2, squares)
    put(tile, 4, count)
    pay_ref[...] = jnp.broadcast_to(tile[...][None], pay_ref.shape)


def parts_kernel(wg_ref, we_ref, wr_ref, *refs):
    vectors, wg_refs, (weh_ref, wel_ref, wrh_ref, wrl_ref, par_ref) = refs[:-9], refs[-9:-5], refs[-5:]
    row = 0
    for vector in vectors:
        put(par_ref, row, vector[...])
        row += vector.shape[1] // 128
    half = wg_ref.shape[1] // 2
    for i in range(len(wg_ref.parts)):
        for j, part in enumerate(split(wg_ref.chunk(i))):
            for g in range(2):
                wg_refs[2 * g + j].put(i, part[:, g * half : (g + 1) * half])
    for source, high_ref, low_ref in ((we_ref, weh_ref, wel_ref), (wr_ref, wrh_ref, wrl_ref)):
        for i in range(len(source.parts)):
            high, low = split(source.chunk(i))
            high_ref.put(i, high)
            low_ref.put(i, low)


def turned_kernel(x_ref, high_ref, low_ref):
    high_ref[...], low_ref[...] = split(x_ref[...].T)


def moved(values, step):
    count = values.shape[0]
    at = lax.broadcasted_iota(jnp.int32, values.shape, 0) & 15
    if step == 0:
        return values
    if step > 0:
        return jnp.where(at < 15, pltpu.roll(values, count - 1, 0), 0.0)
    return jnp.where(at > 0, pltpu.roll(values, 1, 0), 0.0)


def window(extended, images, row, width):
    tall = extended.shape[0] // images // 16
    cells = extended.reshape(images, tall, 16, extended.shape[1])
    return cells[:, row : row + tall - 2, :, width].reshape(images * (tall - 2) * 16, -1)


def extend(place, cells, above, below):
    images, tall, broad, width = place.shape
    place[:, 1 : tall - 1] = cells[...].reshape(images, tall - 2, broad, width)
    place[:, 0] = above[...].reshape(images, broad, width)
    place[:, tall - 1] = below[...].reshape(images, broad, width)
    return place[...].reshape(-1, width)


def conv_kernel(g1_ref, par_ref, z_ref, ext_ref, above_ref, below_ref, own_ref, first_high, first_low, second_high, second_low,
                z2_ref, a_ref, stat_ref, counts_ref, pay_ref, tile, zext):
    images = zext.shape[0]
    tall = zext.shape[1] - 2
    width = z_ref.shape[1]
    group = width // 2
    gathered = g1_ref[...]
    counts = gathered[:, 4, :]
    counts_ref[...] = counts
    mean, inv, total = merge_stats(gathered, counts, width)
    tile[...] = jnp.zeros_like(tile)
    put(tile, 0, mean)
    put(tile, 2, inv)
    put(tile, 4, total[None])
    stat_ref[...] = tile[...]
    y = (extend(zext, z_ref, above_ref, below_ref) - mean) * inv * get(par_ref, 0, 2) + get(par_ref, 2, 2)
    a = y * jax.nn.sigmoid(y) * wide(ext_ref[...].reshape(-1, 128), width)
    a_ref[...] = a
    a_ref.send()
    shifted = [split(moved(a, step)) for step in (-1, 0, 1)]
    half = z2_ref.shape[1] // 2
    for ref in (first_high, first_low, second_high, second_low):
        ref.ready()
    for g in range(2):
        cols = slice(g * group, (g + 1) * group)
        left = [
            jnp.concatenate(
                [window(shifted[tap % 3][part], images, tap // 3, cols) for tap in range(9)], axis=1
            )
            for part in range(2)
        ]
        outs = slice(g * half, (g + 1) * half)
        right = [ref[...] for ref in ((first_high, first_low), (second_high, second_low))[g]]
        z2_ref[:, outs] = product(left, right, NN)
    z2_ref.send()
    z2 = z2_ref[...]
    own = own_ref[...]
    sums, squares = local_stats(z2, wide(own, z2.shape[1]), wide(column_sum(own), z2.shape[1]))
    put(tile, 0, sums)
    put(tile, 4, squares)
    pay_ref[...] = jnp.broadcast_to(tile[...][None], pay_ref.shape)


def taps_kernel(images, a_ref, high_ref, low_ref):
    group = a_ref.shape[1] // 2
    a = a_ref[...]
    shifted = [moved(a, step) for step in (-1, 0, 1)]
    for g in range(2):
        cols = slice(g * group, (g + 1) * group)
        for tap in range(9):
            high, low = split(window(shifted[tap % 3], images, tap // 3, cols).T)
            high_ref[g, tap * group : (tap + 1) * group, :] = high
            low_ref[g, tap * group : (tap + 1) * group, :] = low
        high_ref.send(g)
        low_ref.send(g)


def pixel_count(rows_ref, cols_ref):
    rows = jnp.sum(rows_ref[...].astype(f32), axis=1, keepdims=True)
    return rows * jnp.sum(cols_ref[...].astype(f32), axis=1, keepdims=True)


def pool_kernel(g2_ref, counts_ref, par_ref, rows_ref, cols_ref, z_ref, own_ref, w_ref, a_ref, stat_ref, pooled_ref, pay_ref):
    images = rows_ref.shape[0]
    width = z_ref.shape[1]
    mid = width // 2
    mean, inv, total = merge_stats(g2_ref[...], counts_ref[...], width)
    put(stat_ref, 0, mean)
    put(stat_ref, 4, inv)
    gain, shift = get(par_ref, 4, 4), get(par_ref, 8, 4)
    pieces = len(z_ref.parts)
    sums = []
    for i in range(pieces):
        y = (z_ref.chunk(i) - mean) * inv * gain + shift
        a = y * jax.nn.sigmoid(y) * wide(own_ref.chunk(i), width)
        a_ref.put(i, a)
        sums.append(image_sum(a, images // pieces))
    sums = jnp.concatenate(sums, axis=0)
    pooled = (sums[:, :mid] + sums[:, mid:]) / pixel_count(rows_ref, cols_ref)
    pooled_ref[...] = pooled
    pay_ref[...] = jnp.broadcast_to(exact(pooled, w_ref[...], NN)[None], pay_ref.shape)


def slope_of(values, mean, inv, gain, shift):
    normed = (values - mean) * inv
    y = normed * gain + shift
    sigma = jax.nn.sigmoid(y)
    return sigma * (1.0 + y * (1.0 - sigma)), normed, y * sigma


def slope_kernel(stat_ref, par_ref, rows_ref, cols_ref, own_ref, z_ref, slope_ref, normed_ref, lead_ref, sums_ref):
    images = rows_ref.shape[0]
    width = z_ref.shape[1]
    mean, inv = get(stat_ref, 0, 4), get(stat_ref, 4, 4)
    gain, shift = get(par_ref, 4, 4), get(par_ref, 8, 4)
    pieces = len(z_ref.parts)
    sums, cross = [], []
    for i in range(pieces):
        slope, normed, a = slope_of(z_ref.chunk(i), mean, inv, gain, shift)
        mask = wide(own_ref.chunk(i), width)
        slope, a = slope * mask, a * mask
        lead_ref.put(i, a[:, : width // 2] - a[:, width // 2 :])
        normed_ref.put(i, normed)
        slope_ref.put(i, slope)
        sums.append(image_sum(slope, images // pieces))
        cross.append(image_sum(slope * normed, images // pieces))
    pixels = pixel_count(rows_ref, cols_ref)
    sums_ref[:, :width] = jnp.concatenate(sums, axis=0) / pixels
    sums_ref[:, width:] = jnp.concatenate(cross, axis=0) / pixels


def expand_kernel(g3_ref, par_ref, w_ref, a_ref, wh_ref, wl_ref, own_ref,
                  mixed_ref, z_ref, weights_ref, normed_ref, pre_ref, act_ref, inv_ref, pay_ref, tile, acts):
    own_images = weights_ref.shape[0]
    mid = mixed_ref.shape[1]
    devices = g3_ref.shape[0]
    rows = lax.axis_size("rows")
    f_one = jnp.sum(g3_ref[...].reshape(rows, devices // rows * own_images, -1), axis=0)
    mean = jnp.mean(f_one, axis=0, keepdims=True)
    centered = f_one - mean
    inv = lax.rsqrt(jnp.mean(centered * centered, axis=0, keepdims=True) + epsilon)
    normed = centered * inv
    pre = normed * par_ref[12:13, :] + par_ref[13:14, :]
    normed_ref[...] = normed
    pre_ref[...] = pre
    inv_ref[...] = inv
    acts[...] = pre * jax.nn.sigmoid(pre)
    at = pl.multiple_of(lax.axis_index("batch") * own_images, own_images)
    act = acts[pl.ds(at, own_images), :]
    act_ref[...] = act
    logits = exact(act, w_ref[...], NN) + get(par_ref, 14, 4)
    lead = logits[:, :mid] - logits[:, mid:]
    first, second = jax.nn.sigmoid(lead), jax.nn.sigmoid(-lead)
    weights_ref[:, :mid] = first
    weights_ref[:, mid:] = second
    a = a_ref[...]
    mixed = per_image(first, a) * a[:, :mid] + per_image(second, a) * a[:, mid:]
    mixed_ref[...] = mixed
    mixed_ref.send()
    left, right = split(mixed), (wh_ref[...], wl_ref[...])
    for i, part in enumerate(z_ref.parts):
        rows = slice(part.start, part.start + part.size)
        z_ref.put(i, product([each[rows] for each in left], right, NN))
    z = z_ref[...]
    width = z.shape[1]
    own = wide(own_ref[...], width)
    sums, squares = local_stats(z, own, wide(column_sum(own_ref[...]), width))
    put(tile, 0, sums)
    put(tile, width // 128, squares)
    pay_ref[...] = jnp.broadcast_to(tile[...][None], pay_ref.shape)


def output_kernel(g4_ref, counts_ref, par_ref, own_ref, z_ref, x_ref, cot_ref, *refs):
    slope_refs, (grad_ref, stat_ref, slopes_ref, pay_ref, tile) = refs[:-5], refs[-5:]
    width = z_ref.shape[1]
    groups = width // 128
    mean, inv, total = merge_stats(g4_ref[...], counts_ref[...], width)
    put(stat_ref, 0, mean)
    put(stat_ref, groups, inv)
    gain, shift = get(par_ref, 18, groups), get(par_ref, 26, groups)
    flat, cross = 0.0, 0.0
    for i in range(len(z_ref.parts)):
        own = wide(own_ref.chunk(i), width)
        normed = (z_ref.chunk(i) - mean) * inv
        pre = normed * gain + shift + x_ref.chunk(i)
        sigma = jax.nn.sigmoid(pre)
        grad = cot_ref.chunk(i) * own * (sigma * (1.0 + pre * (1.0 - sigma)))
        grad_ref.put(i, grad)
        flat = flat + column_sum(grad)
        cross = cross + column_sum(grad * normed)
    put(tile, 0, flat)
    put(tile, groups, cross)
    pay_ref[...] = jnp.broadcast_to(tile[...][None], pay_ref.shape)
    sum_kernel(*slope_refs, slopes_ref)


def result_kernel(stat_ref, par_ref, own_ref, z_ref, x_ref, out_ref, mark_ref):
    width = z_ref.shape[1]
    groups = width // 128
    mean, inv = get(stat_ref, 0, groups), get(stat_ref, groups, groups)
    gain, shift = get(par_ref, 18, groups), get(par_ref, 26, groups)
    for i in range(len(z_ref.parts)):
        pre = (z_ref.chunk(i) - mean) * inv * gain + shift + x_ref.chunk(i)
        out_ref.put(i, pre * jax.nn.sigmoid(pre) * wide(own_ref.chunk(i), width))
    mark_ref[...] = own_ref[:8, :]


def mixed_kernel(digit, g5_ref, stat1_ref, stat3_ref, par_ref, own_ref, grad_ref, z_ref, wh_ref, wl_ref, a_ref, weights_ref,
                 w_ref, slope_ref, normed_ref, *refs):
    shares, (gm_ref, dsum_ref, grads_ref, gain_ref, shift_ref, slopes_ref, pay_ref, tile) = refs[: digit.size], refs[digit.size :]
    width = z_ref.shape[1]
    mid = gm_ref.shape[1]
    images = weights_ref.shape[0]
    groups = width // 128
    grads_ref[...] = jnp.sum(g5_ref[...], axis=0)
    shift_ref[...] = grads_ref[:groups, :]
    gain_ref[...] = grads_ref[groups:, :]
    count = wide(stat1_ref[4:5, :], width)
    mean, inv = get(stat3_ref, 0, groups), get(stat3_ref, groups, groups)
    flat = get(grads_ref, 0, groups) / count
    cross = get(grads_ref, groups, groups) / count
    scale = get(par_ref, 18, groups) * inv
    for i in range(len(z_ref.parts)):
        normed = (z_ref.chunk(i) - mean) * inv
        dz = scale * (grad_ref.chunk(i) - flat - normed * cross) * wide(own_ref.chunk(i), width)
        gm_ref[z_ref.parts[i]] = product(split(dz), (wh_ref[...], wl_ref[...]), NT)
    gm = gm_ref[...]
    gm_ref.send()
    weights = weights_ref[...]
    gate = image_sum(gm * a_ref[...], images)
    dsum = weights[:, :mid] * weights[:, mid:] * gate
    dsum_ref[...] = dsum
    tile[...] = jnp.zeros_like(tile)
    tile[:images, :] = exact(dsum, w_ref[:, :mid] - w_ref[:, mid:], NT)
    slope = slope_ref[...] * jnp.concatenate([gm, gm], axis=1)
    put(tile, 8, column_sum(weights * image_sum(slope, images)))
    put(tile, 12, column_sum(weights * image_sum(slope * normed_ref[...], images)))
    pay_ref[...] = jnp.broadcast_to(tile[...][None], pay_ref.shape)
    digit.gather(shares, slopes_ref)


def expand_grad_kernel(core, grads_ref, stat1_ref, stat3_ref, par_ref, mixed_ref, act_ref, dsum_ref, own_ref, grad_ref, z_ref,
                       keep_ref, send_ref, excite_ref, term):
    width = z_ref.shape[1]
    groups = width // 128
    count = wide(stat1_ref[4:5, :], width)
    mean, inv = get(stat3_ref, 0, groups), get(stat3_ref, groups, groups)
    flat = get(grads_ref, 0, groups) / count
    cross = get(grads_ref, groups, groups) / count
    scale = get(par_ref, 18, groups) * inv
    left = split(mixed_ref[...].T)
    rows, span = left[0].shape[0], term.shape[1]
    for i, part in enumerate(z_ref.parts):
        normed = (z_ref.chunk(i) - mean) * inv
        dz = scale * (grad_ref.chunk(i) - flat - normed * cross) * wide(own_ref.chunk(i), width)
        right = split(dz)
        some = [each[:, part.start : part.start + part.size] for each in left]
        for j in range(term.shape[0] // rows):
            value = product(some, [each[:, j * span : (j + 1) * span] for each in right], NN)
            if i:
                value = value + term[j * rows : (j + 1) * rows, :]
            term[j * rows : (j + 1) * rows, :] = value
    core.scatter([term], [keep_ref, send_ref])
    excite_ref[...] = exact(act_ref[...], dsum_ref[...], TN)


def turned_rows(left, refs, row, taps):
    return product(left, [ref[row * taps : (row + 1) * taps, :] for ref in refs], NT)


def fold(total, group):
    return moved(total[:, :group], 1) + total[:, group : 2 * group] + moved(total[:, 2 * group :], -1)


def back_kernel(digit, g6_ref, pre_ref, fcn_ref, inv_ref, par_ref, wsq_ref, pooled_ref, stat1_ref, stat2_ref, rows_ref,
                cols_ref, weights_ref, mine_ref, other_ref, own_ref, gm_ref, slope_ref, normed_ref, *refs):
    w_refs, (up_ref, down_ref), dz_refs, (squeeze_ref, gain_ref, flat_ref, fc_gain_ref, fc_flat_ref, gf, owned, slopes) = (
        refs[:4], refs[4:6], refs[6:10], refs[10:]
    )
    images = rows_ref.shape[0]
    tall = dz_refs[0].shape[1] - 2
    width = normed_ref.shape[1]
    mid = width // 2
    groups = width // 128
    rows = lax.axis_size("rows")
    shared = g6_ref[...]
    pre = pre_ref[...]
    fcn = fcn_ref[...]
    sigma = jax.nn.sigmoid(pre)
    total = pre.shape[0]
    grad = jnp.sum(shared[:, :images].reshape(rows, total, -1), axis=0) * (sigma * (1.0 + pre * (1.0 - sigma)))
    flat, cross = column_sum(grad), column_sum(grad * fcn)
    fc_gain_ref[...] = cross
    fc_flat_ref[...] = flat
    gf[...] = par_ref[12:13, :] * inv_ref[...] * (grad - flat / total - fcn * cross / total)
    at = pl.multiple_of(lax.axis_index("batch") * images, images)
    mine = gf[pl.ds(at, images), :]
    squeeze = exact(pooled_ref[...], mine, TN)
    half_rows = squeeze.shape[0] // 2
    squeeze_ref[:, : squeeze.shape[1]] = squeeze[:half_rows]
    squeeze_ref[:, squeeze.shape[1] :] = squeeze[half_rows:]
    spread = exact(gf[...], wsq_ref[...], NT)
    owned[...] = spread
    own_spread = owned[pl.ds(at, images), :] / pixel_count(rows_ref, cols_ref)
    for flipped, half in enumerate((mine_ref, other_ref)):
        for block in range(half.shape[0] // images):
            here = pl.multiple_of((2 * block + (digit.own() ^ flipped)) * images, images)
            slopes[pl.ds(here, images), :] = half[block * images : (block + 1) * images, :]
    base = jnp.sum(shared[:, 8:], axis=0)
    count = wide(stat1_ref[4:5, :], mid)
    weights = weights_ref[...]
    gm = gm_ref[...]
    shared_part = per_image(own_spread, gm)
    mask = wide(own_ref[...], mid)
    zero = jnp.zeros((images, 16, mid), bf16)
    for ref in dz_refs:
        ref[:, 0] = zero
        ref[:, tall + 1] = zero
    for g in range(2):
        outs = slice(g * mid, (g + 1) * mid)
        crosses = slice(width + g * mid, width + (g + 1) * mid)
        half = groups // 2
        flat_two = get(base, g * half, half) + column_sum(spread * slopes[:, outs])
        cross_two = get(base, groups + g * half, half) + column_sum(spread * slopes[:, crosses])
        put(gain_ref, g * half, cross_two)
        put(flat_ref, g * half, flat_two)
        scale = get(par_ref, 4 + g * half, half) * get(stat2_ref, groups + g * half, half)
        upstream = per_image(weights[:, outs], gm) * gm + shared_part
        dz = scale * (upstream * slope_ref[:, outs] - flat_two / count - normed_ref[:, outs] * (cross_two / count)) * mask
        for ref, part in zip(dz_refs[2 * g : 2 * g + 2], split(dz)):
            ref[:, 1 : tall + 1] = part.reshape(images, tall, 16, mid)
            ref.send()
    group = up_ref.shape[1] // 2
    for g in range(2):
        cols = slice(g * group, (g + 1) * group)
        for side, row, tap in ((up_ref, 1, 0), (down_ref, tall, 2)):
            left = [ref[:, row].reshape(-1, mid) for ref in dz_refs[2 * g : 2 * g + 2]]
            side[:, cols] = fold(turned_rows(left, w_refs[2 * g : 2 * g + 2], tap, 3 * group), group)


def group_kernel(core, *refs):
    dz_refs, (squeeze_ref, excite_ref, th_ref, tl_ref, keep_ref, send_ref, out_ref) = refs[:4], refs[4:]
    for ref in (*dz_refs, squeeze_ref, excite_ref, th_ref, tl_ref):
        ref.ready()
    tall = dz_refs[0].shape[1] - 2
    taps = th_ref.shape[1]
    for g in range(2):
        right = [ref[:, 1 : tall + 1].reshape(-1, ref.shape[3]) for ref in dz_refs[2 * g : 2 * g + 2]]
        out_ref[g * taps : (g + 1) * taps, :] = product((th_ref.chunk(g)[0], tl_ref.chunk(g)[0]), right, NN)
    inter = excite_ref.shape[0]
    out_ref[2 * taps : 2 * taps + inter, :] = excite_ref[...]
    out_ref[2 * taps + inter :, :] = squeeze_ref[...]
    core.scatter([out_ref], [keep_ref, send_ref])


def input_grad_kernel(g, par_ref, stat_ref, z_ref, own_ref, above_ref, below_ref, dzh_ref, dzl_ref, wh_ref, wl_ref, *refs):
    images, tall = dzh_ref.shape[0], dzh_ref.shape[1] - 2
    group = z_ref.shape[1] // 2
    cols = slice(g * group, (g + 1) * group)
    total = None
    for row in range(3):
        left = [ref[:, 2 - row : 2 - row + tall].reshape(-1, ref.shape[3]) for ref in (dzh_ref, dzl_ref)]
        term = turned_rows(left, (wh_ref, wl_ref), row, 3 * group)
        total = term if total is None else total + term
    place = refs[-1]
    place[...] = fold(total, group).reshape(place.shape)
    place[:, 0] += above_ref[:, cols].reshape(images, 16, group)
    place[:, tall - 1] += below_ref[:, cols].reshape(images, 16, group)
    grad = place[...].reshape(-1, group)
    mean, inv, gain, shift = [ref[row + g : row + g + 1, :] for ref, row in ((stat_ref, 0), (stat_ref, 2), (par_ref, 0), (par_ref, 2))]
    normed = (z_ref[:, cols] - mean) * inv
    y = normed * gain + shift
    sigma = jax.nn.sigmoid(y)
    dy = grad * wide(own_ref[...], group) * (sigma * (1.0 + y * (1.0 - sigma)))
    if g == 0:
        dy_ref, tile = refs[:2]
        tile[...] = jnp.zeros(tile.shape, f32)
    else:
        dsum_ref, before_ref, dy_ref, pay_ref, tile = refs[:5]
        tile[...] = before_ref[...]
        put(tile, 4, column_sum(dsum_ref[...]))
    dy_ref[...] = dy
    dy_ref.send()
    put(tile, g, column_sum(dy * normed))
    put(tile, 2 + g, column_sum(dy))
    if g:
        pay_ref[...] = jnp.broadcast_to(tile[...][None], pay_ref.shape)


def final_kernel(core, g7_ref, par_ref, stat_ref, first_ref, second_ref, z_ref, own_ref, th_ref, tl_ref,
                 keep_ref, send_ref, dzh_ref, dzl_ref, mark_ref, gain_ref, flat_ref, bias_ref, gains_ref, term):
    width = z_ref.shape[1]
    gains_ref[...] = jnp.sum(g7_ref[...], axis=0)
    mark_ref[...] = gains_ref[...]
    gain_ref[...] = gains_ref[0:2, :]
    flat_ref[...] = gains_ref[2:4, :]
    bias_ref[0:2, :] = gains_ref[4:6, :]
    bias_ref[2:4, :] = -gains_ref[4:6, :]
    cross, flat = get(gains_ref, 0, 2), get(gains_ref, 2, 2)
    count = wide(stat_ref[4:5, :], width)
    mean, inv = get(stat_ref, 0, 2), get(stat_ref, 2, 2)
    normed = (z_ref[...] - mean) * inv
    scale = get(par_ref, 0, 2) * inv
    dy = jnp.concatenate([first_ref[...], second_ref[...]], axis=1)
    dz = scale * (dy - flat / count - normed * (cross / count)) * wide(own_ref[...], width)
    high, low = split(dz)
    dzh_ref[...] = high
    dzl_ref[...] = low
    term[...] = product((th_ref[...], tl_ref[...]), (high, low), NN)
    core.scatter([term], [keep_ref, send_ref])


def images_kernel(dzh_ref, dzl_ref, wh_ref, wl_ref, grad_ref, out_ref):
    for i in range(len(grad_ref.parts)):
        left = [ref.chunk(i) for ref in (dzh_ref, dzl_ref)]
        out_ref.put(i, product(left, (wh_ref[...], wl_ref[...]), NT) + grad_ref.chunk(i))


def deal_kernel(plan, count, *refs):
    outs = list(refs[count:])
    for digit, stretches in plan:
        own = digit.own()
        for j in range(digit.size):
            out, at = outs.pop(0), 0
            for inputs, first, rows in stretches:
                each = rows // digit.size
                here = pl.ds(pl.multiple_of(first + (own ^ j) * each, 8), each)
                total = refs[inputs[0]][here, :]
                for k in inputs[1:]:
                    total = total + refs[k][here, :]
                out[at : at + each, :] = total
                at += each


def deal(plan, ins, **order):
    width = ins[0].shape[1]
    outs = []
    for digit, stretches in plan:
        rows = sum(rows for _, _, rows in stretches) // digit.size
        outs += [((rows, width), f32)] * digit.size
    return local_call(functools.partial(deal_kernel, plan, len(ins)), outs, ins, **order)


def stack_kernel(stretches, *refs):
    refs, out = refs[:-1], refs[-1]
    at = 0
    for inputs, first, rows in stretches:
        each = rows // out.shape[0]
        for d in range(out.shape[0]):
            here = slice(first + d * each, first + (d + 1) * each)
            total = refs[inputs[0]][here, :]
            for k in inputs[1:]:
                total = total + refs[k][here, :]
            out[d, at : at + each, :] = total
        at += each


def extra_pieces(extra, stacked):
    if extra.size == 1:
        return [stacked]
    total = local_call(lambda ref, out: out.__setitem__(Ellipsis, jnp.sum(ref[...], axis=0)), [(stacked.shape[1:], f32)], [stacked])[0]
    return extra.send([total] * extra.size)


def stacked_kernel(count, *refs):
    if count == 1:
        refs[-1][...] = jnp.sum(refs[0][...], axis=0)
    else:
        sum_kernel(*refs)


def halves_kernel(digit, *refs):
    pieces, outs = refs[: digit.size], refs[digit.size :]
    half = pieces[0].shape[0] // 2
    own = digit.own()
    for j, piece in enumerate(pieces):
        at = pl.ds(pl.multiple_of((own ^ j) * half, 8), half)
        for i, out in enumerate(outs):
            out[at, :] = piece[i * half : (i + 1) * half, :]


def pair_kernel(digits, *refs):
    outs = refs[4:]
    for i, digit in enumerate(digits):
        digit.gather(refs[2 * i : 2 * i + 2], outs[i] if len(outs) == 2 else outs[0].at[pl.ds(i * 2 * refs[0].shape[0], 2 * refs[0].shape[0])])


def last_kernel(core, expand_map, group_map, mine_ref, other_ref, expand_ref, group_ref, excite_ref, squeeze_ref, whole):
    core.gather([mine_ref, other_ref], whole)
    taps, mid = group_ref.shape[0], whole.shape[1]
    inter = squeeze_ref.shape[1]
    tall = expand_ref.shape[0]
    places = [
        (taps, lambda rows, value: group_ref.__setitem__((rows, slice(0, mid)), value)),
        (taps, lambda rows, value: group_ref.__setitem__((rows, slice(mid, 2 * mid)), value)),
        (inter, lambda rows, value: excite_ref.__setitem__((rows, slice(0, mid)), value)),
        (inter, lambda rows, value: squeeze_put(squeeze_ref, rows, value)),
    ]
    for at, first, rows in expand_map:
        j, m = first // tall, first % tall
        expand_ref[m : m + rows, j * mid : (j + 1) * mid] = whole[at : at + rows, :]
    for at, first, rows in group_map:
        base = 0
        for length, store in places:
            low, high = max(first, base), min(first + rows, base + length)
            if low < high:
                store(slice(low - base, high - base), whole[at + low - first : at + high - first, :])
            base += length
    excite_ref[:, mid:] = -excite_ref[:, :mid]


def squeeze_put(squeeze_ref, rows, value):
    half = squeeze_ref.shape[0] // 2
    width = squeeze_ref.shape[1]
    squeeze_ref[rows, :] = value[:, :width]
    squeeze_ref[slice(half + rows.start, half + rows.stop), :] = value[:, width:]


def on_device(
    images,
    w_reduce,
    gain_one,
    shift_one,
    w_group,
    gain_two,
    shift_two,
    w_squeeze,
    gain_fc,
    shift_fc,
    w_excite,
    excite_bias,
    w_expand,
    gain_three,
    shift_three,
    valid_rows,
    valid_cols,
    cotangent,
):
    count, tall, broad, chan = images.shape
    mid = w_reduce.shape[1]
    inter = w_squeeze.shape[1]
    duo = 2 * mid
    taps = 9 * mid // 2
    cells = count * tall * broad
    longer = count * (tall + 2) * broad
    edge = count * broad
    devices = lax.axis_size("rows") * lax.axis_size("batch")
    all_images = count * lax.axis_size("batch")
    x = images.reshape(cells, chan)
    cot = cotangent.reshape(cells, chan)
    pay8 = ((devices, 8, 128), f32)
    pay16 = ((devices, 16, 128), f32)
    tile8 = pltpu.VMEM((8, 128), f32)
    tile16 = pltpu.VMEM((16, 128), f32)
    twice = lambda *shape: [(shape, bf16)] * 2
    flat_w = w_group.reshape(taps, duo)
    vectors = (gain_one, shift_one, gain_two, shift_two, gain_fc, shift_fc, excite_bias, gain_three, shift_three)
    core, line, depth, extra = digits()

    z_one, ext, own, first, last, pay = call(
        reduce_kernel,
        [((cells, mid), f32), ((count, tall + 2, broad, 128), f32), ((cells, 128), f32), ((edge, mid), f32),
         ((edge, mid), f32), pay8],
        [valid_rows, valid_cols, w_reduce, x],
        [tile8],
        near_outs=(3, 4, 5),
    )
    g1 = share(pay)
    above, below = halos(first, last)
    *group_parts, weh, wel, wrh, wrl, par = call(
        parts_kernel,
        [*twice(taps, mid), *twice(taps, mid), *twice(mid, chan), *twice(chan, mid), ((40, 128), f32)],
        [flat_w, w_expand, w_reduce, *[v.reshape(1, -1) for v in vectors]],
        chunks={0: 4, 1: 2, 2: 2},
        out_chunks={0: 4, 1: 4, 2: 4, 3: 4, 4: 2, 5: 2, 6: 2, 7: 2},
        after=[z_one],
    )
    z_two, a_one, stat1, counts, pay = call(
        conv_kernel,
        [((cells, duo), f32), ((longer, mid), f32), ((8, 128), f32), ((devices, 128), f32), pay8],
        [g1, par, z_one, ext, above, below, own, *group_parts],
        [tile8, pltpu.VMEM((count, tall + 2, broad, mid), f32)],
        near=(0, 4, 5),
        near_outs=(4,),
    )
    g2 = share(pay)
    xth, xtl = call(turned_kernel, twice(chan, cells), [x], after=[stat1])
    a_two, stat2, pooled, pay = call(
        pool_kernel,
        [((cells, duo), f32), ((8, 128), f32), ((count, mid), f32), ((devices, count, inter), f32)],
        [g2, counts, par, valid_rows, valid_cols, z_two, own, w_squeeze],
        chunks={5: 2, 6: 2},
        out_chunks={0: 2},
        after=[xth],
        near=(0,),
        near_outs=(3,),
    )
    g3 = share(pay)
    slope_two, normed_two, lead_two, slopes = call(
        slope_kernel,
        [((cells, duo), f32), ((cells, duo), f32), ((cells, mid), f32), ((count, 2 * duo), f32)],
        [stat2, par, valid_rows, valid_cols, own, z_two],
        chunks={4: 2, 5: 2},
        out_chunks={0: 2, 1: 2, 2: 2},
    )
    mixed, z_three, weights, fc_normed, fc_pre, fc_act, fc_inv, pay = call(
        expand_kernel,
        [((cells, mid), f32), ((cells, chan), f32), ((count, duo), f32), ((all_images, inter), f32),
         ((all_images, inter), f32), ((count, inter), f32), ((1, inter), f32), pay16],
        [g3, par, w_excite, a_two, weh, wel, own],
        [tile16, pltpu.VMEM((all_images, inter), f32)],
        out_chunks={1: 2},
        after=[slopes],
        near=(0,),
        near_outs=(7,),
    )
    g4 = share(pay)
    slopes = line.send([slopes] * line.size)
    grad_pre, stat3, slopes, pay = call(
        output_kernel,
        [((cells, chan), f32), ((16, 128), f32), ((count, 2 * duo), f32), pay16],
        [g4, counts, par, own, z_three, x, cot, *slopes],
        [tile16],
        chunks={3: 2, 4: 2, 5: 2, 6: 2},
        out_chunks={0: 2},
        near=(0, *range(7, 7 + line.size)),
        near_outs=(2, 3),
    )
    g5 = share(pay)
    slopes = depth.send([slopes] * depth.size)
    tph, tpl = call(functools.partial(taps_kernel, count), twice(2, taps, cells), [a_one], out_chunks={0: 2, 1: 2}, after=[stat3])
    grad_mixed, dsum, grads_three, grad_gain_three, grad_shift_three, slopes, pay = call(
        functools.partial(mixed_kernel, depth),
        [((cells, mid), f32), ((count, mid), f32),
         ((16, 128), f32), ((8, 128), f32), ((8, 128), f32), ((depth.size * count, 2 * duo), f32), pay16],
        [g5, stat1, stat3, par, own, grad_pre, z_three, weh, wel, lead_two, weights, w_excite, slope_two, normed_two, *slopes],
        [tile16],
        after=[tph],
        near=(0, *range(14, 14 + depth.size)),
        near_outs=(5, 6),
    )
    g6 = share(pay)
    *expand_sum, excite_term = call(
        functools.partial(expand_grad_kernel, core),
        [*core.outs(mid * chan // mid, mid), ((inter, mid), f32)],
        [grads_three, stat1, stat3, par, mixed, fc_act, dsum, own, grad_pre, z_three],
        [pltpu.VMEM((chan, mid), f32)],
        chunks={7: 2, 8: 2, 9: 2},
    )
    if extra.size > 1:
        slopes = gather_more(extra, extra.send([slopes] * extra.size))
    slopes = core.send([slopes] * 2)
    packed = 2 * taps + 2 * inter
    up, down, *dz_parts, squeeze_term, grad_gain_two, grad_shift_two, grad_gain_fc, grad_shift_fc = call(
        functools.partial(back_kernel, core),
        [((edge, mid), f32), ((edge, mid), f32), *twice(count, tall + 2, broad, mid), *twice(count, tall + 2, broad, mid), ((inter, mid), f32),
         ((duo // 128, 128), f32), ((duo // 128, 128), f32), ((1, inter), f32), ((1, inter), f32)],
        [g6, fc_pre, fc_normed, fc_inv, par, w_squeeze, pooled, stat1, stat2, valid_rows, valid_cols, weights, *slopes, own,
         grad_mixed, slope_two, normed_two, *group_parts],
        [pltpu.VMEM((all_images, inter), f32), pltpu.VMEM((all_images, mid), f32), pltpu.VMEM((all_images, 2 * duo), f32)],
        after=[excite_term],
        near=(0, 12, 13),
        near_outs=(0, 1),
    )
    above, below = halos(up, down)
    group_sum = call(
        functools.partial(group_kernel, core),
        core.outs(packed, mid),
        [*dz_parts, squeeze_term, excite_term, tph, tpl],
        [pltpu.VMEM((packed, mid), f32)],
        chunks={6: 2, 7: 2},
        near_outs=(0, 1),
    )
    expand_sum = core.send(expand_sum)
    group_sum = core.send([group_sum[0], gate(group_sum[1], [above, below])])
    dy_first, tile = call(
        functools.partial(input_grad_kernel, 0),
        [((cells, mid // 2), f32), ((8, 128), f32)],
        [par, stat1, z_one, own, above, below, *dz_parts[:2], *group_parts[:2]],
        [pltpu.VMEM((count, tall, broad, mid // 2), f32)],
        near=(4, 5),
    )
    first_bit, second_bit = line.bits()
    some, more = expand_sum[0].shape[0] // 2, group_sum[0].shape[0] // 2
    both_of = lambda start, a, b: [((0, 1), start * a, a), ((2, 3), start * b, b)]
    first_half = lambda digit: (digit, both_of(0, some, more))
    second_half = lambda digit: (digit, both_of(1, some, more))
    keep_a, send_a, keep_b, send_b = deal(
        [first_half(first_bit), second_half(second_bit)], [*expand_sum, *group_sum], after=[tile]
    )
    come_a, come_b = first_bit.send([keep_a, send_a]), second_bit.send([keep_b, send_b])
    place = pltpu.VMEM((count, tall, broad, mid // 2), f32)
    dy_second, pay = call(
        functools.partial(input_grad_kernel, 1),
        [((cells, mid // 2), f32), pay8],
        [par, stat1, z_one, own, above, below, *dz_parts[2:], *group_parts[2:], dsum, tile],
        [tile8, place],
        beside=[keep_a],
        near=(4, 5),
        near_outs=(1,),
    )
    g7 = share(pay)
    some, more = some // 2, more // 2
    turn = lambda k: [((k, k + 1), 0, some), ((k, k + 1), some, more)]
    keep_a, send_a, keep_b, send_b = deal([(second_bit, turn(0)), (first_bit, turn(2))], [*come_a, *come_b], after=[dy_second])
    *reduce_sum, dzh, dzl, mark_one, grad_gain_one, grad_shift_one, grad_bias = call(
        functools.partial(final_kernel, core),
        [*core.outs(chan, mid), *twice(cells, mid), ((8, 128), f32), *[((mid // 128, 128), f32)] * 2, ((duo // 128, 128), f32)],
        [g7, par, stat1, dy_first, dy_second, z_one, own, xth, xtl],
        [tile8, pltpu.VMEM((chan, mid), f32)],
        beside=[keep_a],
        near=(0,),
        near_outs=(0, 1),
    )
    come_a, come_b = second_bit.send([keep_a, send_a]), first_bit.send([keep_b, send_b])
    some, more = some // 2, more // 2
    stretches = turn(0) + turn(2)
    (joined,) = local_call(
        functools.partial(stack_kernel, stretches),
        [((depth.size, (some + more) * 2 // depth.size, mid), f32)],
        [*come_a, *come_b],
        after=[mark_one],
    )
    joined = depth.trade(joined)
    reduce_sum = scatter_more(line, core.send(reduce_sum))
    (grad_images,) = call(
        images_kernel,
        [((cells, chan), f32)],
        [dzh, dzl, wrh, wrl, grad_pre],
        chunks={0: 2, 1: 2, 4: 2},
        out_chunks={0: 2},
        beside=[reduce_sum[0]],
    )
    reduce_sum = scatter_more(depth, line.send(reduce_sum), after=[grad_images])
    (joined,) = local_call(
        functools.partial(stacked_kernel, extra.size), [(joined.shape[1:], f32)], extra_pieces(extra, joined), beside=[reduce_sum[0]]
    )
    rows_in = depth.size * joined.shape[0]
    block_out, mark = call(
        result_kernel,
        [((cells, chan), f32), ((8, 128), f32)],
        [stat3, par, own, z_three, x],
        chunks={2: 4, 3: 4, 4: 4},
        out_chunks={0: 4},
        beside=[joined],
    )
    half_a, half_b = local_call(
        functools.partial(halves_kernel, depth),
        [((rows_in // 2, mid), f32)] * 2,
        depth.send([joined] * depth.size),
        after=[mark],
    )
    reduce_sum = finish_sum(depth.send(reduce_sum), extra, beside=[half_a])
    half_a, half_b = local_call(
        functools.partial(pair_kernel, [second_bit, first_bit]),
        [((rows_in, mid), f32)] * 2,
        [*second_bit.send([half_a] * 2), *first_bit.send([half_b] * 2)],
        beside=[reduce_sum],
    )
    reduce_sum = gather_more(depth, depth.send([reduce_sum] * depth.size), beside=[half_a])
    (joined,) = local_call(
        functools.partial(pair_kernel, [first_bit, second_bit]),
        [((4 * rows_in, mid), f32)],
        [*first_bit.send([half_a] * 2), *second_bit.send([half_b] * 2)],
        beside=[reduce_sum],
    )
    expand_map, group_map = [], []
    at = 0
    some, more = some // depth.size, more // depth.size
    for half in range(core.size):
        for part in range(2):
            for outer in range(2):
                for inner in range(2):
                    for deep in range(depth.size):
                        block = (((half * 2 + part) * 2 + outer) * 2 + inner) * depth.size + deep
                        expand_map.append((at, block * some, some))
                        group_map.append((at + some, block * more, more))
                        at += some + more
    grad_w_expand, grad_w_group, grad_w_excite, grad_w_squeeze = call(
        functools.partial(last_kernel, core, expand_map, group_map),
        [((mid, chan), f32), ((taps, duo), f32), ((inter, duo), f32), ((mid, inter), f32)],
        core.send([joined] * 2),
        [pltpu.VMEM((chan + packed, mid), f32)],
        near=(0, 1),
    )
    reduce_sum = gather_more(line, line.send([reduce_sum] * line.size), after=[grad_w_squeeze])
    (grad_w_reduce,) = call(
        functools.partial(gather_kernel, core), [((chan, mid), f32)], core.send([reduce_sum] * 2), near=(0, 1)
    )
    return (
        block_out.reshape(images.shape),
        grad_images.reshape(images.shape),
        grad_w_reduce,
        grad_gain_one.reshape(-1),
        grad_shift_one.reshape(-1),
        grad_w_group.reshape(w_group.shape),
        grad_gain_two.reshape(-1),
        grad_shift_two.reshape(-1),
        grad_w_squeeze,
        grad_gain_fc.reshape(-1),
        grad_shift_fc.reshape(-1),
        grad_w_excite,
        grad_bias.reshape(-1),
        grad_w_expand,
        grad_gain_three.reshape(-1),
        grad_shift_three.reshape(-1),
    )


def solution(mesh):
    maps = P("batch", "rows", None, None)
    return jax.shard_map(
        on_device,
        mesh=mesh,
        in_specs=(maps,) + (P(),) * 14 + (P("batch", None), P("batch", None), maps),
        out_specs=(maps, maps) + (P(),) * 14,
        check_vma=False,
    )
```
